32 devices in a mesh: row: 8 (over z, y), col: 4 (over x, core).
Axes of the slice: x: 2, y: 2, z: 4, core: 2. Of those that a mesh axis runs over, the one named last changes fastest.
Arguments:
- pair: bfloat16 [128, 128, 128], P('row', 'col'), may hold values from -6 to 6
- chain_lengths: int32 [8], replicated, may hold values from 1 to 16, 96 in all
- norm_in_gain: float32 [128], replicated, may hold values from 0.1 to 1.9
- norm_in_bias: float32 [128], replicated, may hold values from -3 to 3
- proj_in: bfloat16 [128, 256], replicated, may hold values from -0.5 to 0.5
- gate_in: bfloat16 [128, 256], replicated, may hold values from -0.5 to 0.5
- norm_out_gain: float32 [128], replicated, may hold values from 0.1 to 1.9
- norm_out_bias: float32 [128], replicated, may hold values from -3 to 3
- proj_out: bfloat16 [128, 128], replicated, may hold values from -0.5 to 0.5
- gate_out: bfloat16 [128, 128], replicated, may hold values from -0.5 to 0.5
Outputs:
- update: bfloat16 [128, 128, 128], P('row', 'col')
The draws below stay inside these ranges and needn't reach their ends.
Inputs may be any that keep to these rules, and one draw needn't show every extreme that they name: Chain c owns token slots c * 16 to (c + 1) * 16 - 1; its first chain_lengths[c] slots are real tokens and the rest padding; the lengths sum to 96 and one of them is 16.
All inputs are finite; a program needn't handle non-finite values.
Results may differ from the reference program's by a relative error of at most 0.0055.
Values may be sent and summed in bfloat16 or wider, within the bound.
No kernel may reach another device: no remote copies, remote signals or barrier semaphores. Data moves between devices by JAX's collectives and lax.ppermute only.
A program may use at most 64 MiB of HBM per device.

```python
import math
import jax
import jax.numpy as jnp
import numpy as np
from jax import lax

C = 128
H = 128
ROWS_DEV = 16
CHAINS = 8
TOKENS = 128
SLOTS = 16


def steps_of(own_key, shape, pieces, low, high):
    factor_of, own = 1.0, jax.random.fold_in(own_key, 6)
    for dim, parts in pieces:
        draws = jnp.exp(jax.random.uniform(jax.random.fold_in(own, dim), (parts,), jnp.float32, low / len(pieces), high / len(pieces)))
        factor_of = factor_of * jnp.repeat(draws, shape[dim] // parts).reshape([-1 if axis == dim else 1 for axis in range(len(shape))])
    return factor_of


def profile(count, total, bound, slope):
    weights = [(1 << 20) // math.isqrt(rank ** slope) + 1 for rank in range(2, count + 1)]
    spare, counts = total - bound - (count - 1), [1] * (count - 1)
    while spare > 0:
        candidates = [i for i in range(count - 1) if counts[i] < bound]
        pool, remaining = sum([weights[i] for i in candidates]), spare
        for i in candidates:
            addition = min(bound - counts[i], max(1, remaining * weights[i] // pool), spare)
            counts[i] = counts[i] + addition
            spare = spare - addition
    return np.array([bound] + counts)


def ragged(key, amount, total, limit, slope):
    if amount == 2:
        one = jax.random.randint(key, (), max(1, total - limit), min(limit, total - 1) + 1)
        return jnp.stack([one, total - one])
    sizes = jnp.asarray(profile(amount, total, limit, slope), jnp.int32)
    couples = (amount - 1) // 2
    source_of, taker = sizes[1:1 + 2 * couples:2], sizes[2:2 + 2 * couples:2]
    room = jnp.minimum(source_of - 1, limit - taker)
    moved = jax.random.randint(jax.random.fold_in(key, 1), (couples,), 0, 1 << 20) % (room + 1)
    sizes = sizes.at[1:1 + 2 * couples:2].set(source_of - moved).at[2:2 + 2 * couples:2].set(taker + moved)
    return sizes[jax.random.permutation(jax.random.fold_in(key, 2), amount)]


def centred(stream_key, dims, width, reach, cuts=(), kind=jnp.bfloat16):
    array = jax.random.normal(stream_key, dims, jnp.float32) * width
    if len(cuts) > 0:
        array = steps_of(stream_key, dims, cuts, -0.22, 0.18) * array
    return jnp.clip(array, min=-reach, max=reach).astype(kind)


def setup_inputs(seed: int = 0) -> dict:
    seeds = jax.random.split(jax.random.key(seed), 11)
    return {
        "pair": centred(seeds[0], (TOKENS, TOKENS, C), 1.0, 6.0, ((0, 8), (1, 4))),
        "chain_lengths": ragged(seeds[1], CHAINS, 3 * TOKENS // 4, SLOTS, 2).astype(jnp.int32),
        "norm_in_gain": jnp.clip(1.0 + 0.18 * jax.random.normal(seeds[2], (C,), jnp.float32), 0.1, 1.9),
        "norm_in_bias": centred(seeds[3], (C,), 0.5, 3.0, (), jnp.float32),
        "proj_in": centred(seeds[4], (C, 2 * H), C ** -0.5, 0.5),
        "gate_in": centred(seeds[5], (C, 2 * H), C ** -0.5, 0.5),
        "norm_out_gain": jnp.clip(1.0 + 0.18 * jax.random.normal(seeds[6], (H,), jnp.float32), 0.1, 1.9),
        "norm_out_bias": centred(seeds[7], (H,), 0.5, 3.0, (), jnp.float32),
        "proj_out": centred(seeds[8], (H, C), H ** -0.5, 0.5),
        "gate_out": centred(seeds[9], (C, C), C ** -0.5, 0.5),
    }


def layer_norm(values, gain, bias):
    mean = lax.optimization_barrier(jnp.mean(values, axis=-1, keepdims=True))
    centered = values - mean
    variance = lax.optimization_barrier(jnp.mean(centered * centered, axis=-1, keepdims=True))
    return centered * jax.lax.rsqrt(variance + 1e-05) * gain + bias

def token_valid(chain_lengths, tokens_idx):
    chain = tokens_idx // SLOTS
    position = tokens_idx % SLOTS
    chain_ids = jnp.arange(CHAINS, dtype=jnp.int32)
    length_of = lax.optimization_barrier(jnp.sum(jnp.where(chain[:, None] == chain_ids[None, :], chain_lengths[None, :], 0), axis=1))
    return (position < length_of).astype(jnp.float32)

def reference(pair, chain_lengths, norm_in_gain, norm_in_bias, proj_in, gate_in, norm_out_gain, norm_out_bias, proj_out, gate_out):
    count = pair.shape[0]
    valid = token_valid(chain_lengths, jnp.arange(count, dtype=jnp.int32))
    pair_mask = valid[:, None] * valid[None, :]
    normed = layer_norm(pair.astype(jnp.float32), norm_in_gain, norm_in_bias).astype(jnp.bfloat16)
    flat = normed.reshape(-1, C)
    values = jnp.dot(flat, proj_in, preferred_element_type=jnp.float32)
    gates = jnp.dot(flat, gate_in, preferred_element_type=jnp.float32)
    mixed = (jax.nn.sigmoid(gates) * values).reshape(count, count, 2 * H) * pair_mask[:, :, None]
    left = mixed[:, :, :H].astype(jnp.bfloat16)
    right = mixed[:, :, H:].astype(jnp.bfloat16)
    block = ROWS_DEV

    def rows_of(start):
        piece = jax.lax.dynamic_slice_in_dim(left, start, block, 0)
        return jnp.einsum('ikh,jkh->ijh', piece.astype(jnp.float32), right.astype(jnp.float32))
    starts = jnp.arange(count // block, dtype=jnp.int32) * block
    triangle = jax.lax.map(rows_of, starts).reshape(count, count, H)
    tri_normed = layer_norm(triangle, norm_out_gain, norm_out_bias).astype(jnp.bfloat16)
    projected = jnp.dot(tri_normed.reshape(-1, H), proj_out, preferred_element_type=jnp.float32)
    gate = jax.nn.sigmoid(jnp.dot(flat, gate_out, preferred_element_type=jnp.float32))
    return (gate * projected).astype(jnp.bfloat16).reshape(count, count, C)
```

```python
import functools
import jax
import jax.numpy as jnp
from jax import lax
from jax.experimental import pallas as pl
from jax.experimental.pallas import tpu as pltpu
from jax.sharding import PartitionSpec as P

LANES = 128
F32 = jnp.float32
BF16 = jnp.bfloat16


def broadcast(value, axis, source):
    kept = jnp.where(lax.axis_index(axis) == source, value, 0).astype(value.dtype)
    return lax.psum(kept, axis)


def layer_norm(values, gain, bias):
    mean = jnp.mean(values, axis=-1, keepdims=True)
    centered = values - mean
    variance = jnp.mean(centered * centered, axis=-1, keepdims=True)
    return centered * lax.rsqrt(variance + 1e-05) * gain + bias


def token_valid(chain_lengths, tokens_idx, slots):
    chain = tokens_idx // slots
    position = tokens_idx % slots
    chain_ids = jnp.arange(chain_lengths.shape[0], dtype=jnp.int32)
    length_of = jnp.sum(
        jnp.where(chain[:, None] == chain_ids[None, :], chain_lengths[None, :], 0), axis=1
    )
    return (position < length_of).astype(jnp.float32)


def gathered(
    pair,
    chain_lengths,
    norm_in_gain,
    norm_in_bias,
    proj_in,
    gate_in,
    norm_out_gain,
    norm_out_bias,
    proj_out,
    gate_out,
):
    row_count = pair.shape[0]
    col_count = pair.shape[1]
    channels = pair.shape[2]
    hidden = proj_out.shape[0]
    row_index = lax.axis_index("row")
    col_index = lax.axis_index("col")
    slots = row_count * lax.axis_size("row") // chain_lengths.shape[0]
    valid_rows = token_valid(
        chain_lengths, row_index * row_count + jnp.arange(row_count, dtype=jnp.int32), slots
    )
    valid_cols = token_valid(
        chain_lengths, col_index * col_count + jnp.arange(col_count, dtype=jnp.int32), slots
    )
    pair_mask = valid_rows[:, None] * valid_cols[None, :]
    normed = layer_norm(pair.astype(jnp.float32), norm_in_gain, norm_in_bias).astype(jnp.bfloat16)
    flat = normed.reshape(-1, channels)
    values = jnp.dot(flat, proj_in, preferred_element_type=jnp.float32)
    gates = jnp.dot(flat, gate_in, preferred_element_type=jnp.float32)
    mixed = (jax.nn.sigmoid(gates) * values).reshape(row_count, col_count, 2 * hidden) * pair_mask[
        :, :, None
    ]
    left_tile = mixed[:, :, :hidden].astype(jnp.bfloat16)
    right_tile = mixed[:, :, hidden:].astype(jnp.bfloat16)
    ratio = lax.axis_size("row") // lax.axis_size("col")
    right_full = lax.all_gather(right_tile, "col", axis=1, tiled=True)
    received = []
    for part in range(ratio):
        received.append(broadcast(right_full, "row", col_index * ratio + part))
    right_mine = jnp.concatenate(received, axis=0)
    triangle = jnp.einsum(
        "ikh,jkh->ijh",
        lax.all_gather(left_tile, "col", axis=1, tiled=True),
        right_mine,
        preferred_element_type=jnp.float32,
    )
    tri_normed = layer_norm(triangle, norm_out_gain, norm_out_bias).astype(jnp.bfloat16)
    projected = jnp.dot(
        tri_normed.reshape(-1, hidden), proj_out, preferred_element_type=jnp.float32
    )
    gate = jax.nn.sigmoid(jnp.dot(flat, gate_out, preferred_element_type=jnp.float32))
    return (gate * projected).astype(jnp.bfloat16).reshape(row_count, col_count, channels)


def iota2(shape):
    return (
        lax.broadcasted_iota(jnp.int32, shape, 0),
        lax.broadcasted_iota(jnp.int32, shape, 1),
    )


def one_hot(condition):
    return jnp.where(condition, 1.0, 0.0).astype(BF16)


def dot(a, b, a_dim=1, b_dim=0):
    return lax.dot_general(a, b, (((a_dim,), (b_dim,)), ((), ())), preferred_element_type=F32)


def mix_kernel(
    slots, chain_ref, pair_ref, gain_ref, bias_ref, proj_ref, gate_ref, sent_ref, normed_ref
):
    rows, cols, channels = pair_ref.shape
    hidden = proj_ref.shape[1] // 2
    cells = rows * cols
    groups = cells // LANES
    chunks = sent_ref.shape[0]
    own = hidden // chunks
    flat = pair_ref[...].reshape(cells, channels).astype(F32)
    normed = layer_norm(flat, gain_ref[...], bias_ref[...]).astype(BF16)
    normed_ref[...] = normed

    cell = lax.broadcasted_iota(jnp.int32, (1, cells), 1)

    def valid(token):
        length = jnp.zeros_like(token)
        for chain in range(chain_ref.shape[0]):
            length = jnp.where(token // slots == chain, chain_ref[chain], length)
        return token % slots < length

    row_ok = valid(lax.axis_index("row") * rows + cell // cols)
    col_ok = valid(lax.axis_index("col") * cols + cell % cols)
    mask = jnp.where(row_ok & col_ok, 1.0, 0.0)

    values = dot(proj_ref[...], normed, 0, 1)
    gates = dot(gate_ref[...], normed, 0, 1)
    mixed = (jax.nn.sigmoid(gates) * values * mask).astype(BF16)

    block = LANES // groups
    out, source = iota2((LANES, LANES))
    order = one_hot((out // groups == source % block) & (out % groups == source // block))
    for side in range(2):
        for part in range(hidden // block):
            first = side * hidden + part * block
            stack = jnp.concatenate(
                [
                    mixed[first : first + block, g * LANES : (g + 1) * LANES]
                    for g in range(groups)
                ],
                axis=0,
            )
            moved = dot(order, stack).astype(BF16)
            count = block // own
            sent_ref[
                part * count : (part + 1) * count, side * own * groups : (side + 1) * own * groups
            ] = moved.reshape(count, own * groups, LANES)


def triangle_kernel(grid_rows, grid_cols, rows, cols, got_ref, sent_ref):
    groups = rows * cols // LANES
    inner = LANES // cols
    own = got_ref.shape[1] // (2 * groups)
    side = own * groups
    got = got_ref[...].reshape(grid_rows, grid_cols, 2 * side, LANES)
    high = grid_rows * side
    ratio = grid_rows // grid_cols
    quarter = ratio * side

    def block(column, which):
        return got[:, column, which * side : (which + 1) * side].reshape(high, LANES)

    left = jnp.concatenate([block(c, 0) for c in range(grid_cols)], axis=1)
    right = jnp.concatenate([block(c, 1) for c in range(grid_cols)], axis=0)

    lane = lax.broadcasted_iota(jnp.int32, (1, grid_cols * LANES), 1)
    left_by = jnp.concatenate(
        [left * one_hot(lane % LANES // cols == i) for i in range(inner)], axis=0
    )
    source, out = iota2((LANES, inner * LANES))
    spread = one_hot((source // cols == out // LANES) & (source % cols == out % cols))
    wide = dot(right, spread).astype(BF16)
    right_by = jnp.concatenate(
        [
            jnp.concatenate(
                [
                    wide[
                        c * high + d * quarter : c * high + (d + 1) * quarter,
                        j * LANES : (j + 1) * LANES,
                    ]
                    for c in range(grid_cols)
                ],
                axis=1,
            )
            for d in range(grid_cols)
            for j in range(inner)
        ],
        axis=0,
    )
    product = dot(left_by, right_by, 1, 1)

    width = inner * quarter
    a, b = iota2((high, width))
    same = jnp.where(a // groups % own == b // groups % own, 1.0, 0.0)
    kept = jnp.concatenate(
        [
            jnp.concatenate(
                [
                    (product[i * high : (i + 1) * high, d * width : (d + 1) * width] * same).astype(
                        BF16
                    )
                    for i in range(inner)
                ],
                axis=1,
            )
            for d in range(grid_cols)
        ],
        axis=0,
    )
    source, out = iota2((inner * width, LANES))
    at = source % width
    token = at % quarter // side * rows + at % groups * inner + at // quarter
    order = one_hot((source // width == out // cols) & (token == out % cols))
    moved = dot(kept, order).astype(BF16).reshape(grid_cols, grid_rows, side, LANES)
    for c in range(grid_cols):
        for r in range(grid_rows):
            sent_ref[r * grid_cols + c] = moved[c, r]


def gate_kernel(normed_ref, gate_ref, out_ref):
    out_ref[...] = jax.nn.sigmoid(dot(normed_ref[...], gate_ref[...]))


def update_kernel(got_ref, open_ref, gain_ref, bias_ref, proj_ref, out_ref):
    rows, cols, channels = out_ref.shape
    hidden = proj_ref.shape[0]
    groups = rows * cols // LANES
    inner = LANES // cols
    block = LANES // groups
    got = got_ref[...].reshape(hidden * groups, LANES)
    out, source = iota2((LANES, LANES))
    order = one_hot((source // groups == out % block) & (source % groups == out // block))
    pieces = [
        dot(order, got[part * LANES : (part + 1) * LANES]) for part in range(hidden // block)
    ]
    a, b = iota2((hidden, hidden))
    gain = jnp.sum(jnp.where(a == b, gain_ref[...], 0.0), axis=1, keepdims=True)
    bias = jnp.sum(jnp.where(a == b, bias_ref[...], 0.0), axis=1, keepdims=True)
    for g in range(groups):
        values = jnp.concatenate([piece[g * block : (g + 1) * block] for piece in pieces], axis=0)
        mean = jnp.mean(values, axis=0, keepdims=True)
        centered = values - mean
        variance = jnp.mean(centered * centered, axis=0, keepdims=True)
        tri_normed = (centered * lax.rsqrt(variance + 1e-05) * gain + bias).astype(BF16)
        projected = dot(tri_normed, proj_ref[...], 0, 0)
        update = (open_ref[g * LANES : (g + 1) * LANES] * projected).astype(BF16)
        out_ref[g * inner : (g + 1) * inner] = update.reshape(inner, cols, channels)


VMEM = pl.BlockSpec(memory_space=pltpu.VMEM)
SMEM = pl.BlockSpec(memory_space=pltpu.SMEM)
PARAMS = pltpu.CompilerParams(vmem_limit_bytes=40 * 1024 * 1024)


def exchanged(
    pair,
    chain_lengths,
    norm_in_gain,
    norm_in_bias,
    proj_in,
    gate_in,
    norm_out_gain,
    norm_out_bias,
    proj_out,
    gate_out,
):
    rows, cols, channels = pair.shape
    hidden = proj_out.shape[0]
    grid_rows, grid_cols = lax.axis_size("row"), lax.axis_size("col")
    devices = grid_rows * grid_cols
    groups = rows * cols // LANES
    side = hidden // devices * groups
    slots = rows * grid_rows // chain_lengths.shape[0]
    sent, normed = pl.pallas_call(
        functools.partial(mix_kernel, slots),
        out_shape=(
            jax.ShapeDtypeStruct((devices, 2 * side, LANES), BF16),
            jax.ShapeDtypeStruct((rows * cols, channels), BF16),
        ),
        in_specs=[SMEM] + [VMEM] * 5,
        out_specs=(VMEM, VMEM),
        compiler_params=PARAMS,
        name="mix",
    )(
        chain_lengths,
        pair,
        norm_in_gain.reshape(1, channels),
        norm_in_bias.reshape(1, channels),
        proj_in,
        gate_in,
    )
    got = lax.all_to_all(sent, ("row", "col"), 0, 0, tiled=True)
    opened = pl.pallas_call(
        gate_kernel,
        out_shape=jax.ShapeDtypeStruct((rows * cols, channels), F32),
        in_specs=[VMEM] * 2,
        out_specs=VMEM,
        compiler_params=PARAMS,
        name="gate",
    )(normed, gate_out)
    sums = pl.pallas_call(
        functools.partial(triangle_kernel, grid_rows, grid_cols, rows, cols),
        out_shape=jax.ShapeDtypeStruct((devices, side, LANES), BF16),
        in_specs=[VMEM],
        out_specs=VMEM,
        compiler_params=PARAMS,
        name="triangle",
    )(got)
    mine = lax.all_to_all(sums, ("row", "col"), 0, 0, tiled=True)
    return pl.pallas_call(
        update_kernel,
        out_shape=jax.ShapeDtypeStruct((rows, cols, channels), BF16),
        in_specs=[VMEM] * 5,
        out_specs=VMEM,
        compiler_params=PARAMS,
        name="update",
    )(mine, opened, norm_out_gain.reshape(1, hidden), norm_out_bias.reshape(1, hidden), proj_out)


def solution(mesh):
    devices = mesh.shape["row"] * mesh.shape["col"]

    def shards(*arrays):
        rows, cols, _ = arrays[0].shape
        hidden = arrays[8].shape[0]
        fits = (
            hidden % devices == 0
            and LANES % cols == 0
            and rows * cols % LANES == 0
            and mesh.shape["row"] % mesh.shape["col"] == 0
            and mesh.shape["row"] // mesh.shape["col"] * rows == cols
            and hidden // devices * (rows * cols // LANES) % 16 == 0
        )
        return exchanged(*arrays) if fits else gathered(*arrays)

    return jax.shard_map(
        shards,
        mesh=mesh,
        in_specs=(P("row", "col", None), P(), P(), P(), P(), P(), P(), P(), P(), P()),
        out_specs=P("row", "col", None),
        check_vma=False,
    )
```

```python
import functools
import jax
import jax.numpy as jnp
from jax import lax
from jax.experimental import pallas as pl
from jax.experimental.pallas import tpu as pltpu
from jax.sharding import PartitionSpec as P

LANES = 128
F32 = jnp.float32
BF16 = jnp.bfloat16


def broadcast(value, axis, source):
    kept = jnp.where(lax.axis_index(axis) == source, value, 0).astype(value.dtype)
    return lax.psum(kept, axis)


def layer_norm(values, gain, bias):
    mean = jnp.mean(values, axis=-1, keepdims=True)
    centered = values - mean
    variance = jnp.mean(centered * centered, axis=-1, keepdims=True)
    return centered * lax.rsqrt(variance + 1e-05) * gain + bias


def token_valid(chain_lengths, tokens_idx, slots):
    chain = tokens_idx // slots
    position = tokens_idx % slots
    chain_ids = jnp.arange(chain_lengths.shape[0], dtype=jnp.int32)
    length_of = jnp.sum(
        jnp.where(chain[:, None] == chain_ids[None, :], chain_lengths[None, :], 0), axis=1
    )
    return (position < length_of).astype(jnp.float32)


def gathered(
    pair,
    chain_lengths,
    norm_in_gain,
    norm_in_bias,
    proj_in,
    gate_in,
    norm_out_gain,
    norm_out_bias,
    proj_out,
    gate_out,
):
    row_count = pair.shape[0]
    col_count = pair.shape[1]
    channels = pair.shape[2]
    hidden = proj_out.shape[0]
    row_index = lax.axis_index("row")
    col_index = lax.axis_index("col")
    slots = row_count * lax.axis_size("row") // chain_lengths.shape[0]
    valid_rows = token_valid(
        chain_lengths, row_index * row_count + jnp.arange(row_count, dtype=jnp.int32), slots
    )
    valid_cols = token_valid(
        chain_lengths, col_index * col_count + jnp.arange(col_count, dtype=jnp.int32), slots
    )
    pair_mask = valid_rows[:, None] * valid_cols[None, :]
    normed = layer_norm(pair.astype(jnp.float32), norm_in_gain, norm_in_bias).astype(jnp.bfloat16)
    flat = normed.reshape(-1, channels)
    values = jnp.dot(flat, proj_in, preferred_element_type=jnp.float32)
    gates = jnp.dot(flat, gate_in, preferred_element_type=jnp.float32)
    mixed = (jax.nn.sigmoid(gates) * values).reshape(row_count, col_count, 2 * hidden) * pair_mask[
        :, :, None
    ]
    left_tile = mixed[:, :, :hidden].astype(jnp.bfloat16)
    right_tile = mixed[:, :, hidden:].astype(jnp.bfloat16)
    ratio = lax.axis_size("row") // lax.axis_size("col")
    right_full = lax.all_gather(right_tile, "col", axis=1, tiled=True)
    received = []
    for part in range(ratio):
        received.append(broadcast(right_full, "row", col_index * ratio + part))
    right_mine = jnp.concatenate(received, axis=0)
    triangle = jnp.einsum(
        "ikh,jkh->ijh",
        lax.all_gather(left_tile, "col", axis=1, tiled=True),
        right_mine,
        preferred_element_type=jnp.float32,
    )
    tri_normed = layer_norm(triangle, norm_out_gain, norm_out_bias).astype(jnp.bfloat16)
    projected = jnp.dot(
        tri_normed.reshape(-1, hidden), proj_out, preferred_element_type=jnp.float32
    )
    gate = jax.nn.sigmoid(jnp.dot(flat, gate_out, preferred_element_type=jnp.float32))
    return (gate * projected).astype(jnp.bfloat16).reshape(row_count, col_count, channels)


def iota2(shape):
    return (
        lax.broadcasted_iota(jnp.int32, shape, 0),
        lax.broadcasted_iota(jnp.int32, shape, 1),
    )


def one_hot(condition):
    return jnp.where(condition, 1.0, 0.0).astype(BF16)


def dot(a, b, a_dim=1, b_dim=0):
    return lax.dot_general(a, b, (((a_dim,), (b_dim,)), ((), ())), preferred_element_type=F32)


def fetch(sources, targets, sems):
    copies = [
        pltpu.make_async_copy(source, target, sems.at[n])
        for n, (source, target) in enumerate(zip(sources, targets))
    ]
    for copy in copies:
        copy.start()
    return copies


def mix_kernel(
    slots,
    chain_hbm,
    pair_hbm,
    gain_hbm,
    bias_hbm,
    proj_hbm,
    gate_hbm,
    sent_ref,
    normed_ref,
    chain_ref,
    pair_ref,
    gain_ref,
    bias_ref,
    proj_ref,
    gate_ref,
    sems,
):
    copies = fetch(
        (pair_hbm, gain_hbm, bias_hbm, chain_hbm, proj_hbm, gate_hbm),
        (pair_ref, gain_ref, bias_ref, chain_ref, proj_ref, gate_ref),
        sems,
    )
    rows, cols, channels = pair_ref.shape
    hidden = proj_ref.shape[1] // 2
    cells = rows * cols
    groups = cells // LANES
    chunks = sent_ref.shape[0]
    own = hidden // chunks
    for copy in copies:
        copy.wait()
    flat = pair_ref[...].reshape(cells, channels).astype(F32)
    normed = layer_norm(flat, gain_ref[...], bias_ref[...]).astype(BF16)
    normed_ref[...] = normed

    cell = lax.broadcasted_iota(jnp.int32, (1, cells), 1)

    def valid(token):
        length = jnp.zeros_like(token)
        for chain in range(chain_ref.shape[0]):
            length = jnp.where(token // slots == chain, chain_ref[chain], length)
        return token % slots < length

    row_ok = valid(lax.axis_index(("high", "low")) * rows + cell // cols)
    col_ok = valid(lax.axis_index("col") * cols + cell % cols)
    mask = jnp.where(row_ok & col_ok, 1.0, 0.0)

    values = dot(proj_ref[...], normed, 0, 1)
    gates = dot(gate_ref[...], normed, 0, 1)
    mixed = (jax.nn.sigmoid(gates) * values * mask).astype(BF16)

    block = LANES // groups
    out, source = iota2((LANES, LANES))
    order = one_hot((out // groups == source % block) & (out % groups == source // block))
    for side in range(2):
        for part in range(hidden // block):
            first = side * hidden + part * block
            stack = jnp.concatenate(
                [
                    mixed[first : first + block, g * LANES : (g + 1) * LANES]
                    for g in range(groups)
                ],
                axis=0,
            )
            moved = dot(order, stack).astype(BF16)
            count = block // own
            sent_ref[
                part * count : (part + 1) * count, side * own * groups : (side + 1) * own * groups
            ] = moved.reshape(count, own * groups, LANES)


def triangle_kernel(split, grid_cols, rows, cols, got_ref, sent_ref):
    grid_rows = split[0] * split[1]
    groups = rows * cols // LANES
    inner = LANES // cols
    own = got_ref.shape[1] // (2 * groups)
    side = own * groups
    got = got_ref[...].reshape(grid_cols, split[1], split[0], 2 * side, LANES)
    high = grid_rows * side
    ratio = grid_rows // grid_cols
    quarter = ratio * side

    def block(column, which):
        part = got[column, :, :, which * side : (which + 1) * side]
        return jnp.concatenate(
            [part[y, z] for z in range(split[0]) for y in range(split[1])], axis=0
        )

    left = jnp.concatenate([block(c, 0) for c in range(grid_cols)], axis=1)
    right = jnp.concatenate([block(c, 1) for c in range(grid_cols)], axis=0)

    lane = lax.broadcasted_iota(jnp.int32, (1, grid_cols * LANES), 1)
    left_by = jnp.concatenate(
        [left * one_hot(lane % LANES // cols == i) for i in range(inner)], axis=0
    )
    source, out = iota2((LANES, inner * LANES))
    spread = one_hot((source // cols == out // LANES) & (source % cols == out % cols))
    wide = dot(right, spread).astype(BF16)
    right_by = jnp.concatenate(
        [
            jnp.concatenate(
                [
                    wide[
                        c * high + d * quarter : c * high + (d + 1) * quarter,
                        j * LANES : (j + 1) * LANES,
                    ]
                    for c in range(grid_cols)
                ],
                axis=1,
            )
            for d in range(grid_cols)
            for j in range(inner)
        ],
        axis=0,
    )
    product = dot(left_by, right_by, 1, 1)

    width = inner * quarter
    a, b = iota2((high, width))
    same = jnp.where(a // groups % own == b // groups % own, 1.0, 0.0)
    kept = jnp.concatenate(
        [
            jnp.concatenate(
                [
                    (product[i * high : (i + 1) * high, d * width : (d + 1) * width] * same).astype(
                        BF16
                    )
                    for i in range(inner)
                ],
                axis=1,
            )
            for d in range(grid_cols)
        ],
        axis=0,
    )
    source, out = iota2((inner * width, LANES))
    at = source % width
    token = at % quarter // side * rows + at % groups * inner + at // quarter
    order = one_hot((source // width == out // cols) & (token == out % cols))
    moved = dot(kept, order).astype(BF16).reshape(grid_cols, grid_rows, side, LANES)
    for c in range(grid_cols):
        for r in range(grid_rows):
            z, y = r // split[1], r % split[1]
            sent_ref[(c * split[1] + y) * split[0] + z] = moved[c, r]


def gate_kernel(
    normed_ref,
    gate_hbm,
    gain_hbm,
    bias_hbm,
    proj_hbm,
    open_ref,
    gain_out,
    bias_out,
    proj_out,
    gate_ref,
    gain_ref,
    bias_ref,
    sems,
):
    copies = fetch(
        (gate_hbm, gain_hbm, bias_hbm, proj_hbm), (gate_ref, gain_ref, bias_ref, proj_out), sems
    )
    for copy in copies:
        copy.wait()
    open_ref[...] = jax.nn.sigmoid(dot(normed_ref[...], gate_ref[...]))
    a, b = iota2(gain_out.shape)
    for source, target in ((gain_ref, gain_out), (bias_ref, bias_out)):
        column = jnp.sum(jnp.where(a == b, source[...], 0.0), axis=1, keepdims=True)
        target[...] = jnp.broadcast_to(column, target.shape)


def update_kernel(got_ref, open_ref, gain_ref, bias_ref, proj_ref, out_ref):
    rows, cols, channels = out_ref.shape
    hidden = proj_ref.shape[0]
    groups = rows * cols // LANES
    inner = LANES // cols
    block = LANES // groups
    got = got_ref[...].reshape(hidden * groups, LANES)
    out, source = iota2((LANES, LANES))
    order = one_hot((source // groups == out % block) & (source % groups == out // block))
    pieces = [
        dot(order, got[part * LANES : (part + 1) * LANES]) for part in range(hidden // block)
    ]
    gain, bias = gain_ref[...], bias_ref[...]
    for g in range(groups):
        values = jnp.concatenate([piece[g * block : (g + 1) * block] for piece in pieces], axis=0)
        mean = jnp.mean(values, axis=0, keepdims=True)
        centered = values - mean
        variance = jnp.mean(centered * centered, axis=0, keepdims=True)
        tri_normed = (centered * lax.rsqrt(variance + 1e-05) * gain + bias).astype(BF16)
        projected = dot(tri_normed, proj_ref[...], 0, 0)
        update = (open_ref[g * LANES : (g + 1) * LANES] * projected).astype(BF16)
        out_ref[g * inner : (g + 1) * inner] = update.reshape(inner, cols, channels)


VMEM = pl.BlockSpec(memory_space=pltpu.VMEM)
ANY = pl.BlockSpec(memory_space=pl.ANY)
PARAMS = pltpu.CompilerParams(vmem_limit_bytes=40 * 1024 * 1024)


def exchanged(
    split,
    grid_cols,
    pair,
    chain_lengths,
    norm_in_gain,
    norm_in_bias,
    proj_in,
    gate_in,
    norm_out_gain,
    norm_out_bias,
    proj_out,
    gate_out,
):
    rows, cols, channels = pair.shape
    hidden = proj_out.shape[0]
    grid_rows = split[0] * split[1]
    devices = grid_rows * grid_cols
    groups = rows * cols // LANES
    side = hidden // devices * groups
    slots = rows * grid_rows // chain_lengths.shape[0]
    sent, normed = pl.pallas_call(
        functools.partial(mix_kernel, slots),
        out_shape=(
            jax.ShapeDtypeStruct((devices, 2 * side, LANES), BF16),
            jax.ShapeDtypeStruct((rows * cols, channels), BF16),
        ),
        in_specs=[ANY] * 6,
        out_specs=(VMEM, VMEM),
        scratch_shapes=[
            pltpu.SMEM(chain_lengths.shape, jnp.int32),
            pltpu.VMEM(pair.shape, BF16),
            pltpu.VMEM((1, channels), F32),
            pltpu.VMEM((1, channels), F32),
            pltpu.VMEM(proj_in.shape, BF16),
            pltpu.VMEM(gate_in.shape, BF16),
            pltpu.SemaphoreType.DMA((6,)),
        ],
        compiler_params=PARAMS,
        name="mix",
    )(
        chain_lengths,
        pair,
        norm_in_gain.reshape(1, channels),
        norm_in_bias.reshape(1, channels),
        proj_in,
        gate_in,
    )
    order = ("col", "low", "high")
    got = lax.all_to_all(sent, order, 0, 0, tiled=True)
    opened, gain, bias, proj = pl.pallas_call(
        gate_kernel,
        out_shape=(
            jax.ShapeDtypeStruct((rows * cols, channels), F32),
            jax.ShapeDtypeStruct((hidden, LANES), F32),
            jax.ShapeDtypeStruct((hidden, LANES), F32),
            jax.ShapeDtypeStruct(proj_out.shape, BF16),
        ),
        in_specs=[VMEM] + [ANY] * 4,
        out_specs=[VMEM] * 4,
        scratch_shapes=[
            pltpu.VMEM(gate_out.shape, BF16),
            pltpu.VMEM((1, hidden), F32),
            pltpu.VMEM((1, hidden), F32),
            pltpu.SemaphoreType.DMA((4,)),
        ],
        compiler_params=PARAMS,
        name="gate",
    )(normed, gate_out, norm_out_gain.reshape(1, hidden), norm_out_bias.reshape(1, hidden), proj_out)
    sums = pl.pallas_call(
        functools.partial(triangle_kernel, split, grid_cols, rows, cols),
        out_shape=jax.ShapeDtypeStruct((devices, side, LANES), BF16),
        in_specs=[VMEM],
        out_specs=VMEM,
        compiler_params=PARAMS,
        name="triangle",
    )(got)
    mine = lax.all_to_all(sums, order, 0, 0, tiled=True)
    return pl.pallas_call(
        update_kernel,
        out_shape=jax.ShapeDtypeStruct((rows, cols, channels), BF16),
        in_specs=[VMEM] * 5,
        out_specs=VMEM,
        compiler_params=PARAMS,
        name="update",
    )(mine, opened, gain, bias, proj)


def solution(mesh):
    grid_rows, grid_cols = mesh.shape["row"], mesh.shape["col"]
    split = (grid_rows // 2, 2)
    fine = jax.sharding.Mesh(
        mesh.devices.reshape(split + (grid_cols,)), ("high", "low", "col")
    )

    def fits(rows, cols, hidden):
        devices = grid_rows * grid_cols
        return (
            hidden % devices == 0
            and hidden == LANES
            and LANES % cols == 0
            and rows * cols % LANES == 0
            and grid_rows % grid_cols == 0
            and grid_rows // grid_cols * rows == cols
            and hidden // devices * (rows * cols // LANES) % 16 == 0
        )

    def call(*arrays):
        tokens, _, _ = arrays[0].shape
        hidden = arrays[8].shape[0]
        if fits(tokens // grid_rows, tokens // grid_cols, hidden):
            return jax.shard_map(
                functools.partial(exchanged, split, grid_cols),
                mesh=fine,
                in_specs=(P(("high", "low"), "col", None),) + (P(),) * 9,
                out_specs=P(("high", "low"), "col", None),
                check_vma=False,
            )(*arrays)
        return jax.shard_map(
            gathered,
            mesh=mesh,
            in_specs=(P("row", "col", None),) + (P(),) * 9,
            out_specs=P("row", "col", None),
            check_vma=False,
        )(*arrays)

    return call
```

```python
import functools
import jax
import jax.numpy as jnp
from jax import lax
from jax.experimental import pallas as pl
from jax.experimental.pallas import tpu as pltpu
from jax.sharding import PartitionSpec as P

LANES = 128
F32 = jnp.float32
BF16 = jnp.bfloat16


def broadcast(value, axis, source):
    kept = jnp.where(lax.axis_index(axis) == source, value, 0).astype(value.dtype)
    return lax.psum(kept, axis)


def layer_norm(values, gain, bias):
    mean = jnp.mean(values, axis=-1, keepdims=True)
    centered = values - mean
    variance = jnp.mean(centered * centered, axis=-1, keepdims=True)
    return centered * lax.rsqrt(variance + 1e-05) * gain + bias


def token_valid(chain_lengths, tokens_idx, slots):
    chain = tokens_idx // slots
    position = tokens_idx % slots
    chain_ids = jnp.arange(chain_lengths.shape[0], dtype=jnp.int32)
    length_of = jnp.sum(
        jnp.where(chain[:, None] == chain_ids[None, :], chain_lengths[None, :], 0), axis=1
    )
    return (position < length_of).astype(jnp.float32)


def gathered(
    pair,
    chain_lengths,
    norm_in_gain,
    norm_in_bias,
    proj_in,
    gate_in,
    norm_out_gain,
    norm_out_bias,
    proj_out,
    gate_out,
):
    row_count = pair.shape[0]
    col_count = pair.shape[1]
    channels = pair.shape[2]
    hidden = proj_out.shape[0]
    row_index = lax.axis_index("row")
    col_index = lax.axis_index("col")
    slots = row_count * lax.axis_size("row") // chain_lengths.shape[0]
    valid_rows = token_valid(
        chain_lengths, row_index * row_count + jnp.arange(row_count, dtype=jnp.int32), slots
    )
    valid_cols = token_valid(
        chain_lengths, col_index * col_count + jnp.arange(col_count, dtype=jnp.int32), slots
    )
    pair_mask = valid_rows[:, None] * valid_cols[None, :]
    normed = layer_norm(pair.astype(jnp.float32), norm_in_gain, norm_in_bias).astype(jnp.bfloat16)
    flat = normed.reshape(-1, channels)
    values = jnp.dot(flat, proj_in, preferred_element_type=jnp.float32)
    gates = jnp.dot(flat, gate_in, preferred_element_type=jnp.float32)
    mixed = (jax.nn.sigmoid(gates) * values).reshape(row_count, col_count, 2 * hidden) * pair_mask[
        :, :, None
    ]
    left_tile = mixed[:, :, :hidden].astype(jnp.bfloat16)
    right_tile = mixed[:, :, hidden:].astype(jnp.bfloat16)
    ratio = lax.axis_size("row") // lax.axis_size("col")
    right_full = lax.all_gather(right_tile, "col", axis=1, tiled=True)
    received = []
    for part in range(ratio):
        received.append(broadcast(right_full, "row", col_index * ratio + part))
    right_mine = jnp.concatenate(received, axis=0)
    triangle = jnp.einsum(
        "ikh,jkh->ijh",
        lax.all_gather(left_tile, "col", axis=1, tiled=True),
        right_mine,
        preferred_element_type=jnp.float32,
    )
    tri_normed = layer_norm(triangle, norm_out_gain, norm_out_bias).astype(jnp.bfloat16)
    projected = jnp.dot(
        tri_normed.reshape(-1, hidden), proj_out, preferred_element_type=jnp.float32
    )
    gate = jax.nn.sigmoid(jnp.dot(flat, gate_out, preferred_element_type=jnp.float32))
    return (gate * projected).astype(jnp.bfloat16).reshape(row_count, col_count, channels)


def iota2(shape):
    return (
        lax.broadcasted_iota(jnp.int32, shape, 0),
        lax.broadcasted_iota(jnp.int32, shape, 1),
    )


def one_hot(condition):
    return jnp.where(condition, 1.0, 0.0).astype(BF16)


def dot(a, b, a_dim=1, b_dim=0):
    return lax.dot_general(a, b, (((a_dim,), (b_dim,)), ((), ())), preferred_element_type=F32)


def fetch(sources, targets, sems):
    copies = [
        pltpu.make_async_copy(source, target, sems.at[n])
        for n, (source, target) in enumerate(zip(sources, targets))
    ]
    for copy in copies:
        copy.start()
    return copies


def mix_kernel(
    slots,
    chain_hbm,
    pair_hbm,
    gain_hbm,
    bias_hbm,
    proj_hbm,
    gate_hbm,
    sent_ref,
    normed_ref,
    chain_ref,
    pair_ref,
    gain_ref,
    bias_ref,
    proj_ref,
    gate_ref,
    sems,
):
    copies = fetch(
        (pair_hbm, gain_hbm, bias_hbm, chain_hbm, proj_hbm, gate_hbm),
        (pair_ref, gain_ref, bias_ref, chain_ref, proj_ref, gate_ref),
        sems,
    )
    rows, cols, channels = pair_ref.shape
    hidden = proj_ref.shape[1] // 2
    cells = rows * cols
    groups = cells // LANES
    chunks = sent_ref.shape[0]
    own = hidden // chunks
    for copy in copies:
        copy.wait()
    flat = pair_ref[...].reshape(cells, channels).astype(F32)
    normed = layer_norm(flat, gain_ref[...], bias_ref[...]).astype(BF16)
    normed_ref[...] = normed

    cell = lax.broadcasted_iota(jnp.int32, (1, cells), 1)

    def valid(token):
        length = jnp.zeros_like(token)
        for chain in range(chain_ref.shape[0]):
            length = jnp.where(token // slots == chain, chain_ref[chain], length)
        return token % slots < length

    row_ok = valid(lax.axis_index(("high", "low")) * rows + cell // cols)
    col_ok = valid(lax.axis_index("col") * cols + cell % cols)
    mask = jnp.where(row_ok & col_ok, 1.0, 0.0)

    values = dot(proj_ref[...], normed, 0, 1)
    gates = dot(gate_ref[...], normed, 0, 1)
    mixed = (jax.nn.sigmoid(gates) * values * mask).astype(BF16)

    block = LANES // groups
    out, source = iota2((LANES, LANES))
    order = one_hot((out // groups == source % block) & (out % groups == source // block))
    for side in range(2):
        for part in range(hidden // block):
            first = side * hidden + part * block
            stack = jnp.concatenate(
                [
                    mixed[first : first + block, g * LANES : (g + 1) * LANES]
                    for g in range(groups)
                ],
                axis=0,
            )
            moved = dot(order, stack).astype(BF16)
            count = block // own
            sent_ref[
                part * count : (part + 1) * count, side * own * groups : (side + 1) * own * groups
            ] = moved.reshape(count, own * groups, LANES)


def pick_kernel(grid_cols, got_ref, right_ref):
    side = got_ref.shape[1] // 2
    blocks = side // 16
    lows = got_ref.shape[0] // grid_cols
    for q in range(blocks):
        for y in range(lows):
            for c in range(grid_cols):
                right_ref[(q * lows + y) * 16 : (q * lows + y + 1) * 16, c * LANES : (c + 1) * LANES] = (
                    got_ref[y * grid_cols + c, side + q * 16 : side + (q + 1) * 16]
                )


def triangle_kernel(planes, grid_cols, rows, cols, got_ref, *refs):
    own_ref, below, above = refs[0], refs[1:planes], refs[planes : 2 * planes - 1]
    sent_ref, right_ref = refs[2 * planes - 1 :]
    height = own_ref.shape[0]
    place = lax.axis_index("high")
    for p in range(planes):
        for here in range(planes):
            source = own_ref if here == p else below[here - p - 1] if here > p else above[p - here - 1]

            @pl.when(place == here)
            def _(p=p, source=source):
                right_ref[p * height : (p + 1) * height] = source[...]

    groups = rows * cols // LANES
    inner = LANES // cols
    side = got_ref.shape[1] // 2
    blocks = side // 16
    some = 16 // groups
    lows = got_ref.shape[0] // grid_cols
    here = lows * 16
    high = planes * here
    lane = lax.broadcasted_iota(jnp.int32, (1, grid_cols * LANES), 1)
    own = [one_hot(lane % LANES // cols == i) for i in range(inner)]
    a, b = iota2((here, high))
    same = jnp.where(a // groups % some == b // groups % some, 1.0, 0.0)
    kept = []
    for q in range(blocks):
        left = jnp.concatenate(
            [
                jnp.concatenate(
                    [
                        got_ref[y * grid_cols + c, q * 16 : (q + 1) * 16]
                        for c in range(grid_cols)
                    ],
                    axis=1,
                )
                for y in range(lows)
            ],
            axis=0,
        )
        left_by = jnp.concatenate([left * mask for mask in own], axis=0)
        right = jnp.concatenate(
            [
                right_ref[(p * blocks + q) * here : (p * blocks + q + 1) * here]
                for p in range(planes)
            ],
            axis=0,
        ).astype(F32)
        turned = []
        for turn in range(inner):
            turned.append(
                jnp.concatenate(
                    [
                        pltpu.roll(right[:, c * LANES : (c + 1) * LANES], turn * cols, 1)
                        if turn
                        else right[:, c * LANES : (c + 1) * LANES]
                        for c in range(grid_cols)
                    ],
                    axis=1,
                ).astype(BF16)
            )
        product = dot(left_by, jnp.concatenate(turned, axis=0), 1, 1)
        for d in range(grid_cols):
            kept.append(
                jnp.concatenate(
                    [
                        (
                            product[
                                i * here : (i + 1) * here,
                                t * high + d * here : t * high + (d + 1) * here,
                            ]
                            * same[:, :here]
                        ).astype(BF16)
                        for i in range(inner)
                        for t in range(inner)
                    ],
                    axis=1,
                )
            )
    source, out = iota2((inner * inner * here, LANES))
    at = source % here
    i, turn = source // (inner * here), source // here % inner
    token = at // 16 * rows + at % groups * inner + (i + inner - turn) % inner
    order = one_hot((i == out // cols) & (token == out % cols))
    moved = dot(jnp.concatenate(kept, axis=0), order).astype(BF16)
    for q in range(blocks):
        for d in range(grid_cols):
            for y in range(lows):
                at = (q * grid_cols + d) * here + y * 16
                sent_ref[y * grid_cols + d, q * 16 : (q + 1) * 16] = moved[at : at + 16]


def gate_kernel(
    normed_ref,
    gate_hbm,
    gain_hbm,
    bias_hbm,
    proj_hbm,
    open_ref,
    gain_out,
    bias_out,
    proj_out,
    gate_ref,
    gain_ref,
    bias_ref,
    sems,
):
    copies = fetch(
        (gate_hbm, gain_hbm, bias_hbm, proj_hbm), (gate_ref, gain_ref, bias_ref, proj_out), sems
    )
    for copy in copies:
        copy.wait()
    open_ref[...] = jax.nn.sigmoid(dot(normed_ref[...], gate_ref[...]))
    a, b = iota2(gain_out.shape)
    for source, target in ((gain_ref, gain_out), (bias_ref, bias_out)):
        column = jnp.sum(jnp.where(a == b, source[...], 0.0), axis=1, keepdims=True)
        target[...] = jnp.broadcast_to(column, target.shape)


def update_kernel(got_ref, open_ref, gain_ref, bias_ref, proj_ref, out_ref):
    rows, cols, channels = out_ref.shape
    hidden = proj_ref.shape[0]
    groups = rows * cols // LANES
    inner = LANES // cols
    block = LANES // groups
    got = got_ref[...].reshape(hidden * groups, LANES)
    out, source = iota2((LANES, LANES))
    order = one_hot((source // groups == out % block) & (source % groups == out // block))
    pieces = [
        dot(order, got[part * LANES : (part + 1) * LANES]) for part in range(hidden // block)
    ]
    gain, bias = gain_ref[...], bias_ref[...]
    for g in range(groups):
        values = jnp.concatenate([piece[g * block : (g + 1) * block] for piece in pieces], axis=0)
        mean = jnp.mean(values, axis=0, keepdims=True)
        centered = values - mean
        variance = jnp.mean(centered * centered, axis=0, keepdims=True)
        tri_normed = (centered * lax.rsqrt(variance + 1e-05) * gain + bias).astype(BF16)
        projected = dot(tri_normed, proj_ref[...], 0, 0)
        update = (open_ref[g * LANES : (g + 1) * LANES] * projected).astype(BF16)
        out_ref[g * inner : (g + 1) * inner] = update.reshape(inner, cols, channels)


VMEM = pl.BlockSpec(memory_space=pltpu.VMEM)
HBM = pl.BlockSpec(memory_space=pltpu.HBM)
PARAMS = pltpu.CompilerParams(vmem_limit_bytes=32 * 1024 * 1024)
FETCHING = pltpu.CompilerParams(vmem_limit_bytes=60 * 1024 * 1024)


def exchanged(
    split,
    grid_cols,
    pair,
    chain_lengths,
    norm_in_gain,
    norm_in_bias,
    proj_in,
    gate_in,
    norm_out_gain,
    norm_out_bias,
    proj_out,
    gate_out,
):
    rows, cols, channels = pair.shape
    hidden = proj_out.shape[0]
    grid_rows = split[0] * split[1]
    planes, lows = split
    devices = lows * grid_cols
    groups = rows * cols // LANES
    side = hidden // devices * groups
    slots = rows * grid_rows // chain_lengths.shape[0]
    sent, normed = pl.pallas_call(
        functools.partial(mix_kernel, slots),
        out_shape=(
            jax.ShapeDtypeStruct((devices, 2 * side, LANES), BF16),
            jax.ShapeDtypeStruct((rows * cols, channels), BF16),
        ),
        in_specs=[HBM] * 6,
        out_specs=(VMEM, VMEM),
        scratch_shapes=[
            pltpu.SMEM(chain_lengths.shape, jnp.int32),
            pltpu.VMEM(pair.shape, BF16),
            pltpu.VMEM((1, channels), F32),
            pltpu.VMEM((1, channels), F32),
            pltpu.VMEM(proj_in.shape, BF16),
            pltpu.VMEM(gate_in.shape, BF16),
            pltpu.SemaphoreType.DMA((6,)),
        ],
        compiler_params=FETCHING,
        name="mix",
    )(
        chain_lengths,
        pair,
        norm_in_gain.reshape(1, channels),
        norm_in_bias.reshape(1, channels),
        proj_in,
        gate_in,
    )
    order = ("low", "col")
    got = lax.all_to_all(sent, order, 0, 0, tiled=True)
    right = pl.pallas_call(
        functools.partial(pick_kernel, grid_cols),
        out_shape=jax.ShapeDtypeStruct((side * lows, grid_cols * LANES), BF16),
        in_specs=[VMEM],
        out_specs=VMEM,
        compiler_params=PARAMS,
        name="pick",
    )(got)
    below, above = [right], [right]
    for step in range(1, planes):
        below.append(
            lax.ppermute(below[-1], "high", [(p, p + 1) for p in range(step - 1, planes - 1)])
        )
        above.append(
            lax.ppermute(above[-1], "high", [(p, p - 1) for p in range(1, planes - step + 1)])
        )
    opened, gain, bias, proj = pl.pallas_call(
        gate_kernel,
        out_shape=(
            jax.ShapeDtypeStruct((rows * cols, channels), F32),
            jax.ShapeDtypeStruct((hidden, LANES), F32),
            jax.ShapeDtypeStruct((hidden, LANES), F32),
            jax.ShapeDtypeStruct(proj_out.shape, BF16),
        ),
        in_specs=[VMEM] + [HBM] * 4,
        out_specs=[VMEM] * 4,
        scratch_shapes=[
            pltpu.VMEM(gate_out.shape, BF16),
            pltpu.VMEM((1, hidden), F32),
            pltpu.VMEM((1, hidden), F32),
            pltpu.SemaphoreType.DMA((4,)),
        ],
        compiler_params=FETCHING,
        name="gate",
    )(normed, gate_out, norm_out_gain.reshape(1, hidden), norm_out_bias.reshape(1, hidden), proj_out)
    sums = pl.pallas_call(
        functools.partial(triangle_kernel, planes, grid_cols, rows, cols),
        out_shape=jax.ShapeDtypeStruct((devices, side, LANES), BF16),
        in_specs=[VMEM] * (2 * planes),
        out_specs=VMEM,
        scratch_shapes=[pltpu.VMEM((planes * side * lows, grid_cols * LANES), BF16)],
        compiler_params=PARAMS,
        name="triangle",
    )(got, *below, *above[1:])
    mine = lax.all_to_all(sums, order, 0, 0, tiled=True)
    return pl.pallas_call(
        update_kernel,
        out_shape=jax.ShapeDtypeStruct((rows, cols, channels), BF16),
        in_specs=[VMEM] * 5,
        out_specs=VMEM,
        compiler_params=PARAMS,
        name="update",
    )(mine, opened, gain, bias, proj)


def solution(mesh):
    grid_rows, grid_cols = mesh.shape["row"], mesh.shape["col"]
    split = (grid_rows // 2, 2)
    fine = jax.sharding.Mesh(
        mesh.devices.reshape(split + (grid_cols,)), ("high", "low", "col")
    )

    def fits(rows, cols, hidden):
        devices = split[1] * grid_cols
        return (
            hidden % devices == 0
            and hidden == LANES
            and LANES % cols == 0
            and rows * cols % LANES == 0
            and split[0] == grid_cols
            and split[1] * rows == cols
            and 16 % (rows * cols // LANES) == 0
            and hidden // devices * (rows * cols // LANES) % 16 == 0
        )

    def call(*arrays):
        tokens, _, _ = arrays[0].shape
        hidden = arrays[8].shape[0]
        if fits(tokens // grid_rows, tokens // grid_cols, hidden):
            return jax.shard_map(
                functools.partial(exchanged, split, grid_cols),
                mesh=fine,
                in_specs=(P(("high", "low"), "col", None),) + (P(),) * 9,
                out_specs=P(("high", "low"), "col", None),
                check_vma=False,
            )(*arrays)
        return jax.shard_map(
            gathered,
            mesh=mesh,
            in_specs=(P("row", "col", None),) + (P(),) * 9,
            out_specs=P("row", "col", None),
            check_vma=False,
        )(*arrays)

    return call
```

```python
import functools
import jax
import jax.numpy as jnp
from jax import lax
from jax.experimental import pallas as pl
from jax.experimental.pallas import tpu as pltpu
from jax.sharding import PartitionSpec as P

LANES = 128
F32 = jnp.float32
BF16 = jnp.bfloat16


def broadcast(value, axis, source):
    kept = jnp.where(lax.axis_index(axis) == source, value, 0).astype(value.dtype)
    return lax.psum(kept, axis)


def layer_norm(values, gain, bias):
    mean = jnp.mean(values, axis=-1, keepdims=True)
    centered = values - mean
    variance = jnp.mean(centered * centered, axis=-1, keepdims=True)
    return centered * lax.rsqrt(variance + 1e-05) * gain + bias


def token_valid(chain_lengths, tokens_idx, slots):
    chain = tokens_idx // slots
    position = tokens_idx % slots
    chain_ids = jnp.arange(chain_lengths.shape[0], dtype=jnp.int32)
    length_of = jnp.sum(
        jnp.where(chain[:, None] == chain_ids[None, :], chain_lengths[None, :], 0), axis=1
    )
    return (position < length_of).astype(jnp.float32)


def gathered(
    pair,
    chain_lengths,
    norm_in_gain,
    norm_in_bias,
    proj_in,
    gate_in,
    norm_out_gain,
    norm_out_bias,
    proj_out,
    gate_out,
):
    row_count = pair.shape[0]
    col_count = pair.shape[1]
    channels = pair.shape[2]
    hidden = proj_out.shape[0]
    row_index = lax.axis_index("row")
    col_index = lax.axis_index("col")
    slots = row_count * lax.axis_size("row") // chain_lengths.shape[0]
    valid_rows = token_valid(
        chain_lengths, row_index * row_count + jnp.arange(row_count, dtype=jnp.int32), slots
    )
    valid_cols = token_valid(
        chain_lengths, col_index * col_count + jnp.arange(col_count, dtype=jnp.int32), slots
    )
    pair_mask = valid_rows[:, None] * valid_cols[None, :]
    normed = layer_norm(pair.astype(jnp.float32), norm_in_gain, norm_in_bias).astype(jnp.bfloat16)
    flat = normed.reshape(-1, channels)
    values = jnp.dot(flat, proj_in, preferred_element_type=jnp.float32)
    gates = jnp.dot(flat, gate_in, preferred_element_type=jnp.float32)
    mixed = (jax.nn.sigmoid(gates) * values).reshape(row_count, col_count, 2 * hidden) * pair_mask[
        :, :, None
    ]
    left_tile = mixed[:, :, :hidden].astype(jnp.bfloat16)
    right_tile = mixed[:, :, hidden:].astype(jnp.bfloat16)
    ratio = lax.axis_size("row") // lax.axis_size("col")
    right_full = lax.all_gather(right_tile, "col", axis=1, tiled=True)
    received = []
    for part in range(ratio):
        received.append(broadcast(right_full, "row", col_index * ratio + part))
    right_mine = jnp.concatenate(received, axis=0)
    triangle = jnp.einsum(
        "ikh,jkh->ijh",
        lax.all_gather(left_tile, "col", axis=1, tiled=True),
        right_mine,
        preferred_element_type=jnp.float32,
    )
    tri_normed = layer_norm(triangle, norm_out_gain, norm_out_bias).astype(jnp.bfloat16)
    projected = jnp.dot(
        tri_normed.reshape(-1, hidden), proj_out, preferred_element_type=jnp.float32
    )
    gate = jax.nn.sigmoid(jnp.dot(flat, gate_out, preferred_element_type=jnp.float32))
    return (gate * projected).astype(jnp.bfloat16).reshape(row_count, col_count, channels)


def iota2(shape):
    return (
        lax.broadcasted_iota(jnp.int32, shape, 0),
        lax.broadcasted_iota(jnp.int32, shape, 1),
    )


def one_hot(condition):
    return jnp.where(condition, 1.0, 0.0).astype(BF16)


def dot(a, b, a_dim=1, b_dim=0):
    return lax.dot_general(a, b, (((a_dim,), (b_dim,)), ((), ())), preferred_element_type=F32)


def fetch(sources, targets, sems):
    copies = [
        pltpu.make_async_copy(source, target, sems.at[n])
        for n, (source, target) in enumerate(zip(sources, targets))
    ]
    for copy in copies:
        copy.start()
    return copies


def mix_kernel(
    slots,
    chain_hbm,
    pair_hbm,
    gain_hbm,
    bias_hbm,
    proj_hbm,
    gate_hbm,
    sent_ref,
    normed_ref,
    chain_ref,
    pair_ref,
    gain_ref,
    bias_ref,
    proj_ref,
    gate_ref,
    sems,
):
    copies = fetch(
        (pair_hbm, gain_hbm, bias_hbm, chain_hbm, proj_hbm, gate_hbm),
        (pair_ref, gain_ref, bias_ref, chain_ref, proj_ref, gate_ref),
        sems,
    )
    rows, cols, channels = pair_ref.shape
    hidden = proj_ref.shape[1] // 2
    cells = rows * cols
    groups = cells // LANES
    chunks = sent_ref.shape[0]
    own = hidden // chunks
    for copy in copies:
        copy.wait()
    flat = pair_ref[...].reshape(cells, channels).astype(F32)
    normed = layer_norm(flat, gain_ref[...], bias_ref[...]).astype(BF16)
    normed_ref[...] = normed

    cell = lax.broadcasted_iota(jnp.int32, (1, cells), 1)

    def valid(token):
        length = jnp.zeros_like(token)
        for chain in range(chain_ref.shape[0]):
            length = jnp.where(token // slots == chain, chain_ref[chain], length)
        return token % slots < length

    row_ok = valid(lax.axis_index(("high", "low")) * rows + cell // cols)
    col_ok = valid(lax.axis_index("col") * cols + cell % cols)
    mask = jnp.where(row_ok & col_ok, 1.0, 0.0)

    values = dot(proj_ref[...], normed, 0, 1)
    gates = dot(gate_ref[...], normed, 0, 1)
    mixed = (jax.nn.sigmoid(gates) * values * mask).astype(BF16)

    block = LANES // groups
    out, source = iota2((LANES, LANES))
    order = one_hot((out // groups == source % block) & (out % groups == source // block))
    for side in range(2):
        for part in range(hidden // block):
            first = side * hidden + part * block
            stack = jnp.concatenate(
                [
                    mixed[first : first + block, g * LANES : (g + 1) * LANES]
                    for g in range(groups)
                ],
                axis=0,
            )
            moved = dot(order, stack).astype(BF16)
            count = block // own
            sent_ref[
                part * count : (part + 1) * count, side * own * groups : (side + 1) * own * groups
            ] = moved.reshape(count, own * groups, LANES)


def triangle_kernel(split, grid_cols, rows, cols, got_ref, sent_ref):
    grid_rows = split[0] * split[1]
    groups = rows * cols // LANES
    inner = LANES // cols
    own = got_ref.shape[1] // (2 * groups)
    side = own * groups
    got = got_ref[...].reshape(grid_cols, split[1], split[0], 2 * side, LANES)
    high = grid_rows * side
    ratio = grid_rows // grid_cols
    quarter = ratio * side

    def block(column, which):
        part = got[column, :, :, which * side : (which + 1) * side]
        return jnp.concatenate(
            [part[y, z] for z in range(split[0]) for y in range(split[1])], axis=0
        )

    left = jnp.concatenate([block(c, 0) for c in range(grid_cols)], axis=1)
    right = jnp.concatenate([block(c, 1) for c in range(grid_cols)], axis=0)

    lane = lax.broadcasted_iota(jnp.int32, (1, grid_cols * LANES), 1)
    left_by = jnp.concatenate(
        [left * one_hot(lane % LANES // cols == i) for i in range(inner)], axis=0
    )
    right = right.astype(F32)
    turned = [right.astype(BF16)] + [
        pltpu.roll(right, turn * cols, 1).astype(BF16) for turn in range(1, inner)
    ]
    right_by = jnp.concatenate(
        [
            jnp.concatenate(
                [
                    turned[turn][c * high + d * quarter : c * high + (d + 1) * quarter]
                    for c in range(grid_cols)
                ],
                axis=1,
            )
            for d in range(grid_cols)
            for turn in range(inner)
        ],
        axis=0,
    )
    product = dot(left_by, right_by, 1, 1)

    width = inner * quarter
    a, b = iota2((high, width))
    same = jnp.where(a // groups % own == b // groups % own, 1.0, 0.0)
    kept = jnp.concatenate(
        [
            jnp.concatenate(
                [
                    (product[i * high : (i + 1) * high, d * width : (d + 1) * width] * same).astype(
                        BF16
                    )
                    for i in range(inner)
                ],
                axis=1,
            )
            for d in range(grid_cols)
        ],
        axis=0,
    )
    source, out = iota2((inner * width, LANES))
    i, at = source // width, source % width
    j = (i + inner - at // quarter) % inner
    token = at % quarter // side * rows + at % groups * inner + j
    order = one_hot((i == out // cols) & (token == out % cols))
    moved = dot(kept, order).astype(BF16).reshape(grid_cols, grid_rows, side, LANES)
    for c in range(grid_cols):
        for r in range(grid_rows):
            z, y = r // split[1], r % split[1]
            sent_ref[(c * split[1] + y) * split[0] + z] = moved[c, r]


def gate_kernel(
    normed_ref,
    gate_hbm,
    gain_hbm,
    bias_hbm,
    proj_hbm,
    open_ref,
    gain_out,
    bias_out,
    proj_out,
    gate_ref,
    gain_ref,
    bias_ref,
    sems,
):
    copies = fetch(
        (gate_hbm, gain_hbm, bias_hbm, proj_hbm), (gate_ref, gain_ref, bias_ref, proj_out), sems
    )
    for copy in copies:
        copy.wait()
    open_ref[...] = jax.nn.sigmoid(dot(normed_ref[...], gate_ref[...]))
    a, b = iota2(gain_out.shape)
    for source, target in ((gain_ref, gain_out), (bias_ref, bias_out)):
        column = jnp.sum(jnp.where(a == b, source[...], 0.0), axis=1, keepdims=True)
        target[...] = jnp.broadcast_to(column, target.shape)


def update_kernel(got_ref, open_ref, gain_ref, bias_ref, proj_ref, out_ref):
    rows, cols, channels = out_ref.shape
    hidden = proj_ref.shape[0]
    groups = rows * cols // LANES
    inner = LANES // cols
    block = LANES // groups
    got = got_ref[...].reshape(hidden * groups, LANES)
    out, source = iota2((LANES, LANES))
    order = one_hot((source // groups == out % block) & (source % groups == out // block))
    pieces = [
        dot(order, got[part * LANES : (part + 1) * LANES]) for part in range(hidden // block)
    ]
    gain, bias = gain_ref[...], bias_ref[...]
    for g in range(groups):
        values = jnp.concatenate([piece[g * block : (g + 1) * block] for piece in pieces], axis=0)
        mean = jnp.mean(values, axis=0, keepdims=True)
        centered = values - mean
        variance = jnp.mean(centered * centered, axis=0, keepdims=True)
        tri_normed = (centered * lax.rsqrt(variance + 1e-05) * gain + bias).astype(BF16)
        projected = dot(tri_normed, proj_ref[...], 0, 0)
        update = (open_ref[g * LANES : (g + 1) * LANES] * projected).astype(BF16)
        out_ref[g * inner : (g + 1) * inner] = update.reshape(inner, cols, channels)


VMEM = pl.BlockSpec(memory_space=pltpu.VMEM)
HBM = pl.BlockSpec(memory_space=pltpu.HBM)
PARAMS = pltpu.CompilerParams(vmem_limit_bytes=32 * 1024 * 1024)
FETCHING = pltpu.CompilerParams(vmem_limit_bytes=60 * 1024 * 1024)


def exchanged(
    split,
    grid_cols,
    pair,
    chain_lengths,
    norm_in_gain,
    norm_in_bias,
    proj_in,
    gate_in,
    norm_out_gain,
    norm_out_bias,
    proj_out,
    gate_out,
):
    rows, cols, channels = pair.shape
    hidden = proj_out.shape[0]
    grid_rows = split[0] * split[1]
    devices = grid_rows * grid_cols
    groups = rows * cols // LANES
    side = hidden // devices * groups
    slots = rows * grid_rows // chain_lengths.shape[0]
    sent, normed = pl.pallas_call(
        functools.partial(mix_kernel, slots),
        out_shape=(
            jax.ShapeDtypeStruct((devices, 2 * side, LANES), BF16),
            jax.ShapeDtypeStruct((rows * cols, channels), BF16),
        ),
        in_specs=[HBM] * 6,
        out_specs=(VMEM, VMEM),
        scratch_shapes=[
            pltpu.SMEM(chain_lengths.shape, jnp.int32),
            pltpu.VMEM(pair.shape, BF16),
            pltpu.VMEM((1, channels), F32),
            pltpu.VMEM((1, channels), F32),
            pltpu.VMEM(proj_in.shape, BF16),
            pltpu.VMEM(gate_in.shape, BF16),
            pltpu.SemaphoreType.DMA((6,)),
        ],
        compiler_params=FETCHING,
        name="mix",
    )(
        chain_lengths,
        pair,
        norm_in_gain.reshape(1, channels),
        norm_in_bias.reshape(1, channels),
        proj_in,
        gate_in,
    )
    order = ("col", "low", "high")
    got = lax.all_to_all(sent, order, 0, 0, tiled=True)
    opened, gain, bias, proj = pl.pallas_call(
        gate_kernel,
        out_shape=(
            jax.ShapeDtypeStruct((rows * cols, channels), F32),
            jax.ShapeDtypeStruct((hidden, LANES), F32),
            jax.ShapeDtypeStruct((hidden, LANES), F32),
            jax.ShapeDtypeStruct(proj_out.shape, BF16),
        ),
        in_specs=[VMEM] + [HBM] * 4,
        out_specs=[VMEM] * 4,
        scratch_shapes=[
            pltpu.VMEM(gate_out.shape, BF16),
            pltpu.VMEM((1, hidden), F32),
            pltpu.VMEM((1, hidden), F32),
            pltpu.SemaphoreType.DMA((4,)),
        ],
        compiler_params=PARAMS,
        name="gate",
    )(normed, gate_out, norm_out_gain.reshape(1, hidden), norm_out_bias.reshape(1, hidden), proj_out)
    sums = pl.pallas_call(
        functools.partial(triangle_kernel, split, grid_cols, rows, cols),
        out_shape=jax.ShapeDtypeStruct((devices, side, LANES), BF16),
        in_specs=[VMEM],
        out_specs=VMEM,
        compiler_params=PARAMS,
        name="triangle",
    )(got)
    mine = lax.all_to_all(sums, order, 0, 0, tiled=True)
    return pl.pallas_call(
        update_kernel,
        out_shape=jax.ShapeDtypeStruct((rows, cols, channels), BF16),
        in_specs=[VMEM] * 5,
        out_specs=VMEM,
        compiler_params=PARAMS,
        name="update",
    )(mine, opened, gain, bias, proj)


def solution(mesh):
    grid_rows, grid_cols = mesh.shape["row"], mesh.shape["col"]
    split = (grid_rows // 2, 2)
    fine = jax.sharding.Mesh(
        mesh.devices.reshape(split + (grid_cols,)), ("high", "low", "col")
    )

    def fits(rows, cols, hidden):
        devices = grid_rows * grid_cols
        return (
            hidden % devices == 0
            and hidden == LANES
            and LANES % cols == 0
            and rows * cols % LANES == 0
            and grid_rows % grid_cols == 0
            and grid_rows // grid_cols * rows == cols
            and hidden // devices * (rows * cols // LANES) % 16 == 0
        )

    def call(*arrays):
        tokens, _, _ = arrays[0].shape
        hidden = arrays[8].shape[0]
        if fits(tokens // grid_rows, tokens // grid_cols, hidden):
            return jax.shard_map(
                functools.partial(exchanged, split, grid_cols),
                mesh=fine,
                in_specs=(P(("high", "low"), "col", None),) + (P(),) * 9,
                out_specs=P(("high", "low"), "col", None),
                check_vma=False,
            )(*arrays)
        return jax.shard_map(
            gathered,
            mesh=mesh,
            in_specs=(P("row", "col", None),) + (P(),) * 9,
            out_specs=P("row", "col", None),
            check_vma=False,
        )(*arrays)

    return call
```

```python
import functools
import jax
import jax.numpy as jnp
from jax import lax
from jax.experimental import pallas as pl
from jax.experimental.pallas import tpu as pltpu
from jax.sharding import PartitionSpec as P

LANES = 128
F32 = jnp.float32
BF16 = jnp.bfloat16


def broadcast(value, axis, source):
    kept = jnp.where(lax.axis_index(axis) == source, value, 0).astype(value.dtype)
    return lax.psum(kept, axis)


def layer_norm(values, gain, bias):
    mean = jnp.mean(values, axis=-1, keepdims=True)
    centered = values - mean
    variance = jnp.mean(centered * centered, axis=-1, keepdims=True)
    return centered * lax.rsqrt(variance + 1e-05) * gain + bias


def token_valid(chain_lengths, tokens_idx, slots):
    chain = tokens_idx // slots
    position = tokens_idx % slots
    chain_ids = jnp.arange(chain_lengths.shape[0], dtype=jnp.int32)
    length_of = jnp.sum(
        jnp.where(chain[:, None] == chain_ids[None, :], chain_lengths[None, :], 0), axis=1
    )
    return (position < length_of).astype(jnp.float32)


def gathered(
    pair,
    chain_lengths,
    norm_in_gain,
    norm_in_bias,
    proj_in,
    gate_in,
    norm_out_gain,
    norm_out_bias,
    proj_out,
    gate_out,
):
    row_count = pair.shape[0]
    col_count = pair.shape[1]
    channels = pair.shape[2]
    hidden = proj_out.shape[0]
    row_index = lax.axis_index("row")
    col_index = lax.axis_index("col")
    slots = row_count * lax.axis_size("row") // chain_lengths.shape[0]
    valid_rows = token_valid(
        chain_lengths, row_index * row_count + jnp.arange(row_count, dtype=jnp.int32), slots
    )
    valid_cols = token_valid(
        chain_lengths, col_index * col_count + jnp.arange(col_count, dtype=jnp.int32), slots
    )
    pair_mask = valid_rows[:, None] * valid_cols[None, :]
    normed = layer_norm(pair.astype(jnp.float32), norm_in_gain, norm_in_bias).astype(jnp.bfloat16)
    flat = normed.reshape(-1, channels)
    values = jnp.dot(flat, proj_in, preferred_element_type=jnp.float32)
    gates = jnp.dot(flat, gate_in, preferred_element_type=jnp.float32)
    mixed = (jax.nn.sigmoid(gates) * values).reshape(row_count, col_count, 2 * hidden) * pair_mask[
        :, :, None
    ]
    left_tile = mixed[:, :, :hidden].astype(jnp.bfloat16)
    right_tile = mixed[:, :, hidden:].astype(jnp.bfloat16)
    ratio = lax.axis_size("row") // lax.axis_size("col")
    right_full = lax.all_gather(right_tile, "col", axis=1, tiled=True)
    received = []
    for part in range(ratio):
        received.append(broadcast(right_full, "row", col_index * ratio + part))
    right_mine = jnp.concatenate(received, axis=0)
    triangle = jnp.einsum(
        "ikh,jkh->ijh",
        lax.all_gather(left_tile, "col", axis=1, tiled=True),
        right_mine,
        preferred_element_type=jnp.float32,
    )
    tri_normed = layer_norm(triangle, norm_out_gain, norm_out_bias).astype(jnp.bfloat16)
    projected = jnp.dot(
        tri_normed.reshape(-1, hidden), proj_out, preferred_element_type=jnp.float32
    )
    gate = jax.nn.sigmoid(jnp.dot(flat, gate_out, preferred_element_type=jnp.float32))
    return (gate * projected).astype(jnp.bfloat16).reshape(row_count, col_count, channels)


def iota2(shape):
    return (
        lax.broadcasted_iota(jnp.int32, shape, 0),
        lax.broadcasted_iota(jnp.int32, shape, 1),
    )


def one_hot(condition):
    return jnp.where(condition, 1.0, 0.0).astype(BF16)


def dot(a, b, a_dim=1, b_dim=0):
    return lax.dot_general(a, b, (((a_dim,), (b_dim,)), ((), ())), preferred_element_type=F32)


def fetch(sources, targets, sems):
    copies = [
        pltpu.make_async_copy(source, target, sems.at[n])
        for n, (source, target) in enumerate(zip(sources, targets))
    ]
    for copy in copies:
        copy.start()
    return copies


def exchange_blocks(arrays, cols):
    lane = lax.broadcasted_iota(jnp.int32, (1, LANES), 1) // cols
    arrays, step = list(arrays), 1
    while step < len(arrays):
        upper = lane // step % 2 == 1
        for n in range(len(arrays)):
            if n // step % 2 == 0:
                a, b = arrays[n], arrays[n + step]
                arrays[n] = jnp.where(upper, pltpu.roll(b, step * cols, 1), a)
                arrays[n + step] = jnp.where(upper, b, pltpu.roll(a, LANES - step * cols, 1))
        step *= 2
    return arrays


def mix_kernel(
    slots,
    chain_hbm,
    pair_hbm,
    gain_hbm,
    bias_hbm,
    proj_hbm,
    gate_hbm,
    sent_hbm,
    normed_hbm,
    chain_ref,
    pair_ref,
    gain_ref,
    bias_ref,
    proj_ref,
    gate_ref,
    sent_ref,
    normed_ref,
    sems,
    out_sems,
):
    copies = fetch(
        (pair_hbm, gain_hbm, bias_hbm, chain_hbm, proj_hbm, gate_hbm),
        (pair_ref, gain_ref, bias_ref, chain_ref, proj_ref, gate_ref),
        sems,
    )
    rows, cols, channels = pair_ref.shape
    hidden = proj_ref.shape[1] // 2
    cells = rows * cols
    inner = LANES // cols
    groups = rows // inner
    chunks = sent_ref.shape[0]
    some = LANES // rows
    out, source = iota2((LANES, LANES))
    order = one_hot((out // rows == source % some) & (out % rows == source // some))
    cell = lax.broadcasted_iota(jnp.int32, (1, cells), 1)
    for copy in copies:
        copy.wait()
    flat = pair_ref[...].reshape(cells, channels).astype(F32)
    normed = layer_norm(flat, gain_ref[...], bias_ref[...]).astype(BF16)
    normed_ref[...] = normed
    results = [pltpu.make_async_copy(normed_ref, normed_hbm, out_sems.at[0])]
    results[0].start()

    def valid(token):
        length = jnp.zeros_like(token)
        for chain in range(chain_ref.shape[0]):
            length = jnp.where(token // slots == chain, chain_ref[chain], length)
        return token % slots < length

    row_ok = valid(lax.axis_index(("high", "low")) * rows + cell // cols)
    col_ok = valid(lax.axis_index("col") * cols + cell % cols)
    mask = jnp.where(row_ok & col_ok, 1.0, 0.0)

    values = dot(proj_ref[...], normed, 0, 1)
    gates = dot(gate_ref[...], normed, 0, 1)
    mixed = jax.nn.sigmoid(gates) * values * mask

    by_row = []
    for side in range(2):
        lines = []
        for g in range(groups):
            lines += exchange_blocks(
                [
                    mixed[
                        side * hidden + n * chunks : side * hidden + (n + 1) * chunks,
                        g * LANES : (g + 1) * LANES,
                    ]
                    for n in range(inner)
                ],
                cols,
            )
        by_row.append(lines)
    for part in range(chunks // some):
        here = pl.ds(part * some, some)
        for side in range(2):
            stack = jnp.concatenate(
                [line[part * some : (part + 1) * some] for line in by_row[side]], axis=0
            ).astype(BF16)
            moved = dot(order, stack).astype(BF16)
            sent_ref[here, side * rows : (side + 1) * rows] = moved.reshape(some, rows, LANES)
        results.append(
            pltpu.make_async_copy(sent_ref.at[here], sent_hbm.at[here], out_sems.at[part + 1])
        )
        results[-1].start()
    for copy in results:
        copy.wait()


def triangle_kernel(split, grid_cols, rows, cols, got_ref, sent_ref):
    inner = LANES // cols

    def place(r, c):
        z, y = r // split[1], r % split[1]
        return (c * split[1] + y) * split[0] + z

    def side(which):
        return jnp.concatenate(
            [
                jnp.concatenate(
                    [
                        got_ref[place(r, c), which * rows : (which + 1) * rows]
                        for r in range(split[0] * split[1])
                    ],
                    axis=0,
                )
                for c in range(grid_cols)
            ],
            axis=1,
        )

    left, right = side(0), side(1)
    lane = lax.broadcasted_iota(jnp.int32, (1, grid_cols * LANES), 1)
    by_channel = [right * one_hot(lane % LANES // cols == n) for n in range(inner)]
    right_by = jnp.concatenate(
        [
            by_channel[n][c * cols : (c + 1) * cols]
            for c in range(grid_cols)
            for n in range(inner)
        ],
        axis=0,
    )
    sums = dot(left, right_by, 1, 1).astype(BF16)
    for c in range(grid_cols):
        for r in range(split[0] * split[1]):
            sent_ref[place(r, c)] = sums[r * rows : (r + 1) * rows, c * LANES : (c + 1) * LANES]


def gate_kernel(
    normed_ref,
    gate_hbm,
    gain_hbm,
    bias_hbm,
    proj_hbm,
    open_ref,
    gain_out,
    bias_out,
    proj_out,
    gate_ref,
    gain_ref,
    bias_ref,
    sems,
):
    copies = fetch(
        (gate_hbm, gain_hbm, bias_hbm, proj_hbm), (gate_ref, gain_ref, bias_ref, proj_out), sems
    )
    for copy in copies:
        copy.wait()
    open_ref[...] = jax.nn.sigmoid(dot(normed_ref[...], gate_ref[...]))
    a, b = iota2(gain_out.shape)
    for source, target in ((gain_ref, gain_out), (bias_ref, bias_out)):
        column = jnp.sum(jnp.where(a == b, source[...], 0.0), axis=1, keepdims=True)
        target[...] = jnp.broadcast_to(column, target.shape)


def update_kernel(
    got_ref, open_ref, gain_ref, bias_ref, proj_ref, out_hbm, out_ref, out_sems
):
    rows, cols, channels = out_ref.shape
    chunks = got_ref.shape[0]
    inner = LANES // cols
    groups = rows // inner
    some = LANES // rows
    out, source = iota2((LANES, LANES))
    order = one_hot((out // some == source % rows) & (out % some == source // rows))
    parts = [
        dot(order, got_ref[part * some : (part + 1) * some].reshape(LANES, LANES))
        for part in range(chunks // some)
    ]
    lines = [
        jnp.concatenate([part[row * some : (row + 1) * some] for part in parts], axis=0)
        for row in range(rows)
    ]
    gain, bias = gain_ref[...], bias_ref[...]
    results = []
    for g in range(groups):
        values = jnp.concatenate(
            exchange_blocks(lines[g * inner : (g + 1) * inner], cols), axis=0
        )
        mean = jnp.mean(values, axis=0, keepdims=True)
        centered = values - mean
        variance = jnp.mean(centered * centered, axis=0, keepdims=True)
        tri_normed = (centered * lax.rsqrt(variance + 1e-05) * gain + bias).astype(BF16)
        projected = dot(tri_normed, proj_ref[...], 0, 0)
        update = (open_ref[g * LANES : (g + 1) * LANES] * projected).astype(BF16)
        here = pl.ds(g * inner, inner)
        out_ref[here] = update.reshape(inner, cols, channels)
        results.append(pltpu.make_async_copy(out_ref.at[here], out_hbm.at[here], out_sems.at[g]))
        results[-1].start()
    for copy in results:
        copy.wait()


VMEM = pl.BlockSpec(memory_space=pltpu.VMEM)
HBM = pl.BlockSpec(memory_space=pltpu.HBM)
PARAMS = pltpu.CompilerParams(vmem_limit_bytes=32 * 1024 * 1024)
FETCHING = pltpu.CompilerParams(vmem_limit_bytes=60 * 1024 * 1024)


def exchanged(
    split,
    grid_cols,
    pair,
    chain_lengths,
    norm_in_gain,
    norm_in_bias,
    proj_in,
    gate_in,
    norm_out_gain,
    norm_out_bias,
    proj_out,
    gate_out,
):
    rows, cols, channels = pair.shape
    hidden = proj_out.shape[0]
    grid_rows = split[0] * split[1]
    devices = grid_rows * grid_cols
    slots = rows * grid_rows // chain_lengths.shape[0]
    sent, normed = pl.pallas_call(
        functools.partial(mix_kernel, slots),
        out_shape=(
            jax.ShapeDtypeStruct((devices, 2 * rows, LANES), BF16),
            jax.ShapeDtypeStruct((rows * cols, channels), BF16),
        ),
        in_specs=[HBM] * 6,
        out_specs=(HBM, HBM),
        scratch_shapes=[
            pltpu.SMEM(chain_lengths.shape, jnp.int32),
            pltpu.VMEM(pair.shape, BF16),
            pltpu.VMEM((1, channels), F32),
            pltpu.VMEM((1, channels), F32),
            pltpu.VMEM(proj_in.shape, BF16),
            pltpu.VMEM(gate_in.shape, BF16),
            pltpu.VMEM((devices, 2 * rows, LANES), BF16),
            pltpu.VMEM((rows * cols, channels), BF16),
            pltpu.SemaphoreType.DMA((6,)),
            pltpu.SemaphoreType.DMA((1 + devices * rows // LANES,)),
        ],
        compiler_params=FETCHING,
        name="mix",
    )(
        chain_lengths,
        pair,
        norm_in_gain.reshape(1, channels),
        norm_in_bias.reshape(1, channels),
        proj_in,
        gate_in,
    )
    order = ("col", "low", "high")
    got = lax.all_to_all(sent, order, 0, 0, tiled=True)
    opened, gain, bias, proj = pl.pallas_call(
        gate_kernel,
        out_shape=(
            jax.ShapeDtypeStruct((rows * cols, channels), F32),
            jax.ShapeDtypeStruct((hidden, LANES), F32),
            jax.ShapeDtypeStruct((hidden, LANES), F32),
            jax.ShapeDtypeStruct(proj_out.shape, BF16),
        ),
        in_specs=[VMEM] + [HBM] * 4,
        out_specs=[VMEM] * 4,
        scratch_shapes=[
            pltpu.VMEM(gate_out.shape, BF16),
            pltpu.VMEM((1, hidden), F32),
            pltpu.VMEM((1, hidden), F32),
            pltpu.SemaphoreType.DMA((4,)),
        ],
        compiler_params=PARAMS,
        name="gate",
    )(normed, gate_out, norm_out_gain.reshape(1, hidden), norm_out_bias.reshape(1, hidden), proj_out)
    sums = pl.pallas_call(
        functools.partial(triangle_kernel, split, grid_cols, rows, cols),
        out_shape=jax.ShapeDtypeStruct((devices, rows, LANES), BF16),
        in_specs=[VMEM],
        out_specs=VMEM,
        compiler_params=PARAMS,
        name="triangle",
    )(got)
    mine = lax.all_to_all(sums, order, 0, 0, tiled=True)
    return pl.pallas_call(
        update_kernel,
        out_shape=jax.ShapeDtypeStruct((rows, cols, channels), BF16),
        in_specs=[VMEM] * 5,
        out_specs=HBM,
        scratch_shapes=[
            pltpu.VMEM((rows, cols, channels), BF16),
            pltpu.SemaphoreType.DMA((rows * cols // LANES,)),
        ],
        compiler_params=PARAMS,
        name="update",
    )(mine, opened, gain, bias, proj)


def solution(mesh):
    grid_rows, grid_cols = mesh.shape["row"], mesh.shape["col"]
    split = (grid_rows // 2, 2)
    fine = jax.sharding.Mesh(
        mesh.devices.reshape(split + (grid_cols,)), ("high", "low", "col")
    )

    def fits(rows, cols, channels, hidden):
        devices = grid_rows * grid_cols
        inner = LANES // cols
        return (
            channels == LANES
            and hidden == LANES
            and inner * cols == LANES
            and inner & (inner - 1) == 0
            and inner * devices == hidden
            and rows % 16 == 0
            and rows % inner == 0
            and LANES % rows == 0
            and devices * rows % LANES == 0
            and LANES // rows % 8 == 0
        )

    def call(*arrays):
        tokens, others, channels = arrays[0].shape
        hidden = arrays[8].shape[0]
        if fits(tokens // grid_rows, others // grid_cols, channels, hidden):
            return jax.shard_map(
                functools.partial(exchanged, split, grid_cols),
                mesh=fine,
                in_specs=(P(("high", "low"), "col", None),) + (P(),) * 9,
                out_specs=P(("high", "low"), "col", None),
                check_vma=False,
            )(*arrays)
        return jax.shard_map(
            gathered,
            mesh=mesh,
            in_specs=(P("row", "col", None),) + (P(),) * 9,
            out_specs=P("row", "col", None),
            check_vma=False,
        )(*arrays)

    return call
```

```python
import functools
import jax
import jax.numpy as jnp
from jax import lax
from jax.experimental import pallas as pl
from jax.experimental.pallas import tpu as pltpu
from jax.sharding import PartitionSpec as P

LANES = 128
F32 = jnp.float32
BF16 = jnp.bfloat16


def broadcast(value, axis, source):
    kept = jnp.where(lax.axis_index(axis) == source, value, 0).astype(value.dtype)
    return lax.psum(kept, axis)


def layer_norm(values, gain, bias):
    mean = jnp.mean(values, axis=-1, keepdims=True)
    centered = values - mean
    variance = jnp.mean(centered * centered, axis=-1, keepdims=True)
    return centered * lax.rsqrt(variance + 1e-05) * gain + bias


def token_valid(chain_lengths, tokens_idx, slots):
    chain = tokens_idx // slots
    position = tokens_idx % slots
    chain_ids = jnp.arange(chain_lengths.shape[0], dtype=jnp.int32)
    length_of = jnp.sum(
        jnp.where(chain[:, None] == chain_ids[None, :], chain_lengths[None, :], 0), axis=1
    )
    return (position < length_of).astype(jnp.float32)


def gathered(
    pair,
    chain_lengths,
    norm_in_gain,
    norm_in_bias,
    proj_in,
    gate_in,
    norm_out_gain,
    norm_out_bias,
    proj_out,
    gate_out,
):
    row_count = pair.shape[0]
    col_count = pair.shape[1]
    channels = pair.shape[2]
    hidden = proj_out.shape[0]
    row_index = lax.axis_index("row")
    col_index = lax.axis_index("col")
    slots = row_count * lax.axis_size("row") // chain_lengths.shape[0]
    valid_rows = token_valid(
        chain_lengths, row_index * row_count + jnp.arange(row_count, dtype=jnp.int32), slots
    )
    valid_cols = token_valid(
        chain_lengths, col_index * col_count + jnp.arange(col_count, dtype=jnp.int32), slots
    )
    pair_mask = valid_rows[:, None] * valid_cols[None, :]
    normed = layer_norm(pair.astype(jnp.float32), norm_in_gain, norm_in_bias).astype(jnp.bfloat16)
    flat = normed.reshape(-1, channels)
    values = jnp.dot(flat, proj_in, preferred_element_type=jnp.float32)
    gates = jnp.dot(flat, gate_in, preferred_element_type=jnp.float32)
    mixed = (jax.nn.sigmoid(gates) * values).reshape(row_count, col_count, 2 * hidden) * pair_mask[
        :, :, None
    ]
    left_tile = mixed[:, :, :hidden].astype(jnp.bfloat16)
    right_tile = mixed[:, :, hidden:].astype(jnp.bfloat16)
    ratio = lax.axis_size("row") // lax.axis_size("col")
    right_full = lax.all_gather(right_tile, "col", axis=1, tiled=True)
    received = []
    for part in range(ratio):
        received.append(broadcast(right_full, "row", col_index * ratio + part))
    right_mine = jnp.concatenate(received, axis=0)
    triangle = jnp.einsum(
        "ikh,jkh->ijh",
        lax.all_gather(left_tile, "col", axis=1, tiled=True),
        right_mine,
        preferred_element_type=jnp.float32,
    )
    tri_normed = layer_norm(triangle, norm_out_gain, norm_out_bias).astype(jnp.bfloat16)
    projected = jnp.dot(
        tri_normed.reshape(-1, hidden), proj_out, preferred_element_type=jnp.float32
    )
    gate = jax.nn.sigmoid(jnp.dot(flat, gate_out, preferred_element_type=jnp.float32))
    return (gate * projected).astype(jnp.bfloat16).reshape(row_count, col_count, channels)


def iota2(shape):
    return (
        lax.broadcasted_iota(jnp.int32, shape, 0),
        lax.broadcasted_iota(jnp.int32, shape, 1),
    )


def one_hot(condition):
    return jnp.where(condition, 1.0, 0.0).astype(BF16)


def dot(a, b, a_dim=1, b_dim=0):
    return lax.dot_general(a, b, (((a_dim,), (b_dim,)), ((), ())), preferred_element_type=F32)


def fetch(sources, targets, sems):
    copies = [
        pltpu.make_async_copy(source, target, sems.at[n])
        for n, (source, target) in enumerate(zip(sources, targets))
    ]
    for copy in copies:
        copy.start()
    return copies


def exchange_blocks(arrays, cols):
    lane = lax.broadcasted_iota(jnp.int32, (1, LANES), 1) // cols
    arrays, step = list(arrays), 1
    while step < len(arrays):
        upper = lane // step % 2 == 1
        for n in range(len(arrays)):
            if n // step % 2 == 0:
                a, b = arrays[n], arrays[n + step]
                arrays[n] = jnp.where(upper, pltpu.roll(b, step * cols, 1), a)
                arrays[n + step] = jnp.where(upper, b, pltpu.roll(a, LANES - step * cols, 1))
        step *= 2
    return arrays


def mix_kernel(
    slots,
    chain_hbm,
    pair_hbm,
    gain_hbm,
    bias_hbm,
    proj_hbm,
    gate_hbm,
    sent_hbm,
    normed_hbm,
    chain_ref,
    pair_ref,
    gain_ref,
    bias_ref,
    proj_ref,
    gate_ref,
    sent_ref,
    normed_ref,
    sems,
    out_sems,
):
    copies = fetch(
        (pair_hbm, gain_hbm, bias_hbm, chain_hbm, proj_hbm, gate_hbm),
        (pair_ref, gain_ref, bias_ref, chain_ref, proj_ref, gate_ref),
        sems,
    )
    rows, cols, channels = pair_ref.shape
    hidden = proj_ref.shape[1] // 2
    cells = rows * cols
    inner = LANES // cols
    groups = rows // inner
    chunks = sent_ref.shape[0]
    some = LANES // rows
    out, source = iota2((LANES, LANES))
    order = one_hot((out // rows == source % some) & (out % rows == source // some))
    cell = lax.broadcasted_iota(jnp.int32, (1, cells), 1)
    for copy in copies:
        copy.wait()
    flat = pair_ref[...].reshape(cells, channels).astype(F32)
    normed = layer_norm(flat, gain_ref[...], bias_ref[...]).astype(BF16)
    normed_ref[...] = normed
    results = [pltpu.make_async_copy(normed_ref, normed_hbm, out_sems.at[0])]
    results[0].start()

    def valid(token):
        length = jnp.zeros_like(token)
        for chain in range(chain_ref.shape[0]):
            length = jnp.where(token // slots == chain, chain_ref[chain], length)
        return token % slots < length

    row_ok = valid(lax.axis_index(("high", "low")) * rows + cell // cols)
    col_ok = valid(lax.axis_index("col") * cols + cell % cols)
    mask = jnp.where(row_ok & col_ok, 1.0, 0.0)

    values = dot(proj_ref[...], normed, 0, 1)
    gates = dot(gate_ref[...], normed, 0, 1)
    mixed = jax.nn.sigmoid(gates) * values * mask

    by_row = []
    for side in range(2):
        lines = []
        for g in range(groups):
            lines += exchange_blocks(
                [
                    mixed[
                        side * hidden + n * chunks : side * hidden + (n + 1) * chunks,
                        g * LANES : (g + 1) * LANES,
                    ]
                    for n in range(inner)
                ],
                cols,
            )
        by_row.append(lines)
    for part in range(chunks // some):
        here = pl.ds(part * some, some)
        for side in range(2):
            stack = jnp.concatenate(
                [line[part * some : (part + 1) * some] for line in by_row[side]], axis=0
            ).astype(BF16)
            moved = dot(order, stack).astype(BF16)
            sent_ref[here, side * rows : (side + 1) * rows] = moved.reshape(some, rows, LANES)
        results.append(
            pltpu.make_async_copy(sent_ref.at[here], sent_hbm.at[here], out_sems.at[part + 1])
        )
        results[-1].start()
    for copy in results:
        copy.wait()


def triangle_kernel(split, grid_cols, rows, cols, got_ref, sent_ref):
    inner = LANES // cols

    def place(r, c):
        z, y = r // split[1], r % split[1]
        return (c * split[1] + y) * split[0] + z

    def side(which):
        return jnp.concatenate(
            [
                jnp.concatenate(
                    [
                        got_ref[place(r, c), which * rows : (which + 1) * rows]
                        for r in range(split[0] * split[1])
                    ],
                    axis=0,
                )
                for c in range(grid_cols)
            ],
            axis=1,
        )

    left, right = side(0), side(1)
    lane = lax.broadcasted_iota(jnp.int32, (1, grid_cols * LANES), 1)
    by_channel = [right * one_hot(lane % LANES // cols == n) for n in range(inner)]
    right_by = jnp.concatenate(
        [
            by_channel[n][c * cols : (c + 1) * cols]
            for c in range(grid_cols)
            for n in range(inner)
        ],
        axis=0,
    )
    sums = dot(left, right_by, 1, 1).astype(BF16)
    for c in range(grid_cols):
        for r in range(split[0] * split[1]):
            sent_ref[place(r, c)] = sums[r * rows : (r + 1) * rows, c * LANES : (c + 1) * LANES]


def gate_kernel(
    normed_ref,
    gate_hbm,
    gain_hbm,
    bias_hbm,
    proj_hbm,
    open_ref,
    gain_out,
    bias_out,
    proj_out,
    gate_ref,
    gain_ref,
    bias_ref,
    sems,
):
    copies = fetch(
        (gate_hbm, gain_hbm, bias_hbm, proj_hbm), (gate_ref, gain_ref, bias_ref, proj_out), sems
    )
    for copy in copies:
        copy.wait()
    open_ref[...] = jax.nn.sigmoid(dot(normed_ref[...], gate_ref[...]))
    a, b = iota2(gain_out.shape)
    for source, target in ((gain_ref, gain_out), (bias_ref, bias_out)):
        column = jnp.sum(jnp.where(a == b, source[...], 0.0), axis=1, keepdims=True)
        target[...] = jnp.broadcast_to(column, target.shape)


def update_kernel(
    got_ref, open_ref, gain_ref, bias_ref, proj_ref, out_hbm, out_ref, out_sems
):
    rows, cols, channels = out_ref.shape
    chunks = got_ref.shape[0]
    inner = LANES // cols
    groups = rows // inner
    some = LANES // rows
    out, source = iota2((LANES, LANES))
    order = one_hot((out // some == source % rows) & (out % some == source // rows))
    parts = [
        dot(order, got_ref[part * some : (part + 1) * some].reshape(LANES, LANES))
        for part in range(chunks // some)
    ]
    lines = [
        jnp.concatenate([part[row * some : (row + 1) * some] for part in parts], axis=0)
        for row in range(rows)
    ]
    gain, bias = gain_ref[...], bias_ref[...]
    results = []
    for g in range(groups):
        values = jnp.concatenate(
            exchange_blocks(lines[g * inner : (g + 1) * inner], cols), axis=0
        )
        mean = jnp.mean(values, axis=0, keepdims=True)
        centered = values - mean
        variance = jnp.mean(centered * centered, axis=0, keepdims=True)
        tri_normed = (centered * lax.rsqrt(variance + 1e-05) * gain + bias).astype(BF16)
        projected = dot(tri_normed, proj_ref[...], 0, 0)
        update = (open_ref[g * LANES : (g + 1) * LANES] * projected).astype(BF16)
        here = pl.ds(g * inner, inner)
        out_ref[here] = update.reshape(inner, cols, channels)
        results.append(pltpu.make_async_copy(out_ref.at[here], out_hbm.at[here], out_sems.at[g]))
        results[-1].start()
    for copy in results:
        copy.wait()


VMEM = pl.BlockSpec(memory_space=pltpu.VMEM)
HBM = pl.BlockSpec(memory_space=pltpu.HBM)
PARAMS = pltpu.CompilerParams(vmem_limit_bytes=32 * 1024 * 1024)
FETCHING = pltpu.CompilerParams(vmem_limit_bytes=60 * 1024 * 1024)


def exchanged(
    split,
    grid_cols,
    pair,
    chain_lengths,
    norm_in_gain,
    norm_in_bias,
    proj_in,
    gate_in,
    norm_out_gain,
    norm_out_bias,
    proj_out,
    gate_out,
):
    rows, cols, channels = pair.shape
    hidden = proj_out.shape[0]
    grid_rows = split[0] * split[1]
    devices = grid_rows * grid_cols
    slots = rows * grid_rows // chain_lengths.shape[0]
    sent, normed = pl.pallas_call(
        functools.partial(mix_kernel, slots),
        out_shape=(
            jax.ShapeDtypeStruct((devices, 2 * rows, LANES), BF16),
            jax.ShapeDtypeStruct((rows * cols, channels), BF16),
        ),
        in_specs=[HBM] * 6,
        out_specs=(HBM, HBM),
        scratch_shapes=[
            pltpu.SMEM(chain_lengths.shape, jnp.int32),
            pltpu.VMEM(pair.shape, BF16),
            pltpu.VMEM((1, channels), F32),
            pltpu.VMEM((1, channels), F32),
            pltpu.VMEM(proj_in.shape, BF16),
            pltpu.VMEM(gate_in.shape, BF16),
            pltpu.VMEM((devices, 2 * rows, LANES), BF16),
            pltpu.VMEM((rows * cols, channels), BF16),
            pltpu.SemaphoreType.DMA((6,)),
            pltpu.SemaphoreType.DMA((1 + devices * rows // LANES,)),
        ],
        compiler_params=FETCHING,
        name="mix",
    )(
        chain_lengths,
        pair,
        norm_in_gain.reshape(1, channels),
        norm_in_bias.reshape(1, channels),
        proj_in,
        gate_in,
    )
    order = ("col", "low", "high")
    got = lax.all_to_all(sent, order, 0, 0, tiled=True)
    opened, gain, bias, proj = pl.pallas_call(
        gate_kernel,
        out_shape=(
            jax.ShapeDtypeStruct((rows * cols, channels), F32),
            jax.ShapeDtypeStruct((hidden, LANES), F32),
            jax.ShapeDtypeStruct((hidden, LANES), F32),
            jax.ShapeDtypeStruct(proj_out.shape, BF16),
        ),
        in_specs=[VMEM] + [HBM] * 4,
        out_specs=[VMEM] * 4,
        scratch_shapes=[
            pltpu.VMEM(gate_out.shape, BF16),
            pltpu.VMEM((1, hidden), F32),
            pltpu.VMEM((1, hidden), F32),
            pltpu.SemaphoreType.DMA((4,)),
        ],
        compiler_params=PARAMS,
        name="gate",
    )(normed, gate_out, norm_out_gain.reshape(1, hidden), norm_out_bias.reshape(1, hidden), proj_out)
    got, opened, gain, bias, proj = lax.optimization_barrier((got, opened, gain, bias, proj))
    sums = pl.pallas_call(
        functools.partial(triangle_kernel, split, grid_cols, rows, cols),
        out_shape=jax.ShapeDtypeStruct((devices, rows, LANES), BF16),
        in_specs=[VMEM],
        out_specs=VMEM,
        compiler_params=PARAMS,
        name="triangle",
    )(got)
    mine = lax.all_to_all(sums, order, 0, 0, tiled=True)
    return pl.pallas_call(
        update_kernel,
        out_shape=jax.ShapeDtypeStruct((rows, cols, channels), BF16),
        in_specs=[VMEM] * 5,
        out_specs=HBM,
        scratch_shapes=[
            pltpu.VMEM((rows, cols, channels), BF16),
            pltpu.SemaphoreType.DMA((rows * cols // LANES,)),
        ],
        compiler_params=PARAMS,
        name="update",
    )(mine, opened, gain, bias, proj)


def solution(mesh):
    grid_rows, grid_cols = mesh.shape["row"], mesh.shape["col"]
    split = (grid_rows // 2, 2)
    fine = jax.sharding.Mesh(
        mesh.devices.reshape(split + (grid_cols,)), ("high", "low", "col")
    )

    def fits(rows, cols, channels, hidden):
        devices = grid_rows * grid_cols
        inner = LANES // cols
        return (
            channels == LANES
            and hidden == LANES
            and inner * cols == LANES
            and inner & (inner - 1) == 0
            and inner * devices == hidden
            and rows % 16 == 0
            and rows % inner == 0
            and LANES % rows == 0
            and devices * rows % LANES == 0
            and LANES // rows % 8 == 0
        )

    def call(*arrays):
        tokens, others, channels = arrays[0].shape
        hidden = arrays[8].shape[0]
        if fits(tokens // grid_rows, others // grid_cols, channels, hidden):
            return jax.shard_map(
                functools.partial(exchanged, split, grid_cols),
                mesh=fine,
                in_specs=(P(("high", "low"), "col", None),) + (P(),) * 9,
                out_specs=P(("high", "low"), "col", None),
                check_vma=False,
            )(*arrays)
        return jax.shard_map(
            gathered,
            mesh=mesh,
            in_specs=(P("row", "col", None),) + (P(),) * 9,
            out_specs=P("row", "col", None),
            check_vma=False,
        )(*arrays)

    return call
```

```python
import functools
import jax
import jax.numpy as jnp
from jax import lax
from jax.experimental import pallas as pl
from jax.experimental.pallas import tpu as pltpu
from jax.sharding import PartitionSpec as P

LANES = 128
F32 = jnp.float32
BF16 = jnp.bfloat16


def broadcast(value, axis, source):
    kept = jnp.where(lax.axis_index(axis) == source, value, 0).astype(value.dtype)
    return lax.psum(kept, axis)


def layer_norm(values, gain, bias):
    mean = jnp.mean(values, axis=-1, keepdims=True)
    centered = values - mean
    variance = jnp.mean(centered * centered, axis=-1, keepdims=True)
    return centered * lax.rsqrt(variance + 1e-05) * gain + bias


def token_valid(chain_lengths, tokens_idx, slots):
    chain = tokens_idx // slots
    position = tokens_idx % slots
    chain_ids = jnp.arange(chain_lengths.shape[0], dtype=jnp.int32)
    length_of = jnp.sum(
        jnp.where(chain[:, None] == chain_ids[None, :], chain_lengths[None, :], 0), axis=1
    )
    return (position < length_of).astype(jnp.float32)


def gathered(
    pair,
    chain_lengths,
    norm_in_gain,
    norm_in_bias,
    proj_in,
    gate_in,
    norm_out_gain,
    norm_out_bias,
    proj_out,
    gate_out,
):
    row_count = pair.shape[0]
    col_count = pair.shape[1]
    channels = pair.shape[2]
    hidden = proj_out.shape[0]
    row_index = lax.axis_index("row")
    col_index = lax.axis_index("col")
    slots = row_count * lax.axis_size("row") // chain_lengths.shape[0]
    valid_rows = token_valid(
        chain_lengths, row_index * row_count + jnp.arange(row_count, dtype=jnp.int32), slots
    )
    valid_cols = token_valid(
        chain_lengths, col_index * col_count + jnp.arange(col_count, dtype=jnp.int32), slots
    )
    pair_mask = valid_rows[:, None] * valid_cols[None, :]
    normed = layer_norm(pair.astype(jnp.float32), norm_in_gain, norm_in_bias).astype(jnp.bfloat16)
    flat = normed.reshape(-1, channels)
    values = jnp.dot(flat, proj_in, preferred_element_type=jnp.float32)
    gates = jnp.dot(flat, gate_in, preferred_element_type=jnp.float32)
    mixed = (jax.nn.sigmoid(gates) * values).reshape(row_count, col_count, 2 * hidden) * pair_mask[
        :, :, None
    ]
    left_tile = mixed[:, :, :hidden].astype(jnp.bfloat16)
    right_tile = mixed[:, :, hidden:].astype(jnp.bfloat16)
    ratio = lax.axis_size("row") // lax.axis_size("col")
    right_full = lax.all_gather(right_tile, "col", axis=1, tiled=True)
    received = []
    for part in range(ratio):
        received.append(broadcast(right_full, "row", col_index * ratio + part))
    right_mine = jnp.concatenate(received, axis=0)
    triangle = jnp.einsum(
        "ikh,jkh->ijh",
        lax.all_gather(left_tile, "col", axis=1, tiled=True),
        right_mine,
        preferred_element_type=jnp.float32,
    )
    tri_normed = layer_norm(triangle, norm_out_gain, norm_out_bias).astype(jnp.bfloat16)
    projected = jnp.dot(
        tri_normed.reshape(-1, hidden), proj_out, preferred_element_type=jnp.float32
    )
    gate = jax.nn.sigmoid(jnp.dot(flat, gate_out, preferred_element_type=jnp.float32))
    return (gate * projected).astype(jnp.bfloat16).reshape(row_count, col_count, channels)


def iota2(shape):
    return (
        lax.broadcasted_iota(jnp.int32, shape, 0),
        lax.broadcasted_iota(jnp.int32, shape, 1),
    )


def one_hot(condition):
    return jnp.where(condition, 1.0, 0.0).astype(BF16)


def dot(a, b, a_dim=1, b_dim=0):
    return lax.dot_general(a, b, (((a_dim,), (b_dim,)), ((), ())), preferred_element_type=F32)


def fetch(sources, targets, sems):
    copies = [
        pltpu.make_async_copy(source, target, sems.at[n])
        for n, (source, target) in enumerate(zip(sources, targets))
    ]
    for copy in copies:
        copy.start()
    return copies


def sigmoid(halved):
    return 0.5 + 0.5 * jnp.tanh(halved)


def column(row_ref):
    a, b = iota2((LANES, LANES))
    return jnp.sum(jnp.where(a == b, row_ref[...], 0.0), axis=1, keepdims=True)


def exchange_blocks(arrays, cols):
    lane = lax.broadcasted_iota(jnp.int32, (1, LANES), 1) // cols
    arrays, step = list(arrays), 1
    while step < len(arrays):
        upper = lane // step % 2 == 1
        for n in range(len(arrays)):
            if n // step % 2 == 0:
                a, b = arrays[n], arrays[n + step]
                arrays[n] = jnp.where(upper, pltpu.roll(b, step * cols, 1), a)
                arrays[n + step] = jnp.where(upper, b, pltpu.roll(a, LANES - step * cols, 1))
        step *= 2
    return arrays


def mix_kernel(
    slots,
    chain_hbm,
    pair_hbm,
    gain_hbm,
    bias_hbm,
    proj_hbm,
    gate_hbm,
    sent_hbm,
    normed_hbm,
    chain_ref,
    pair_ref,
    gain_ref,
    bias_ref,
    proj_ref,
    gate_ref,
    sent_ref,
    normed_ref,
    sems,
    out_sems,
):
    copies = fetch(
        (pair_hbm, gain_hbm, bias_hbm, chain_hbm, proj_hbm, gate_hbm),
        (pair_ref, gain_ref, bias_ref, chain_ref, proj_ref, gate_ref),
        sems,
    )
    rows, cols, channels = pair_ref.shape
    hidden = proj_ref.shape[1] // 2
    cells = rows * cols
    inner = LANES // cols
    groups = rows // inner
    chunks = sent_ref.shape[0]
    some = 16
    out, source = iota2((some * rows, some * rows))
    order = one_hot((out // rows == source % some) & (out % rows == source // some))
    a, b = iota2((channels, channels))
    eye = one_hot(a == b)
    cell = lax.broadcasted_iota(jnp.int32, (1, cells), 1)
    for copy in copies:
        copy.wait()
    flat = dot(eye, pair_ref[...].reshape(cells, channels), 1, 1)
    centered = flat - jnp.mean(flat, axis=0, keepdims=True)
    variance = jnp.mean(centered * centered, axis=0, keepdims=True)
    normed = centered * lax.rsqrt(variance + 1e-05) * column(gain_ref) + column(bias_ref)
    normed = normed.astype(BF16)
    normed_ref[...] = normed
    results = [pltpu.make_async_copy(normed_ref, normed_hbm, out_sems.at[0])]
    results[0].start()

    def valid(token):
        length = jnp.zeros_like(token)
        for chain in range(chain_ref.shape[0]):
            length = jnp.where(token // slots == chain, chain_ref[chain], length)
        return token % slots < length

    row_ok = valid(lax.axis_index(("high", "low")) * rows + cell // cols)
    col_ok = valid(lax.axis_index("col") * cols + cell % cols)
    mask = jnp.where(row_ok & col_ok, 1.0, 0.0)

    values = dot(proj_ref[...], normed, 0, 0)
    gates = dot(gate_ref[...] * 0.5, normed, 0, 0)
    mixed = (sigmoid(gates) * values * mask).astype(BF16)

    by_row = []
    for side in range(2):
        lines = []
        for g in range(groups):
            lines += exchange_blocks(
                [
                    mixed[
                        side * hidden + n * chunks : side * hidden + (n + 1) * chunks,
                        g * LANES : (g + 1) * LANES,
                    ]
                    for n in range(inner)
                ],
                cols,
            )
        by_row.append(lines)
    for part in range(chunks // some):
        here = pl.ds(part * some, some)
        for side in range(2):
            stack = jnp.concatenate(
                [line[part * some : (part + 1) * some] for line in by_row[side]], axis=0
            )
            moved = dot(order, stack).astype(BF16)
            sent_ref[here, side * rows : (side + 1) * rows] = moved.reshape(some, rows, LANES)
        results.append(
            pltpu.make_async_copy(sent_ref.at[here], sent_hbm.at[here], out_sems.at[part + 1])
        )
        results[-1].start()
    for copy in results:
        copy.wait()


def triangle_kernel(split, grid_cols, rows, cols, got_ref, sent_ref):
    inner = LANES // cols

    def place(r, c):
        z, y = r // split[1], r % split[1]
        return (c * split[1] + y) * split[0] + z

    def side(which):
        return jnp.concatenate(
            [
                jnp.concatenate(
                    [
                        got_ref[place(r, c), which * rows : (which + 1) * rows]
                        for r in range(split[0] * split[1])
                    ],
                    axis=0,
                )
                for c in range(grid_cols)
            ],
            axis=1,
        )

    left, right = side(0), side(1)
    lane = lax.broadcasted_iota(jnp.int32, (1, grid_cols * LANES), 1)
    by_channel = [right * one_hot(lane % LANES // cols == n) for n in range(inner)]
    right_by = jnp.concatenate(
        [
            by_channel[n][c * cols : (c + 1) * cols]
            for c in range(grid_cols)
            for n in range(inner)
        ],
        axis=0,
    )
    sums = dot(left, right_by, 1, 1).astype(BF16)
    for c in range(grid_cols):
        for r in range(split[0] * split[1]):
            sent_ref[place(r, c)] = sums[r * rows : (r + 1) * rows, c * LANES : (c + 1) * LANES]


def gate_kernel(
    normed_ref,
    gate_hbm,
    gain_hbm,
    bias_hbm,
    proj_hbm,
    open_ref,
    gain_out,
    bias_out,
    proj_out,
    gate_ref,
    gain_ref,
    bias_ref,
    sems,
):
    copies = fetch(
        (gate_hbm, gain_hbm, bias_hbm, proj_hbm), (gate_ref, gain_ref, bias_ref, proj_out), sems
    )
    for copy in copies:
        copy.wait()
    open_ref[...] = sigmoid(dot(normed_ref[...], gate_ref[...] * 0.5, 0, 0))
    gain_out[...] = jnp.broadcast_to(column(gain_ref), gain_out.shape)
    bias_out[...] = jnp.broadcast_to(column(bias_ref), bias_out.shape)


def update_kernel(
    got_ref, open_ref, gain_ref, bias_ref, proj_ref, out_hbm, out_ref, out_sems
):
    rows, cols, channels = out_ref.shape
    chunks = got_ref.shape[0]
    inner = LANES // cols
    groups = rows // inner
    some = 16
    out, source = iota2((some * rows, some * rows))
    order = one_hot((out // some == source % rows) & (out % some == source // rows))
    parts = [
        dot(order, got_ref[part * some : (part + 1) * some].reshape(some * rows, LANES)).astype(BF16)
        for part in range(chunks // some)
    ]
    lines = [
        jnp.concatenate([part[row * some : (row + 1) * some] for part in parts], axis=0)
        for row in range(rows)
    ]
    gain, bias = gain_ref[...], bias_ref[...]
    results = []
    for g in range(groups):
        values = jnp.concatenate(
            exchange_blocks(lines[g * inner : (g + 1) * inner], cols), axis=0
        ).astype(F32)
        mean = jnp.mean(values, axis=0, keepdims=True)
        centered = values - mean
        variance = jnp.mean(centered * centered, axis=0, keepdims=True)
        tri_normed = (centered * lax.rsqrt(variance + 1e-05) * gain + bias).astype(BF16)
        projected = dot(tri_normed, proj_ref[...], 0, 0)
        update = (open_ref[g * LANES : (g + 1) * LANES] * projected).astype(BF16)
        here = pl.ds(g * inner, inner)
        out_ref[here] = update.reshape(inner, cols, channels)
        results.append(pltpu.make_async_copy(out_ref.at[here], out_hbm.at[here], out_sems.at[g]))
        results[-1].start()
    for copy in results:
        copy.wait()


VMEM = pl.BlockSpec(memory_space=pltpu.VMEM)
HBM = pl.BlockSpec(memory_space=pltpu.HBM)
PARAMS = pltpu.CompilerParams(vmem_limit_bytes=32 * 1024 * 1024)
FETCHING = pltpu.CompilerParams(vmem_limit_bytes=60 * 1024 * 1024)


def exchanged(
    split,
    grid_cols,
    pair,
    chain_lengths,
    norm_in_gain,
    norm_in_bias,
    proj_in,
    gate_in,
    norm_out_gain,
    norm_out_bias,
    proj_out,
    gate_out,
):
    rows, cols, channels = pair.shape
    hidden = proj_out.shape[0]
    grid_rows = split[0] * split[1]
    devices = grid_rows * grid_cols
    slots = rows * grid_rows // chain_lengths.shape[0]
    sent, normed = pl.pallas_call(
        functools.partial(mix_kernel, slots),
        out_shape=(
            jax.ShapeDtypeStruct((devices, 2 * rows, LANES), BF16),
            jax.ShapeDtypeStruct((channels, rows * cols), BF16),
        ),
        in_specs=[HBM] * 6,
        out_specs=(HBM, HBM),
        scratch_shapes=[
            pltpu.SMEM(chain_lengths.shape, jnp.int32),
            pltpu.VMEM(pair.shape, BF16),
            pltpu.VMEM((1, channels), F32),
            pltpu.VMEM((1, channels), F32),
            pltpu.VMEM(proj_in.shape, BF16),
            pltpu.VMEM(gate_in.shape, BF16),
            pltpu.VMEM((devices, 2 * rows, LANES), BF16),
            pltpu.VMEM((channels, rows * cols), BF16),
            pltpu.SemaphoreType.DMA((6,)),
            pltpu.SemaphoreType.DMA((1 + devices // 16,)),
        ],
        compiler_params=FETCHING,
        name="mix",
    )(
        chain_lengths,
        pair,
        norm_in_gain.reshape(1, channels),
        norm_in_bias.reshape(1, channels),
        proj_in,
        gate_in,
    )
    order = ("col", "low", "high")
    got = lax.all_to_all(sent, order, 0, 0, tiled=True)
    opened, gain, bias, proj = pl.pallas_call(
        gate_kernel,
        out_shape=(
            jax.ShapeDtypeStruct((rows * cols, channels), F32),
            jax.ShapeDtypeStruct((hidden, LANES), F32),
            jax.ShapeDtypeStruct((hidden, LANES), F32),
            jax.ShapeDtypeStruct(proj_out.shape, BF16),
        ),
        in_specs=[VMEM] + [HBM] * 4,
        out_specs=[VMEM] * 4,
        scratch_shapes=[
            pltpu.VMEM(gate_out.shape, BF16),
            pltpu.VMEM((1, hidden), F32),
            pltpu.VMEM((1, hidden), F32),
            pltpu.SemaphoreType.DMA((4,)),
        ],
        compiler_params=PARAMS,
        name="gate",
    )(normed, gate_out, norm_out_gain.reshape(1, hidden), norm_out_bias.reshape(1, hidden), proj_out)
    got, opened, gain, bias, proj = lax.optimization_barrier((got, opened, gain, bias, proj))
    sums = pl.pallas_call(
        functools.partial(triangle_kernel, split, grid_cols, rows, cols),
        out_shape=jax.ShapeDtypeStruct((devices, rows, LANES), BF16),
        in_specs=[VMEM],
        out_specs=VMEM,
        compiler_params=PARAMS,
        name="triangle",
    )(got)
    mine = lax.all_to_all(sums, order, 0, 0, tiled=True)
    return pl.pallas_call(
        update_kernel,
        out_shape=jax.ShapeDtypeStruct((rows, cols, channels), BF16),
        in_specs=[VMEM] * 5,
        out_specs=HBM,
        scratch_shapes=[
            pltpu.VMEM((rows, cols, channels), BF16),
            pltpu.SemaphoreType.DMA((rows * cols // LANES,)),
        ],
        compiler_params=PARAMS,
        name="update",
    )(mine, opened, gain, bias, proj)


def solution(mesh):
    grid_rows, grid_cols = mesh.shape["row"], mesh.shape["col"]
    split = (grid_rows // 2, 2)
    fine = jax.sharding.Mesh(
        mesh.devices.reshape(split + (grid_cols,)), ("high", "low", "col")
    )

    def fits(rows, cols, channels, hidden):
        devices = grid_rows * grid_cols
        inner = LANES // cols
        return (
            channels == LANES
            and hidden == LANES
            and inner * cols == LANES
            and inner & (inner - 1) == 0
            and inner * devices == hidden
            and rows % 16 == 0
            and rows % inner == 0
            and devices % 16 == 0
        )

    def call(*arrays):
        tokens, others, channels = arrays[0].shape
        hidden = arrays[8].shape[0]
        if fits(tokens // grid_rows, others // grid_cols, channels, hidden):
            return jax.shard_map(
                functools.partial(exchanged, split, grid_cols),
                mesh=fine,
                in_specs=(P(("high", "low"), "col", None),) + (P(),) * 9,
                out_specs=P(("high", "low"), "col", None),
                check_vma=False,
            )(*arrays)
        return jax.shard_map(
            gathered,
            mesh=mesh,
            in_specs=(P("row", "col", None),) + (P(),) * 9,
            out_specs=P("row", "col", None),
            check_vma=False,
        )(*arrays)

    return call
```

```python
import functools
import jax
import jax.numpy as jnp
from jax import lax
from jax.experimental import pallas as pl
from jax.experimental.pallas import tpu as pltpu
from jax.sharding import PartitionSpec as P

LANES = 128
F32 = jnp.float32
BF16 = jnp.bfloat16


def broadcast(value, axis, source):
    kept = jnp.where(lax.axis_index(axis) == source, value, 0).astype(value.dtype)
    return lax.psum(kept, axis)


def layer_norm(values, gain, bias):
    mean = jnp.mean(values, axis=-1, keepdims=True)
    centered = values - mean
    variance = jnp.mean(centered * centered, axis=-1, keepdims=True)
    return centered * lax.rsqrt(variance + 1e-05) * gain + bias


def token_valid(chain_lengths, tokens_idx, slots):
    chain = tokens_idx // slots
    position = tokens_idx % slots
    chain_ids = jnp.arange(chain_lengths.shape[0], dtype=jnp.int32)
    length_of = jnp.sum(
        jnp.where(chain[:, None] == chain_ids[None, :], chain_lengths[None, :], 0), axis=1
    )
    return (position < length_of).astype(jnp.float32)


def gathered(
    pair,
    chain_lengths,
    norm_in_gain,
    norm_in_bias,
    proj_in,
    gate_in,
    norm_out_gain,
    norm_out_bias,
    proj_out,
    gate_out,
):
    row_count = pair.shape[0]
    col_count = pair.shape[1]
    channels = pair.shape[2]
    hidden = proj_out.shape[0]
    row_index = lax.axis_index("row")
    col_index = lax.axis_index("col")
    slots = row_count * lax.axis_size("row") // chain_lengths.shape[0]
    valid_rows = token_valid(
        chain_lengths, row_index * row_count + jnp.arange(row_count, dtype=jnp.int32), slots
    )
    valid_cols = token_valid(
        chain_lengths, col_index * col_count + jnp.arange(col_count, dtype=jnp.int32), slots
    )
    pair_mask = valid_rows[:, None] * valid_cols[None, :]
    normed = layer_norm(pair.astype(jnp.float32), norm_in_gain, norm_in_bias).astype(jnp.bfloat16)
    flat = normed.reshape(-1, channels)
    values = jnp.dot(flat, proj_in, preferred_element_type=jnp.float32)
    gates = jnp.dot(flat, gate_in, preferred_element_type=jnp.float32)
    mixed = (jax.nn.sigmoid(gates) * values).reshape(row_count, col_count, 2 * hidden) * pair_mask[
        :, :, None
    ]
    left_tile = mixed[:, :, :hidden].astype(jnp.bfloat16)
    right_tile = mixed[:, :, hidden:].astype(jnp.bfloat16)
    ratio = lax.axis_size("row") // lax.axis_size("col")
    right_full = lax.all_gather(right_tile, "col", axis=1, tiled=True)
    received = []
    for part in range(ratio):
        received.append(broadcast(right_full, "row", col_index * ratio + part))
    right_mine = jnp.concatenate(received, axis=0)
    triangle = jnp.einsum(
        "ikh,jkh->ijh",
        lax.all_gather(left_tile, "col", axis=1, tiled=True),
        right_mine,
        preferred_element_type=jnp.float32,
    )
    tri_normed = layer_norm(triangle, norm_out_gain, norm_out_bias).astype(jnp.bfloat16)
    projected = jnp.dot(
        tri_normed.reshape(-1, hidden), proj_out, preferred_element_type=jnp.float32
    )
    gate = jax.nn.sigmoid(jnp.dot(flat, gate_out, preferred_element_type=jnp.float32))
    return (gate * projected).astype(jnp.bfloat16).reshape(row_count, col_count, channels)


def iota2(shape):
    return (
        lax.broadcasted_iota(jnp.int32, shape, 0),
        lax.broadcasted_iota(jnp.int32, shape, 1),
    )


def one_hot(condition):
    return jnp.where(condition, 1.0, 0.0).astype(BF16)


def dot(a, b, a_dim=1, b_dim=0):
    return lax.dot_general(a, b, (((a_dim,), (b_dim,)), ((), ())), preferred_element_type=F32)


def fetch(sources, targets, sems):
    copies = [
        pltpu.make_async_copy(source, target, sems.at[n])
        for n, (source, target) in enumerate(zip(sources, targets))
    ]
    for copy in copies:
        copy.start()
    return copies


def sigmoid(halved):
    return 0.5 + 0.5 * jnp.tanh(halved)


def column(row_ref):
    a, b = iota2((LANES, LANES))
    return jnp.sum(jnp.where(a == b, row_ref[...], 0.0), axis=1, keepdims=True)


def exchange_blocks(arrays, cols):
    lane = lax.broadcasted_iota(jnp.int32, (1, LANES), 1) // cols
    arrays, step = list(arrays), 1
    while step < len(arrays):
        upper = lane // step % 2 == 1
        for n in range(len(arrays)):
            if n // step % 2 == 0:
                a, b = arrays[n], arrays[n + step]
                arrays[n] = jnp.where(upper, pltpu.roll(b, step * cols, 1), a)
                arrays[n + step] = jnp.where(upper, b, pltpu.roll(a, LANES - step * cols, 1))
        step *= 2
    return arrays


def mix_kernel(
    slots,
    chain_hbm,
    pair_hbm,
    gain_hbm,
    bias_hbm,
    proj_hbm,
    gate_hbm,
    sent_hbm,
    normed_hbm,
    chain_ref,
    pair_ref,
    gain_ref,
    bias_ref,
    proj_ref,
    gate_ref,
    sent_ref,
    normed_ref,
    sems,
    out_sems,
):
    copies = fetch(
        (pair_hbm, gain_hbm, bias_hbm, chain_hbm, proj_hbm, gate_hbm),
        (pair_ref, gain_ref, bias_ref, chain_ref, proj_ref, gate_ref),
        sems,
    )
    rows, cols, channels = pair_ref.shape
    hidden = proj_ref.shape[1] // 2
    cells = rows * cols
    inner = LANES // cols
    groups = rows // inner
    chunks = sent_ref.shape[0]
    some = 16
    out, source = iota2((some * rows, some * rows))
    order = one_hot((out // rows == source % some) & (out % rows == source // some))
    a, b = iota2((channels, channels))
    eye = one_hot(a == b)
    cell = lax.broadcasted_iota(jnp.int32, (1, cells), 1)
    for copy in copies:
        copy.wait()
    flat = dot(eye, pair_ref[...].reshape(cells, channels), 1, 1)
    centered = flat - jnp.mean(flat, axis=0, keepdims=True)
    variance = jnp.mean(centered * centered, axis=0, keepdims=True)
    normed = centered * lax.rsqrt(variance + 1e-05) * column(gain_ref) + column(bias_ref)
    normed = normed.astype(BF16)
    normed_ref[...] = normed
    results = [pltpu.make_async_copy(normed_ref, normed_hbm, out_sems.at[0])]
    results[0].start()

    def valid(token):
        length = jnp.zeros_like(token)
        for chain in range(chain_ref.shape[0]):
            length = jnp.where(token // slots == chain, chain_ref[chain], length)
        return token % slots < length

    row_ok = valid(lax.axis_index("row") * rows + cell // cols)
    col_ok = valid(lax.axis_index("col") * cols + cell % cols)
    mask = jnp.where(row_ok & col_ok, 1.0, 0.0)

    values = dot(proj_ref[...], normed, 0, 0)
    gates = dot(gate_ref[...] * 0.5, normed, 0, 0)
    mixed = (sigmoid(gates) * values * mask).astype(BF16)

    by_row = []
    for side in range(2):
        lines = []
        for g in range(groups):
            lines += exchange_blocks(
                [
                    mixed[
                        side * hidden + n * chunks : side * hidden + (n + 1) * chunks,
                        g * LANES : (g + 1) * LANES,
                    ]
                    for n in range(inner)
                ],
                cols,
            )
        by_row.append(lines)
    for part in range(chunks // some):
        here = pl.ds(part * some, some)
        for side in range(2):
            stack = jnp.concatenate(
                [line[part * some : (part + 1) * some] for line in by_row[side]], axis=0
            )
            moved = dot(order, stack).astype(BF16)
            sent_ref[here, side * rows : (side + 1) * rows] = moved.reshape(some, rows, LANES)
        results.append(
            pltpu.make_async_copy(sent_ref.at[here], sent_hbm.at[here], out_sems.at[part + 1])
        )
        results[-1].start()
    for copy in results:
        copy.wait()


def triangle_kernel(order, grid_rows, grid_cols, rows, cols, got_ref, sent_ref):
    inner = LANES // cols

    def place(r, c):
        return order.index(r * grid_cols + c)

    def side(which):
        return jnp.concatenate(
            [
                jnp.concatenate(
                    [
                        got_ref[place(r, c), which * rows : (which + 1) * rows]
                        for r in range(grid_rows)
                    ],
                    axis=0,
                )
                for c in range(grid_cols)
            ],
            axis=1,
        )

    left, right = side(0), side(1)
    lane = lax.broadcasted_iota(jnp.int32, (1, grid_cols * LANES), 1)
    by_channel = [right * one_hot(lane % LANES // cols == n) for n in range(inner)]
    right_by = jnp.concatenate(
        [
            by_channel[n][c * cols : (c + 1) * cols]
            for c in range(grid_cols)
            for n in range(inner)
        ],
        axis=0,
    )
    sums = dot(left, right_by, 1, 1).astype(BF16)
    for c in range(grid_cols):
        for r in range(grid_rows):
            sent_ref[place(r, c)] = sums[r * rows : (r + 1) * rows, c * LANES : (c + 1) * LANES]


def gate_kernel(
    normed_ref,
    gate_hbm,
    gain_hbm,
    bias_hbm,
    proj_hbm,
    open_ref,
    gain_out,
    bias_out,
    proj_out,
    gate_ref,
    gain_ref,
    bias_ref,
    sems,
):
    copies = fetch(
        (gate_hbm, gain_hbm, bias_hbm, proj_hbm), (gate_ref, gain_ref, bias_ref, proj_out), sems
    )
    for copy in copies:
        copy.wait()
    open_ref[...] = sigmoid(dot(normed_ref[...], gate_ref[...] * 0.5, 0, 0))
    gain_out[...] = jnp.broadcast_to(column(gain_ref), gain_out.shape)
    bias_out[...] = jnp.broadcast_to(column(bias_ref), bias_out.shape)


def update_kernel(
    got_ref, open_ref, gain_ref, bias_ref, proj_ref, out_hbm, out_ref, out_sems
):
    rows, cols, channels = out_ref.shape
    chunks = got_ref.shape[0]
    inner = LANES // cols
    groups = rows // inner
    some = 16
    out, source = iota2((some * rows, some * rows))
    order = one_hot((out // some == source % rows) & (out % some == source // rows))
    parts = [
        dot(order, got_ref[part * some : (part + 1) * some].reshape(some * rows, LANES)).astype(BF16)
        for part in range(chunks // some)
    ]
    lines = [
        jnp.concatenate([part[row * some : (row + 1) * some] for part in parts], axis=0)
        for row in range(rows)
    ]
    gain, bias = gain_ref[...], bias_ref[...]
    results = []
    for g in range(groups):
        values = jnp.concatenate(
            exchange_blocks(lines[g * inner : (g + 1) * inner], cols), axis=0
        ).astype(F32)
        mean = jnp.mean(values, axis=0, keepdims=True)
        centered = values - mean
        variance = jnp.mean(centered * centered, axis=0, keepdims=True)
        tri_normed = (centered * lax.rsqrt(variance + 1e-05) * gain + bias).astype(BF16)
        projected = dot(tri_normed, proj_ref[...], 0, 0)
        update = (open_ref[g * LANES : (g + 1) * LANES] * projected).astype(BF16)
        here = pl.ds(g * inner, inner)
        out_ref[here] = update.reshape(inner, cols, channels)
        results.append(pltpu.make_async_copy(out_ref.at[here], out_hbm.at[here], out_sems.at[g]))
        results[-1].start()
    for copy in results:
        copy.wait()


VMEM = pl.BlockSpec(memory_space=pltpu.VMEM)
HBM = pl.BlockSpec(memory_space=pltpu.HBM)
PARAMS = pltpu.CompilerParams(vmem_limit_bytes=32 * 1024 * 1024)
FETCHING = pltpu.CompilerParams(vmem_limit_bytes=60 * 1024 * 1024)


def exchanged(
    grid_rows,
    grid_cols,
    pair,
    chain_lengths,
    norm_in_gain,
    norm_in_bias,
    proj_in,
    gate_in,
    norm_out_gain,
    norm_out_bias,
    proj_out,
    gate_out,
):
    rows, cols, channels = pair.shape
    hidden = proj_out.shape[0]
    devices = grid_rows * grid_cols
    slots = rows * grid_rows // chain_lengths.shape[0]
    sent, normed = pl.pallas_call(
        functools.partial(mix_kernel, slots),
        out_shape=(
            jax.ShapeDtypeStruct((devices, 2 * rows, LANES), BF16),
            jax.ShapeDtypeStruct((channels, rows * cols), BF16),
        ),
        in_specs=[HBM] * 6,
        out_specs=(HBM, HBM),
        scratch_shapes=[
            pltpu.SMEM(chain_lengths.shape, jnp.int32),
            pltpu.VMEM(pair.shape, BF16),
            pltpu.VMEM((1, channels), F32),
            pltpu.VMEM((1, channels), F32),
            pltpu.VMEM(proj_in.shape, BF16),
            pltpu.VMEM(gate_in.shape, BF16),
            pltpu.VMEM((devices, 2 * rows, LANES), BF16),
            pltpu.VMEM((channels, rows * cols), BF16),
            pltpu.SemaphoreType.DMA((6,)),
            pltpu.SemaphoreType.DMA((1 + devices // 16,)),
        ],
        compiler_params=FETCHING,
        name="mix",
    )(
        chain_lengths,
        pair,
        norm_in_gain.reshape(1, channels),
        norm_in_bias.reshape(1, channels),
        proj_in,
        gate_in,
    )
    order = list(range(devices - 1, -1, -1))

    def exchange(chunks):
        return lax.all_to_all(
            chunks, ("row", "col"), 0, 0, tiled=True, axis_index_groups=[order]
        )

    got = exchange(sent)
    opened, gain, bias, proj = pl.pallas_call(
        gate_kernel,
        out_shape=(
            jax.ShapeDtypeStruct((rows * cols, channels), F32),
            jax.ShapeDtypeStruct((hidden, LANES), F32),
            jax.ShapeDtypeStruct((hidden, LANES), F32),
            jax.ShapeDtypeStruct(proj_out.shape, BF16),
        ),
        in_specs=[VMEM] + [HBM] * 4,
        out_specs=[VMEM] * 4,
        scratch_shapes=[
            pltpu.VMEM(gate_out.shape, BF16),
            pltpu.VMEM((1, hidden), F32),
            pltpu.VMEM((1, hidden), F32),
            pltpu.SemaphoreType.DMA((4,)),
        ],
        compiler_params=PARAMS,
        name="gate",
    )(normed, gate_out, norm_out_gain.reshape(1, hidden), norm_out_bias.reshape(1, hidden), proj_out)
    got, opened, gain, bias, proj = lax.optimization_barrier((got, opened, gain, bias, proj))
    sums = pl.pallas_call(
        functools.partial(triangle_kernel, order, grid_rows, grid_cols, rows, cols),
        out_shape=jax.ShapeDtypeStruct((devices, rows, LANES), BF16),
        in_specs=[VMEM],
        out_specs=VMEM,
        compiler_params=PARAMS,
        name="triangle",
    )(got)
    mine = exchange(sums)
    return pl.pallas_call(
        update_kernel,
        out_shape=jax.ShapeDtypeStruct((rows, cols, channels), BF16),
        in_specs=[VMEM] * 5,
        out_specs=HBM,
        scratch_shapes=[
            pltpu.VMEM((rows, cols, channels), BF16),
            pltpu.SemaphoreType.DMA((rows * cols // LANES,)),
        ],
        compiler_params=PARAMS,
        name="update",
    )(mine, opened, gain, bias, proj)


def solution(mesh):
    grid_rows, grid_cols = mesh.shape["row"], mesh.shape["col"]
    def fits(rows, cols, channels, hidden):
        devices = grid_rows * grid_cols
        inner = LANES // cols
        return (
            channels == LANES
            and hidden == LANES
            and inner * cols == LANES
            and inner & (inner - 1) == 0
            and inner * devices == hidden
            and rows % 16 == 0
            and rows % inner == 0
            and devices % 16 == 0
        )

    def call(*arrays):
        tokens, others, channels = arrays[0].shape
        hidden = arrays[8].shape[0]
        if fits(tokens // grid_rows, others // grid_cols, channels, hidden):
            return jax.shard_map(
                functools.partial(exchanged, grid_rows, grid_cols),
                mesh=mesh,
                in_specs=(P("row", "col", None),) + (P(),) * 9,
                out_specs=P("row", "col", None),
                check_vma=False,
            )(*arrays)
        return jax.shard_map(
            gathered,
            mesh=mesh,
            in_specs=(P("row", "col", None),) + (P(),) * 9,
            out_specs=P("row", "col", None),
            check_vma=False,
        )(*arrays)

    return call
```

```python
import functools
import jax
import jax.numpy as jnp
from jax import lax
from jax.experimental import pallas as pl
from jax.experimental.pallas import tpu as pltpu
from jax.sharding import PartitionSpec as P

LANES = 128
SOME = 16
F32 = jnp.float32
BF16 = jnp.bfloat16


def broadcast(value, axis, source):
    kept = jnp.where(lax.axis_index(axis) == source, value, 0).astype(value.dtype)
    return lax.psum(kept, axis)


def layer_norm(values, gain, bias):
    mean = jnp.mean(values, axis=-1, keepdims=True)
    centered = values - mean
    variance = jnp.mean(centered * centered, axis=-1, keepdims=True)
    return centered * lax.rsqrt(variance + 1e-05) * gain + bias


def token_valid(chain_lengths, tokens_idx, slots):
    chain = tokens_idx // slots
    position = tokens_idx % slots
    chain_ids = jnp.arange(chain_lengths.shape[0], dtype=jnp.int32)
    length_of = jnp.sum(
        jnp.where(chain[:, None] == chain_ids[None, :], chain_lengths[None, :], 0), axis=1
    )
    return (position < length_of).astype(jnp.float32)


def gathered(
    pair,
    chain_lengths,
    norm_in_gain,
    norm_in_bias,
    proj_in,
    gate_in,
    norm_out_gain,
    norm_out_bias,
    proj_out,
    gate_out,
):
    row_count = pair.shape[0]
    col_count = pair.shape[1]
    channels = pair.shape[2]
    hidden = proj_out.shape[0]
    row_index = lax.axis_index("row")
    col_index = lax.axis_index("col")
    slots = row_count * lax.axis_size("row") // chain_lengths.shape[0]
    valid_rows = token_valid(
        chain_lengths, row_index * row_count + jnp.arange(row_count, dtype=jnp.int32), slots
    )
    valid_cols = token_valid(
        chain_lengths, col_index * col_count + jnp.arange(col_count, dtype=jnp.int32), slots
    )
    pair_mask = valid_rows[:, None] * valid_cols[None, :]
    normed = layer_norm(pair.astype(jnp.float32), norm_in_gain, norm_in_bias).astype(jnp.bfloat16)
    flat = normed.reshape(-1, channels)
    values = jnp.dot(flat, proj_in, preferred_element_type=jnp.float32)
    gates = jnp.dot(flat, gate_in, preferred_element_type=jnp.float32)
    mixed = (jax.nn.sigmoid(gates) * values).reshape(row_count, col_count, 2 * hidden) * pair_mask[
        :, :, None
    ]
    left_tile = mixed[:, :, :hidden].astype(jnp.bfloat16)
    right_tile = mixed[:, :, hidden:].astype(jnp.bfloat16)
    ratio = lax.axis_size("row") // lax.axis_size("col")
    right_full = lax.all_gather(right_tile, "col", axis=1, tiled=True)
    received = []
    for part in range(ratio):
        received.append(broadcast(right_full, "row", col_index * ratio + part))
    right_mine = jnp.concatenate(received, axis=0)
    triangle = jnp.einsum(
        "ikh,jkh->ijh",
        lax.all_gather(left_tile, "col", axis=1, tiled=True),
        right_mine,
        preferred_element_type=jnp.float32,
    )
    tri_normed = layer_norm(triangle, norm_out_gain, norm_out_bias).astype(jnp.bfloat16)
    projected = jnp.dot(
        tri_normed.reshape(-1, hidden), proj_out, preferred_element_type=jnp.float32
    )
    gate = jax.nn.sigmoid(jnp.dot(flat, gate_out, preferred_element_type=jnp.float32))
    return (gate * projected).astype(jnp.bfloat16).reshape(row_count, col_count, channels)


def iota2(shape):
    return (
        lax.broadcasted_iota(jnp.int32, shape, 0),
        lax.broadcasted_iota(jnp.int32, shape, 1),
    )


def one_hot(condition):
    return jnp.where(condition, 1.0, 0.0).astype(BF16)


def dot(a, b, a_dim=1, b_dim=0):
    return lax.dot_general(a, b, (((a_dim,), (b_dim,)), ((), ())), preferred_element_type=F32)


def fetch(sources, targets, sems):
    copies = [
        pltpu.make_async_copy(source, target, sems.at[n])
        for n, (source, target) in enumerate(zip(sources, targets))
    ]
    for copy in copies:
        copy.start()
    return copies


def sigmoid(halved):
    return 0.5 + 0.5 * jnp.tanh(halved)


def column(row_ref):
    a, b = iota2((LANES, LANES))
    return jnp.sum(jnp.where(a == b, row_ref[...], 0.0), axis=1, keepdims=True)


def exchange_blocks(arrays, cols):
    lane = lax.broadcasted_iota(jnp.int32, (1, LANES), 1) // cols
    arrays, step = list(arrays), 1
    while step < len(arrays):
        upper = lane // step % 2 == 1
        for n in range(len(arrays)):
            if n // step % 2 == 0:
                a, b = arrays[n], arrays[n + step]
                arrays[n] = jnp.where(upper, pltpu.roll(b, step * cols, 1), a)
                arrays[n + step] = jnp.where(upper, b, pltpu.roll(a, LANES - step * cols, 1))
        step *= 2
    return arrays


def cell_mask(chain_ref, slots, rows, cols):
    cell = lax.broadcasted_iota(jnp.int32, (1, rows * cols), 1)

    def valid(token):
        length = jnp.zeros_like(token)
        for chain in range(chain_ref.shape[0]):
            length = jnp.where(token // slots == chain, chain_ref[chain], length)
        return token % slots < length

    row_ok = valid(lax.axis_index("row") * rows + cell // cols)
    col_ok = valid(lax.axis_index("col") * cols + cell % cols)
    return jnp.where(row_ok & col_ok, 1.0, 0.0)


def chunks_of(normed, proj, gate, mask, rows, cols):
    hidden = proj.shape[1]
    inner = LANES // cols
    chunks = hidden // inner
    out, source = iota2((SOME * rows, SOME * rows))
    order = one_hot((out // rows == source % SOME) & (out % rows == source // SOME))
    values = dot(proj, normed, 0, 0)
    gates = dot(gate * 0.5, normed, 0, 0)
    mixed = (sigmoid(gates) * values * mask).astype(BF16)
    lines = []
    for g in range(rows // inner):
        lines += exchange_blocks(
            [
                mixed[n * chunks : (n + 1) * chunks, g * LANES : (g + 1) * LANES]
                for n in range(inner)
            ],
            cols,
        )
    for part in range(chunks // SOME):
        stack = jnp.concatenate(
            [line[part * SOME : (part + 1) * SOME] for line in lines], axis=0
        )
        yield dot(order, stack).astype(BF16).reshape(SOME, rows, LANES)


def right_kernel(
    slots,
    halves,
    chain_hbm,
    pair_hbm,
    gain_hbm,
    bias_hbm,
    proj_hbm,
    gate_hbm,
    sent_hbm,
    normed_hbm,
    chain_ref,
    pair_ref,
    gain_ref,
    bias_ref,
    proj_ref,
    gate_ref,
    sent_ref,
    normed_ref,
    sems,
    out_sems,
):
    rows, cols, channels = pair_ref.shape
    hidden = proj_ref.shape[1]
    members = sent_ref.shape[0]
    second = pl.ds(hidden, hidden)
    copies = fetch(
        (
            pair_hbm,
            gain_hbm,
            bias_hbm,
            chain_hbm,
            proj_hbm.at[:, second],
            gate_hbm.at[:, second],
        ),
        (pair_ref, gain_ref, bias_ref, chain_ref, proj_ref, gate_ref),
        sems,
    )
    a, b = iota2((channels, channels))
    eye = one_hot(a == b)
    for copy in copies:
        copy.wait()
    flat = dot(eye, pair_ref[...].reshape(rows * cols, channels), 1, 1)
    centered = flat - jnp.mean(flat, axis=0, keepdims=True)
    variance = jnp.mean(centered * centered, axis=0, keepdims=True)
    normed = centered * lax.rsqrt(variance + 1e-05) * column(gain_ref) + column(bias_ref)
    normed = normed.astype(BF16)
    normed_ref[...] = normed
    results = [pltpu.make_async_copy(normed_ref, normed_hbm, out_sems.at[0])]
    results[0].start()
    mask = cell_mask(chain_ref, slots, rows, cols)
    blocks = chunks_of(normed, proj_ref[...], gate_ref[...], mask, rows, cols)
    for part, block in enumerate(blocks):
        first, sub = part * SOME % members, part * SOME // members
        here = (pl.ds(first, SOME), pl.ds(sub * rows, rows))
        sent_ref[here] = block
        for half in range(halves):
            there = (pl.ds(half * members + first, SOME), here[1])
            results.append(
                pltpu.make_async_copy(
                    sent_ref.at[here], sent_hbm.at[there], out_sems.at[len(results)]
                )
            )
            results[-1].start()
    for copy in results:
        copy.wait()


def left_kernel(
    slots,
    rows,
    cols,
    chain_ref,
    normed_ref,
    proj_ref,
    gate_ref,
    open_weight_ref,
    gain_ref,
    bias_ref,
    sent_ref,
    open_ref,
    gain_out,
    bias_out,
):
    hidden = proj_ref.shape[1] // 2
    members = sent_ref.shape[0]
    normed = normed_ref[...]
    mask = cell_mask(chain_ref, slots, rows, cols)
    blocks = chunks_of(normed, proj_ref[:, :hidden], gate_ref[:, :hidden], mask, rows, cols)
    for part, block in enumerate(blocks):
        first, sub = part * SOME % members, part * SOME // members
        sent_ref[first : first + SOME, sub * rows : (sub + 1) * rows] = block
    open_ref[...] = sigmoid(dot(normed, open_weight_ref[...] * 0.5, 0, 0))
    gain_out[...] = jnp.broadcast_to(column(gain_ref), gain_out.shape)
    bias_out[...] = jnp.broadcast_to(column(bias_ref), bias_out.shape)


def triangle_kernel(grid_cols, rows, cols, left_ref, right_ref, sent_ref):
    inner = LANES // cols
    lane = lax.broadcasted_iota(jnp.int32, (1, grid_cols * LANES), 1)
    own = [one_hot(lane % LANES // cols == n) for n in range(inner)]

    def whole(ref, sub):
        return jnp.concatenate(
            [
                jnp.concatenate(
                    [
                        ref[r * grid_cols + c, sub * rows : (sub + 1) * rows]
                        for r in range(ref.shape[0] // grid_cols)
                    ],
                    axis=0,
                )
                for c in range(grid_cols)
            ],
            axis=1,
        )

    for sub in range(left_ref.shape[1] // rows):
        right = whole(right_ref, sub)
        by_channel = [right * mask for mask in own]
        right_by = jnp.concatenate(
            [
                by_channel[n][c * cols : (c + 1) * cols]
                for c in range(grid_cols)
                for n in range(inner)
            ],
            axis=0,
        )
        sums = dot(whole(left_ref, sub), right_by, 1, 1).astype(BF16)
        for r in range(left_ref.shape[0] // grid_cols):
            for c in range(grid_cols):
                sent_ref[r * grid_cols + c, sub * rows : (sub + 1) * rows] = sums[
                    r * rows : (r + 1) * rows, c * LANES : (c + 1) * LANES
                ]


def update_kernel(
    got_ref, open_ref, gain_ref, bias_ref, proj_ref, out_hbm, out_ref, out_sems
):
    rows, cols, channels = out_ref.shape
    members = got_ref.shape[0]
    inner = LANES // cols
    groups = rows // inner
    out, source = iota2((SOME * rows, SOME * rows))
    order = one_hot((out // SOME == source % rows) & (out % SOME == source // rows))
    parts = [
        dot(
            order,
            got_ref[first : first + SOME, sub * rows : (sub + 1) * rows].reshape(-1, LANES),
        ).astype(BF16)
        for sub in range(got_ref.shape[1] // rows)
        for first in range(0, members, SOME)
    ]
    lines = [
        jnp.concatenate([part[row * SOME : (row + 1) * SOME] for part in parts], axis=0)
        for row in range(rows)
    ]
    gain, bias = gain_ref[...], bias_ref[...]
    results = []
    for g in range(groups):
        values = jnp.concatenate(
            exchange_blocks(lines[g * inner : (g + 1) * inner], cols), axis=0
        ).astype(F32)
        mean = jnp.mean(values, axis=0, keepdims=True)
        centered = values - mean
        variance = jnp.mean(centered * centered, axis=0, keepdims=True)
        tri_normed = (centered * lax.rsqrt(variance + 1e-05) * gain + bias).astype(BF16)
        projected = dot(tri_normed, proj_ref[...], 0, 0)
        update = (open_ref[g * LANES : (g + 1) * LANES] * projected).astype(BF16)
        here = pl.ds(g * inner, inner)
        out_ref[here] = update.reshape(inner, cols, channels)
        results.append(pltpu.make_async_copy(out_ref.at[here], out_hbm.at[here], out_sems.at[g]))
        results[-1].start()
    for copy in results:
        copy.wait()


VMEM = pl.BlockSpec(memory_space=pltpu.VMEM)
SMEM = pl.BlockSpec(memory_space=pltpu.SMEM)
HBM = pl.BlockSpec(memory_space=pltpu.HBM)
PARAMS = pltpu.CompilerParams(vmem_limit_bytes=32 * 1024 * 1024)
FETCHING = pltpu.CompilerParams(vmem_limit_bytes=60 * 1024 * 1024)


def exchanged(
    grid_rows,
    grid_cols,
    halves,
    pair,
    chain_lengths,
    norm_in_gain,
    norm_in_bias,
    proj_in,
    gate_in,
    norm_out_gain,
    norm_out_bias,
    proj_out,
    gate_out,
):
    rows, cols, channels = pair.shape
    hidden = proj_out.shape[0]
    devices = grid_rows * grid_cols
    members = devices // halves
    slots = rows * grid_rows // chain_lengths.shape[0]
    chunk = (halves * rows, LANES)

    def exchange(chunks, groups):
        return lax.all_to_all(
            chunks, ("row", "col"), 0, 0, tiled=True, axis_index_groups=groups
        )

    by_half = [list(range(h * members, (h + 1) * members)) for h in range(halves)]
    right, normed = pl.pallas_call(
        functools.partial(right_kernel, slots, halves),
        out_shape=(
            jax.ShapeDtypeStruct((devices,) + chunk, BF16),
            jax.ShapeDtypeStruct((channels, rows * cols), BF16),
        ),
        in_specs=[HBM] * 6,
        out_specs=(HBM, HBM),
        scratch_shapes=[
            pltpu.SMEM(chain_lengths.shape, jnp.int32),
            pltpu.VMEM(pair.shape, BF16),
            pltpu.VMEM((1, channels), F32),
            pltpu.VMEM((1, channels), F32),
            pltpu.VMEM((channels, hidden), BF16),
            pltpu.VMEM((channels, hidden), BF16),
            pltpu.VMEM((members,) + chunk, BF16),
            pltpu.VMEM((channels, rows * cols), BF16),
            pltpu.SemaphoreType.DMA((6,)),
            pltpu.SemaphoreType.DMA((1 + devices // SOME * halves,)),
        ],
        compiler_params=FETCHING,
        name="right",
    )(
        chain_lengths,
        pair,
        norm_in_gain.reshape(1, channels),
        norm_in_bias.reshape(1, channels),
        proj_in,
        gate_in,
    )
    got_right = exchange(right, None)
    left, opened, gain, bias = pl.pallas_call(
        functools.partial(left_kernel, slots, rows, cols),
        out_shape=(
            jax.ShapeDtypeStruct((members,) + chunk, BF16),
            jax.ShapeDtypeStruct((rows * cols, channels), F32),
            jax.ShapeDtypeStruct((hidden, LANES), F32),
            jax.ShapeDtypeStruct((hidden, LANES), F32),
        ),
        in_specs=[SMEM] + [VMEM] * 6,
        out_specs=[VMEM] * 4,
        compiler_params=PARAMS,
        name="left",
    )(
        chain_lengths,
        normed,
        proj_in,
        gate_in,
        gate_out,
        norm_out_gain.reshape(1, hidden),
        norm_out_bias.reshape(1, hidden),
    )
    got_left = exchange(left, by_half)
    sums = pl.pallas_call(
        functools.partial(triangle_kernel, grid_cols, rows, cols),
        out_shape=jax.ShapeDtypeStruct((members,) + chunk, BF16),
        in_specs=[VMEM] * 2,
        out_specs=VMEM,
        compiler_params=PARAMS,
        name="triangle",
    )(got_left, got_right)
    mine = exchange(sums, by_half)
    return pl.pallas_call(
        update_kernel,
        out_shape=jax.ShapeDtypeStruct((rows, cols, channels), BF16),
        in_specs=[VMEM] * 5,
        out_specs=HBM,
        scratch_shapes=[
            pltpu.VMEM((rows, cols, channels), BF16),
            pltpu.SemaphoreType.DMA((rows * cols // LANES,)),
        ],
        compiler_params=PARAMS,
        name="update",
    )(mine, opened, gain, bias, proj_out)


def solution(mesh):
    grid_rows, grid_cols = mesh.shape["row"], mesh.shape["col"]
    halves = 2

    def fits(rows, cols, channels, hidden):
        devices = grid_rows * grid_cols
        inner = LANES // cols
        return (
            channels == LANES
            and hidden == LANES
            and inner * cols == LANES
            and inner & (inner - 1) == 0
            and inner * devices == hidden
            and rows % 16 == 0
            and rows % inner == 0
            and grid_rows % halves == 0
            and devices // halves % SOME == 0
        )

    def call(*arrays):
        tokens, others, channels = arrays[0].shape
        hidden = arrays[8].shape[0]
        if fits(tokens // grid_rows, others // grid_cols, channels, hidden):
            return jax.shard_map(
                functools.partial(exchanged, grid_rows, grid_cols, halves),
                mesh=mesh,
                in_specs=(P("row", "col", None),) + (P(),) * 9,
                out_specs=P("row", "col", None),
                check_vma=False,
            )(*arrays)
        return jax.shard_map(
            gathered,
            mesh=mesh,
            in_specs=(P("row", "col", None),) + (P(),) * 9,
            out_specs=P("row", "col", None),
            check_vma=False,
        )(*arrays)

    return call
```

```python
import functools
import jax
import jax.numpy as jnp
from jax import lax
from jax.experimental import pallas as pl
from jax.experimental.pallas import tpu as pltpu
from jax.sharding import PartitionSpec as P

LANES = 128
F32 = jnp.float32
BF16 = jnp.bfloat16


def broadcast(value, axis, source):
    kept = jnp.where(lax.axis_index(axis) == source, value, 0).astype(value.dtype)
    return lax.psum(kept, axis)


def layer_norm(values, gain, bias):
    mean = jnp.mean(values, axis=-1, keepdims=True)
    centered = values - mean
    variance = jnp.mean(centered * centered, axis=-1, keepdims=True)
    return centered * lax.rsqrt(variance + 1e-05) * gain + bias


def token_valid(chain_lengths, tokens_idx, slots):
    chain = tokens_idx // slots
    position = tokens_idx % slots
    chain_ids = jnp.arange(chain_lengths.shape[0], dtype=jnp.int32)
    length_of = jnp.sum(
        jnp.where(chain[:, None] == chain_ids[None, :], chain_lengths[None, :], 0), axis=1
    )
    return (position < length_of).astype(jnp.float32)


def gathered(
    pair,
    chain_lengths,
    norm_in_gain,
    norm_in_bias,
    proj_in,
    gate_in,
    norm_out_gain,
    norm_out_bias,
    proj_out,
    gate_out,
):
    row_count = pair.shape[0]
    col_count = pair.shape[1]
    channels = pair.shape[2]
    hidden = proj_out.shape[0]
    row_index = lax.axis_index("row")
    col_index = lax.axis_index("col")
    slots = row_count * lax.axis_size("row") // chain_lengths.shape[0]
    valid_rows = token_valid(
        chain_lengths, row_index * row_count + jnp.arange(row_count, dtype=jnp.int32), slots
    )
    valid_cols = token_valid(
        chain_lengths, col_index * col_count + jnp.arange(col_count, dtype=jnp.int32), slots
    )
    pair_mask = valid_rows[:, None] * valid_cols[None, :]
    normed = layer_norm(pair.astype(jnp.float32), norm_in_gain, norm_in_bias).astype(jnp.bfloat16)
    flat = normed.reshape(-1, channels)
    values = jnp.dot(flat, proj_in, preferred_element_type=jnp.float32)
    gates = jnp.dot(flat, gate_in, preferred_element_type=jnp.float32)
    mixed = (jax.nn.sigmoid(gates) * values).reshape(row_count, col_count, 2 * hidden) * pair_mask[
        :, :, None
    ]
    left_tile = mixed[:, :, :hidden].astype(jnp.bfloat16)
    right_tile = mixed[:, :, hidden:].astype(jnp.bfloat16)
    ratio = lax.axis_size("row") // lax.axis_size("col")
    right_full = lax.all_gather(right_tile, "col", axis=1, tiled=True)
    received = []
    for part in range(ratio):
        received.append(broadcast(right_full, "row", col_index * ratio + part))
    right_mine = jnp.concatenate(received, axis=0)
    triangle = jnp.einsum(
        "ikh,jkh->ijh",
        lax.all_gather(left_tile, "col", axis=1, tiled=True),
        right_mine,
        preferred_element_type=jnp.float32,
    )
    tri_normed = layer_norm(triangle, norm_out_gain, norm_out_bias).astype(jnp.bfloat16)
    projected = jnp.dot(
        tri_normed.reshape(-1, hidden), proj_out, preferred_element_type=jnp.float32
    )
    gate = jax.nn.sigmoid(jnp.dot(flat, gate_out, preferred_element_type=jnp.float32))
    return (gate * projected).astype(jnp.bfloat16).reshape(row_count, col_count, channels)


def iota2(shape):
    return (
        lax.broadcasted_iota(jnp.int32, shape, 0),
        lax.broadcasted_iota(jnp.int32, shape, 1),
    )


def one_hot(condition):
    return jnp.where(condition, 1.0, 0.0).astype(BF16)


def dot(a, b, a_dim=1, b_dim=0):
    return lax.dot_general(a, b, (((a_dim,), (b_dim,)), ((), ())), preferred_element_type=F32)


def over(value, size):
    if size & (size - 1):
        return value // size
    return lax.shift_right_logical(value, jnp.full_like(value, size.bit_length() - 1))


def rest(value, size):
    return value % size if size & (size - 1) else value & (size - 1)


def fetch(sources, targets, sems):
    copies = [
        pltpu.make_async_copy(source, target, sems.at[n])
        for n, (source, target) in enumerate(zip(sources, targets))
    ]
    for copy in copies:
        copy.start()
    return copies


def sigmoid(halved):
    return 0.5 + 0.5 * jnp.tanh(halved)


def column(row_ref):
    a, b = iota2((LANES, LANES))
    return jnp.sum(jnp.where(a == b, row_ref[...], 0.0), axis=1, keepdims=True)


def exchange_blocks(arrays, cols):
    lane = over(lax.broadcasted_iota(jnp.int32, (1, LANES), 1), cols)
    arrays, step = list(arrays), 1
    while step < len(arrays):
        upper = lane & step != 0
        for n in range(len(arrays)):
            if n // step % 2 == 0:
                a, b = arrays[n], arrays[n + step]
                arrays[n] = jnp.where(upper, pltpu.roll(b, step * cols, 1), a)
                arrays[n + step] = jnp.where(upper, b, pltpu.roll(a, LANES - step * cols, 1))
        step *= 2
    return arrays


def mix_kernel(
    slots,
    chain_hbm,
    pair_hbm,
    gain_hbm,
    bias_hbm,
    proj_hbm,
    gate_hbm,
    sent_hbm,
    normed_hbm,
    chain_ref,
    pair_ref,
    gain_ref,
    bias_ref,
    proj_ref,
    gate_ref,
    sent_ref,
    normed_ref,
    sems,
    out_sems,
):
    copies = fetch(
        (pair_hbm, gain_hbm, bias_hbm, chain_hbm, proj_hbm, gate_hbm),
        (pair_ref, gain_ref, bias_ref, chain_ref, proj_ref, gate_ref),
        sems,
    )
    rows, cols, channels = pair_ref.shape
    hidden = proj_ref.shape[1] // 2
    cells = rows * cols
    inner = LANES // cols
    groups = rows // inner
    chunks = sent_ref.shape[0]
    some = 16
    out, source = iota2((some * rows, some * rows))
    order = one_hot(
        (over(out, rows) == rest(source, some)) & (rest(out, rows) == over(source, some))
    )
    a, b = iota2((channels, channels))
    eye = one_hot(a == b)
    cell = lax.broadcasted_iota(jnp.int32, (1, cells), 1)
    for copy in copies:
        copy.wait()
    flat = dot(eye, pair_ref[...].reshape(cells, channels), 1, 1)
    centered = flat - jnp.mean(flat, axis=0, keepdims=True)
    variance = jnp.mean(centered * centered, axis=0, keepdims=True)
    normed = centered * lax.rsqrt(variance + 1e-05) * column(gain_ref) + column(bias_ref)
    normed = normed.astype(BF16)
    normed_ref[...] = normed
    results = [pltpu.make_async_copy(normed_ref, normed_hbm, out_sems.at[0])]
    results[0].start()

    def valid(token):
        length = jnp.zeros_like(token)
        for chain in range(chain_ref.shape[0]):
            length = jnp.where(over(token, slots) == chain, chain_ref[chain], length)
        return rest(token, slots) < length

    row_ok = valid(lax.axis_index(("high", "low")) * rows + over(cell, cols))
    col_ok = valid(lax.axis_index("col") * cols + rest(cell, cols))
    mask = jnp.where(row_ok & col_ok, 1.0, 0.0)

    values = dot(proj_ref[...], normed, 0, 0)
    gates = dot(gate_ref[...] * 0.5, normed, 0, 0)
    mixed = (sigmoid(gates) * values * mask).astype(BF16)

    by_row = []
    for side in range(2):
        lines = []
        for g in range(groups):
            lines += exchange_blocks(
                [
                    mixed[
                        side * hidden + n * chunks : side * hidden + (n + 1) * chunks,
                        g * LANES : (g + 1) * LANES,
                    ]
                    for n in range(inner)
                ],
                cols,
            )
        by_row.append(lines)
    for part in range(chunks // some):
        here = pl.ds(part * some, some)
        for side in range(2):
            stack = jnp.concatenate(
                [line[part * some : (part + 1) * some] for line in by_row[side]], axis=0
            )
            moved = dot(order, stack).astype(BF16)
            sent_ref[here, side * rows : (side + 1) * rows] = moved.reshape(some, rows, LANES)
        results.append(
            pltpu.make_async_copy(sent_ref.at[here], sent_hbm.at[here], out_sems.at[part + 1])
        )
        results[-1].start()
    for copy in results:
        copy.wait()


def triangle_kernel(split, grid_cols, rows, cols, got_ref, sent_ref):
    inner = LANES // cols

    def place(r, c):
        z, y = r // split[1], r % split[1]
        return (c * split[1] + y) * split[0] + z

    def side(which):
        return jnp.concatenate(
            [
                jnp.concatenate(
                    [
                        got_ref[place(r, c), which * rows : (which + 1) * rows]
                        for r in range(split[0] * split[1])
                    ],
                    axis=0,
                )
                for c in range(grid_cols)
            ],
            axis=1,
        )

    left, right = side(0), side(1)
    lane = lax.broadcasted_iota(jnp.int32, (1, grid_cols * LANES), 1)
    by_channel = [right * one_hot(over(rest(lane, LANES), cols) == n) for n in range(inner)]
    right_by = jnp.concatenate(
        [
            by_channel[n][c * cols : (c + 1) * cols]
            for c in range(grid_cols)
            for n in range(inner)
        ],
        axis=0,
    )
    sums = dot(left, right_by, 1, 1).astype(BF16)
    for c in range(grid_cols):
        for r in range(split[0] * split[1]):
            sent_ref[place(r, c)] = sums[r * rows : (r + 1) * rows, c * LANES : (c + 1) * LANES]


def gate_kernel(
    normed_ref,
    gate_hbm,
    gain_hbm,
    bias_hbm,
    proj_hbm,
    open_ref,
    gain_out,
    bias_out,
    proj_out,
    gate_ref,
    gain_ref,
    bias_ref,
    sems,
):
    copies = fetch(
        (gate_hbm, gain_hbm, bias_hbm, proj_hbm), (gate_ref, gain_ref, bias_ref, proj_out), sems
    )
    for copy in copies:
        copy.wait()
    open_ref[...] = sigmoid(dot(normed_ref[...], gate_ref[...] * 0.5, 0, 0))
    gain_out[...] = jnp.broadcast_to(column(gain_ref), gain_out.shape)
    bias_out[...] = jnp.broadcast_to(column(bias_ref), bias_out.shape)


def update_kernel(
    got_ref, open_ref, gain_ref, bias_ref, proj_ref, out_hbm, out_ref, out_sems
):
    rows, cols, channels = out_ref.shape
    chunks = got_ref.shape[0]
    inner = LANES // cols
    groups = rows // inner
    some = 16
    out, source = iota2((some * rows, some * rows))
    order = one_hot(
        (over(out, some) == rest(source, rows)) & (rest(out, some) == over(source, rows))
    )
    parts = [
        dot(order, got_ref[part * some : (part + 1) * some].reshape(some * rows, LANES)).astype(BF16)
        for part in range(chunks // some)
    ]
    lines = [
        jnp.concatenate([part[row * some : (row + 1) * some] for part in parts], axis=0)
        for row in range(rows)
    ]
    gain, bias = gain_ref[...], bias_ref[...]
    results = []
    for g in range(groups):
        values = jnp.concatenate(
            exchange_blocks(lines[g * inner : (g + 1) * inner], cols), axis=0
        ).astype(F32)
        mean = jnp.mean(values, axis=0, keepdims=True)
        centered = values - mean
        variance = jnp.mean(centered * centered, axis=0, keepdims=True)
        tri_normed = (centered * lax.rsqrt(variance + 1e-05) * gain + bias).astype(BF16)
        projected = dot(tri_normed, proj_ref[...], 0, 0)
        update = (open_ref[g * LANES : (g + 1) * LANES] * projected).astype(BF16)
        here = pl.ds(g * inner, inner)
        out_ref[here] = update.reshape(inner, cols, channels)
        results.append(pltpu.make_async_copy(out_ref.at[here], out_hbm.at[here], out_sems.at[g]))
        results[-1].start()
    for copy in results:
        copy.wait()


VMEM = pl.BlockSpec(memory_space=pltpu.VMEM)
HBM = pl.BlockSpec(memory_space=pltpu.HBM)
PARAMS = pltpu.CompilerParams(vmem_limit_bytes=32 * 1024 * 1024)
FETCHING = pltpu.CompilerParams(vmem_limit_bytes=60 * 1024 * 1024)


def exchanged(
    split,
    grid_cols,
    pair,
    chain_lengths,
    norm_in_gain,
    norm_in_bias,
    proj_in,
    gate_in,
    norm_out_gain,
    norm_out_bias,
    proj_out,
    gate_out,
):
    rows, cols, channels = pair.shape
    hidden = proj_out.shape[0]
    grid_rows = split[0] * split[1]
    devices = grid_rows * grid_cols
    slots = rows * grid_rows // chain_lengths.shape[0]
    sent, normed = pl.pallas_call(
        functools.partial(mix_kernel, slots),
        out_shape=(
            jax.ShapeDtypeStruct((devices, 2 * rows, LANES), BF16),
            jax.ShapeDtypeStruct((channels, rows * cols), BF16),
        ),
        in_specs=[HBM] * 6,
        out_specs=(HBM, HBM),
        scratch_shapes=[
            pltpu.SMEM(chain_lengths.shape, jnp.int32),
            pltpu.VMEM(pair.shape, BF16),
            pltpu.VMEM((1, channels), F32),
            pltpu.VMEM((1, channels), F32),
            pltpu.VMEM(proj_in.shape, BF16),
            pltpu.VMEM(gate_in.shape, BF16),
            pltpu.VMEM((devices, 2 * rows, LANES), BF16),
            pltpu.VMEM((channels, rows * cols), BF16),
            pltpu.SemaphoreType.DMA((6,)),
            pltpu.SemaphoreType.DMA((1 + devices // 16,)),
        ],
        compiler_params=FETCHING,
        name="mix",
    )(
        chain_lengths,
        pair,
        norm_in_gain.reshape(1, channels),
        norm_in_bias.reshape(1, channels),
        proj_in,
        gate_in,
    )
    order = ("col", "low", "high")
    got = lax.all_to_all(sent, order, 0, 0, tiled=True)
    opened, gain, bias, proj = pl.pallas_call(
        gate_kernel,
        out_shape=(
            jax.ShapeDtypeStruct((rows * cols, channels), F32),
            jax.ShapeDtypeStruct((hidden, LANES), F32),
            jax.ShapeDtypeStruct((hidden, LANES), F32),
            jax.ShapeDtypeStruct(proj_out.shape, BF16),
        ),
        in_specs=[VMEM] + [HBM] * 4,
        out_specs=[VMEM] * 4,
        scratch_shapes=[
            pltpu.VMEM(gate_out.shape, BF16),
            pltpu.VMEM((1, hidden), F32),
            pltpu.VMEM((1, hidden), F32),
            pltpu.SemaphoreType.DMA((4,)),
        ],
        compiler_params=PARAMS,
        name="gate",
    )(normed, gate_out, norm_out_gain.reshape(1, hidden), norm_out_bias.reshape(1, hidden), proj_out)
    got, opened, gain, bias, proj = lax.optimization_barrier((got, opened, gain, bias, proj))
    sums = pl.pallas_call(
        functools.partial(triangle_kernel, split, grid_cols, rows, cols),
        out_shape=jax.ShapeDtypeStruct((devices, rows, LANES), BF16),
        in_specs=[VMEM],
        out_specs=VMEM,
        compiler_params=PARAMS,
        name="triangle",
    )(got)
    mine = lax.all_to_all(sums, order, 0, 0, tiled=True)
    return pl.pallas_call(
        update_kernel,
        out_shape=jax.ShapeDtypeStruct((rows, cols, channels), BF16),
        in_specs=[VMEM] * 5,
        out_specs=HBM,
        scratch_shapes=[
            pltpu.VMEM((rows, cols, channels), BF16),
            pltpu.SemaphoreType.DMA((rows * cols // LANES,)),
        ],
        compiler_params=PARAMS,
        name="update",
    )(mine, opened, gain, bias, proj)


def solution(mesh):
    grid_rows, grid_cols = mesh.shape["row"], mesh.shape["col"]
    split = (grid_rows // 2, 2)
    fine = jax.sharding.Mesh(
        mesh.devices.reshape(split + (grid_cols,)), ("high", "low", "col")
    )

    def fits(rows, cols, channels, hidden):
        devices = grid_rows * grid_cols
        inner = LANES // cols
        return (
            channels == LANES
            and hidden == LANES
            and inner * cols == LANES
            and inner & (inner - 1) == 0
            and inner * devices == hidden
            and rows % 16 == 0
            and rows % inner == 0
            and devices % 16 == 0
        )

    def call(*arrays):
        tokens, others, channels = arrays[0].shape
        hidden = arrays[8].shape[0]
        if fits(tokens // grid_rows, others // grid_cols, channels, hidden):
            return jax.shard_map(
                functools.partial(exchanged, split, grid_cols),
                mesh=fine,
                in_specs=(P(("high", "low"), "col", None),) + (P(),) * 9,
                out_specs=P(("high", "low"), "col", None),
                check_vma=False,
            )(*arrays)
        return jax.shard_map(
            gathered,
            mesh=mesh,
            in_specs=(P("row", "col", None),) + (P(),) * 9,
            out_specs=P("row", "col", None),
            check_vma=False,
        )(*arrays)

    return call
```

```python
import functools
import jax
import jax.numpy as jnp
from jax import lax
from jax.experimental import pallas as pl
from jax.experimental.pallas import tpu as pltpu
from jax.sharding import PartitionSpec as P

LANES = 128
SOME = 16
F32 = jnp.float32
BF16 = jnp.bfloat16


def broadcast(value, axis, source):
    kept = jnp.where(lax.axis_index(axis) == source, value, 0).astype(value.dtype)
    return lax.psum(kept, axis)


def layer_norm(values, gain, bias):
    mean = jnp.mean(values, axis=-1, keepdims=True)
    centered = values - mean
    variance = jnp.mean(centered * centered, axis=-1, keepdims=True)
    return centered * lax.rsqrt(variance + 1e-05) * gain + bias


def token_valid(chain_lengths, tokens_idx, slots):
    chain = tokens_idx // slots
    position = tokens_idx % slots
    chain_ids = jnp.arange(chain_lengths.shape[0], dtype=jnp.int32)
    length_of = jnp.sum(
        jnp.where(chain[:, None] == chain_ids[None, :], chain_lengths[None, :], 0), axis=1
    )
    return (position < length_of).astype(jnp.float32)


def gathered(
    pair,
    chain_lengths,
    norm_in_gain,
    norm_in_bias,
    proj_in,
    gate_in,
    norm_out_gain,
    norm_out_bias,
    proj_out,
    gate_out,
):
    row_count = pair.shape[0]
    col_count = pair.shape[1]
    channels = pair.shape[2]
    hidden = proj_out.shape[0]
    row_index = lax.axis_index("row")
    col_index = lax.axis_index("col")
    slots = row_count * lax.axis_size("row") // chain_lengths.shape[0]
    valid_rows = token_valid(
        chain_lengths, row_index * row_count + jnp.arange(row_count, dtype=jnp.int32), slots
    )
    valid_cols = token_valid(
        chain_lengths, col_index * col_count + jnp.arange(col_count, dtype=jnp.int32), slots
    )
    pair_mask = valid_rows[:, None] * valid_cols[None, :]
    normed = layer_norm(pair.astype(jnp.float32), norm_in_gain, norm_in_bias).astype(jnp.bfloat16)
    flat = normed.reshape(-1, channels)
    values = jnp.dot(flat, proj_in, preferred_element_type=jnp.float32)
    gates = jnp.dot(flat, gate_in, preferred_element_type=jnp.float32)
    mixed = (jax.nn.sigmoid(gates) * values).reshape(row_count, col_count, 2 * hidden) * pair_mask[
        :, :, None
    ]
    left_tile = mixed[:, :, :hidden].astype(jnp.bfloat16)
    right_tile = mixed[:, :, hidden:].astype(jnp.bfloat16)
    ratio = lax.axis_size("row") // lax.axis_size("col")
    right_full = lax.all_gather(right_tile, "col", axis=1, tiled=True)
    received = []
    for part in range(ratio):
        received.append(broadcast(right_full, "row", col_index * ratio + part))
    right_mine = jnp.concatenate(received, axis=0)
    triangle = jnp.einsum(
        "ikh,jkh->ijh",
        lax.all_gather(left_tile, "col", axis=1, tiled=True),
        right_mine,
        preferred_element_type=jnp.float32,
    )
    tri_normed = layer_norm(triangle, norm_out_gain, norm_out_bias).astype(jnp.bfloat16)
    projected = jnp.dot(
        tri_normed.reshape(-1, hidden), proj_out, preferred_element_type=jnp.float32
    )
    gate = jax.nn.sigmoid(jnp.dot(flat, gate_out, preferred_element_type=jnp.float32))
    return (gate * projected).astype(jnp.bfloat16).reshape(row_count, col_count, channels)


def iota2(shape):
    return (
        lax.broadcasted_iota(jnp.int32, shape, 0),
        lax.broadcasted_iota(jnp.int32, shape, 1),
    )


def one_hot(condition):
    return jnp.where(condition, 1.0, 0.0).astype(BF16)


def dot(a, b, a_dim=1, b_dim=0):
    return lax.dot_general(a, b, (((a_dim,), (b_dim,)), ((), ())), preferred_element_type=F32)


def over(value, size):
    if size & (size - 1):
        return value // size
    return lax.shift_right_logical(value, jnp.full_like(value, size.bit_length() - 1))


def rest(value, size):
    return value % size if size & (size - 1) else value & (size - 1)


def over(value, size):
    if size & (size - 1):
        return value // size
    return lax.shift_right_logical(value, jnp.full_like(value, size.bit_length() - 1))


def rest(value, size):
    return value % size if size & (size - 1) else value & (size - 1)


def fetch(sources, targets, sems):
    copies = [
        pltpu.make_async_copy(source, target, sems.at[n])
        for n, (source, target) in enumerate(zip(sources, targets))
    ]
    for copy in copies:
        copy.start()
    return copies


def sigmoid(halved):
    return 0.5 + 0.5 * jnp.tanh(halved)


def exchange_blocks(arrays, cols):
    lane = over(lax.broadcasted_iota(jnp.int32, (1, LANES), 1), cols)
    arrays, step = list(arrays), 1
    while step < len(arrays):
        upper = lane & step != 0
        for n in range(len(arrays)):
            if n // step % 2 == 0:
                a, b = arrays[n], arrays[n + step]
                arrays[n] = jnp.where(upper, pltpu.roll(b, step * cols, 1), a)
                arrays[n + step] = jnp.where(upper, b, pltpu.roll(a, LANES - step * cols, 1))
        step *= 2
    return arrays


def orders_kernel(order_ref, eye_ref):
    out, source = iota2(order_ref.shape)
    order_ref[...] = one_hot(
        (over(out, SOME) == rest(source, SOME)) & (rest(out, SOME) == over(source, SOME))
    )
    a, b = iota2(eye_ref.shape)
    eye_ref[...] = one_hot(a == b)


def prepare_kernel(slots, cols, chain_ref, *refs):
    *rows_in, mask_ref = refs[:5]
    cell = lax.broadcasted_iota(jnp.int32, mask_ref.shape, 1)

    def valid(token):
        length = jnp.zeros_like(token)
        for chain in range(chain_ref.shape[0]):
            length = jnp.where(over(token, slots) == chain, chain_ref[chain], length)
        return rest(token, slots) < length

    rows = mask_ref.shape[1] // cols
    row_ok = valid(lax.axis_index(("high", "low")) * rows + over(cell, cols))
    col_ok = valid(lax.axis_index("col") * cols + rest(cell, cols))
    mask_ref[...] = jnp.where(row_ok & col_ok, 1.0, 0.0)
    a, b = iota2((LANES, LANES))
    for source, target in zip(rows_in, refs[5:]):
        column = jnp.sum(jnp.where(a == b, source[...], 0.0), axis=1, keepdims=True)
        target[...] = jnp.broadcast_to(column, target.shape)


def mix_kernel(
    order_ref,
    eye_ref,
    mask_ref,
    pair_ref,
    gain_ref,
    bias_ref,
    proj_ref,
    gate_ref,
    sent_ref,
    normed_ref,
):
    rows, cols, channels = pair_ref.shape
    hidden = proj_ref.shape[1] // 2
    cells = rows * cols
    inner = LANES // cols
    groups = rows // inner
    chunks = sent_ref.shape[0]
    flat = dot(eye_ref[...], pair_ref[...].reshape(cells, channels), 1, 1)
    centered = flat - jnp.mean(flat, axis=0, keepdims=True)
    variance = jnp.mean(centered * centered, axis=0, keepdims=True)
    scaled = centered * lax.rsqrt(variance + 1e-05)
    gain, bias = gain_ref[...], bias_ref[...]
    normed = jnp.concatenate(
        [
            (scaled[:, g * LANES : (g + 1) * LANES] * gain + bias).astype(BF16)
            for g in range(groups)
        ],
        axis=1,
    )
    normed_ref[...] = normed

    values = dot(proj_ref[...], normed, 0, 0)
    gates = dot(gate_ref[...] * 0.5, normed, 0, 0)
    mixed = (sigmoid(gates) * values * mask_ref[...]).astype(BF16)

    by_row = []
    for side in range(2):
        lines = []
        for g in range(groups):
            lines += exchange_blocks(
                [
                    mixed[
                        side * hidden + n * chunks : side * hidden + (n + 1) * chunks,
                        g * LANES : (g + 1) * LANES,
                    ]
                    for n in range(inner)
                ],
                cols,
            )
        by_row.append(lines)
    order = order_ref[...]
    for part in range(chunks // SOME):
        for side in range(2):
            stack = jnp.concatenate(
                [line[part * SOME : (part + 1) * SOME] for line in by_row[side]], axis=0
            )
            sent_ref[part * SOME : (part + 1) * SOME, side * rows : (side + 1) * rows] = (
                dot(order, stack).astype(BF16).reshape(SOME, rows, LANES)
            )


def triangle_kernel(split, grid_cols, rows, cols, got_ref, sent_ref):
    inner = LANES // cols

    def place(r, c):
        z, y = r // split[1], r % split[1]
        return (c * split[1] + y) * split[0] + z

    def side(which):
        return jnp.concatenate(
            [
                jnp.concatenate(
                    [
                        got_ref[place(r, c), which * rows : (which + 1) * rows]
                        for r in range(split[0] * split[1])
                    ],
                    axis=0,
                )
                for c in range(grid_cols)
            ],
            axis=1,
        )

    left, right = side(0), side(1)
    lane = lax.broadcasted_iota(jnp.int32, (1, grid_cols * LANES), 1)
    by_channel = [right * one_hot(over(rest(lane, LANES), cols) == n) for n in range(inner)]
    right_by = jnp.concatenate(
        [
            by_channel[n][c * cols : (c + 1) * cols]
            for c in range(grid_cols)
            for n in range(inner)
        ],
        axis=0,
    )
    sums = dot(left, right_by, 1, 1).astype(BF16)
    for c in range(grid_cols):
        for r in range(split[0] * split[1]):
            sent_ref[place(r, c)] = sums[r * rows : (r + 1) * rows, c * LANES : (c + 1) * LANES]


def update_kernel(
    got_ref,
    order_ref,
    normed_ref,
    gain_ref,
    bias_ref,
    proj_ref,
    gate_ref,
    out_hbm,
    out_ref,
    out_sems,
):
    rows, cols, channels = out_ref.shape
    chunks = got_ref.shape[0]
    inner = LANES // cols
    groups = rows // inner
    order = order_ref[...]
    parts = [
        dot(order, got_ref[part * SOME : (part + 1) * SOME].reshape(SOME * rows, LANES)).astype(BF16)
        for part in range(chunks // SOME)
    ]
    lines = [
        jnp.concatenate([part[row * SOME : (row + 1) * SOME] for part in parts], axis=0)
        for row in range(rows)
    ]
    gain, bias = gain_ref[...], bias_ref[...]
    opened = sigmoid(dot(normed_ref[...], gate_ref[...] * 0.5, 0, 0))
    results = []
    for g in range(groups):
        values = jnp.concatenate(
            exchange_blocks(lines[g * inner : (g + 1) * inner], cols), axis=0
        ).astype(F32)
        mean = jnp.mean(values, axis=0, keepdims=True)
        centered = values - mean
        variance = jnp.mean(centered * centered, axis=0, keepdims=True)
        tri_normed = (centered * lax.rsqrt(variance + 1e-05) * gain + bias).astype(BF16)
        projected = dot(tri_normed, proj_ref[...], 0, 0)
        update = (opened[g * LANES : (g + 1) * LANES] * projected).astype(BF16)
        here = pl.ds(g * inner, inner)
        out_ref[here] = update.reshape(inner, cols, channels)
        results.append(pltpu.make_async_copy(out_ref.at[here], out_hbm.at[here], out_sems.at[g]))
        results[-1].start()
    for copy in results:
        copy.wait()


VMEM = pl.BlockSpec(memory_space=pltpu.VMEM)
SMEM = pl.BlockSpec(memory_space=pltpu.SMEM)
HBM = pl.BlockSpec(memory_space=pltpu.HBM)
PARAMS = pltpu.CompilerParams(vmem_limit_bytes=32 * 1024 * 1024)


def exchanged(
    split,
    grid_cols,
    pair,
    chain_lengths,
    norm_in_gain,
    norm_in_bias,
    proj_in,
    gate_in,
    norm_out_gain,
    norm_out_bias,
    proj_out,
    gate_out,
):
    rows, cols, channels = pair.shape
    hidden = proj_out.shape[0]
    grid_rows = split[0] * split[1]
    devices = grid_rows * grid_cols
    slots = rows * grid_rows // chain_lengths.shape[0]
    order, eye = pl.pallas_call(
        orders_kernel,
        out_shape=(
            jax.ShapeDtypeStruct((SOME * SOME, SOME * SOME), BF16),
            jax.ShapeDtypeStruct((LANES, LANES), BF16),
        ),
        out_specs=[VMEM] * 2,
        compiler_params=PARAMS,
        cost_estimate=pl.CostEstimate(flops=10**9, bytes_accessed=10**6, transcendentals=0),
        name="orders",
    )()
    square = jax.ShapeDtypeStruct((LANES, LANES), F32)
    mask, *columns = pl.pallas_call(
        functools.partial(prepare_kernel, slots, cols),
        out_shape=(jax.ShapeDtypeStruct((1, rows * cols), F32),) + (square,) * 4,
        in_specs=[SMEM] + [VMEM] * 4,
        out_specs=[VMEM] * 5,
        compiler_params=PARAMS,
        name="prepare",
    )(
        chain_lengths,
        *(
            row.reshape(1, LANES)
            for row in (norm_in_gain, norm_in_bias, norm_out_gain, norm_out_bias)
        ),
    )
    sent, normed = pl.pallas_call(
        mix_kernel,
        out_shape=(
            jax.ShapeDtypeStruct((devices, 2 * rows, LANES), BF16),
            jax.ShapeDtypeStruct((channels, rows * cols), BF16),
        ),
        in_specs=[VMEM] * 8,
        out_specs=(VMEM, VMEM),
        compiler_params=PARAMS,
        name="mix",
    )(order, eye, mask, pair, *columns[:2], proj_in, gate_in)
    axes = ("col", "low", "high")
    got = lax.all_to_all(sent, axes, 0, 0, tiled=True)
    sums = pl.pallas_call(
        functools.partial(triangle_kernel, split, grid_cols, rows, cols),
        out_shape=jax.ShapeDtypeStruct((devices, rows, LANES), BF16),
        in_specs=[VMEM],
        out_specs=VMEM,
        compiler_params=PARAMS,
        name="triangle",
    )(got)
    mine = lax.all_to_all(sums, axes, 0, 0, tiled=True)
    return pl.pallas_call(
        update_kernel,
        out_shape=jax.ShapeDtypeStruct((rows, cols, channels), BF16),
        in_specs=[VMEM] * 7,
        out_specs=HBM,
        scratch_shapes=[
            pltpu.VMEM((rows, cols, channels), BF16),
            pltpu.SemaphoreType.DMA((rows * cols // LANES,)),
        ],
        compiler_params=PARAMS,
        name="update",
    )(mine, order, normed, *columns[2:], proj_out, gate_out)


def solution(mesh):
    grid_rows, grid_cols = mesh.shape["row"], mesh.shape["col"]
    split = (grid_rows // 2, 2)
    fine = jax.sharding.Mesh(
        mesh.devices.reshape(split + (grid_cols,)), ("high", "low", "col")
    )

    def fits(rows, cols, channels, hidden):
        devices = grid_rows * grid_cols
        inner = LANES // cols
        return (
            channels == LANES
            and hidden == LANES
            and inner * cols == LANES
            and inner & (inner - 1) == 0
            and inner * devices == hidden
            and rows == SOME
            and rows % inner == 0
            and devices % SOME == 0
        )

    def call(*arrays):
        tokens, others, channels = arrays[0].shape
        hidden = arrays[8].shape[0]
        if fits(tokens // grid_rows, others // grid_cols, channels, hidden):
            return jax.shard_map(
                functools.partial(exchanged, split, grid_cols),
                mesh=fine,
                in_specs=(P(("high", "low"), "col", None),) + (P(),) * 9,
                out_specs=P(("high", "low"), "col", None),
                check_vma=False,
            )(*arrays)
        return jax.shard_map(
            gathered,
            mesh=mesh,
            in_specs=(P("row", "col", None),) + (P(),) * 9,
            out_specs=P("row", "col", None),
            check_vma=False,
        )(*arrays)

    return call
```

```python
import functools
import jax
import jax.numpy as jnp
from jax import lax
from jax.experimental import pallas as pl
from jax.experimental.pallas import tpu as pltpu
from jax.sharding import PartitionSpec as P

LANES = 128
SOME = 16
F32 = jnp.float32
BF16 = jnp.bfloat16


def broadcast(value, axis, source):
    kept = jnp.where(lax.axis_index(axis) == source, value, 0).astype(value.dtype)
    return lax.psum(kept, axis)


def layer_norm(values, gain, bias):
    mean = jnp.mean(values, axis=-1, keepdims=True)
    centered = values - mean
    variance = jnp.mean(centered * centered, axis=-1, keepdims=True)
    return centered * lax.rsqrt(variance + 1e-05) * gain + bias


def token_valid(chain_lengths, tokens_idx, slots):
    chain = tokens_idx // slots
    position = tokens_idx % slots
    chain_ids = jnp.arange(chain_lengths.shape[0], dtype=jnp.int32)
    length_of = jnp.sum(
        jnp.where(chain[:, None] == chain_ids[None, :], chain_lengths[None, :], 0), axis=1
    )
    return (position < length_of).astype(jnp.float32)


def gathered(
    pair,
    chain_lengths,
    norm_in_gain,
    norm_in_bias,
    proj_in,
    gate_in,
    norm_out_gain,
    norm_out_bias,
    proj_out,
    gate_out,
):
    row_count = pair.shape[0]
    col_count = pair.shape[1]
    channels = pair.shape[2]
    hidden = proj_out.shape[0]
    row_index = lax.axis_index("row")
    col_index = lax.axis_index("col")
    slots = row_count * lax.axis_size("row") // chain_lengths.shape[0]
    valid_rows = token_valid(
        chain_lengths, row_index * row_count + jnp.arange(row_count, dtype=jnp.int32), slots
    )
    valid_cols = token_valid(
        chain_lengths, col_index * col_count + jnp.arange(col_count, dtype=jnp.int32), slots
    )
    pair_mask = valid_rows[:, None] * valid_cols[None, :]
    normed = layer_norm(pair.astype(jnp.float32), norm_in_gain, norm_in_bias).astype(jnp.bfloat16)
    flat = normed.reshape(-1, channels)
    values = jnp.dot(flat, proj_in, preferred_element_type=jnp.float32)
    gates = jnp.dot(flat, gate_in, preferred_element_type=jnp.float32)
    mixed = (jax.nn.sigmoid(gates) * values).reshape(row_count, col_count, 2 * hidden) * pair_mask[
        :, :, None
    ]
    left_tile = mixed[:, :, :hidden].astype(jnp.bfloat16)
    right_tile = mixed[:, :, hidden:].astype(jnp.bfloat16)
    ratio = lax.axis_size("row") // lax.axis_size("col")
    right_full = lax.all_gather(right_tile, "col", axis=1, tiled=True)
    received = []
    for part in range(ratio):
        received.append(broadcast(right_full, "row", col_index * ratio + part))
    right_mine = jnp.concatenate(received, axis=0)
    triangle = jnp.einsum(
        "ikh,jkh->ijh",
        lax.all_gather(left_tile, "col", axis=1, tiled=True),
        right_mine,
        preferred_element_type=jnp.float32,
    )
    tri_normed = layer_norm(triangle, norm_out_gain, norm_out_bias).astype(jnp.bfloat16)
    projected = jnp.dot(
        tri_normed.reshape(-1, hidden), proj_out, preferred_element_type=jnp.float32
    )
    gate = jax.nn.sigmoid(jnp.dot(flat, gate_out, preferred_element_type=jnp.float32))
    return (gate * projected).astype(jnp.bfloat16).reshape(row_count, col_count, channels)


def iota2(shape):
    return (
        lax.broadcasted_iota(jnp.int32, shape, 0),
        lax.broadcasted_iota(jnp.int32, shape, 1),
    )


def one_hot(condition):
    return jnp.where(condition, 1.0, 0.0).astype(BF16)


def dot(a, b, a_dim=1, b_dim=0):
    return lax.dot_general(a, b, (((a_dim,), (b_dim,)), ((), ())), preferred_element_type=F32)


def over(value, size):
    if size & (size - 1):
        return value // size
    return lax.shift_right_logical(value, jnp.full_like(value, size.bit_length() - 1))


def rest(value, size):
    return value % size if size & (size - 1) else value & (size - 1)


def over(value, size):
    if size & (size - 1):
        return value // size
    return lax.shift_right_logical(value, jnp.full_like(value, size.bit_length() - 1))


def rest(value, size):
    return value % size if size & (size - 1) else value & (size - 1)


def fetch(sources, targets, sems):
    copies = [
        pltpu.make_async_copy(source, target, sems.at[n])
        for n, (source, target) in enumerate(zip(sources, targets))
    ]
    for copy in copies:
        copy.start()
    return copies


def sigmoid(halved):
    return 0.5 + 0.5 * jnp.tanh(halved)


def exchange_blocks(arrays, cols):
    lane = over(lax.broadcasted_iota(jnp.int32, (1, LANES), 1), cols)
    arrays, step = list(arrays), 1
    while step < len(arrays):
        upper = lane & step != 0
        for n in range(len(arrays)):
            if n // step % 2 == 0:
                a, b = arrays[n], arrays[n + step]
                arrays[n] = jnp.where(upper, pltpu.roll(b, step * cols, 1), a)
                arrays[n + step] = jnp.where(upper, b, pltpu.roll(a, LANES - step * cols, 1))
        step *= 2
    return arrays


def orders_kernel(order_ref, eye_ref):
    out, source = iota2(order_ref.shape)
    order_ref[...] = one_hot(
        (over(out, SOME) == rest(source, SOME)) & (rest(out, SOME) == over(source, SOME))
    )
    a, b = iota2(eye_ref.shape)
    eye_ref[...] = one_hot(a == b)


def column(row):
    a, b = iota2((LANES, LANES))
    return jnp.sum(jnp.where(a == b, row, 0.0), axis=1, keepdims=True)


def cell_mask(lengths, slots, rows, cols):
    cell = lax.broadcasted_iota(jnp.int32, (1, rows * cols), 1)

    def valid(token):
        length = jnp.zeros_like(token)
        for chain in range(lengths.shape[1]):
            length = jnp.where(
                over(token, slots) == chain, lengths[:, chain : chain + 1], length
            )
        return rest(token, slots) < length

    row_ok = valid(lax.axis_index(("high", "low")) * rows + over(cell, cols))
    col_ok = valid(lax.axis_index("col") * cols + rest(cell, cols))
    return jnp.where(row_ok & col_ok, 1.0, 0.0)


def mix_kernel(
    slots,
    order_ref,
    eye_ref,
    chain_ref,
    pair_ref,
    gain_ref,
    bias_ref,
    proj_ref,
    gate_ref,
    last_gain_ref,
    last_bias_ref,
    sent_ref,
    normed_ref,
    last_gain_out,
    last_bias_out,
):
    rows, cols, channels = pair_ref.shape
    hidden = proj_ref.shape[1] // 2
    cells = rows * cols
    inner = LANES // cols
    groups = rows // inner
    chunks = sent_ref.shape[0]
    flat = dot(eye_ref[...], pair_ref[...].reshape(cells, channels), 1, 1)
    centered = flat - jnp.mean(flat, axis=0, keepdims=True)
    variance = jnp.mean(centered * centered, axis=0, keepdims=True)
    gain, bias = column(gain_ref[...]), column(bias_ref[...])
    normed = (centered * lax.rsqrt(variance + 1e-05) * gain + bias).astype(BF16)
    normed_ref[...] = normed
    for source, target in ((last_gain_ref, last_gain_out), (last_bias_ref, last_bias_out)):
        target[...] = jnp.broadcast_to(column(source[...]), target.shape)

    values = dot(proj_ref[...], normed, 0, 0)
    gates = dot(gate_ref[...] * 0.5, normed, 0, 0)
    mask = cell_mask(chain_ref[...], slots, rows, cols)
    mixed = (sigmoid(gates) * values * mask).astype(BF16)

    by_row = []
    for side in range(2):
        lines = []
        for g in range(groups):
            lines += exchange_blocks(
                [
                    mixed[
                        side * hidden + n * chunks : side * hidden + (n + 1) * chunks,
                        g * LANES : (g + 1) * LANES,
                    ]
                    for n in range(inner)
                ],
                cols,
            )
        by_row.append(lines)
    order = order_ref[...]
    for part in range(chunks // SOME):
        for side in range(2):
            stack = jnp.concatenate(
                [line[part * SOME : (part + 1) * SOME] for line in by_row[side]], axis=0
            )
            sent_ref[part * SOME : (part + 1) * SOME, side * rows : (side + 1) * rows] = (
                dot(order, stack).astype(BF16).reshape(SOME, rows, LANES)
            )


def triangle_kernel(split, grid_cols, rows, cols, got_ref, sent_ref):
    inner = LANES // cols

    def place(r, c):
        z, y = r // split[1], r % split[1]
        return (c * split[1] + y) * split[0] + z

    def side(which):
        return jnp.concatenate(
            [
                jnp.concatenate(
                    [
                        got_ref[place(r, c), which * rows : (which + 1) * rows]
                        for r in range(split[0] * split[1])
                    ],
                    axis=0,
                )
                for c in range(grid_cols)
            ],
            axis=1,
        )

    left, right = side(0), side(1)
    lane = lax.broadcasted_iota(jnp.int32, (1, grid_cols * LANES), 1)
    by_channel = [right * one_hot(over(rest(lane, LANES), cols) == n) for n in range(inner)]
    right_by = jnp.concatenate(
        [
            by_channel[n][c * cols : (c + 1) * cols]
            for c in range(grid_cols)
            for n in range(inner)
        ],
        axis=0,
    )
    sums = dot(left, right_by, 1, 1).astype(BF16)
    for c in range(grid_cols):
        for r in range(split[0] * split[1]):
            sent_ref[place(r, c)] = sums[r * rows : (r + 1) * rows, c * LANES : (c + 1) * LANES]


def update_kernel(
    got_ref,
    order_ref,
    normed_ref,
    gain_ref,
    bias_ref,
    proj_ref,
    gate_ref,
    out_hbm,
    out_ref,
    out_sems,
):
    rows, cols, channels = out_ref.shape
    chunks = got_ref.shape[0]
    inner = LANES // cols
    groups = rows // inner
    order = order_ref[...]
    parts = [
        dot(order, got_ref[part * SOME : (part + 1) * SOME].reshape(SOME * rows, LANES)).astype(BF16)
        for part in range(chunks // SOME)
    ]
    lines = [
        jnp.concatenate([part[row * SOME : (row + 1) * SOME] for part in parts], axis=0)
        for row in range(rows)
    ]
    gain, bias = gain_ref[...], bias_ref[...]
    opened = sigmoid(dot(normed_ref[...], gate_ref[...] * 0.5, 0, 0))
    results = []
    for g in range(groups):
        values = jnp.concatenate(
            exchange_blocks(lines[g * inner : (g + 1) * inner], cols), axis=0
        ).astype(F32)
        mean = jnp.mean(values, axis=0, keepdims=True)
        centered = values - mean
        variance = jnp.mean(centered * centered, axis=0, keepdims=True)
        tri_normed = (centered * lax.rsqrt(variance + 1e-05) * gain + bias).astype(BF16)
        projected = dot(tri_normed, proj_ref[...], 0, 0)
        update = (opened[g * LANES : (g + 1) * LANES] * projected).astype(BF16)
        here = pl.ds(g * inner, inner)
        out_ref[here] = update.reshape(inner, cols, channels)
        results.append(pltpu.make_async_copy(out_ref.at[here], out_hbm.at[here], out_sems.at[g]))
        results[-1].start()
    for copy in results:
        copy.wait()


VMEM = pl.BlockSpec(memory_space=pltpu.VMEM)
HBM = pl.BlockSpec(memory_space=pltpu.HBM)
PARAMS = pltpu.CompilerParams(vmem_limit_bytes=32 * 1024 * 1024)


def exchanged(
    split,
    grid_cols,
    pair,
    chain_lengths,
    norm_in_gain,
    norm_in_bias,
    proj_in,
    gate_in,
    norm_out_gain,
    norm_out_bias,
    proj_out,
    gate_out,
):
    rows, cols, channels = pair.shape
    hidden = proj_out.shape[0]
    grid_rows = split[0] * split[1]
    devices = grid_rows * grid_cols
    slots = rows * grid_rows // chain_lengths.shape[0]
    order, eye = pl.pallas_call(
        orders_kernel,
        out_shape=(
            jax.ShapeDtypeStruct((SOME * SOME, SOME * SOME), BF16),
            jax.ShapeDtypeStruct((LANES, LANES), BF16),
        ),
        out_specs=[VMEM] * 2,
        compiler_params=PARAMS,
        cost_estimate=pl.CostEstimate(flops=10**9, bytes_accessed=10**6, transcendentals=0),
        name="orders",
    )()
    square = jax.ShapeDtypeStruct((LANES, LANES), F32)
    sent, normed, last_gain, last_bias = pl.pallas_call(
        functools.partial(mix_kernel, slots),
        out_shape=(
            jax.ShapeDtypeStruct((devices, 2 * rows, LANES), BF16),
            jax.ShapeDtypeStruct((channels, rows * cols), BF16),
            square,
            square,
        ),
        in_specs=[VMEM] * 10,
        out_specs=[VMEM] * 4,
        compiler_params=PARAMS,
        name="mix",
    )(
        order,
        eye,
        chain_lengths.reshape(1, -1),
        pair,
        norm_in_gain.reshape(1, LANES),
        norm_in_bias.reshape(1, LANES),
        proj_in,
        gate_in,
        norm_out_gain.reshape(1, LANES),
        norm_out_bias.reshape(1, LANES),
    )
    axes = ("col", "low", "high")
    got = lax.all_to_all(sent, axes, 0, 0, tiled=True)
    sums = pl.pallas_call(
        functools.partial(triangle_kernel, split, grid_cols, rows, cols),
        out_shape=jax.ShapeDtypeStruct((devices, rows, LANES), BF16),
        in_specs=[VMEM],
        out_specs=VMEM,
        compiler_params=PARAMS,
        name="triangle",
    )(got)
    mine = lax.all_to_all(sums, axes, 0, 0, tiled=True)
    return pl.pallas_call(
        update_kernel,
        out_shape=jax.ShapeDtypeStruct((rows, cols, channels), BF16),
        in_specs=[VMEM] * 7,
        out_specs=HBM,
        scratch_shapes=[
            pltpu.VMEM((rows, cols, channels), BF16),
            pltpu.SemaphoreType.DMA((rows * cols // LANES,)),
        ],
        compiler_params=PARAMS,
        name="update",
    )(mine, order, normed, last_gain, last_bias, proj_out, gate_out)


def solution(mesh):
    grid_rows, grid_cols = mesh.shape["row"], mesh.shape["col"]
    split = (grid_rows // 2, 2)
    fine = jax.sharding.Mesh(
        mesh.devices.reshape(split + (grid_cols,)), ("high", "low", "col")
    )

    def fits(rows, cols, channels, hidden):
        devices = grid_rows * grid_cols
        inner = LANES // cols
        return (
            channels == LANES
            and hidden == LANES
            and inner * cols == LANES
            and inner & (inner - 1) == 0
            and inner * devices == hidden
            and rows == SOME
            and rows % inner == 0
            and devices % SOME == 0
        )

    def call(*arrays):
        tokens, others, channels = arrays[0].shape
        hidden = arrays[8].shape[0]
        if fits(tokens // grid_rows, others // grid_cols, channels, hidden):
            return jax.shard_map(
                functools.partial(exchanged, split, grid_cols),
                mesh=fine,
                in_specs=(P(("high", "low"), "col", None),) + (P(),) * 9,
                out_specs=P(("high", "low"), "col", None),
                check_vma=False,
            )(*arrays)
        return jax.shard_map(
            gathered,
            mesh=mesh,
            in_specs=(P("row", "col", None),) + (P(),) * 9,
            out_specs=P("row", "col", None),
            check_vma=False,
        )(*arrays)

    return call
```

```python
import functools
import jax
import jax.numpy as jnp
from jax import lax
from jax.experimental import pallas as pl
from jax.experimental.pallas import tpu as pltpu
from jax.sharding import PartitionSpec as P

LANES = 128
SOME = 16
F32 = jnp.float32
BF16 = jnp.bfloat16


def broadcast(value, axis, source):
    kept = jnp.where(lax.axis_index(axis) == source, value, 0).astype(value.dtype)
    return lax.psum(kept, axis)


def layer_norm(values, gain, bias):
    mean = jnp.mean(values, axis=-1, keepdims=True)
    centered = values - mean
    variance = jnp.mean(centered * centered, axis=-1, keepdims=True)
    return centered * lax.rsqrt(variance + 1e-05) * gain + bias


def token_valid(chain_lengths, tokens_idx, slots):
    chain = tokens_idx // slots
    position = tokens_idx % slots
    chain_ids = jnp.arange(chain_lengths.shape[0], dtype=jnp.int32)
    length_of = jnp.sum(
        jnp.where(chain[:, None] == chain_ids[None, :], chain_lengths[None, :], 0), axis=1
    )
    return (position < length_of).astype(jnp.float32)


def gathered(
    pair,
    chain_lengths,
    norm_in_gain,
    norm_in_bias,
    proj_in,
    gate_in,
    norm_out_gain,
    norm_out_bias,
    proj_out,
    gate_out,
):
    row_count = pair.shape[0]
    col_count = pair.shape[1]
    channels = pair.shape[2]
    hidden = proj_out.shape[0]
    row_index = lax.axis_index("row")
    col_index = lax.axis_index("col")
    slots = row_count * lax.axis_size("row") // chain_lengths.shape[0]
    valid_rows = token_valid(
        chain_lengths, row_index * row_count + jnp.arange(row_count, dtype=jnp.int32), slots
    )
    valid_cols = token_valid(
        chain_lengths, col_index * col_count + jnp.arange(col_count, dtype=jnp.int32), slots
    )
    pair_mask = valid_rows[:, None] * valid_cols[None, :]
    normed = layer_norm(pair.astype(jnp.float32), norm_in_gain, norm_in_bias).astype(jnp.bfloat16)
    flat = normed.reshape(-1, channels)
    values = jnp.dot(flat, proj_in, preferred_element_type=jnp.float32)
    gates = jnp.dot(flat, gate_in, preferred_element_type=jnp.float32)
    mixed = (jax.nn.sigmoid(gates) * values).reshape(row_count, col_count, 2 * hidden) * pair_mask[
        :, :, None
    ]
    left_tile = mixed[:, :, :hidden].astype(jnp.bfloat16)
    right_tile = mixed[:, :, hidden:].astype(jnp.bfloat16)
    ratio = lax.axis_size("row") // lax.axis_size("col")
    right_full = lax.all_gather(right_tile, "col", axis=1, tiled=True)
    received = []
    for part in range(ratio):
        received.append(broadcast(right_full, "row", col_index * ratio + part))
    right_mine = jnp.concatenate(received, axis=0)
    triangle = jnp.einsum(
        "ikh,jkh->ijh",
        lax.all_gather(left_tile, "col", axis=1, tiled=True),
        right_mine,
        preferred_element_type=jnp.float32,
    )
    tri_normed = layer_norm(triangle, norm_out_gain, norm_out_bias).astype(jnp.bfloat16)
    projected = jnp.dot(
        tri_normed.reshape(-1, hidden), proj_out, preferred_element_type=jnp.float32
    )
    gate = jax.nn.sigmoid(jnp.dot(flat, gate_out, preferred_element_type=jnp.float32))
    return (gate * projected).astype(jnp.bfloat16).reshape(row_count, col_count, channels)


def iota2(shape):
    return (
        lax.broadcasted_iota(jnp.int32, shape, 0),
        lax.broadcasted_iota(jnp.int32, shape, 1),
    )


def one_hot(condition):
    return jnp.where(condition, 1.0, 0.0).astype(BF16)


def dot(a, b, a_dim=1, b_dim=0):
    return lax.dot_general(a, b, (((a_dim,), (b_dim,)), ((), ())), preferred_element_type=F32)


def over(value, size):
    if size & (size - 1):
        return value // size
    return lax.shift_right_logical(value, jnp.full_like(value, size.bit_length() - 1))


def rest(value, size):
    return value % size if size & (size - 1) else value & (size - 1)


def over(value, size):
    if size & (size - 1):
        return value // size
    return lax.shift_right_logical(value, jnp.full_like(value, size.bit_length() - 1))


def rest(value, size):
    return value % size if size & (size - 1) else value & (size - 1)


def fetch(sources, targets, sems):
    copies = [
        pltpu.make_async_copy(source, target, sems.at[n])
        for n, (source, target) in enumerate(zip(sources, targets))
    ]
    for copy in copies:
        copy.start()
    return copies


def sigmoid(halved):
    return 0.5 + 0.5 * jnp.tanh(halved)


def exchange_blocks(arrays, cols):
    lane = over(lax.broadcasted_iota(jnp.int32, (1, LANES), 1), cols)
    arrays, step = list(arrays), 1
    while step < len(arrays):
        upper = lane & step != 0
        for n in range(len(arrays)):
            if n // step % 2 == 0:
                a, b = arrays[n], arrays[n + step]
                arrays[n] = jnp.where(upper, pltpu.roll(b, step * cols, 1), a)
                arrays[n + step] = jnp.where(upper, b, pltpu.roll(a, LANES - step * cols, 1))
        step *= 2
    return arrays


def order_kernel(order_ref):
    out, source = iota2(order_ref.shape)
    order_ref[...] = one_hot(
        (over(out, SOME) == rest(source, SOME)) & (rest(out, SOME) == over(source, SOME))
    )


def column(row):
    a, b = iota2((LANES, LANES))
    return jnp.sum(jnp.where(a == b, row, 0.0), axis=1, keepdims=True)


def cell_mask(lengths, slots, rows, cols):
    cell = lax.broadcasted_iota(jnp.int32, (1, rows * cols), 1)

    def valid(token):
        length = jnp.zeros_like(token)
        for chain in range(lengths.shape[1]):
            length = jnp.where(
                over(token, slots) == chain, lengths[:, chain : chain + 1], length
            )
        return rest(token, slots) < length

    row_ok = valid(lax.axis_index(("high", "low")) * rows + over(cell, cols))
    col_ok = valid(lax.axis_index("col") * cols + rest(cell, cols))
    return jnp.where(row_ok & col_ok, 1.0, 0.0)


def mix_kernel(
    slots,
    order_ref,
    chain_ref,
    pair_ref,
    gain_ref,
    bias_ref,
    proj_ref,
    gate_ref,
    last_gain_ref,
    last_bias_ref,
    sent_ref,
    normed_ref,
    last_gain_out,
    last_bias_out,
):
    rows, cols, channels = pair_ref.shape
    hidden = proj_ref.shape[1] // 2
    cells = rows * cols
    inner = LANES // cols
    groups = rows // inner
    chunks = sent_ref.shape[0]
    flat = pair_ref[...].reshape(cells, channels).astype(F32)
    normed = layer_norm(flat, gain_ref[...], bias_ref[...]).astype(BF16)
    normed_ref[...] = normed
    for source, target in ((last_gain_ref, last_gain_out), (last_bias_ref, last_bias_out)):
        target[...] = jnp.broadcast_to(column(source[...]), target.shape)

    values = dot(proj_ref[...], normed, 0, 1)
    gates = dot(gate_ref[...] * 0.5, normed, 0, 1)
    mask = cell_mask(chain_ref[...], slots, rows, cols)
    mixed = (sigmoid(gates) * values * mask).astype(BF16)

    by_row = []
    for side in range(2):
        lines = []
        for g in range(groups):
            lines += exchange_blocks(
                [
                    mixed[
                        side * hidden + n * chunks : side * hidden + (n + 1) * chunks,
                        g * LANES : (g + 1) * LANES,
                    ]
                    for n in range(inner)
                ],
                cols,
            )
        by_row.append(lines)
    order = order_ref[...]
    for part in range(chunks // SOME):
        for side in range(2):
            stack = jnp.concatenate(
                [line[part * SOME : (part + 1) * SOME] for line in by_row[side]], axis=0
            )
            sent_ref[part * SOME : (part + 1) * SOME, side * rows : (side + 1) * rows] = (
                dot(order, stack).astype(BF16).reshape(SOME, rows, LANES)
            )


def triangle_kernel(split, grid_cols, rows, cols, got_ref, sent_ref):
    inner = LANES // cols

    def place(r, c):
        z, y = r // split[1], r % split[1]
        return (c * split[1] + y) * split[0] + z

    def side(which):
        return jnp.concatenate(
            [
                jnp.concatenate(
                    [
                        got_ref[place(r, c), which * rows : (which + 1) * rows]
                        for r in range(split[0] * split[1])
                    ],
                    axis=0,
                )
                for c in range(grid_cols)
            ],
            axis=1,
        )

    left, right = side(0), side(1)
    lane = lax.broadcasted_iota(jnp.int32, (1, grid_cols * LANES), 1)
    by_channel = [right * one_hot(over(rest(lane, LANES), cols) == n) for n in range(inner)]
    right_by = jnp.concatenate(
        [
            by_channel[n][c * cols : (c + 1) * cols]
            for c in range(grid_cols)
            for n in range(inner)
        ],
        axis=0,
    )
    sums = dot(left, right_by, 1, 1).astype(BF16)
    for c in range(grid_cols):
        for r in range(split[0] * split[1]):
            sent_ref[place(r, c)] = sums[r * rows : (r + 1) * rows, c * LANES : (c + 1) * LANES]


def update_kernel(
    got_ref,
    order_ref,
    normed_ref,
    gain_ref,
    bias_ref,
    proj_ref,
    gate_ref,
    out_hbm,
    out_ref,
    out_sems,
):
    rows, cols, channels = out_ref.shape
    chunks = got_ref.shape[0]
    inner = LANES // cols
    groups = rows // inner
    order = order_ref[...]
    parts = [
        dot(order, got_ref[part * SOME : (part + 1) * SOME].reshape(SOME * rows, LANES)).astype(BF16)
        for part in range(chunks // SOME)
    ]
    lines = [
        jnp.concatenate([part[row * SOME : (row + 1) * SOME] for part in parts], axis=0)
        for row in range(rows)
    ]
    gain, bias = gain_ref[...], bias_ref[...]
    opened = sigmoid(dot(normed_ref[...], gate_ref[...] * 0.5))
    results = []
    for g in range(groups):
        values = jnp.concatenate(
            exchange_blocks(lines[g * inner : (g + 1) * inner], cols), axis=0
        ).astype(F32)
        mean = jnp.mean(values, axis=0, keepdims=True)
        centered = values - mean
        variance = jnp.mean(centered * centered, axis=0, keepdims=True)
        tri_normed = (centered * lax.rsqrt(variance + 1e-05) * gain + bias).astype(BF16)
        projected = dot(tri_normed, proj_ref[...], 0, 0)
        update = (opened[g * LANES : (g + 1) * LANES] * projected).astype(BF16)
        here = pl.ds(g * inner, inner)
        out_ref[here] = update.reshape(inner, cols, channels)
        results.append(pltpu.make_async_copy(out_ref.at[here], out_hbm.at[here], out_sems.at[g]))
        results[-1].start()
    for copy in results:
        copy.wait()


VMEM = pl.BlockSpec(memory_space=pltpu.VMEM)
HBM = pl.BlockSpec(memory_space=pltpu.HBM)
PARAMS = pltpu.CompilerParams(vmem_limit_bytes=32 * 1024 * 1024)


def exchanged(
    split,
    grid_cols,
    pair,
    chain_lengths,
    norm_in_gain,
    norm_in_bias,
    proj_in,
    gate_in,
    norm_out_gain,
    norm_out_bias,
    proj_out,
    gate_out,
):
    rows, cols, channels = pair.shape
    hidden = proj_out.shape[0]
    grid_rows = split[0] * split[1]
    devices = grid_rows * grid_cols
    slots = rows * grid_rows // chain_lengths.shape[0]
    order = pl.pallas_call(
        order_kernel,
        out_shape=jax.ShapeDtypeStruct((SOME * SOME, SOME * SOME), BF16),
        out_specs=VMEM,
        compiler_params=PARAMS,
        cost_estimate=pl.CostEstimate(flops=10**9, bytes_accessed=10**6, transcendentals=0),
        name="order",
    )()
    square = jax.ShapeDtypeStruct((LANES, LANES), F32)
    sent, normed, last_gain, last_bias = pl.pallas_call(
        functools.partial(mix_kernel, slots),
        out_shape=(
            jax.ShapeDtypeStruct((devices, 2 * rows, LANES), BF16),
            jax.ShapeDtypeStruct((rows * cols, channels), BF16),
            square,
            square,
        ),
        in_specs=[VMEM] * 9,
        out_specs=[VMEM] * 4,
        compiler_params=PARAMS,
        name="mix",
    )(
        order,
        chain_lengths.reshape(1, -1),
        pair,
        norm_in_gain.reshape(1, LANES),
        norm_in_bias.reshape(1, LANES),
        proj_in,
        gate_in,
        norm_out_gain.reshape(1, LANES),
        norm_out_bias.reshape(1, LANES),
    )
    axes = ("col", "low", "high")
    got = lax.all_to_all(sent, axes, 0, 0, tiled=True)
    sums = pl.pallas_call(
        functools.partial(triangle_kernel, split, grid_cols, rows, cols),
        out_shape=jax.ShapeDtypeStruct((devices, rows, LANES), BF16),
        in_specs=[VMEM],
        out_specs=VMEM,
        compiler_params=PARAMS,
        name="triangle",
    )(got)
    mine = lax.all_to_all(sums, axes, 0, 0, tiled=True)
    return pl.pallas_call(
        update_kernel,
        out_shape=jax.ShapeDtypeStruct((rows, cols, channels), BF16),
        in_specs=[VMEM] * 7,
        out_specs=HBM,
        scratch_shapes=[
            pltpu.VMEM((rows, cols, channels), BF16),
            pltpu.SemaphoreType.DMA((rows * cols // LANES,)),
        ],
        compiler_params=PARAMS,
        name="update",
    )(mine, order, normed, last_gain, last_bias, proj_out, gate_out)


def solution(mesh):
    grid_rows, grid_cols = mesh.shape["row"], mesh.shape["col"]
    split = (grid_rows // 2, 2)
    fine = jax.sharding.Mesh(
        mesh.devices.reshape(split + (grid_cols,)), ("high", "low", "col")
    )

    def fits(rows, cols, channels, hidden):
        devices = grid_rows * grid_cols
        inner = LANES // cols
        return (
            channels == LANES
            and hidden == LANES
            and inner * cols == LANES
            and inner & (inner - 1) == 0
            and inner * devices == hidden
            and rows == SOME
            and rows % inner == 0
            and devices % SOME == 0
        )

    def call(*arrays):
        tokens, others, channels = arrays[0].shape
        hidden = arrays[8].shape[0]
        if fits(tokens // grid_rows, others // grid_cols, channels, hidden):
            return jax.shard_map(
                functools.partial(exchanged, split, grid_cols),
                mesh=fine,
                in_specs=(P(("high", "low"), "col", None),) + (P(),) * 9,
                out_specs=P(("high", "low"), "col", None),
                check_vma=False,
            )(*arrays)
        return jax.shard_map(
            gathered,
            mesh=mesh,
            in_specs=(P("row", "col", None),) + (P(),) * 9,
            out_specs=P("row", "col", None),
            check_vma=False,
        )(*arrays)

    return call
```

```python
import functools
import jax
import jax.numpy as jnp
from jax import lax
from jax.experimental import pallas as pl
from jax.experimental.pallas import tpu as pltpu
from jax.sharding import PartitionSpec as P

LANES = 128
SOME = 16
F32 = jnp.float32
BF16 = jnp.bfloat16


def broadcast(value, axis, source):
    kept = jnp.where(lax.axis_index(axis) == source, value, 0).astype(value.dtype)
    return lax.psum(kept, axis)


def layer_norm(values, gain, bias):
    mean = jnp.mean(values, axis=-1, keepdims=True)
    centered = values - mean
    variance = jnp.mean(centered * centered, axis=-1, keepdims=True)
    return centered * lax.rsqrt(variance + 1e-05) * gain + bias


def token_valid(chain_lengths, tokens_idx, slots):
    chain = tokens_idx // slots
    position = tokens_idx % slots
    chain_ids = jnp.arange(chain_lengths.shape[0], dtype=jnp.int32)
    length_of = jnp.sum(
        jnp.where(chain[:, None] == chain_ids[None, :], chain_lengths[None, :], 0), axis=1
    )
    return (position < length_of).astype(jnp.float32)


def gathered(
    pair,
    chain_lengths,
    norm_in_gain,
    norm_in_bias,
    proj_in,
    gate_in,
    norm_out_gain,
    norm_out_bias,
    proj_out,
    gate_out,
):
    row_count = pair.shape[0]
    col_count = pair.shape[1]
    channels = pair.shape[2]
    hidden = proj_out.shape[0]
    row_index = lax.axis_index("row")
    col_index = lax.axis_index("col")
    slots = row_count * lax.axis_size("row") // chain_lengths.shape[0]
    valid_rows = token_valid(
        chain_lengths, row_index * row_count + jnp.arange(row_count, dtype=jnp.int32), slots
    )
    valid_cols = token_valid(
        chain_lengths, col_index * col_count + jnp.arange(col_count, dtype=jnp.int32), slots
    )
    pair_mask = valid_rows[:, None] * valid_cols[None, :]
    normed = layer_norm(pair.astype(jnp.float32), norm_in_gain, norm_in_bias).astype(jnp.bfloat16)
    flat = normed.reshape(-1, channels)
    values = jnp.dot(flat, proj_in, preferred_element_type=jnp.float32)
    gates = jnp.dot(flat, gate_in, preferred_element_type=jnp.float32)
    mixed = (jax.nn.sigmoid(gates) * values).reshape(row_count, col_count, 2 * hidden) * pair_mask[
        :, :, None
    ]
    left_tile = mixed[:, :, :hidden].astype(jnp.bfloat16)
    right_tile = mixed[:, :, hidden:].astype(jnp.bfloat16)
    ratio = lax.axis_size("row") // lax.axis_size("col")
    right_full = lax.all_gather(right_tile, "col", axis=1, tiled=True)
    received = []
    for part in range(ratio):
        received.append(broadcast(right_full, "row", col_index * ratio + part))
    right_mine = jnp.concatenate(received, axis=0)
    triangle = jnp.einsum(
        "ikh,jkh->ijh",
        lax.all_gather(left_tile, "col", axis=1, tiled=True),
        right_mine,
        preferred_element_type=jnp.float32,
    )
    tri_normed = layer_norm(triangle, norm_out_gain, norm_out_bias).astype(jnp.bfloat16)
    projected = jnp.dot(
        tri_normed.reshape(-1, hidden), proj_out, preferred_element_type=jnp.float32
    )
    gate = jax.nn.sigmoid(jnp.dot(flat, gate_out, preferred_element_type=jnp.float32))
    return (gate * projected).astype(jnp.bfloat16).reshape(row_count, col_count, channels)


def iota2(shape):
    return (
        lax.broadcasted_iota(jnp.int32, shape, 0),
        lax.broadcasted_iota(jnp.int32, shape, 1),
    )


def one_hot(condition):
    return jnp.where(condition, 1.0, 0.0).astype(BF16)


def dot(a, b, a_dim=1, b_dim=0):
    return lax.dot_general(a, b, (((a_dim,), (b_dim,)), ((), ())), preferred_element_type=F32)


def over(value, size):
    if size & (size - 1):
        return value // size
    return lax.shift_right_logical(value, jnp.full_like(value, size.bit_length() - 1))


def rest(value, size):
    return value % size if size & (size - 1) else value & (size - 1)


def over(value, size):
    if size & (size - 1):
        return value // size
    return lax.shift_right_logical(value, jnp.full_like(value, size.bit_length() - 1))


def rest(value, size):
    return value % size if size & (size - 1) else value & (size - 1)


def fetch(sources, targets, sems):
    copies = [
        pltpu.make_async_copy(source, target, sems.at[n])
        for n, (source, target) in enumerate(zip(sources, targets))
    ]
    for copy in copies:
        copy.start()
    return copies


def sigmoid(halved):
    return 0.5 + 0.5 * jnp.tanh(halved)


def exchange_blocks(arrays, cols):
    lane = over(lax.broadcasted_iota(jnp.int32, (1, LANES), 1), cols)
    arrays, step = list(arrays), 1
    while step < len(arrays):
        upper = lane & step != 0
        for n in range(len(arrays)):
            if n // step % 2 == 0:
                a, b = arrays[n], arrays[n + step]
                arrays[n] = jnp.where(upper, pltpu.roll(b, step * cols, 1), a)
                arrays[n + step] = jnp.where(upper, b, pltpu.roll(a, LANES - step * cols, 1))
        step *= 2
    return arrays


def order_kernel(order_ref):
    out, source = iota2(order_ref.shape)
    order_ref[...] = one_hot(
        (over(out, SOME) == rest(source, SOME)) & (rest(out, SOME) == over(source, SOME))
    )


def column(row):
    a, b = iota2((LANES, LANES))
    return jnp.sum(jnp.where(a == b, row, 0.0), axis=1, keepdims=True)


def cell_mask(lengths, slots, rows, cols):
    cell = lax.broadcasted_iota(jnp.int32, (1, rows * cols), 1)

    def valid(token):
        length = jnp.zeros_like(token)
        for chain in range(lengths.shape[1]):
            length = jnp.where(
                over(token, slots) == chain, lengths[:, chain : chain + 1], length
            )
        return rest(token, slots) < length

    row_ok = valid(lax.axis_index("row") * rows + over(cell, cols))
    col_ok = valid(lax.axis_index("col") * cols + rest(cell, cols))
    return jnp.where(row_ok & col_ok, 1.0, 0.0)


def mix_kernel(
    slots,
    order_ref,
    chain_ref,
    pair_ref,
    gain_ref,
    bias_ref,
    proj_ref,
    gate_ref,
    last_gain_ref,
    last_bias_ref,
    sent_ref,
    normed_ref,
    last_gain_out,
    last_bias_out,
):
    rows, cols, channels = pair_ref.shape
    hidden = proj_ref.shape[1] // 2
    cells = rows * cols
    inner = LANES // cols
    groups = rows // inner
    chunks = sent_ref.shape[0]
    flat = pair_ref[...].reshape(cells, channels).astype(F32)
    normed = layer_norm(flat, gain_ref[...], bias_ref[...]).astype(BF16)
    normed_ref[...] = normed
    for source, target in ((last_gain_ref, last_gain_out), (last_bias_ref, last_bias_out)):
        target[...] = jnp.broadcast_to(column(source[...]), target.shape)

    values = dot(proj_ref[...], normed, 0, 1)
    gates = dot(gate_ref[...] * 0.5, normed, 0, 1)
    mask = cell_mask(chain_ref[...], slots, rows, cols)
    mixed = (sigmoid(gates) * values * mask).astype(BF16)

    by_row = []
    for side in range(2):
        lines = []
        for g in range(groups):
            lines += exchange_blocks(
                [
                    mixed[
                        side * hidden + n * chunks : side * hidden + (n + 1) * chunks,
                        g * LANES : (g + 1) * LANES,
                    ]
                    for n in range(inner)
                ],
                cols,
            )
        by_row.append(lines)
    order = order_ref[...]
    for part in range(chunks // SOME):
        for side in range(2):
            stack = jnp.concatenate(
                [line[part * SOME : (part + 1) * SOME] for line in by_row[side]], axis=0
            )
            sent_ref[part * SOME : (part + 1) * SOME, side * rows : (side + 1) * rows] = (
                dot(order, stack).astype(BF16).reshape(SOME, rows, LANES)
            )


def triangle_kernel(grid_rows, grid_cols, rows, cols, got_ref, sent_ref):
    inner = LANES // cols

    def place(r, c):
        return r * grid_cols + c

    def side(which):
        return jnp.concatenate(
            [
                jnp.concatenate(
                    [
                        got_ref[place(r, c), which * rows : (which + 1) * rows]
                        for r in range(grid_rows)
                    ],
                    axis=0,
                )
                for c in range(grid_cols)
            ],
            axis=1,
        )

    left, right = side(0), side(1)
    lane = lax.broadcasted_iota(jnp.int32, (1, grid_cols * LANES), 1)
    by_channel = [right * one_hot(over(rest(lane, LANES), cols) == n) for n in range(inner)]
    right_by = jnp.concatenate(
        [
            by_channel[n][c * cols : (c + 1) * cols]
            for c in range(grid_cols)
            for n in range(inner)
        ],
        axis=0,
    )
    sums = dot(left, right_by, 1, 1).astype(BF16)
    for c in range(grid_cols):
        for r in range(grid_rows):
            sent_ref[place(r, c)] = sums[r * rows : (r + 1) * rows, c * LANES : (c + 1) * LANES]


def update_kernel(
    got_ref,
    order_ref,
    normed_ref,
    gain_ref,
    bias_ref,
    proj_ref,
    gate_ref,
    out_hbm,
    out_ref,
    out_sems,
):
    rows, cols, channels = out_ref.shape
    chunks = got_ref.shape[0]
    inner = LANES // cols
    groups = rows // inner
    order = order_ref[...]
    parts = [
        dot(order, got_ref[part * SOME : (part + 1) * SOME].reshape(SOME * rows, LANES)).astype(BF16)
        for part in range(chunks // SOME)
    ]
    lines = [
        jnp.concatenate([part[row * SOME : (row + 1) * SOME] for part in parts], axis=0)
        for row in range(rows)
    ]
    gain, bias = gain_ref[...], bias_ref[...]
    opened = sigmoid(dot(normed_ref[...], gate_ref[...] * 0.5))
    results = []
    for g in range(groups):
        values = jnp.concatenate(
            exchange_blocks(lines[g * inner : (g + 1) * inner], cols), axis=0
        ).astype(F32)
        mean = jnp.mean(values, axis=0, keepdims=True)
        centered = values - mean
        variance = jnp.mean(centered * centered, axis=0, keepdims=True)
        tri_normed = (centered * lax.rsqrt(variance + 1e-05) * gain + bias).astype(BF16)
        projected = dot(tri_normed, proj_ref[...], 0, 0)
        update = (opened[g * LANES : (g + 1) * LANES] * projected).astype(BF16)
        here = pl.ds(g * inner, inner)
        out_ref[here] = update.reshape(inner, cols, channels)
        results.append(pltpu.make_async_copy(out_ref.at[here], out_hbm.at[here], out_sems.at[g]))
        results[-1].start()
    for copy in results:
        copy.wait()


VMEM = pl.BlockSpec(memory_space=pltpu.VMEM)
HBM = pl.BlockSpec(memory_space=pltpu.HBM)
PARAMS = pltpu.CompilerParams(vmem_limit_bytes=32 * 1024 * 1024)


def exchanged(
    grid_rows,
    grid_cols,
    pair,
    chain_lengths,
    norm_in_gain,
    norm_in_bias,
    proj_in,
    gate_in,
    norm_out_gain,
    norm_out_bias,
    proj_out,
    gate_out,
):
    rows, cols, channels = pair.shape
    hidden = proj_out.shape[0]
    devices = grid_rows * grid_cols
    slots = rows * grid_rows // chain_lengths.shape[0]
    order = pl.pallas_call(
        order_kernel,
        out_shape=jax.ShapeDtypeStruct((SOME * SOME, SOME * SOME), BF16),
        out_specs=VMEM,
        compiler_params=PARAMS,
        cost_estimate=pl.CostEstimate(flops=10**9, bytes_accessed=10**6, transcendentals=0),
        name="order",
    )()
    square = jax.ShapeDtypeStruct((LANES, LANES), F32)
    sent, normed, last_gain, last_bias = pl.pallas_call(
        functools.partial(mix_kernel, slots),
        out_shape=(
            jax.ShapeDtypeStruct((devices, 2 * rows, LANES), BF16),
            jax.ShapeDtypeStruct((rows * cols, channels), BF16),
            square,
            square,
        ),
        in_specs=[VMEM] * 9,
        out_specs=[VMEM] * 4,
        compiler_params=PARAMS,
        name="mix",
    )(
        order,
        chain_lengths.reshape(1, -1),
        pair,
        norm_in_gain.reshape(1, LANES),
        norm_in_bias.reshape(1, LANES),
        proj_in,
        gate_in,
        norm_out_gain.reshape(1, LANES),
        norm_out_bias.reshape(1, LANES),
    )
    axes = ("row", "col")
    got = lax.all_to_all(sent, axes, 0, 0, tiled=True)
    sums = pl.pallas_call(
        functools.partial(triangle_kernel, grid_rows, grid_cols, rows, cols),
        out_shape=jax.ShapeDtypeStruct((devices, rows, LANES), BF16),
        in_specs=[VMEM],
        out_specs=VMEM,
        compiler_params=PARAMS,
        name="triangle",
    )(got)
    mine = lax.all_to_all(sums, axes, 0, 0, tiled=True)
    return pl.pallas_call(
        update_kernel,
        out_shape=jax.ShapeDtypeStruct((rows, cols, channels), BF16),
        in_specs=[VMEM] * 7,
        out_specs=HBM,
        scratch_shapes=[
            pltpu.VMEM((rows, cols, channels), BF16),
            pltpu.SemaphoreType.DMA((rows * cols // LANES,)),
        ],
        compiler_params=PARAMS,
        name="update",
    )(mine, order, normed, last_gain, last_bias, proj_out, gate_out)


def solution(mesh):
    grid_rows, grid_cols = mesh.shape["row"], mesh.shape["col"]
    def fits(rows, cols, channels, hidden):
        devices = grid_rows * grid_cols
        inner = LANES // cols
        return (
            channels == LANES
            and hidden == LANES
            and inner * cols == LANES
            and inner & (inner - 1) == 0
            and inner * devices == hidden
            and rows == SOME
            and rows % inner == 0
            and devices % SOME == 0
        )

    def call(*arrays):
        tokens, others, channels = arrays[0].shape
        hidden = arrays[8].shape[0]
        if fits(tokens // grid_rows, others // grid_cols, channels, hidden):
            return jax.shard_map(
                functools.partial(exchanged, grid_rows, grid_cols),
                mesh=mesh,
                in_specs=(P("row", "col", None),) + (P(),) * 9,
                out_specs=P("row", "col", None),
                check_vma=False,
            )(*arrays)
        return jax.shard_map(
            gathered,
            mesh=mesh,
            in_specs=(P("row", "col", None),) + (P(),) * 9,
            out_specs=P("row", "col", None),
            check_vma=False,
        )(*arrays)

    return call
```

```python
import functools
import jax
import jax.numpy as jnp
from jax import lax
from jax.experimental import pallas as pl
from jax.experimental.pallas import tpu as pltpu
from jax.sharding import PartitionSpec as P

LANES = 128
SOME = 16
F32 = jnp.float32
BF16 = jnp.bfloat16


def broadcast(value, axis, source):
    kept = jnp.where(lax.axis_index(axis) == source, value, 0).astype(value.dtype)
    return lax.psum(kept, axis)


def layer_norm(values, gain, bias):
    mean = jnp.mean(values, axis=-1, keepdims=True)
    centered = values - mean
    variance = jnp.mean(centered * centered, axis=-1, keepdims=True)
    return centered * lax.rsqrt(variance + 1e-05) * gain + bias


def token_valid(chain_lengths, tokens_idx, slots):
    chain = tokens_idx // slots
    position = tokens_idx % slots
    chain_ids = jnp.arange(chain_lengths.shape[0], dtype=jnp.int32)
    length_of = jnp.sum(
        jnp.where(chain[:, None] == chain_ids[None, :], chain_lengths[None, :], 0), axis=1
    )
    return (position < length_of).astype(jnp.float32)


def gathered(
    pair,
    chain_lengths,
    norm_in_gain,
    norm_in_bias,
    proj_in,
    gate_in,
    norm_out_gain,
    norm_out_bias,
    proj_out,
    gate_out,
):
    row_count = pair.shape[0]
    col_count = pair.shape[1]
    channels = pair.shape[2]
    hidden = proj_out.shape[0]
    row_index = lax.axis_index("row")
    col_index = lax.axis_index("col")
    slots = row_count * lax.axis_size("row") // chain_lengths.shape[0]
    valid_rows = token_valid(
        chain_lengths, row_index * row_count + jnp.arange(row_count, dtype=jnp.int32), slots
    )
    valid_cols = token_valid(
        chain_lengths, col_index * col_count + jnp.arange(col_count, dtype=jnp.int32), slots
    )
    pair_mask = valid_rows[:, None] * valid_cols[None, :]
    normed = layer_norm(pair.astype(jnp.float32), norm_in_gain, norm_in_bias).astype(jnp.bfloat16)
    flat = normed.reshape(-1, channels)
    values = jnp.dot(flat, proj_in, preferred_element_type=jnp.float32)
    gates = jnp.dot(flat, gate_in, preferred_element_type=jnp.float32)
    mixed = (jax.nn.sigmoid(gates) * values).reshape(row_count, col_count, 2 * hidden) * pair_mask[
        :, :, None
    ]
    left_tile = mixed[:, :, :hidden].astype(jnp.bfloat16)
    right_tile = mixed[:, :, hidden:].astype(jnp.bfloat16)
    ratio = lax.axis_size("row") // lax.axis_size("col")
    right_full = lax.all_gather(right_tile, "col", axis=1, tiled=True)
    received = []
    for part in range(ratio):
        received.append(broadcast(right_full, "row", col_index * ratio + part))
    right_mine = jnp.concatenate(received, axis=0)
    triangle = jnp.einsum(
        "ikh,jkh->ijh",
        lax.all_gather(left_tile, "col", axis=1, tiled=True),
        right_mine,
        preferred_element_type=jnp.float32,
    )
    tri_normed = layer_norm(triangle, norm_out_gain, norm_out_bias).astype(jnp.bfloat16)
    projected = jnp.dot(
        tri_normed.reshape(-1, hidden), proj_out, preferred_element_type=jnp.float32
    )
    gate = jax.nn.sigmoid(jnp.dot(flat, gate_out, preferred_element_type=jnp.float32))
    return (gate * projected).astype(jnp.bfloat16).reshape(row_count, col_count, channels)


def iota2(shape):
    return (
        lax.broadcasted_iota(jnp.int32, shape, 0),
        lax.broadcasted_iota(jnp.int32, shape, 1),
    )


def one_hot(condition):
    return jnp.where(condition, 1.0, 0.0).astype(BF16)


def dot(a, b, a_dim=1, b_dim=0):
    return lax.dot_general(a, b, (((a_dim,), (b_dim,)), ((), ())), preferred_element_type=F32)


def over(value, size):
    if size & (size - 1):
        return value // size
    return lax.shift_right_logical(value, jnp.full_like(value, size.bit_length() - 1))


def rest(value, size):
    return value % size if size & (size - 1) else value & (size - 1)


def over(value, size):
    if size & (size - 1):
        return value // size
    return lax.shift_right_logical(value, jnp.full_like(value, size.bit_length() - 1))


def rest(value, size):
    return value % size if size & (size - 1) else value & (size - 1)


def fetch(sources, targets, sems):
    copies = [
        pltpu.make_async_copy(source, target, sems.at[n])
        for n, (source, target) in enumerate(zip(sources, targets))
    ]
    for copy in copies:
        copy.start()
    return copies


def sigmoid(halved):
    return 0.5 + 0.5 * jnp.tanh(halved)


def exchange_blocks(arrays, cols):
    lane = over(lax.broadcasted_iota(jnp.int32, (1, LANES), 1), cols)
    arrays, step = list(arrays), 1
    while step < len(arrays):
        upper = lane & step != 0
        for n in range(len(arrays)):
            if n // step % 2 == 0:
                a, b = arrays[n], arrays[n + step]
                arrays[n] = jnp.where(upper, pltpu.roll(b, step * cols, 1), a)
                arrays[n + step] = jnp.where(upper, b, pltpu.roll(a, LANES - step * cols, 1))
        step *= 2
    return arrays


def order_kernel(order_ref):
    out, source = iota2(order_ref.shape)
    order_ref[...] = one_hot(
        (over(out, SOME) == rest(source, SOME)) & (rest(out, SOME) == over(source, SOME))
    )


def column(row):
    a, b = iota2((LANES, LANES))
    return jnp.sum(jnp.where(a == b, row, 0.0), axis=1, keepdims=True)


def cell_mask(lengths, slots, rows, cols):
    cell = lax.broadcasted_iota(jnp.int32, (1, rows * cols), 1)

    def valid(token):
        length = jnp.zeros_like(token)
        for chain in range(lengths.shape[1]):
            length = jnp.where(
                over(token, slots) == chain, lengths[:, chain : chain + 1], length
            )
        return rest(token, slots) < length

    row_ok = valid(lax.axis_index(("high", "low")) * rows + over(cell, cols))
    col_ok = valid(lax.axis_index("col") * cols + rest(cell, cols))
    return jnp.where(row_ok & col_ok, 1.0, 0.0)


def mix_kernel(
    slots,
    order_ref,
    chain_ref,
    pair_ref,
    gain_ref,
    bias_ref,
    proj_ref,
    gate_ref,
    last_gain_ref,
    last_bias_ref,
    sent_ref,
    normed_ref,
    last_gain_out,
    last_bias_out,
):
    rows, cols, channels = pair_ref.shape
    hidden = proj_ref.shape[1] // 2
    cells = rows * cols
    inner = LANES // cols
    groups = rows // inner
    chunks = sent_ref.shape[0]
    flat = pair_ref[...].reshape(cells, channels).astype(F32)
    normed = layer_norm(flat, gain_ref[...], bias_ref[...]).astype(BF16)
    normed_ref[...] = normed
    for source, target in ((last_gain_ref, last_gain_out), (last_bias_ref, last_bias_out)):
        target[...] = jnp.broadcast_to(column(source[...]), target.shape)

    values = dot(proj_ref[...], normed, 0, 1)
    gates = dot(gate_ref[...] * 0.5, normed, 0, 1)
    mask = cell_mask(chain_ref[...], slots, rows, cols)
    mixed = (sigmoid(gates) * values * mask).astype(BF16)

    by_row = []
    for side in range(2):
        lines = []
        for g in range(groups):
            lines += exchange_blocks(
                [
                    mixed[
                        side * hidden + n * chunks : side * hidden + (n + 1) * chunks,
                        g * LANES : (g + 1) * LANES,
                    ]
                    for n in range(inner)
                ],
                cols,
            )
        by_row.append(lines)
    order = order_ref[...]
    for part in range(chunks // SOME):
        for side in range(2):
            stack = jnp.concatenate(
                [line[part * SOME : (part + 1) * SOME] for line in by_row[side]], axis=0
            )
            sent_ref[part * SOME : (part + 1) * SOME, side * rows : (side + 1) * rows] = (
                dot(order, stack).astype(BF16).reshape(SOME, rows, LANES)
            )


def triangle_kernel(split, grid_cols, rows, cols, got_ref, sent_ref):
    inner = LANES // cols

    def place(r, c):
        z, y = r // split[1], r % split[1]
        return (c * split[1] + y) * split[0] + z

    def side(which):
        return jnp.concatenate(
            [
                jnp.concatenate(
                    [
                        got_ref[place(r, c), which * rows : (which + 1) * rows]
                        for r in range(split[0] * split[1])
                    ],
                    axis=0,
                )
                for c in range(grid_cols)
            ],
            axis=1,
        )

    left, right = side(0), side(1)
    lane = lax.broadcasted_iota(jnp.int32, (1, grid_cols * LANES), 1)
    by_channel = [right * one_hot(over(rest(lane, LANES), cols) == n) for n in range(inner)]
    right_by = jnp.concatenate(
        [
            by_channel[n][c * cols : (c + 1) * cols]
            for c in range(grid_cols)
            for n in range(inner)
        ],
        axis=0,
    )
    sums = dot(left, right_by, 1, 1).astype(BF16)
    for c in range(grid_cols):
        for r in range(split[0] * split[1]):
            sent_ref[place(r, c)] = sums[r * rows : (r + 1) * rows, c * LANES : (c + 1) * LANES]


def update_kernel(
    got_ref,
    order_ref,
    normed_ref,
    gain_ref,
    bias_ref,
    proj_ref,
    gate_ref,
    out_hbm,
    out_ref,
    out_sems,
):
    rows, cols, channels = out_ref.shape
    chunks = got_ref.shape[0]
    inner = LANES // cols
    groups = rows // inner
    order = order_ref[...]
    parts = [
        dot(order, got_ref[part * SOME : (part + 1) * SOME].reshape(SOME * rows, LANES)).astype(BF16)
        for part in range(chunks // SOME)
    ]
    lines = [
        jnp.concatenate([part[row * SOME : (row + 1) * SOME] for part in parts], axis=0)
        for row in range(rows)
    ]
    opened = sigmoid(dot(normed_ref[...], gate_ref[...] * 0.5))
    values = jnp.concatenate(
        [
            jnp.concatenate(
                exchange_blocks(lines[g * inner : (g + 1) * inner], cols), axis=0
            )
            for g in range(groups)
        ],
        axis=1,
    ).astype(F32)
    mean = jnp.mean(values, axis=0, keepdims=True)
    centered = values - mean
    variance = jnp.mean(centered * centered, axis=0, keepdims=True)
    scaled = centered * lax.rsqrt(variance + 1e-05)
    tri_normed = (scaled * gain_ref[:, :1] + bias_ref[:, :1]).astype(BF16)
    update = (opened * dot(tri_normed, proj_ref[...], 0, 0)).astype(BF16)
    results = []
    for g in range(groups):
        here = pl.ds(g * inner, inner)
        out_ref[here] = update[g * LANES : (g + 1) * LANES].reshape(inner, cols, channels)
        results.append(pltpu.make_async_copy(out_ref.at[here], out_hbm.at[here], out_sems.at[g]))
        results[-1].start()
    for copy in results:
        copy.wait()


VMEM = pl.BlockSpec(memory_space=pltpu.VMEM)
HBM = pl.BlockSpec(memory_space=pltpu.HBM)
PARAMS = pltpu.CompilerParams(vmem_limit_bytes=32 * 1024 * 1024)


def exchanged(
    split,
    grid_cols,
    pair,
    chain_lengths,
    norm_in_gain,
    norm_in_bias,
    proj_in,
    gate_in,
    norm_out_gain,
    norm_out_bias,
    proj_out,
    gate_out,
):
    rows, cols, channels = pair.shape
    hidden = proj_out.shape[0]
    grid_rows = split[0] * split[1]
    devices = grid_rows * grid_cols
    slots = rows * grid_rows // chain_lengths.shape[0]
    order = pl.pallas_call(
        order_kernel,
        out_shape=jax.ShapeDtypeStruct((SOME * SOME, SOME * SOME), BF16),
        out_specs=VMEM,
        compiler_params=PARAMS,
        cost_estimate=pl.CostEstimate(flops=10**9, bytes_accessed=10**6, transcendentals=0),
        name="order",
    )()
    square = jax.ShapeDtypeStruct((LANES, LANES), F32)
    sent, normed, last_gain, last_bias = pl.pallas_call(
        functools.partial(mix_kernel, slots),
        out_shape=(
            jax.ShapeDtypeStruct((devices, 2 * rows, LANES), BF16),
            jax.ShapeDtypeStruct((rows * cols, channels), BF16),
            square,
            square,
        ),
        in_specs=[VMEM] * 9,
        out_specs=[VMEM] * 4,
        compiler_params=PARAMS,
        name="mix",
    )(
        order,
        chain_lengths.reshape(1, -1),
        pair,
        norm_in_gain.reshape(1, LANES),
        norm_in_bias.reshape(1, LANES),
        proj_in,
        gate_in,
        norm_out_gain.reshape(1, LANES),
        norm_out_bias.reshape(1, LANES),
    )
    axes = ("col", "low", "high")
    got = lax.all_to_all(sent, axes, 0, 0, tiled=True)
    sums = pl.pallas_call(
        functools.partial(triangle_kernel, split, grid_cols, rows, cols),
        out_shape=jax.ShapeDtypeStruct((devices, rows, LANES), BF16),
        in_specs=[VMEM],
        out_specs=VMEM,
        compiler_params=PARAMS,
        name="triangle",
    )(got)
    mine = lax.all_to_all(sums, axes, 0, 0, tiled=True)
    return pl.pallas_call(
        update_kernel,
        out_shape=jax.ShapeDtypeStruct((rows, cols, channels), BF16),
        in_specs=[VMEM] * 7,
        out_specs=HBM,
        scratch_shapes=[
            pltpu.VMEM((rows, cols, channels), BF16),
            pltpu.SemaphoreType.DMA((rows * cols // LANES,)),
        ],
        compiler_params=PARAMS,
        name="update",
    )(mine, order, normed, last_gain, last_bias, proj_out, gate_out)


def solution(mesh):
    grid_rows, grid_cols = mesh.shape["row"], mesh.shape["col"]
    split = (grid_rows // 2, 2)
    fine = jax.sharding.Mesh(
        mesh.devices.reshape(split + (grid_cols,)), ("high", "low", "col")
    )

    def fits(rows, cols, channels, hidden):
        devices = grid_rows * grid_cols
        inner = LANES // cols
        return (
            channels == LANES
            and hidden == LANES
            and inner * cols == LANES
            and inner & (inner - 1) == 0
            and inner * devices == hidden
            and rows == SOME
            and rows % inner == 0
            and devices % SOME == 0
        )

    def call(*arrays):
        tokens, others, channels = arrays[0].shape
        hidden = arrays[8].shape[0]
        if fits(tokens // grid_rows, others // grid_cols, channels, hidden):
            return jax.shard_map(
                functools.partial(exchanged, split, grid_cols),
                mesh=fine,
                in_specs=(P(("high", "low"), "col", None),) + (P(),) * 9,
                out_specs=P(("high", "low"), "col", None),
                check_vma=False,
            )(*arrays)
        return jax.shard_map(
            gathered,
            mesh=mesh,
            in_specs=(P("row", "col", None),) + (P(),) * 9,
            out_specs=P("row", "col", None),
            check_vma=False,
        )(*arrays)

    return call
```

```python
import functools
import jax
import jax.numpy as jnp
from jax import lax
from jax.experimental import pallas as pl
from jax.experimental.pallas import tpu as pltpu
from jax.sharding import PartitionSpec as P

LANES = 128
SOME = 16
F32 = jnp.float32
BF16 = jnp.bfloat16


def broadcast(value, axis, source):
    kept = jnp.where(lax.axis_index(axis) == source, value, 0).astype(value.dtype)
    return lax.psum(kept, axis)


def layer_norm(values, gain, bias):
    mean = jnp.mean(values, axis=-1, keepdims=True)
    centered = values - mean
    variance = jnp.mean(centered * centered, axis=-1, keepdims=True)
    return centered * lax.rsqrt(variance + 1e-05) * gain + bias


def token_valid(chain_lengths, tokens_idx, slots):
    chain = tokens_idx // slots
    position = tokens_idx % slots
    chain_ids = jnp.arange(chain_lengths.shape[0], dtype=jnp.int32)
    length_of = jnp.sum(
        jnp.where(chain[:, None] == chain_ids[None, :], chain_lengths[None, :], 0), axis=1
    )
    return (position < length_of).astype(jnp.float32)


def gathered(
    pair,
    chain_lengths,
    norm_in_gain,
    norm_in_bias,
    proj_in,
    gate_in,
    norm_out_gain,
    norm_out_bias,
    proj_out,
    gate_out,
):
    row_count = pair.shape[0]
    col_count = pair.shape[1]
    channels = pair.shape[2]
    hidden = proj_out.shape[0]
    row_index = lax.axis_index("row")
    col_index = lax.axis_index("col")
    slots = row_count * lax.axis_size("row") // chain_lengths.shape[0]
    valid_rows = token_valid(
        chain_lengths, row_index * row_count + jnp.arange(row_count, dtype=jnp.int32), slots
    )
    valid_cols = token_valid(
        chain_lengths, col_index * col_count + jnp.arange(col_count, dtype=jnp.int32), slots
    )
    pair_mask = valid_rows[:, None] * valid_cols[None, :]
    normed = layer_norm(pair.astype(jnp.float32), norm_in_gain, norm_in_bias).astype(jnp.bfloat16)
    flat = normed.reshape(-1, channels)
    values = jnp.dot(flat, proj_in, preferred_element_type=jnp.float32)
    gates = jnp.dot(flat, gate_in, preferred_element_type=jnp.float32)
    mixed = (jax.nn.sigmoid(gates) * values).reshape(row_count, col_count, 2 * hidden) * pair_mask[
        :, :, None
    ]
    left_tile = mixed[:, :, :hidden].astype(jnp.bfloat16)
    right_tile = mixed[:, :, hidden:].astype(jnp.bfloat16)
    ratio = lax.axis_size("row") // lax.axis_size("col")
    right_full = lax.all_gather(right_tile, "col", axis=1, tiled=True)
    received = []
    for part in range(ratio):
        received.append(broadcast(right_full, "row", col_index * ratio + part))
    right_mine = jnp.concatenate(received, axis=0)
    triangle = jnp.einsum(
        "ikh,jkh->ijh",
        lax.all_gather(left_tile, "col", axis=1, tiled=True),
        right_mine,
        preferred_element_type=jnp.float32,
    )
    tri_normed = layer_norm(triangle, norm_out_gain, norm_out_bias).astype(jnp.bfloat16)
    projected = jnp.dot(
        tri_normed.reshape(-1, hidden), proj_out, preferred_element_type=jnp.float32
    )
    gate = jax.nn.sigmoid(jnp.dot(flat, gate_out, preferred_element_type=jnp.float32))
    return (gate * projected).astype(jnp.bfloat16).reshape(row_count, col_count, channels)


def iota2(shape):
    return (
        lax.broadcasted_iota(jnp.int32, shape, 0),
        lax.broadcasted_iota(jnp.int32, shape, 1),
    )


def one_hot(condition):
    return jnp.where(condition, 1.0, 0.0).astype(BF16)


def dot(a, b, a_dim=1, b_dim=0):
    return lax.dot_general(a, b, (((a_dim,), (b_dim,)), ((), ())), preferred_element_type=F32)


def over(value, size):
    if size & (size - 1):
        return value // size
    return lax.shift_right_logical(value, jnp.full_like(value, size.bit_length() - 1))


def rest(value, size):
    return value % size if size & (size - 1) else value & (size - 1)


def over(value, size):
    if size & (size - 1):
        return value // size
    return lax.shift_right_logical(value, jnp.full_like(value, size.bit_length() - 1))


def rest(value, size):
    return value % size if size & (size - 1) else value & (size - 1)


def fetch(sources, targets, sems):
    copies = [
        pltpu.make_async_copy(source, target, sems.at[n])
        for n, (source, target) in enumerate(zip(sources, targets))
    ]
    for copy in copies:
        copy.start()
    return copies


def sigmoid(halved):
    return 0.5 + 0.5 * jnp.tanh(halved)


def exchange_blocks(arrays, cols):
    lane = over(lax.broadcasted_iota(jnp.int32, (1, LANES), 1), cols)
    arrays, step = list(arrays), 1
    while step < len(arrays):
        upper = lane & step != 0
        for n in range(len(arrays)):
            if n // step % 2 == 0:
                a, b = arrays[n], arrays[n + step]
                arrays[n] = jnp.where(upper, pltpu.roll(b, step * cols, 1), a)
                arrays[n + step] = jnp.where(upper, b, pltpu.roll(a, LANES - step * cols, 1))
        step *= 2
    return arrays


def order_kernel(order_ref):
    out, source = iota2(order_ref.shape)
    order_ref[...] = one_hot(
        (over(out, SOME) == rest(source, SOME)) & (rest(out, SOME) == over(source, SOME))
    )


def column(row):
    a, b = iota2((LANES, LANES))
    return jnp.sum(jnp.where(a == b, row, 0.0), axis=1, keepdims=True)


def cell_mask(lengths, slots, rows, cols):
    cell = lax.broadcasted_iota(jnp.int32, (1, rows * cols), 1)

    def valid(token):
        length = jnp.zeros_like(token)
        for chain in range(lengths.shape[1]):
            length = jnp.where(
                over(token, slots) == chain, lengths[:, chain : chain + 1], length
            )
        return rest(token, slots) < length

    row_ok = valid(lax.axis_index("row") * rows + over(cell, cols))
    col_ok = valid(lax.axis_index("col") * cols + rest(cell, cols))
    return jnp.where(row_ok & col_ok, 1.0, 0.0)


def mix_kernel(
    slots,
    order_ref,
    chain_ref,
    pair_ref,
    gain_ref,
    bias_ref,
    proj_ref,
    gate_ref,
    last_gain_ref,
    last_bias_ref,
    sent_ref,
    normed_ref,
    last_gain_out,
    last_bias_out,
):
    rows, cols, channels = pair_ref.shape
    hidden = proj_ref.shape[1] // 2
    cells = rows * cols
    inner = LANES // cols
    groups = rows // inner
    chunks = sent_ref.shape[0]
    flat = pair_ref[...].reshape(cells, channels).astype(F32)
    normed = layer_norm(flat, gain_ref[...], bias_ref[...]).astype(BF16)
    normed_ref[...] = normed
    for source, target in ((last_gain_ref, last_gain_out), (last_bias_ref, last_bias_out)):
        target[...] = jnp.broadcast_to(column(source[...]), target.shape)

    values = dot(proj_ref[...], normed, 0, 1)
    gates = dot(gate_ref[...] * 0.5, normed, 0, 1)
    mask = cell_mask(chain_ref[...], slots, rows, cols)
    mixed = (sigmoid(gates) * values * mask).astype(BF16)

    by_row = []
    for side in range(2):
        lines = []
        for g in range(groups):
            lines += exchange_blocks(
                [
                    mixed[
                        side * hidden + n * chunks : side * hidden + (n + 1) * chunks,
                        g * LANES : (g + 1) * LANES,
                    ]
                    for n in range(inner)
                ],
                cols,
            )
        by_row.append(lines)
    order = order_ref[...]
    for part in range(chunks // SOME):
        for side in range(2):
            stack = jnp.concatenate(
                [line[part * SOME : (part + 1) * SOME] for line in by_row[side]], axis=0
            )
            sent_ref[part * SOME : (part + 1) * SOME, side * rows : (side + 1) * rows] = (
                dot(order, stack).astype(BF16).reshape(SOME, rows, LANES)
            )


def triangle_kernel(ring, grid_rows, grid_cols, rows, cols, got_ref, sent_ref):
    inner = LANES // cols

    def place(r, c):
        return ring.index(r * grid_cols + c)

    def side(which):
        return jnp.concatenate(
            [
                jnp.concatenate(
                    [
                        got_ref[place(r, c), which * rows : (which + 1) * rows]
                        for r in range(grid_rows)
                    ],
                    axis=0,
                )
                for c in range(grid_cols)
            ],
            axis=1,
        )

    left, right = side(0), side(1)
    lane = lax.broadcasted_iota(jnp.int32, (1, grid_cols * LANES), 1)
    by_channel = [right * one_hot(over(rest(lane, LANES), cols) == n) for n in range(inner)]
    right_by = jnp.concatenate(
        [
            by_channel[n][c * cols : (c + 1) * cols]
            for c in range(grid_cols)
            for n in range(inner)
        ],
        axis=0,
    )
    sums = dot(left, right_by, 1, 1).astype(BF16)
    for c in range(grid_cols):
        for r in range(grid_rows):
            sent_ref[place(r, c)] = sums[r * rows : (r + 1) * rows, c * LANES : (c + 1) * LANES]


def update_kernel(
    got_ref,
    order_ref,
    normed_ref,
    gain_ref,
    bias_ref,
    proj_ref,
    gate_ref,
    out_hbm,
    out_ref,
    out_sems,
):
    rows, cols, channels = out_ref.shape
    chunks = got_ref.shape[0]
    inner = LANES // cols
    groups = rows // inner
    order = order_ref[...]
    parts = [
        dot(order, got_ref[part * SOME : (part + 1) * SOME].reshape(SOME * rows, LANES)).astype(BF16)
        for part in range(chunks // SOME)
    ]
    lines = [
        jnp.concatenate([part[row * SOME : (row + 1) * SOME] for part in parts], axis=0)
        for row in range(rows)
    ]
    gain, bias = gain_ref[...], bias_ref[...]
    opened = sigmoid(dot(normed_ref[...], gate_ref[...] * 0.5))
    results = []
    for g in range(groups):
        values = jnp.concatenate(
            exchange_blocks(lines[g * inner : (g + 1) * inner], cols), axis=0
        ).astype(F32)
        mean = jnp.mean(values, axis=0, keepdims=True)
        centered = values - mean
        variance = jnp.mean(centered * centered, axis=0, keepdims=True)
        tri_normed = (centered * lax.rsqrt(variance + 1e-05) * gain + bias).astype(BF16)
        projected = dot(tri_normed, proj_ref[...], 0, 0)
        update = (opened[g * LANES : (g + 1) * LANES] * projected).astype(BF16)
        here = pl.ds(g * inner, inner)
        out_ref[here] = update.reshape(inner, cols, channels)
        results.append(pltpu.make_async_copy(out_ref.at[here], out_hbm.at[here], out_sems.at[g]))
        results[-1].start()
    for copy in results:
        copy.wait()


VMEM = pl.BlockSpec(memory_space=pltpu.VMEM)
HBM = pl.BlockSpec(memory_space=pltpu.HBM)
PARAMS = pltpu.CompilerParams(vmem_limit_bytes=32 * 1024 * 1024)


def ring_of(grid_rows, grid_cols):
    return [
        (z * 2 + y) * grid_cols + x * 2 + core
        for x in range(grid_cols // 2)
        for y in range(2)
        for z in range(grid_rows // 2)
        for core in range(2)
    ]


def exchanged(
    grid_rows,
    grid_cols,
    pair,
    chain_lengths,
    norm_in_gain,
    norm_in_bias,
    proj_in,
    gate_in,
    norm_out_gain,
    norm_out_bias,
    proj_out,
    gate_out,
):
    rows, cols, channels = pair.shape
    hidden = proj_out.shape[0]
    devices = grid_rows * grid_cols
    slots = rows * grid_rows // chain_lengths.shape[0]
    order = pl.pallas_call(
        order_kernel,
        out_shape=jax.ShapeDtypeStruct((SOME * SOME, SOME * SOME), BF16),
        out_specs=VMEM,
        compiler_params=PARAMS,
        cost_estimate=pl.CostEstimate(flops=10**9, bytes_accessed=10**6, transcendentals=0),
        name="order",
    )()
    square = jax.ShapeDtypeStruct((LANES, LANES), F32)
    sent, normed, last_gain, last_bias = pl.pallas_call(
        functools.partial(mix_kernel, slots),
        out_shape=(
            jax.ShapeDtypeStruct((devices, 2 * rows, LANES), BF16),
            jax.ShapeDtypeStruct((rows * cols, channels), BF16),
            square,
            square,
        ),
        in_specs=[VMEM] * 9,
        out_specs=[VMEM] * 4,
        compiler_params=PARAMS,
        name="mix",
    )(
        order,
        chain_lengths.reshape(1, -1),
        pair,
        norm_in_gain.reshape(1, LANES),
        norm_in_bias.reshape(1, LANES),
        proj_in,
        gate_in,
        norm_out_gain.reshape(1, LANES),
        norm_out_bias.reshape(1, LANES),
    )
    ring = ring_of(grid_rows, grid_cols)

    def exchange(chunks):
        return lax.all_to_all(
            chunks, ("row", "col"), 0, 0, tiled=True, axis_index_groups=[ring]
        )

    got = exchange(sent)
    sums = pl.pallas_call(
        functools.partial(triangle_kernel, ring, grid_rows, grid_cols, rows, cols),
        out_shape=jax.ShapeDtypeStruct((devices, rows, LANES), BF16),
        in_specs=[VMEM],
        out_specs=VMEM,
        compiler_params=PARAMS,
        name="triangle",
    )(got)
    mine = exchange(sums)
    return pl.pallas_call(
        update_kernel,
        out_shape=jax.ShapeDtypeStruct((rows, cols, channels), BF16),
        in_specs=[VMEM] * 7,
        out_specs=HBM,
        scratch_shapes=[
            pltpu.VMEM((rows, cols, channels), BF16),
            pltpu.SemaphoreType.DMA((rows * cols // LANES,)),
        ],
        compiler_params=PARAMS,
        name="update",
    )(mine, order, normed, last_gain, last_bias, proj_out, gate_out)


def solution(mesh):
    grid_rows, grid_cols = mesh.shape["row"], mesh.shape["col"]
    def fits(rows, cols, channels, hidden):
        devices = grid_rows * grid_cols
        inner = LANES // cols
        return (
            channels == LANES
            and hidden == LANES
            and inner * cols == LANES
            and inner & (inner - 1) == 0
            and inner * devices == hidden
            and rows == SOME
            and rows % inner == 0
            and devices % SOME == 0
            and grid_rows % 2 == 0
            and grid_cols % 2 == 0
        )

    def call(*arrays):
        tokens, others, channels = arrays[0].shape
        hidden = arrays[8].shape[0]
        if fits(tokens // grid_rows, others // grid_cols, channels, hidden):
            return jax.shard_map(
                functools.partial(exchanged, grid_rows, grid_cols),
                mesh=mesh,
                in_specs=(P("row", "col", None),) + (P(),) * 9,
                out_specs=P("row", "col", None),
                check_vma=False,
            )(*arrays)
        return jax.shard_map(
            gathered,
            mesh=mesh,
            in_specs=(P("row", "col", None),) + (P(),) * 9,
            out_specs=P("row", "col", None),
            check_vma=False,
        )(*arrays)

    return call
```

```python
import functools
import jax
import jax.numpy as jnp
from jax import lax
from jax.experimental import pallas as pl
from jax.experimental.pallas import tpu as pltpu
from jax.sharding import PartitionSpec as P

LANES = 128
SOME = 16
F32 = jnp.float32
BF16 = jnp.bfloat16


def broadcast(value, axis, source):
    kept = jnp.where(lax.axis_index(axis) == source, value, 0).astype(value.dtype)
    return lax.psum(kept, axis)


def layer_norm(values, gain, bias):
    mean = jnp.mean(values, axis=-1, keepdims=True)
    centered = values - mean
    variance = jnp.mean(centered * centered, axis=-1, keepdims=True)
    return centered * lax.rsqrt(variance + 1e-05) * gain + bias


def token_valid(chain_lengths, tokens_idx, slots):
    chain = tokens_idx // slots
    position = tokens_idx % slots
    chain_ids = jnp.arange(chain_lengths.shape[0], dtype=jnp.int32)
    length_of = jnp.sum(
        jnp.where(chain[:, None] == chain_ids[None, :], chain_lengths[None, :], 0), axis=1
    )
    return (position < length_of).astype(jnp.float32)


def gathered(
    pair,
    chain_lengths,
    norm_in_gain,
    norm_in_bias,
    proj_in,
    gate_in,
    norm_out_gain,
    norm_out_bias,
    proj_out,
    gate_out,
):
    row_count = pair.shape[0]
    col_count = pair.shape[1]
    channels = pair.shape[2]
    hidden = proj_out.shape[0]
    row_index = lax.axis_index("row")
    col_index = lax.axis_index("col")
    slots = row_count * lax.axis_size("row") // chain_lengths.shape[0]
    valid_rows = token_valid(
        chain_lengths, row_index * row_count + jnp.arange(row_count, dtype=jnp.int32), slots
    )
    valid_cols = token_valid(
        chain_lengths, col_index * col_count + jnp.arange(col_count, dtype=jnp.int32), slots
    )
    pair_mask = valid_rows[:, None] * valid_cols[None, :]
    normed = layer_norm(pair.astype(jnp.float32), norm_in_gain, norm_in_bias).astype(jnp.bfloat16)
    flat = normed.reshape(-1, channels)
    values = jnp.dot(flat, proj_in, preferred_element_type=jnp.float32)
    gates = jnp.dot(flat, gate_in, preferred_element_type=jnp.float32)
    mixed = (jax.nn.sigmoid(gates) * values).reshape(row_count, col_count, 2 * hidden) * pair_mask[
        :, :, None
    ]
    left_tile = mixed[:, :, :hidden].astype(jnp.bfloat16)
    right_tile = mixed[:, :, hidden:].astype(jnp.bfloat16)
    ratio = lax.axis_size("row") // lax.axis_size("col")
    right_full = lax.all_gather(right_tile, "col", axis=1, tiled=True)
    received = []
    for part in range(ratio):
        received.append(broadcast(right_full, "row", col_index * ratio + part))
    right_mine = jnp.concatenate(received, axis=0)
    triangle = jnp.einsum(
        "ikh,jkh->ijh",
        lax.all_gather(left_tile, "col", axis=1, tiled=True),
        right_mine,
        preferred_element_type=jnp.float32,
    )
    tri_normed = layer_norm(triangle, norm_out_gain, norm_out_bias).astype(jnp.bfloat16)
    projected = jnp.dot(
        tri_normed.reshape(-1, hidden), proj_out, preferred_element_type=jnp.float32
    )
    gate = jax.nn.sigmoid(jnp.dot(flat, gate_out, preferred_element_type=jnp.float32))
    return (gate * projected).astype(jnp.bfloat16).reshape(row_count, col_count, channels)


def iota2(shape):
    return (
        lax.broadcasted_iota(jnp.int32, shape, 0),
        lax.broadcasted_iota(jnp.int32, shape, 1),
    )


def one_hot(condition):
    return jnp.where(condition, 1.0, 0.0).astype(BF16)


def dot(a, b, a_dim=1, b_dim=0):
    return lax.dot_general(a, b, (((a_dim,), (b_dim,)), ((), ())), preferred_element_type=F32)


def over(value, size):
    if size & (size - 1):
        return value // size
    return lax.shift_right_logical(value, jnp.full_like(value, size.bit_length() - 1))


def rest(value, size):
    return value % size if size & (size - 1) else value & (size - 1)


def over(value, size):
    if size & (size - 1):
        return value // size
    return lax.shift_right_logical(value, jnp.full_like(value, size.bit_length() - 1))


def rest(value, size):
    return value % size if size & (size - 1) else value & (size - 1)


def fetch(sources, targets, sems):
    copies = [
        pltpu.make_async_copy(source, target, sems.at[n])
        for n, (source, target) in enumerate(zip(sources, targets))
    ]
    for copy in copies:
        copy.start()
    return copies


def sigmoid(halved):
    return 0.5 + 0.5 * jnp.tanh(halved)


def exchange_blocks(arrays, cols):
    lane = over(lax.broadcasted_iota(jnp.int32, (1, LANES), 1), cols)
    arrays, step = list(arrays), 1
    while step < len(arrays):
        upper = lane & step != 0
        for n in range(len(arrays)):
            if n // step % 2 == 0:
                a, b = arrays[n], arrays[n + step]
                arrays[n] = jnp.where(upper, pltpu.roll(b, step * cols, 1), a)
                arrays[n + step] = jnp.where(upper, b, pltpu.roll(a, LANES - step * cols, 1))
        step *= 2
    return arrays


def order_kernel(order_ref):
    out, source = iota2(order_ref.shape)
    order_ref[...] = one_hot(
        (over(out, SOME) == rest(source, SOME)) & (rest(out, SOME) == over(source, SOME))
    )


def column(row):
    a, b = iota2((LANES, LANES))
    return jnp.sum(jnp.where(a == b, row, 0.0), axis=1, keepdims=True)


def cell_mask(lengths, slots, rows, cols):
    cell = lax.broadcasted_iota(jnp.int32, (1, rows * cols), 1)

    def valid(token):
        length = jnp.zeros_like(token)
        for chain in range(lengths.shape[1]):
            length = jnp.where(
                over(token, slots) == chain, lengths[:, chain : chain + 1], length
            )
        return rest(token, slots) < length

    row_ok = valid(lax.axis_index("row") * rows + over(cell, cols))
    col_ok = valid(lax.axis_index("col") * cols + rest(cell, cols))
    return jnp.where(row_ok & col_ok, 1.0, 0.0)


def mix_kernel(
    slots,
    order_ref,
    chain_ref,
    pair_ref,
    gain_ref,
    bias_ref,
    proj_ref,
    gate_ref,
    last_gain_ref,
    last_bias_ref,
    sent_ref,
    normed_ref,
    last_gain_out,
    last_bias_out,
):
    rows, cols, channels = pair_ref.shape
    hidden = proj_ref.shape[1] // 2
    cells = rows * cols
    inner = LANES // cols
    groups = rows // inner
    chunks = sent_ref.shape[0]
    flat = pair_ref[...].reshape(cells, channels).astype(F32)
    normed = layer_norm(flat, gain_ref[...], bias_ref[...]).astype(BF16)
    normed_ref[...] = normed
    for source, target in ((last_gain_ref, last_gain_out), (last_bias_ref, last_bias_out)):
        target[...] = jnp.broadcast_to(column(source[...]), target.shape)

    values = dot(proj_ref[...], normed, 0, 1)
    gates = dot(gate_ref[...] * 0.5, normed, 0, 1)
    mask = cell_mask(chain_ref[...], slots, rows, cols)
    mixed = (sigmoid(gates) * values * mask).astype(BF16)

    by_row = []
    for side in range(2):
        lines = []
        for g in range(groups):
            lines += exchange_blocks(
                [
                    mixed[
                        side * hidden + n * chunks : side * hidden + (n + 1) * chunks,
                        g * LANES : (g + 1) * LANES,
                    ]
                    for n in range(inner)
                ],
                cols,
            )
        by_row.append(lines)
    order = order_ref[...]
    for part in range(chunks // SOME):
        for side in range(2):
            stack = jnp.concatenate(
                [line[part * SOME : (part + 1) * SOME] for line in by_row[side]], axis=0
            )
            sent_ref[part * SOME : (part + 1) * SOME, side * rows : (side + 1) * rows] = (
                dot(order, stack).astype(BF16).reshape(SOME, rows, LANES)
            )


def triangle_kernel(ring_in, ring_out, grid_rows, grid_cols, rows, cols, got_ref, sent_ref):
    inner = LANES // cols

    def place(ring, r, c):
        return ring.index(r * grid_cols + c)

    def side(which):
        return jnp.concatenate(
            [
                jnp.concatenate(
                    [
                        got_ref[place(ring_in, r, c), which * rows : (which + 1) * rows]
                        for r in range(grid_rows)
                    ],
                    axis=0,
                )
                for c in range(grid_cols)
            ],
            axis=1,
        )

    left, right = side(0), side(1)
    lane = lax.broadcasted_iota(jnp.int32, (1, grid_cols * LANES), 1)
    by_channel = [right * one_hot(over(rest(lane, LANES), cols) == n) for n in range(inner)]
    right_by = jnp.concatenate(
        [
            by_channel[n][c * cols : (c + 1) * cols]
            for c in range(grid_cols)
            for n in range(inner)
        ],
        axis=0,
    )
    sums = dot(left, right_by, 1, 1).astype(BF16)
    for c in range(grid_cols):
        for r in range(grid_rows):
            sent_ref[place(ring_out, r, c)] = sums[r * rows : (r + 1) * rows, c * LANES : (c + 1) * LANES]


def update_kernel(
    places,
    got_ref,
    order_ref,
    normed_ref,
    gain_ref,
    bias_ref,
    proj_ref,
    gate_ref,
    out_hbm,
    out_ref,
    out_sems,
):
    rows, cols, channels = out_ref.shape
    chunks = got_ref.shape[0]
    inner = LANES // cols
    groups = rows // inner
    order = order_ref[...]
    parts = [
        dot(
            order,
            jnp.concatenate(
                [got_ref[place] for place in places[part * SOME : (part + 1) * SOME]], axis=0
            ),
        ).astype(BF16)
        for part in range(chunks // SOME)
    ]
    lines = [
        jnp.concatenate([part[row * SOME : (row + 1) * SOME] for part in parts], axis=0)
        for row in range(rows)
    ]
    gain, bias = gain_ref[...], bias_ref[...]
    opened = sigmoid(dot(normed_ref[...], gate_ref[...] * 0.5))
    results = []
    for g in range(groups):
        values = jnp.concatenate(
            exchange_blocks(lines[g * inner : (g + 1) * inner], cols), axis=0
        ).astype(F32)
        mean = jnp.mean(values, axis=0, keepdims=True)
        centered = values - mean
        variance = jnp.mean(centered * centered, axis=0, keepdims=True)
        tri_normed = (centered * lax.rsqrt(variance + 1e-05) * gain + bias).astype(BF16)
        projected = dot(tri_normed, proj_ref[...], 0, 0)
        update = (opened[g * LANES : (g + 1) * LANES] * projected).astype(BF16)
        here = pl.ds(g * inner, inner)
        out_ref[here] = update.reshape(inner, cols, channels)
        results.append(pltpu.make_async_copy(out_ref.at[here], out_hbm.at[here], out_sems.at[g]))
        results[-1].start()
    for copy in results:
        copy.wait()


VMEM = pl.BlockSpec(memory_space=pltpu.VMEM)
HBM = pl.BlockSpec(memory_space=pltpu.HBM)
PARAMS = pltpu.CompilerParams(vmem_limit_bytes=32 * 1024 * 1024)


def ring_of(axes, grid_rows, grid_cols):
    sizes = {"z": grid_rows // 2, "y": 2, "x": grid_cols // 2, "c": 2}
    strides = {"z": 2 * grid_cols, "y": grid_cols, "x": 2, "c": 1}
    ring = [0]
    for axis in axes:
        ring = [device + n * strides[axis] for device in ring for n in range(sizes[axis])]
    return ring


def exchanged(
    grid_rows,
    grid_cols,
    pair,
    chain_lengths,
    norm_in_gain,
    norm_in_bias,
    proj_in,
    gate_in,
    norm_out_gain,
    norm_out_bias,
    proj_out,
    gate_out,
):
    rows, cols, channels = pair.shape
    hidden = proj_out.shape[0]
    devices = grid_rows * grid_cols
    slots = rows * grid_rows // chain_lengths.shape[0]
    order = pl.pallas_call(
        order_kernel,
        out_shape=jax.ShapeDtypeStruct((SOME * SOME, SOME * SOME), BF16),
        out_specs=VMEM,
        compiler_params=PARAMS,
        cost_estimate=pl.CostEstimate(flops=10**9, bytes_accessed=10**6, transcendentals=0),
        name="order",
    )()
    square = jax.ShapeDtypeStruct((LANES, LANES), F32)
    sent, normed, last_gain, last_bias = pl.pallas_call(
        functools.partial(mix_kernel, slots),
        out_shape=(
            jax.ShapeDtypeStruct((devices, 2 * rows, LANES), BF16),
            jax.ShapeDtypeStruct((rows * cols, channels), BF16),
            square,
            square,
        ),
        in_specs=[VMEM] * 9,
        out_specs=[VMEM] * 4,
        compiler_params=PARAMS,
        name="mix",
    )(
        order,
        chain_lengths.reshape(1, -1),
        pair,
        norm_in_gain.reshape(1, LANES),
        norm_in_bias.reshape(1, LANES),
        proj_in,
        gate_in,
        norm_out_gain.reshape(1, LANES),
        norm_out_bias.reshape(1, LANES),
    )
    ring_in = ring_of("xyzc", grid_rows, grid_cols)
    ring_out = ring_of("xcyz", grid_rows, grid_cols)

    def exchange(chunks, ring):
        return lax.all_to_all(
            chunks, ("row", "col"), 0, 0, tiled=True, axis_index_groups=[ring]
        )

    got = exchange(sent, ring_in)
    sums = pl.pallas_call(
        functools.partial(triangle_kernel, ring_in, ring_out, grid_rows, grid_cols, rows, cols),
        out_shape=jax.ShapeDtypeStruct((devices, rows, LANES), BF16),
        in_specs=[VMEM],
        out_specs=VMEM,
        compiler_params=PARAMS,
        name="triangle",
    )(got)
    mine = exchange(sums, ring_out)
    places = [ring_out.index(device) for device in ring_in]
    return pl.pallas_call(
        functools.partial(update_kernel, places),
        out_shape=jax.ShapeDtypeStruct((rows, cols, channels), BF16),
        in_specs=[VMEM] * 7,
        out_specs=HBM,
        scratch_shapes=[
            pltpu.VMEM((rows, cols, channels), BF16),
            pltpu.SemaphoreType.DMA((rows * cols // LANES,)),
        ],
        compiler_params=PARAMS,
        name="update",
    )(mine, order, normed, last_gain, last_bias, proj_out, gate_out)


def solution(mesh):
    grid_rows, grid_cols = mesh.shape["row"], mesh.shape["col"]
    def fits(rows, cols, channels, hidden):
        devices = grid_rows * grid_cols
        inner = LANES // cols
        return (
            channels == LANES
            and hidden == LANES
            and inner * cols == LANES
            and inner & (inner - 1) == 0
            and inner * devices == hidden
            and rows == SOME
            and rows % inner == 0
            and devices % SOME == 0
            and grid_rows % 2 == 0
            and grid_cols % 2 == 0
        )

    def call(*arrays):
        tokens, others, channels = arrays[0].shape
        hidden = arrays[8].shape[0]
        if fits(tokens // grid_rows, others // grid_cols, channels, hidden):
            return jax.shard_map(
                functools.partial(exchanged, grid_rows, grid_cols),
                mesh=mesh,
                in_specs=(P("row", "col", None),) + (P(),) * 9,
                out_specs=P("row", "col", None),
                check_vma=False,
            )(*arrays)
        return jax.shard_map(
            gathered,
            mesh=mesh,
            in_specs=(P("row", "col", None),) + (P(),) * 9,
            out_specs=P("row", "col", None),
            check_vma=False,
        )(*arrays)

    return call
```

```python
import functools
import jax
import jax.numpy as jnp
from jax import lax
from jax.experimental import pallas as pl
from jax.experimental.pallas import tpu as pltpu
from jax.sharding import PartitionSpec as P

LANES = 128
SOME = 16
F32 = jnp.float32
BF16 = jnp.bfloat16


def broadcast(value, axis, source):
    kept = jnp.where(lax.axis_index(axis) == source, value, 0).astype(value.dtype)
    return lax.psum(kept, axis)


def layer_norm(values, gain, bias):
    mean = jnp.mean(values, axis=-1, keepdims=True)
    centered = values - mean
    variance = jnp.mean(centered * centered, axis=-1, keepdims=True)
    return centered * lax.rsqrt(variance + 1e-05) * gain + bias


def token_valid(chain_lengths, tokens_idx, slots):
    chain = tokens_idx // slots
    position = tokens_idx % slots
    chain_ids = jnp.arange(chain_lengths.shape[0], dtype=jnp.int32)
    length_of = jnp.sum(
        jnp.where(chain[:, None] == chain_ids[None, :], chain_lengths[None, :], 0), axis=1
    )
    return (position < length_of).astype(jnp.float32)


def gathered(
    pair,
    chain_lengths,
    norm_in_gain,
    norm_in_bias,
    proj_in,
    gate_in,
    norm_out_gain,
    norm_out_bias,
    proj_out,
    gate_out,
):
    row_count = pair.shape[0]
    col_count = pair.shape[1]
    channels = pair.shape[2]
    hidden = proj_out.shape[0]
    row_index = lax.axis_index("row")
    col_index = lax.axis_index("col")
    slots = row_count * lax.axis_size("row") // chain_lengths.shape[0]
    valid_rows = token_valid(
        chain_lengths, row_index * row_count + jnp.arange(row_count, dtype=jnp.int32), slots
    )
    valid_cols = token_valid(
        chain_lengths, col_index * col_count + jnp.arange(col_count, dtype=jnp.int32), slots
    )
    pair_mask = valid_rows[:, None] * valid_cols[None, :]
    normed = layer_norm(pair.astype(jnp.float32), norm_in_gain, norm_in_bias).astype(jnp.bfloat16)
    flat = normed.reshape(-1, channels)
    values = jnp.dot(flat, proj_in, preferred_element_type=jnp.float32)
    gates = jnp.dot(flat, gate_in, preferred_element_type=jnp.float32)
    mixed = (jax.nn.sigmoid(gates) * values).reshape(row_count, col_count, 2 * hidden) * pair_mask[
        :, :, None
    ]
    left_tile = mixed[:, :, :hidden].astype(jnp.bfloat16)
    right_tile = mixed[:, :, hidden:].astype(jnp.bfloat16)
    ratio = lax.axis_size("row") // lax.axis_size("col")
    right_full = lax.all_gather(right_tile, "col", axis=1, tiled=True)
    received = []
    for part in range(ratio):
        received.append(broadcast(right_full, "row", col_index * ratio + part))
    right_mine = jnp.concatenate(received, axis=0)
    triangle = jnp.einsum(
        "ikh,jkh->ijh",
        lax.all_gather(left_tile, "col", axis=1, tiled=True),
        right_mine,
        preferred_element_type=jnp.float32,
    )
    tri_normed = layer_norm(triangle, norm_out_gain, norm_out_bias).astype(jnp.bfloat16)
    projected = jnp.dot(
        tri_normed.reshape(-1, hidden), proj_out, preferred_element_type=jnp.float32
    )
    gate = jax.nn.sigmoid(jnp.dot(flat, gate_out, preferred_element_type=jnp.float32))
    return (gate * projected).astype(jnp.bfloat16).reshape(row_count, col_count, channels)


def iota2(shape):
    return (
        lax.broadcasted_iota(jnp.int32, shape, 0),
        lax.broadcasted_iota(jnp.int32, shape, 1),
    )


def one_hot(condition):
    return jnp.where(condition, 1.0, 0.0).astype(BF16)


def dot(a, b, a_dim=1, b_dim=0):
    return lax.dot_general(a, b, (((a_dim,), (b_dim,)), ((), ())), preferred_element_type=F32)


def over(value, size):
    if size & (size - 1):
        return value // size
    return lax.shift_right_logical(value, jnp.full_like(value, size.bit_length() - 1))


def rest(value, size):
    return value % size if size & (size - 1) else value & (size - 1)


def over(value, size):
    if size & (size - 1):
        return value // size
    return lax.shift_right_logical(value, jnp.full_like(value, size.bit_length() - 1))


def rest(value, size):
    return value % size if size & (size - 1) else value & (size - 1)


def fetch(sources, targets, sems):
    copies = [
        pltpu.make_async_copy(source, target, sems.at[n])
        for n, (source, target) in enumerate(zip(sources, targets))
    ]
    for copy in copies:
        copy.start()
    return copies


def sigmoid(halved):
    return 0.5 + 0.5 * jnp.tanh(halved)


def exchange_blocks(arrays, cols):
    lane = over(lax.broadcasted_iota(jnp.int32, (1, LANES), 1), cols)
    arrays, step = list(arrays), 1
    while step < len(arrays):
        upper = lane & step != 0
        for n in range(len(arrays)):
            if n // step % 2 == 0:
                a, b = arrays[n], arrays[n + step]
                arrays[n] = jnp.where(upper, pltpu.roll(b, step * cols, 1), a)
                arrays[n + step] = jnp.where(upper, b, pltpu.roll(a, LANES - step * cols, 1))
        step *= 2
    return arrays


def order_kernel(order_ref):
    out, source = iota2(order_ref.shape)
    order_ref[...] = one_hot(
        (over(out, SOME) == rest(source, SOME)) & (rest(out, SOME) == over(source, SOME))
    )


def column(row):
    a, b = iota2((LANES, LANES))
    return jnp.sum(jnp.where(a == b, row, 0.0), axis=1, keepdims=True)


def cell_mask(lengths, slots, rows, cols):
    cell = lax.broadcasted_iota(jnp.int32, (1, rows * cols), 1)

    def valid(token):
        length = jnp.zeros_like(token)
        for chain in range(lengths.shape[1]):
            length = jnp.where(
                over(token, slots) == chain, lengths[:, chain : chain + 1], length
            )
        return rest(token, slots) < length

    row_ok = valid(lax.axis_index(("z", "y")) * rows + over(cell, cols))
    col_ok = valid(lax.axis_index(("x", "c")) * cols + rest(cell, cols))
    return jnp.where(row_ok & col_ok, 1.0, 0.0)


def mix_kernel(
    slots,
    order_ref,
    chain_ref,
    pair_ref,
    gain_ref,
    bias_ref,
    proj_ref,
    gate_ref,
    last_gain_ref,
    last_bias_ref,
    sent_ref,
    normed_ref,
    last_gain_out,
    last_bias_out,
):
    rows, cols, channels = pair_ref.shape
    hidden = proj_ref.shape[1] // 2
    cells = rows * cols
    inner = LANES // cols
    groups = rows // inner
    chunks = sent_ref.shape[0]
    flat = pair_ref[...].reshape(cells, channels).astype(F32)
    normed = layer_norm(flat, gain_ref[...], bias_ref[...]).astype(BF16)
    normed_ref[...] = normed
    for source, target in ((last_gain_ref, last_gain_out), (last_bias_ref, last_bias_out)):
        target[...] = jnp.broadcast_to(column(source[...]), target.shape)

    values = dot(proj_ref[...], normed, 0, 1)
    gates = dot(gate_ref[...] * 0.5, normed, 0, 1)
    mask = cell_mask(chain_ref[...], slots, rows, cols)
    mixed = (sigmoid(gates) * values * mask).astype(BF16)

    by_row = []
    for side in range(2):
        lines = []
        for g in range(groups):
            lines += exchange_blocks(
                [
                    mixed[
                        side * hidden + n * chunks : side * hidden + (n + 1) * chunks,
                        g * LANES : (g + 1) * LANES,
                    ]
                    for n in range(inner)
                ],
                cols,
            )
        by_row.append(lines)
    order = order_ref[...]
    for part in range(chunks // SOME):
        for side in range(2):
            stack = jnp.concatenate(
                [line[part * SOME : (part + 1) * SOME] for line in by_row[side]], axis=0
            )
            sent_ref[part * SOME : (part + 1) * SOME, side * rows : (side + 1) * rows] = (
                dot(order, stack).astype(BF16).reshape(SOME, rows, LANES)
            )


def triangle_kernel(ring_in, ring_out, grid_rows, grid_cols, rows, cols, got_ref, sent_ref):
    inner = LANES // cols

    def place(ring, r, c):
        return ring.index(r * grid_cols + c)

    def side(which):
        return jnp.concatenate(
            [
                jnp.concatenate(
                    [
                        got_ref[place(ring_in, r, c), which * rows : (which + 1) * rows]
                        for r in range(grid_rows)
                    ],
                    axis=0,
                )
                for c in range(grid_cols)
            ],
            axis=1,
        )

    left, right = side(0), side(1)
    lane = lax.broadcasted_iota(jnp.int32, (1, grid_cols * LANES), 1)
    by_channel = [right * one_hot(over(rest(lane, LANES), cols) == n) for n in range(inner)]
    right_by = jnp.concatenate(
        [
            by_channel[n][c * cols : (c + 1) * cols]
            for c in range(grid_cols)
            for n in range(inner)
        ],
        axis=0,
    )
    sums = dot(left, right_by, 1, 1).astype(BF16)
    for c in range(grid_cols):
        for r in range(grid_rows):
            sent_ref[place(ring_out, r, c)] = sums[r * rows : (r + 1) * rows, c * LANES : (c + 1) * LANES]


def update_kernel(
    places,
    got_ref,
    order_ref,
    normed_ref,
    gain_ref,
    bias_ref,
    proj_ref,
    gate_ref,
    out_hbm,
    out_ref,
    out_sems,
):
    rows, cols, channels = out_ref.shape
    chunks = got_ref.shape[0]
    inner = LANES // cols
    groups = rows // inner
    order = order_ref[...]
    parts = [
        dot(
            order,
            jnp.concatenate(
                [got_ref[place] for place in places[part * SOME : (part + 1) * SOME]], axis=0
            ),
        ).astype(BF16)
        for part in range(chunks // SOME)
    ]
    lines = [
        jnp.concatenate([part[row * SOME : (row + 1) * SOME] for part in parts], axis=0)
        for row in range(rows)
    ]
    gain, bias = gain_ref[...], bias_ref[...]
    opened = sigmoid(dot(normed_ref[...], gate_ref[...] * 0.5))
    results = []
    for g in range(groups):
        values = jnp.concatenate(
            exchange_blocks(lines[g * inner : (g + 1) * inner], cols), axis=0
        ).astype(F32)
        mean = jnp.mean(values, axis=0, keepdims=True)
        centered = values - mean
        variance = jnp.mean(centered * centered, axis=0, keepdims=True)
        tri_normed = (centered * lax.rsqrt(variance + 1e-05) * gain + bias).astype(BF16)
        projected = dot(tri_normed, proj_ref[...], 0, 0)
        update = (opened[g * LANES : (g + 1) * LANES] * projected).astype(BF16)
        here = pl.ds(g * inner, inner)
        out_ref[here] = update.reshape(inner, cols, channels)
        results.append(pltpu.make_async_copy(out_ref.at[here], out_hbm.at[here], out_sems.at[g]))
        results[-1].start()
    for copy in results:
        copy.wait()


VMEM = pl.BlockSpec(memory_space=pltpu.VMEM)
HBM = pl.BlockSpec(memory_space=pltpu.HBM)
PARAMS = pltpu.CompilerParams(vmem_limit_bytes=32 * 1024 * 1024)


def ring_of(axes, grid_rows, grid_cols):
    sizes = {"z": grid_rows // 2, "y": 2, "x": grid_cols // 2, "c": 2}
    strides = {"z": 2 * grid_cols, "y": grid_cols, "x": 2, "c": 1}
    ring = [0]
    for axis in axes:
        ring = [device + n * strides[axis] for device in ring for n in range(sizes[axis])]
    return ring


def exchanged(
    grid_rows,
    grid_cols,
    pair,
    chain_lengths,
    norm_in_gain,
    norm_in_bias,
    proj_in,
    gate_in,
    norm_out_gain,
    norm_out_bias,
    proj_out,
    gate_out,
):
    rows, cols, channels = pair.shape
    hidden = proj_out.shape[0]
    devices = grid_rows * grid_cols
    slots = rows * grid_rows // chain_lengths.shape[0]
    order = pl.pallas_call(
        order_kernel,
        out_shape=jax.ShapeDtypeStruct((SOME * SOME, SOME * SOME), BF16),
        out_specs=VMEM,
        compiler_params=PARAMS,
        cost_estimate=pl.CostEstimate(flops=10**9, bytes_accessed=10**6, transcendentals=0),
        name="order",
    )()
    square = jax.ShapeDtypeStruct((LANES, LANES), F32)
    sent, normed, last_gain, last_bias = pl.pallas_call(
        functools.partial(mix_kernel, slots),
        out_shape=(
            jax.ShapeDtypeStruct((devices, 2 * rows, LANES), BF16),
            jax.ShapeDtypeStruct((rows * cols, channels), BF16),
            square,
            square,
        ),
        in_specs=[VMEM] * 9,
        out_specs=[VMEM] * 4,
        compiler_params=PARAMS,
        name="mix",
    )(
        order,
        chain_lengths.reshape(1, -1),
        pair,
        norm_in_gain.reshape(1, LANES),
        norm_in_bias.reshape(1, LANES),
        proj_in,
        gate_in,
        norm_out_gain.reshape(1, LANES),
        norm_out_bias.reshape(1, LANES),
    )
    axes_in, axes_out = "xyzc", "xcyz"
    ring_in = ring_of(axes_in, grid_rows, grid_cols)
    ring_out = ring_of(axes_out, grid_rows, grid_cols)
    got = lax.all_to_all(sent, tuple(axes_in), 0, 0, tiled=True)
    sums = pl.pallas_call(
        functools.partial(triangle_kernel, ring_in, ring_out, grid_rows, grid_cols, rows, cols),
        out_shape=jax.ShapeDtypeStruct((devices, rows, LANES), BF16),
        in_specs=[VMEM],
        out_specs=VMEM,
        compiler_params=PARAMS,
        name="triangle",
    )(got)
    mine = lax.all_to_all(sums, tuple(axes_out), 0, 0, tiled=True)
    places = [ring_out.index(device) for device in ring_in]
    return pl.pallas_call(
        functools.partial(update_kernel, places),
        out_shape=jax.ShapeDtypeStruct((rows, cols, channels), BF16),
        in_specs=[VMEM] * 7,
        out_specs=HBM,
        scratch_shapes=[
            pltpu.VMEM((rows, cols, channels), BF16),
            pltpu.SemaphoreType.DMA((rows * cols // LANES,)),
        ],
        compiler_params=PARAMS,
        name="update",
    )(mine, order, normed, last_gain, last_bias, proj_out, gate_out)


def solution(mesh):
    grid_rows, grid_cols = mesh.shape["row"], mesh.shape["col"]
    fine = jax.sharding.Mesh(
        mesh.devices.reshape(max(grid_rows // 2, 1), -1, max(grid_cols // 2, 1), min(grid_cols, 2)),
        ("z", "y", "x", "c"),
    )

    def fits(rows, cols, channels, hidden):
        devices = grid_rows * grid_cols
        inner = LANES // cols
        return (
            channels == LANES
            and hidden == LANES
            and inner * cols == LANES
            and inner & (inner - 1) == 0
            and inner * devices == hidden
            and rows == SOME
            and rows % inner == 0
            and devices % SOME == 0
            and grid_rows % 2 == 0
            and grid_cols % 2 == 0
        )

    def call(*arrays):
        tokens, others, channels = arrays[0].shape
        hidden = arrays[8].shape[0]
        if fits(tokens // grid_rows, others // grid_cols, channels, hidden):
            return jax.shard_map(
                functools.partial(exchanged, grid_rows, grid_cols),
                mesh=fine,
                in_specs=(P(("z", "y"), ("x", "c"), None),) + (P(),) * 9,
                out_specs=P(("z", "y"), ("x", "c"), None),
                check_vma=False,
            )(*arrays)
        return jax.shard_map(
            gathered,
            mesh=mesh,
            in_specs=(P("row", "col", None),) + (P(),) * 9,
            out_specs=P("row", "col", None),
            check_vma=False,
        )(*arrays)

    return call
```

```python
import functools
import jax
import jax.numpy as jnp
from jax import lax
from jax.experimental import pallas as pl
from jax.experimental.pallas import tpu as pltpu
from jax.sharding import PartitionSpec as P

LANES = 128
SOME = 16
F32 = jnp.float32
BF16 = jnp.bfloat16


def broadcast(value, axis, source):
    kept = jnp.where(lax.axis_index(axis) == source, value, 0).astype(value.dtype)
    return lax.psum(kept, axis)


def layer_norm(values, gain, bias):
    mean = jnp.mean(values, axis=-1, keepdims=True)
    centered = values - mean
    variance = jnp.mean(centered * centered, axis=-1, keepdims=True)
    return centered * lax.rsqrt(variance + 1e-05) * gain + bias


def token_valid(chain_lengths, tokens_idx, slots):
    chain = tokens_idx // slots
    position = tokens_idx % slots
    chain_ids = jnp.arange(chain_lengths.shape[0], dtype=jnp.int32)
    length_of = jnp.sum(
        jnp.where(chain[:, None] == chain_ids[None, :], chain_lengths[None, :], 0), axis=1
    )
    return (position < length_of).astype(jnp.float32)


def gathered(
    pair,
    chain_lengths,
    norm_in_gain,
    norm_in_bias,
    proj_in,
    gate_in,
    norm_out_gain,
    norm_out_bias,
    proj_out,
    gate_out,
):
    row_count = pair.shape[0]
    col_count = pair.shape[1]
    channels = pair.shape[2]
    hidden = proj_out.shape[0]
    row_index = lax.axis_index("row")
    col_index = lax.axis_index("col")
    slots = row_count * lax.axis_size("row") // chain_lengths.shape[0]
    valid_rows = token_valid(
        chain_lengths, row_index * row_count + jnp.arange(row_count, dtype=jnp.int32), slots
    )
    valid_cols = token_valid(
        chain_lengths, col_index * col_count + jnp.arange(col_count, dtype=jnp.int32), slots
    )
    pair_mask = valid_rows[:, None] * valid_cols[None, :]
    normed = layer_norm(pair.astype(jnp.float32), norm_in_gain, norm_in_bias).astype(jnp.bfloat16)
    flat = normed.reshape(-1, channels)
    values = jnp.dot(flat, proj_in, preferred_element_type=jnp.float32)
    gates = jnp.dot(flat, gate_in, preferred_element_type=jnp.float32)
    mixed = (jax.nn.sigmoid(gates) * values).reshape(row_count, col_count, 2 * hidden) * pair_mask[
        :, :, None
    ]
    left_tile = mixed[:, :, :hidden].astype(jnp.bfloat16)
    right_tile = mixed[:, :, hidden:].astype(jnp.bfloat16)
    ratio = lax.axis_size("row") // lax.axis_size("col")
    right_full = lax.all_gather(right_tile, "col", axis=1, tiled=True)
    received = []
    for part in range(ratio):
        received.append(broadcast(right_full, "row", col_index * ratio + part))
    right_mine = jnp.concatenate(received, axis=0)
    triangle = jnp.einsum(
        "ikh,jkh->ijh",
        lax.all_gather(left_tile, "col", axis=1, tiled=True),
        right_mine,
        preferred_element_type=jnp.float32,
    )
    tri_normed = layer_norm(triangle, norm_out_gain, norm_out_bias).astype(jnp.bfloat16)
    projected = jnp.dot(
        tri_normed.reshape(-1, hidden), proj_out, preferred_element_type=jnp.float32
    )
    gate = jax.nn.sigmoid(jnp.dot(flat, gate_out, preferred_element_type=jnp.float32))
    return (gate * projected).astype(jnp.bfloat16).reshape(row_count, col_count, channels)


def iota2(shape):
    return (
        lax.broadcasted_iota(jnp.int32, shape, 0),
        lax.broadcasted_iota(jnp.int32, shape, 1),
    )


def one_hot(condition):
    return jnp.where(condition, 1.0, 0.0).astype(BF16)


def dot(a, b, a_dim=1, b_dim=0):
    return lax.dot_general(a, b, (((a_dim,), (b_dim,)), ((), ())), preferred_element_type=F32)


def over(value, size):
    if size & (size - 1):
        return value // size
    return lax.shift_right_logical(value, jnp.full_like(value, size.bit_length() - 1))


def rest(value, size):
    return value % size if size & (size - 1) else value & (size - 1)


def over(value, size):
    if size & (size - 1):
        return value // size
    return lax.shift_right_logical(value, jnp.full_like(value, size.bit_length() - 1))


def rest(value, size):
    return value % size if size & (size - 1) else value & (size - 1)


def fetch(sources, targets, sems):
    copies = [
        pltpu.make_async_copy(source, target, sems.at[n])
        for n, (source, target) in enumerate(zip(sources, targets))
    ]
    for copy in copies:
        copy.start()
    return copies


def sigmoid(halved):
    return 0.5 + 0.5 * jnp.tanh(halved)


def exchange_blocks(arrays, cols):
    lane = over(lax.broadcasted_iota(jnp.int32, (1, LANES), 1), cols)
    arrays, step = list(arrays), 1
    while step < len(arrays):
        upper = lane & step != 0
        for n in range(len(arrays)):
            if n // step % 2 == 0:
                a, b = arrays[n], arrays[n + step]
                arrays[n] = jnp.where(upper, pltpu.roll(b, step * cols, 1), a)
                arrays[n + step] = jnp.where(upper, b, pltpu.roll(a, LANES - step * cols, 1))
        step *= 2
    return arrays


def order_kernel(order_ref):
    out, source = iota2(order_ref.shape)
    order_ref[...] = one_hot(
        (over(out, SOME) == rest(source, SOME)) & (rest(out, SOME) == over(source, SOME))
    )


def column(row):
    a, b = iota2((LANES, LANES))
    return jnp.sum(jnp.where(a == b, row, 0.0), axis=1, keepdims=True)


def cell_mask(lengths, slots, rows, cols):
    cell = lax.broadcasted_iota(jnp.int32, (1, rows * cols), 1)

    def valid(token):
        length = jnp.zeros_like(token)
        for chain in range(lengths.shape[1]):
            length = jnp.where(
                over(token, slots) == chain, lengths[:, chain : chain + 1], length
            )
        return rest(token, slots) < length

    row_ok = valid(lax.axis_index(("z", "y")) * rows + over(cell, cols))
    col_ok = valid(lax.axis_index(("x", "c")) * cols + rest(cell, cols))
    return jnp.where(row_ok & col_ok, 1.0, 0.0)


def mix_kernel(
    slots,
    order_ref,
    chain_ref,
    pair_ref,
    gain_ref,
    bias_ref,
    proj_ref,
    gate_ref,
    last_gain_ref,
    last_bias_ref,
    sent_ref,
    normed_ref,
    last_gain_out,
    last_bias_out,
):
    rows, cols, channels = pair_ref.shape
    hidden = proj_ref.shape[1] // 2
    cells = rows * cols
    inner = LANES // cols
    groups = rows // inner
    chunks = sent_ref.shape[0]
    flat = pair_ref[...].reshape(cells, channels).astype(F32)
    normed = layer_norm(flat, gain_ref[...], bias_ref[...]).astype(BF16)
    normed_ref[...] = normed
    for source, target in ((last_gain_ref, last_gain_out), (last_bias_ref, last_bias_out)):
        target[...] = jnp.broadcast_to(column(source[...]), target.shape)

    values = dot(proj_ref[...], normed, 0, 1)
    gates = dot(gate_ref[...] * 0.5, normed, 0, 1)
    mask = cell_mask(chain_ref[...], slots, rows, cols)
    mixed = (sigmoid(gates) * values * mask).astype(BF16)

    by_row = []
    for side in range(2):
        lines = []
        for g in range(groups):
            lines += exchange_blocks(
                [
                    mixed[
                        side * hidden + n * chunks : side * hidden + (n + 1) * chunks,
                        g * LANES : (g + 1) * LANES,
                    ]
                    for n in range(inner)
                ],
                cols,
            )
        by_row.append(lines)
    order = order_ref[...]
    for part in range(chunks // SOME):
        for side in range(2):
            stack = jnp.concatenate(
                [line[part * SOME : (part + 1) * SOME] for line in by_row[side]], axis=0
            )
            sent_ref[part * SOME : (part + 1) * SOME, side * rows : (side + 1) * rows] = (
                dot(order, stack).astype(BF16).reshape(SOME, rows, LANES)
            )


def triangle_kernel(ring_in, ring_out, grid_rows, grid_cols, rows, cols, got_ref, sent_ref):
    inner = LANES // cols

    def place(ring, r, c):
        return ring.index(r * grid_cols + c)

    def side(which):
        return jnp.concatenate(
            [
                jnp.concatenate(
                    [
                        got_ref[place(ring_in, r, c), which * rows : (which + 1) * rows]
                        for r in range(grid_rows)
                    ],
                    axis=0,
                )
                for c in range(grid_cols)
            ],
            axis=1,
        )

    left, right = side(0), side(1)
    lane = lax.broadcasted_iota(jnp.int32, (1, grid_cols * LANES), 1)
    by_channel = [right * one_hot(over(rest(lane, LANES), cols) == n) for n in range(inner)]
    right_by = jnp.concatenate(
        [
            by_channel[n][c * cols : (c + 1) * cols]
            for c in range(grid_cols)
            for n in range(inner)
        ],
        axis=0,
    )
    sums = dot(left, right_by, 1, 1).astype(BF16)
    for c in range(grid_cols):
        for r in range(grid_rows):
            sent_ref[place(ring_out, r, c)] = sums[r * rows : (r + 1) * rows, c * LANES : (c + 1) * LANES]


def update_kernel(
    places,
    got_ref,
    order_ref,
    normed_ref,
    gain_ref,
    bias_ref,
    proj_ref,
    gate_ref,
    out_hbm,
    out_ref,
    out_sems,
):
    rows, cols, channels = out_ref.shape
    chunks = got_ref.shape[0]
    inner = LANES // cols
    groups = rows // inner
    order = order_ref[...]
    parts = [
        dot(
            order,
            jnp.concatenate(
                [got_ref[place] for place in places[part * SOME : (part + 1) * SOME]], axis=0
            ),
        ).astype(BF16)
        for part in range(chunks // SOME)
    ]
    lines = [
        jnp.concatenate([part[row * SOME : (row + 1) * SOME] for part in parts], axis=0)
        for row in range(rows)
    ]
    gain, bias = gain_ref[...], bias_ref[...]
    opened = sigmoid(dot(normed_ref[...], gate_ref[...] * 0.5))
    results = []
    for g in range(groups):
        values = jnp.concatenate(
            exchange_blocks(lines[g * inner : (g + 1) * inner], cols), axis=0
        ).astype(F32)
        mean = jnp.mean(values, axis=0, keepdims=True)
        centered = values - mean
        variance = jnp.mean(centered * centered, axis=0, keepdims=True)
        tri_normed = (centered * lax.rsqrt(variance + 1e-05) * gain + bias).astype(BF16)
        projected = dot(tri_normed, proj_ref[...], 0, 0)
        update = (opened[g * LANES : (g + 1) * LANES] * projected).astype(BF16)
        here = pl.ds(g * inner, inner)
        out_ref[here] = update.reshape(inner, cols, channels)
        results.append(pltpu.make_async_copy(out_ref.at[here], out_hbm.at[here], out_sems.at[g]))
        results[-1].start()
    for copy in results:
        copy.wait()


VMEM = pl.BlockSpec(memory_space=pltpu.VMEM)
HBM = pl.BlockSpec(memory_space=pltpu.HBM)
PARAMS = pltpu.CompilerParams(vmem_limit_bytes=32 * 1024 * 1024)


def ring_of(axes, grid_rows, grid_cols):
    sizes = {"z": grid_rows // 2, "y": 2, "x": grid_cols // 2, "c": 2}
    strides = {"z": 2 * grid_cols, "y": grid_cols, "x": 2, "c": 1}
    ring = [0]
    for axis in axes:
        ring = [device + n * strides[axis] for device in ring for n in range(sizes[axis])]
    return ring


def exchanged(
    grid_rows,
    grid_cols,
    pair,
    chain_lengths,
    norm_in_gain,
    norm_in_bias,
    proj_in,
    gate_in,
    norm_out_gain,
    norm_out_bias,
    proj_out,
    gate_out,
):
    rows, cols, channels = pair.shape
    hidden = proj_out.shape[0]
    devices = grid_rows * grid_cols
    slots = rows * grid_rows // chain_lengths.shape[0]
    order = pl.pallas_call(
        order_kernel,
        out_shape=jax.ShapeDtypeStruct((SOME * SOME, SOME * SOME), BF16),
        out_specs=VMEM,
        compiler_params=PARAMS,
        cost_estimate=pl.CostEstimate(flops=10**9, bytes_accessed=10**6, transcendentals=0),
        name="order",
    )()
    square = jax.ShapeDtypeStruct((LANES, LANES), F32)
    sent, normed, last_gain, last_bias = pl.pallas_call(
        functools.partial(mix_kernel, slots),
        out_shape=(
            jax.ShapeDtypeStruct((devices, 2 * rows, LANES), BF16),
            jax.ShapeDtypeStruct((rows * cols, channels), BF16),
            square,
            square,
        ),
        in_specs=[VMEM] * 9,
        out_specs=[VMEM] * 4,
        compiler_params=PARAMS,
        name="mix",
    )(
        order,
        chain_lengths.reshape(1, -1),
        pair,
        norm_in_gain.reshape(1, LANES),
        norm_in_bias.reshape(1, LANES),
        proj_in,
        gate_in,
        norm_out_gain.reshape(1, LANES),
        norm_out_bias.reshape(1, LANES),
    )
    axes_in, axes_out = "cxyz", "cxyz"
    ring_in = ring_of(axes_in, grid_rows, grid_cols)
    ring_out = ring_of(axes_out, grid_rows, grid_cols)
    got = lax.all_to_all(sent, tuple(axes_in), 0, 0, tiled=True)
    sums = pl.pallas_call(
        functools.partial(triangle_kernel, ring_in, ring_out, grid_rows, grid_cols, rows, cols),
        out_shape=jax.ShapeDtypeStruct((devices, rows, LANES), BF16),
        in_specs=[VMEM],
        out_specs=VMEM,
        compiler_params=PARAMS,
        name="triangle",
    )(got)
    mine = lax.all_to_all(sums, tuple(axes_out), 0, 0, tiled=True)
    places = [ring_out.index(device) for device in ring_in]
    return pl.pallas_call(
        functools.partial(update_kernel, places),
        out_shape=jax.ShapeDtypeStruct((rows, cols, channels), BF16),
        in_specs=[VMEM] * 7,
        out_specs=HBM,
        scratch_shapes=[
            pltpu.VMEM((rows, cols, channels), BF16),
            pltpu.SemaphoreType.DMA((rows * cols // LANES,)),
        ],
        compiler_params=PARAMS,
        name="update",
    )(mine, order, normed, last_gain, last_bias, proj_out, gate_out)


def solution(mesh):
    grid_rows, grid_cols = mesh.shape["row"], mesh.shape["col"]
    fine = jax.sharding.Mesh(
        mesh.devices.reshape(max(grid_rows // 2, 1), -1, max(grid_cols // 2, 1), min(grid_cols, 2)),
        ("z", "y", "x", "c"),
    )

    def fits(rows, cols, channels, hidden):
        devices = grid_rows * grid_cols
        inner = LANES // cols
        return (
            channels == LANES
            and hidden == LANES
            and inner * cols == LANES
            and inner & (inner - 1) == 0
            and inner * devices == hidden
            and rows == SOME
            and rows % inner == 0
            and devices % SOME == 0
            and grid_rows % 2 == 0
            and grid_cols % 2 == 0
        )

    def call(*arrays):
        tokens, others, channels = arrays[0].shape
        hidden = arrays[8].shape[0]
        if fits(tokens // grid_rows, others // grid_cols, channels, hidden):
            return jax.shard_map(
                functools.partial(exchanged, grid_rows, grid_cols),
                mesh=fine,
                in_specs=(P(("z", "y"), ("x", "c"), None),) + (P(),) * 9,
                out_specs=P(("z", "y"), ("x", "c"), None),
                check_vma=False,
            )(*arrays)
        return jax.shard_map(
            gathered,
            mesh=mesh,
            in_specs=(P("row", "col", None),) + (P(),) * 9,
            out_specs=P("row", "col", None),
            check_vma=False,
        )(*arrays)

    return call
```

```python
import functools
import jax
import jax.numpy as jnp
from jax import lax
from jax.experimental import pallas as pl
from jax.experimental.pallas import tpu as pltpu
from jax.sharding import PartitionSpec as P

LANES = 128
SOME = 16
F32 = jnp.float32
BF16 = jnp.bfloat16


def broadcast(value, axis, source):
    kept = jnp.where(lax.axis_index(axis) == source, value, 0).astype(value.dtype)
    return lax.psum(kept, axis)


def layer_norm(values, gain, bias):
    mean = jnp.mean(values, axis=-1, keepdims=True)
    centered = values - mean
    variance = jnp.mean(centered * centered, axis=-1, keepdims=True)
    return centered * lax.rsqrt(variance + 1e-05) * gain + bias


def token_valid(chain_lengths, tokens_idx, slots):
    chain = tokens_idx // slots
    position = tokens_idx % slots
    chain_ids = jnp.arange(chain_lengths.shape[0], dtype=jnp.int32)
    length_of = jnp.sum(
        jnp.where(chain[:, None] == chain_ids[None, :], chain_lengths[None, :], 0), axis=1
    )
    return (position < length_of).astype(jnp.float32)


def gathered(
    pair,
    chain_lengths,
    norm_in_gain,
    norm_in_bias,
    proj_in,
    gate_in,
    norm_out_gain,
    norm_out_bias,
    proj_out,
    gate_out,
):
    row_count = pair.shape[0]
    col_count = pair.shape[1]
    channels = pair.shape[2]
    hidden = proj_out.shape[0]
    row_index = lax.axis_index("row")
    col_index = lax.axis_index("col")
    slots = row_count * lax.axis_size("row") // chain_lengths.shape[0]
    valid_rows = token_valid(
        chain_lengths, row_index * row_count + jnp.arange(row_count, dtype=jnp.int32), slots
    )
    valid_cols = token_valid(
        chain_lengths, col_index * col_count + jnp.arange(col_count, dtype=jnp.int32), slots
    )
    pair_mask = valid_rows[:, None] * valid_cols[None, :]
    normed = layer_norm(pair.astype(jnp.float32), norm_in_gain, norm_in_bias).astype(jnp.bfloat16)
    flat = normed.reshape(-1, channels)
    values = jnp.dot(flat, proj_in, preferred_element_type=jnp.float32)
    gates = jnp.dot(flat, gate_in, preferred_element_type=jnp.float32)
    mixed = (jax.nn.sigmoid(gates) * values).reshape(row_count, col_count, 2 * hidden) * pair_mask[
        :, :, None
    ]
    left_tile = mixed[:, :, :hidden].astype(jnp.bfloat16)
    right_tile = mixed[:, :, hidden:].astype(jnp.bfloat16)
    ratio = lax.axis_size("row") // lax.axis_size("col")
    right_full = lax.all_gather(right_tile, "col", axis=1, tiled=True)
    received = []
    for part in range(ratio):
        received.append(broadcast(right_full, "row", col_index * ratio + part))
    right_mine = jnp.concatenate(received, axis=0)
    triangle = jnp.einsum(
        "ikh,jkh->ijh",
        lax.all_gather(left_tile, "col", axis=1, tiled=True),
        right_mine,
        preferred_element_type=jnp.float32,
    )
    tri_normed = layer_norm(triangle, norm_out_gain, norm_out_bias).astype(jnp.bfloat16)
    projected = jnp.dot(
        tri_normed.reshape(-1, hidden), proj_out, preferred_element_type=jnp.float32
    )
    gate = jax.nn.sigmoid(jnp.dot(flat, gate_out, preferred_element_type=jnp.float32))
    return (gate * projected).astype(jnp.bfloat16).reshape(row_count, col_count, channels)


def iota2(shape):
    return (
        lax.broadcasted_iota(jnp.int32, shape, 0),
        lax.broadcasted_iota(jnp.int32, shape, 1),
    )


def one_hot(condition):
    return jnp.where(condition, 1.0, 0.0).astype(BF16)


def dot(a, b, a_dim=1, b_dim=0):
    return lax.dot_general(a, b, (((a_dim,), (b_dim,)), ((), ())), preferred_element_type=F32)


def over(value, size):
    if size & (size - 1):
        return value // size
    return lax.shift_right_logical(value, jnp.full_like(value, size.bit_length() - 1))


def rest(value, size):
    return value % size if size & (size - 1) else value & (size - 1)


def over(value, size):
    if size & (size - 1):
        return value // size
    return lax.shift_right_logical(value, jnp.full_like(value, size.bit_length() - 1))


def rest(value, size):
    return value % size if size & (size - 1) else value & (size - 1)


def fetch(sources, targets, sems):
    copies = [
        pltpu.make_async_copy(source, target, sems.at[n])
        for n, (source, target) in enumerate(zip(sources, targets))
    ]
    for copy in copies:
        copy.start()
    return copies


def sigmoid(halved):
    return 0.5 + 0.5 * jnp.tanh(halved)


def exchange_blocks(arrays, cols):
    lane = over(lax.broadcasted_iota(jnp.int32, (1, LANES), 1), cols)
    arrays, step = list(arrays), 1
    while step < len(arrays):
        upper = lane & step != 0
        for n in range(len(arrays)):
            if n // step % 2 == 0:
                a, b = arrays[n], arrays[n + step]
                arrays[n] = jnp.where(upper, pltpu.roll(b, step * cols, 1), a)
                arrays[n + step] = jnp.where(upper, b, pltpu.roll(a, LANES - step * cols, 1))
        step *= 2
    return arrays


def order_kernel(order_ref):
    out, source = iota2(order_ref.shape)
    order_ref[...] = one_hot(
        (over(out, SOME) == rest(source, SOME)) & (rest(out, SOME) == over(source, SOME))
    )


def column(row):
    a, b = iota2((LANES, LANES))
    return jnp.sum(jnp.where(a == b, row, 0.0), axis=1, keepdims=True)


def cell_mask(lengths, slots, rows, cols):
    cell = lax.broadcasted_iota(jnp.int32, (1, rows * cols), 1)

    def valid(token):
        length = jnp.zeros_like(token)
        for chain in range(lengths.shape[1]):
            length = jnp.where(
                over(token, slots) == chain, lengths[:, chain : chain + 1], length
            )
        return rest(token, slots) < length

    row_ok = valid(lax.axis_index(("z", "y")) * rows + over(cell, cols))
    col_ok = valid(lax.axis_index(("x", "c")) * cols + rest(cell, cols))
    return jnp.where(row_ok & col_ok, 1.0, 0.0)


def mix_kernel(
    slots,
    order_ref,
    chain_ref,
    pair_ref,
    gain_ref,
    bias_ref,
    proj_ref,
    gate_ref,
    last_gain_ref,
    last_bias_ref,
    sent_ref,
    normed_ref,
    last_gain_out,
    last_bias_out,
):
    rows, cols, channels = pair_ref.shape
    hidden = proj_ref.shape[1] // 2
    cells = rows * cols
    inner = LANES // cols
    groups = rows // inner
    chunks = sent_ref.shape[0]
    flat = pair_ref[...].reshape(cells, channels).astype(F32)
    normed = layer_norm(flat, gain_ref[...], bias_ref[...]).astype(BF16)
    normed_ref[...] = normed
    for source, target in ((last_gain_ref, last_gain_out), (last_bias_ref, last_bias_out)):
        target[...] = jnp.broadcast_to(column(source[...]), target.shape)

    values = dot(proj_ref[...], normed, 0, 1)
    gates = dot(gate_ref[...] * 0.5, normed, 0, 1)
    mask = cell_mask(chain_ref[...], slots, rows, cols)
    mixed = (sigmoid(gates) * values * mask).astype(BF16)

    by_row = []
    for side in range(2):
        lines = []
        for g in range(groups):
            lines += exchange_blocks(
                [
                    mixed[
                        side * hidden + n * chunks : side * hidden + (n + 1) * chunks,
                        g * LANES : (g + 1) * LANES,
                    ]
                    for n in range(inner)
                ],
                cols,
            )
        by_row.append(lines)
    order = order_ref[...]
    for part in range(chunks // SOME):
        for side in range(2):
            stack = jnp.concatenate(
                [line[part * SOME : (part + 1) * SOME] for line in by_row[side]], axis=0
            )
            sent_ref[part * SOME : (part + 1) * SOME, side * rows : (side + 1) * rows] = (
                dot(order, stack).astype(BF16).reshape(SOME, rows, LANES)
            )


def triangle_kernel(ring_in, ring_out, grid_rows, grid_cols, rows, cols, got_ref, sent_ref):
    inner = LANES // cols

    def place(ring, r, c):
        return ring.index(r * grid_cols + c)

    def side(which):
        return jnp.concatenate(
            [
                jnp.concatenate(
                    [
                        got_ref[place(ring_in, r, c), which * rows : (which + 1) * rows]
                        for r in range(grid_rows)
                    ],
                    axis=0,
                )
                for c in range(grid_cols)
            ],
            axis=1,
        )

    left, right = side(0), side(1)
    lane = lax.broadcasted_iota(jnp.int32, (1, grid_cols * LANES), 1)
    by_channel = [right * one_hot(over(rest(lane, LANES), cols) == n) for n in range(inner)]
    right_by = jnp.concatenate(
        [
            by_channel[n][c * cols : (c + 1) * cols]
            for c in range(grid_cols)
            for n in range(inner)
        ],
        axis=0,
    )
    sums = dot(left, right_by, 1, 1).astype(BF16)
    for c in range(grid_cols):
        for r in range(grid_rows):
            sent_ref[place(ring_out, r, c)] = sums[r * rows : (r + 1) * rows, c * LANES : (c + 1) * LANES]


def update_kernel(
    places,
    got_ref,
    order_ref,
    normed_ref,
    gain_ref,
    bias_ref,
    proj_ref,
    gate_ref,
    out_hbm,
    out_ref,
    out_sems,
):
    rows, cols, channels = out_ref.shape
    chunks = got_ref.shape[0]
    inner = LANES // cols
    groups = rows // inner
    order = order_ref[...]
    parts = [
        dot(
            order,
            jnp.concatenate(
                [got_ref[place] for place in places[part * SOME : (part + 1) * SOME]], axis=0
            ),
        ).astype(BF16)
        for part in range(chunks // SOME)
    ]
    lines = [
        jnp.concatenate([part[row * SOME : (row + 1) * SOME] for part in parts], axis=0)
        for row in range(rows)
    ]
    gain, bias = gain_ref[...], bias_ref[...]
    opened = sigmoid(dot(normed_ref[...], gate_ref[...] * 0.5))
    results = []
    for g in range(groups):
        values = jnp.concatenate(
            exchange_blocks(lines[g * inner : (g + 1) * inner], cols), axis=0
        ).astype(F32)
        mean = jnp.mean(values, axis=0, keepdims=True)
        centered = values - mean
        variance = jnp.mean(centered * centered, axis=0, keepdims=True)
        tri_normed = (centered * lax.rsqrt(variance + 1e-05) * gain + bias).astype(BF16)
        projected = dot(tri_normed, proj_ref[...], 0, 0)
        update = (opened[g * LANES : (g + 1) * LANES] * projected).astype(BF16)
        here = pl.ds(g * inner, inner)
        out_ref[here] = update.reshape(inner, cols, channels)
        results.append(pltpu.make_async_copy(out_ref.at[here], out_hbm.at[here], out_sems.at[g]))
        results[-1].start()
    for copy in results:
        copy.wait()


VMEM = pl.BlockSpec(memory_space=pltpu.VMEM)
HBM = pl.BlockSpec(memory_space=pltpu.HBM)
PARAMS = pltpu.CompilerParams(vmem_limit_bytes=32 * 1024 * 1024)


def ring_of(axes, grid_rows, grid_cols):
    sizes = {"z": grid_rows // 2, "y": 2, "x": grid_cols // 2, "c": 2}
    strides = {"z": 2 * grid_cols, "y": grid_cols, "x": 2, "c": 1}
    ring = [0]
    for axis in axes:
        ring = [device + n * strides[axis] for device in ring for n in range(sizes[axis])]
    return ring


def exchanged(
    grid_rows,
    grid_cols,
    pair,
    chain_lengths,
    norm_in_gain,
    norm_in_bias,
    proj_in,
    gate_in,
    norm_out_gain,
    norm_out_bias,
    proj_out,
    gate_out,
):
    rows, cols, channels = pair.shape
    hidden = proj_out.shape[0]
    devices = grid_rows * grid_cols
    slots = rows * grid_rows // chain_lengths.shape[0]
    order = pl.pallas_call(
        order_kernel,
        out_shape=jax.ShapeDtypeStruct((SOME * SOME, SOME * SOME), BF16),
        out_specs=VMEM,
        compiler_params=PARAMS,
        cost_estimate=pl.CostEstimate(flops=10**9, bytes_accessed=10**6, transcendentals=0),
        name="order",
    )()
    square = jax.ShapeDtypeStruct((LANES, LANES), F32)
    sent, normed, last_gain, last_bias = pl.pallas_call(
        functools.partial(mix_kernel, slots),
        out_shape=(
            jax.ShapeDtypeStruct((devices, 2 * rows, LANES), BF16),
            jax.ShapeDtypeStruct((rows * cols, channels), BF16),
            square,
            square,
        ),
        in_specs=[VMEM] * 9,
        out_specs=[VMEM] * 4,
        compiler_params=PARAMS,
        name="mix",
    )(
        order,
        chain_lengths.reshape(1, -1),
        pair,
        norm_in_gain.reshape(1, LANES),
        norm_in_bias.reshape(1, LANES),
        proj_in,
        gate_in,
        norm_out_gain.reshape(1, LANES),
        norm_out_bias.reshape(1, LANES),
    )
    axes_in, axes_out = "ycxz", "ycxz"
    ring_in = ring_of(axes_in, grid_rows, grid_cols)
    ring_out = ring_of(axes_out, grid_rows, grid_cols)
    got = lax.all_to_all(sent, tuple(axes_in), 0, 0, tiled=True)
    sums = pl.pallas_call(
        functools.partial(triangle_kernel, ring_in, ring_out, grid_rows, grid_cols, rows, cols),
        out_shape=jax.ShapeDtypeStruct((devices, rows, LANES), BF16),
        in_specs=[VMEM],
        out_specs=VMEM,
        compiler_params=PARAMS,
        name="triangle",
    )(got)
    mine = lax.all_to_all(sums, tuple(axes_out), 0, 0, tiled=True)
    places = [ring_out.index(device) for device in ring_in]
    return pl.pallas_call(
        functools.partial(update_kernel, places),
        out_shape=jax.ShapeDtypeStruct((rows, cols, channels), BF16),
        in_specs=[VMEM] * 7,
        out_specs=HBM,
        scratch_shapes=[
            pltpu.VMEM((rows, cols, channels), BF16),
            pltpu.SemaphoreType.DMA((rows * cols // LANES,)),
        ],
        compiler_params=PARAMS,
        name="update",
    )(mine, order, normed, last_gain, last_bias, proj_out, gate_out)


def solution(mesh):
    grid_rows, grid_cols = mesh.shape["row"], mesh.shape["col"]
    fine = jax.sharding.Mesh(
        mesh.devices.reshape(max(grid_rows // 2, 1), -1, max(grid_cols // 2, 1), min(grid_cols, 2)),
        ("z", "y", "x", "c"),
    )

    def fits(rows, cols, channels, hidden):
        devices = grid_rows * grid_cols
        inner = LANES // cols
        return (
            channels == LANES
            and hidden == LANES
            and inner * cols == LANES
            and inner & (inner - 1) == 0
            and inner * devices == hidden
            and rows == SOME
            and rows % inner == 0
            and devices % SOME == 0
            and grid_rows % 2 == 0
            and grid_cols % 2 == 0
        )

    def call(*arrays):
        tokens, others, channels = arrays[0].shape
        hidden = arrays[8].shape[0]
        if fits(tokens // grid_rows, others // grid_cols, channels, hidden):
            return jax.shard_map(
                functools.partial(exchanged, grid_rows, grid_cols),
                mesh=fine,
                in_specs=(P(("z", "y"), ("x", "c"), None),) + (P(),) * 9,
                out_specs=P(("z", "y"), ("x", "c"), None),
                check_vma=False,
            )(*arrays)
        return jax.shard_map(
            gathered,
            mesh=mesh,
            in_specs=(P("row", "col", None),) + (P(),) * 9,
            out_specs=P("row", "col", None),
            check_vma=False,
        )(*arrays)

    return call
```

```python
import functools
import jax
import jax.numpy as jnp
from jax import lax
from jax.experimental import pallas as pl
from jax.experimental.pallas import tpu as pltpu
from jax.sharding import PartitionSpec as P

LANES = 128
SOME = 16
F32 = jnp.float32
BF16 = jnp.bfloat16


def broadcast(value, axis, source):
    kept = jnp.where(lax.axis_index(axis) == source, value, 0).astype(value.dtype)
    return lax.psum(kept, axis)


def layer_norm(values, gain, bias):
    mean = jnp.mean(values, axis=-1, keepdims=True)
    centered = values - mean
    variance = jnp.mean(centered * centered, axis=-1, keepdims=True)
    return centered * lax.rsqrt(variance + 1e-05) * gain + bias


def token_valid(chain_lengths, tokens_idx, slots):
    chain = tokens_idx // slots
    position = tokens_idx % slots
    chain_ids = jnp.arange(chain_lengths.shape[0], dtype=jnp.int32)
    length_of = jnp.sum(
        jnp.where(chain[:, None] == chain_ids[None, :], chain_lengths[None, :], 0), axis=1
    )
    return (position < length_of).astype(jnp.float32)


def gathered(
    pair,
    chain_lengths,
    norm_in_gain,
    norm_in_bias,
    proj_in,
    gate_in,
    norm_out_gain,
    norm_out_bias,
    proj_out,
    gate_out,
):
    row_count = pair.shape[0]
    col_count = pair.shape[1]
    channels = pair.shape[2]
    hidden = proj_out.shape[0]
    row_index = lax.axis_index("row")
    col_index = lax.axis_index("col")
    slots = row_count * lax.axis_size("row") // chain_lengths.shape[0]
    valid_rows = token_valid(
        chain_lengths, row_index * row_count + jnp.arange(row_count, dtype=jnp.int32), slots
    )
    valid_cols = token_valid(
        chain_lengths, col_index * col_count + jnp.arange(col_count, dtype=jnp.int32), slots
    )
    pair_mask = valid_rows[:, None] * valid_cols[None, :]
    normed = layer_norm(pair.astype(jnp.float32), norm_in_gain, norm_in_bias).astype(jnp.bfloat16)
    flat = normed.reshape(-1, channels)
    values = jnp.dot(flat, proj_in, preferred_element_type=jnp.float32)
    gates = jnp.dot(flat, gate_in, preferred_element_type=jnp.float32)
    mixed = (jax.nn.sigmoid(gates) * values).reshape(row_count, col_count, 2 * hidden) * pair_mask[
        :, :, None
    ]
    left_tile = mixed[:, :, :hidden].astype(jnp.bfloat16)
    right_tile = mixed[:, :, hidden:].astype(jnp.bfloat16)
    ratio = lax.axis_size("row") // lax.axis_size("col")
    right_full = lax.all_gather(right_tile, "col", axis=1, tiled=True)
    received = []
    for part in range(ratio):
        received.append(broadcast(right_full, "row", col_index * ratio + part))
    right_mine = jnp.concatenate(received, axis=0)
    triangle = jnp.einsum(
        "ikh,jkh->ijh",
        lax.all_gather(left_tile, "col", axis=1, tiled=True),
        right_mine,
        preferred_element_type=jnp.float32,
    )
    tri_normed = layer_norm(triangle, norm_out_gain, norm_out_bias).astype(jnp.bfloat16)
    projected = jnp.dot(
        tri_normed.reshape(-1, hidden), proj_out, preferred_element_type=jnp.float32
    )
    gate = jax.nn.sigmoid(jnp.dot(flat, gate_out, preferred_element_type=jnp.float32))
    return (gate * projected).astype(jnp.bfloat16).reshape(row_count, col_count, channels)


def iota2(shape):
    return (
        lax.broadcasted_iota(jnp.int32, shape, 0),
        lax.broadcasted_iota(jnp.int32, shape, 1),
    )


def one_hot(condition):
    return jnp.where(condition, 1.0, 0.0).astype(BF16)


def dot(a, b, a_dim=1, b_dim=0):
    return lax.dot_general(a, b, (((a_dim,), (b_dim,)), ((), ())), preferred_element_type=F32)


def over(value, size):
    if size & (size - 1):
        return value // size
    return lax.shift_right_logical(value, jnp.full_like(value, size.bit_length() - 1))


def rest(value, size):
    return value % size if size & (size - 1) else value & (size - 1)


def over(value, size):
    if size & (size - 1):
        return value // size
    return lax.shift_right_logical(value, jnp.full_like(value, size.bit_length() - 1))


def rest(value, size):
    return value % size if size & (size - 1) else value & (size - 1)


def fetch(sources, targets, sems):
    copies = [
        pltpu.make_async_copy(source, target, sems.at[n])
        for n, (source, target) in enumerate(zip(sources, targets))
    ]
    for copy in copies:
        copy.start()
    return copies


def sigmoid(halved):
    return 0.5 + 0.5 * jnp.tanh(halved)


def exchange_blocks(arrays, cols):
    lane = over(lax.broadcasted_iota(jnp.int32, (1, LANES), 1), cols)
    arrays, step = list(arrays), 1
    while step < len(arrays):
        upper = lane & step != 0
        for n in range(len(arrays)):
            if n // step % 2 == 0:
                a, b = arrays[n], arrays[n + step]
                arrays[n] = jnp.where(upper, pltpu.roll(b, step * cols, 1), a)
                arrays[n + step] = jnp.where(upper, b, pltpu.roll(a, LANES - step * cols, 1))
        step *= 2
    return arrays


def order_kernel(order_ref):
    out, source = iota2(order_ref.shape)
    order_ref[...] = one_hot(
        (over(out, SOME) == rest(source, SOME)) & (rest(out, SOME) == over(source, SOME))
    )


def column(row):
    a, b = iota2((LANES, LANES))
    return jnp.sum(jnp.where(a == b, row, 0.0), axis=1, keepdims=True)


def cell_mask(lengths, slots, rows, cols):
    cell = lax.broadcasted_iota(jnp.int32, (1, rows * cols), 1)

    def valid(token):
        length = jnp.zeros_like(token)
        for chain in range(lengths.shape[1]):
            length = jnp.where(
                over(token, slots) == chain, lengths[:, chain : chain + 1], length
            )
        return rest(token, slots) < length

    row_ok = valid(lax.axis_index(("z", "y")) * rows + over(cell, cols))
    col_ok = valid(lax.axis_index(("x", "c")) * cols + rest(cell, cols))
    return jnp.where(row_ok & col_ok, 1.0, 0.0)


def mix_kernel(
    slots,
    order_ref,
    chain_ref,
    pair_ref,
    gain_ref,
    bias_ref,
    proj_ref,
    gate_ref,
    last_gain_ref,
    last_bias_ref,
    sent_ref,
    normed_ref,
    last_gain_out,
    last_bias_out,
):
    rows, cols, channels = pair_ref.shape
    hidden = proj_ref.shape[1] // 2
    cells = rows * cols
    inner = LANES // cols
    groups = rows // inner
    chunks = sent_ref.shape[0]
    flat = pair_ref[...].reshape(cells, channels).astype(F32)
    normed = layer_norm(flat, gain_ref[...], bias_ref[...]).astype(BF16)
    normed_ref[...] = normed
    for source, target in ((last_gain_ref, last_gain_out), (last_bias_ref, last_bias_out)):
        target[...] = jnp.broadcast_to(column(source[...]), target.shape)

    values = dot(proj_ref[...], normed, 0, 1)
    gates = dot(gate_ref[...] * 0.5, normed, 0, 1)
    mask = cell_mask(chain_ref[...], slots, rows, cols)
    mixed = (sigmoid(gates) * values * mask).astype(BF16)

    by_row = []
    for side in range(2):
        lines = []
        for g in range(groups):
            lines += exchange_blocks(
                [
                    mixed[
                        side * hidden + n * chunks : side * hidden + (n + 1) * chunks,
                        g * LANES : (g + 1) * LANES,
                    ]
                    for n in range(inner)
                ],
                cols,
            )
        by_row.append(lines)
    order = order_ref[...]
    for part in range(chunks // SOME):
        for side in range(2):
            stack = jnp.concatenate(
                [line[part * SOME : (part + 1) * SOME] for line in by_row[side]], axis=0
            )
            sent_ref[part * SOME : (part + 1) * SOME, side * rows : (side + 1) * rows] = (
                dot(order, stack).astype(BF16).reshape(SOME, rows, LANES)
            )


def triangle_kernel(ring_in, ring_out, grid_rows, grid_cols, rows, cols, got_ref, sent_ref):
    inner = LANES // cols

    def place(ring, r, c):
        return ring.index(r * grid_cols + c)

    def side(which):
        return jnp.concatenate(
            [
                jnp.concatenate(
                    [
                        got_ref[place(ring_in, r, c), which * rows : (which + 1) * rows]
                        for r in range(grid_rows)
                    ],
                    axis=0,
                )
                for c in range(grid_cols)
            ],
            axis=1,
        )

    left, right = side(0), side(1)
    lane = lax.broadcasted_iota(jnp.int32, (1, grid_cols * LANES), 1)
    by_channel = [right * one_hot(over(rest(lane, LANES), cols) == n) for n in range(inner)]
    right_by = jnp.concatenate(
        [
            by_channel[n][c * cols : (c + 1) * cols]
            for c in range(grid_cols)
            for n in range(inner)
        ],
        axis=0,
    )
    sums = dot(left, right_by, 1, 1).astype(BF16)
    for c in range(grid_cols):
        for r in range(grid_rows):
            sent_ref[place(ring_out, r, c)] = sums[r * rows : (r + 1) * rows, c * LANES : (c + 1) * LANES]


def update_kernel(
    places,
    got_ref,
    order_ref,
    normed_ref,
    gain_ref,
    bias_ref,
    proj_ref,
    gate_ref,
    out_hbm,
    out_ref,
    out_sems,
):
    rows, cols, channels = out_ref.shape
    chunks = got_ref.shape[0]
    inner = LANES // cols
    groups = rows // inner
    order = order_ref[...]
    parts = [
        dot(
            order,
            jnp.concatenate(
                [got_ref[place] for place in places[part * SOME : (part + 1) * SOME]], axis=0
            ),
        ).astype(BF16)
        for part in range(chunks // SOME)
    ]
    lines = [
        jnp.concatenate([part[row * SOME : (row + 1) * SOME] for part in parts], axis=0)
        for row in range(rows)
    ]
    gain, bias = gain_ref[...], bias_ref[...]
    opened = sigmoid(dot(normed_ref[...], gate_ref[...] * 0.5))
    results = []
    for g in range(groups):
        values = jnp.concatenate(
            exchange_blocks(lines[g * inner : (g + 1) * inner], cols), axis=0
        ).astype(F32)
        mean = jnp.mean(values, axis=0, keepdims=True)
        centered = values - mean
        variance = jnp.mean(centered * centered, axis=0, keepdims=True)
        tri_normed = (centered * lax.rsqrt(variance + 1e-05) * gain + bias).astype(BF16)
        projected = dot(tri_normed, proj_ref[...], 0, 0)
        update = (opened[g * LANES : (g + 1) * LANES] * projected).astype(BF16)
        here = pl.ds(g * inner, inner)
        out_ref[here] = update.reshape(inner, cols, channels)
        results.append(pltpu.make_async_copy(out_ref.at[here], out_hbm.at[here], out_sems.at[g]))
        results[-1].start()
    for copy in results:
        copy.wait()


VMEM = pl.BlockSpec(memory_space=pltpu.VMEM)
HBM = pl.BlockSpec(memory_space=pltpu.HBM)
PARAMS = pltpu.CompilerParams(vmem_limit_bytes=32 * 1024 * 1024)


def ring_of(grid_rows, grid_cols):
    planes, xs = grid_rows // 2, grid_cols // 2
    return [
        ((turn + 2 * x + y) % planes * 2 + y) * grid_cols + 2 * x + core
        for core in range(2)
        for turn in range(planes)
        for x in range(xs)
        for y in range(2)
    ]


def exchanged(
    grid_rows,
    grid_cols,
    pair,
    chain_lengths,
    norm_in_gain,
    norm_in_bias,
    proj_in,
    gate_in,
    norm_out_gain,
    norm_out_bias,
    proj_out,
    gate_out,
):
    rows, cols, channels = pair.shape
    hidden = proj_out.shape[0]
    devices = grid_rows * grid_cols
    slots = rows * grid_rows // chain_lengths.shape[0]
    order = pl.pallas_call(
        order_kernel,
        out_shape=jax.ShapeDtypeStruct((SOME * SOME, SOME * SOME), BF16),
        out_specs=VMEM,
        compiler_params=PARAMS,
        cost_estimate=pl.CostEstimate(flops=10**9, bytes_accessed=10**6, transcendentals=0),
        name="order",
    )()
    square = jax.ShapeDtypeStruct((LANES, LANES), F32)
    sent, normed, last_gain, last_bias = pl.pallas_call(
        functools.partial(mix_kernel, slots),
        out_shape=(
            jax.ShapeDtypeStruct((devices, 2 * rows, LANES), BF16),
            jax.ShapeDtypeStruct((rows * cols, channels), BF16),
            square,
            square,
        ),
        in_specs=[VMEM] * 9,
        out_specs=[VMEM] * 4,
        compiler_params=PARAMS,
        name="mix",
    )(
        order,
        chain_lengths.reshape(1, -1),
        pair,
        norm_in_gain.reshape(1, LANES),
        norm_in_bias.reshape(1, LANES),
        proj_in,
        gate_in,
        norm_out_gain.reshape(1, LANES),
        norm_out_bias.reshape(1, LANES),
    )
    ring_in = ring_out = ring_of(grid_rows, grid_cols)

    def exchange(chunks, ring):
        return lax.all_to_all(
            chunks, ("z", "y", "x", "c"), 0, 0, tiled=True, axis_index_groups=[ring]
        )

    got = exchange(sent, ring_in)
    sums = pl.pallas_call(
        functools.partial(triangle_kernel, ring_in, ring_out, grid_rows, grid_cols, rows, cols),
        out_shape=jax.ShapeDtypeStruct((devices, rows, LANES), BF16),
        in_specs=[VMEM],
        out_specs=VMEM,
        compiler_params=PARAMS,
        name="triangle",
    )(got)
    mine = exchange(sums, ring_out)
    places = [ring_out.index(device) for device in ring_in]
    return pl.pallas_call(
        functools.partial(update_kernel, places),
        out_shape=jax.ShapeDtypeStruct((rows, cols, channels), BF16),
        in_specs=[VMEM] * 7,
        out_specs=HBM,
        scratch_shapes=[
            pltpu.VMEM((rows, cols, channels), BF16),
            pltpu.SemaphoreType.DMA((rows * cols // LANES,)),
        ],
        compiler_params=PARAMS,
        name="update",
    )(mine, order, normed, last_gain, last_bias, proj_out, gate_out)


def solution(mesh):
    grid_rows, grid_cols = mesh.shape["row"], mesh.shape["col"]
    fine = jax.sharding.Mesh(
        mesh.devices.reshape(max(grid_rows // 2, 1), -1, max(grid_cols // 2, 1), min(grid_cols, 2)),
        ("z", "y", "x", "c"),
    )

    def fits(rows, cols, channels, hidden):
        devices = grid_rows * grid_cols
        inner = LANES // cols
        return (
            channels == LANES
            and hidden == LANES
            and inner * cols == LANES
            and inner & (inner - 1) == 0
            and inner * devices == hidden
            and rows == SOME
            and rows % inner == 0
            and devices % SOME == 0
            and grid_rows % 2 == 0
            and grid_cols % 2 == 0
        )

    def call(*arrays):
        tokens, others, channels = arrays[0].shape
        hidden = arrays[8].shape[0]
        if fits(tokens // grid_rows, others // grid_cols, channels, hidden):
            return jax.shard_map(
                functools.partial(exchanged, grid_rows, grid_cols),
                mesh=fine,
                in_specs=(P(("z", "y"), ("x", "c"), None),) + (P(),) * 9,
                out_specs=P(("z", "y"), ("x", "c"), None),
                check_vma=False,
            )(*arrays)
        return jax.shard_map(
            gathered,
            mesh=mesh,
            in_specs=(P("row", "col", None),) + (P(),) * 9,
            out_specs=P("row", "col", None),
            check_vma=False,
        )(*arrays)

    return call
```

```python
import functools
import jax
import jax.numpy as jnp
from jax import lax
from jax.experimental import pallas as pl
from jax.experimental.pallas import tpu as pltpu
from jax.sharding import PartitionSpec as P

LANES = 128
SOME = 16
F32 = jnp.float32
BF16 = jnp.bfloat16


def broadcast(value, axis, source):
    kept = jnp.where(lax.axis_index(axis) == source, value, 0).astype(value.dtype)
    return lax.psum(kept, axis)


def layer_norm(values, gain, bias):
    mean = jnp.mean(values, axis=-1, keepdims=True)
    centered = values - mean
    variance = jnp.mean(centered * centered, axis=-1, keepdims=True)
    return centered * lax.rsqrt(variance + 1e-05) * gain + bias


def token_valid(chain_lengths, tokens_idx, slots):
    chain = tokens_idx // slots
    position = tokens_idx % slots
    chain_ids = jnp.arange(chain_lengths.shape[0], dtype=jnp.int32)
    length_of = jnp.sum(
        jnp.where(chain[:, None] == chain_ids[None, :], chain_lengths[None, :], 0), axis=1
    )
    return (position < length_of).astype(jnp.float32)


def gathered(
    pair,
    chain_lengths,
    norm_in_gain,
    norm_in_bias,
    proj_in,
    gate_in,
    norm_out_gain,
    norm_out_bias,
    proj_out,
    gate_out,
):
    row_count = pair.shape[0]
    col_count = pair.shape[1]
    channels = pair.shape[2]
    hidden = proj_out.shape[0]
    row_index = lax.axis_index("row")
    col_index = lax.axis_index("col")
    slots = row_count * lax.axis_size("row") // chain_lengths.shape[0]
    valid_rows = token_valid(
        chain_lengths, row_index * row_count + jnp.arange(row_count, dtype=jnp.int32), slots
    )
    valid_cols = token_valid(
        chain_lengths, col_index * col_count + jnp.arange(col_count, dtype=jnp.int32), slots
    )
    pair_mask = valid_rows[:, None] * valid_cols[None, :]
    normed = layer_norm(pair.astype(jnp.float32), norm_in_gain, norm_in_bias).astype(jnp.bfloat16)
    flat = normed.reshape(-1, channels)
    values = jnp.dot(flat, proj_in, preferred_element_type=jnp.float32)
    gates = jnp.dot(flat, gate_in, preferred_element_type=jnp.float32)
    mixed = (jax.nn.sigmoid(gates) * values).reshape(row_count, col_count, 2 * hidden) * pair_mask[
        :, :, None
    ]
    left_tile = mixed[:, :, :hidden].astype(jnp.bfloat16)
    right_tile = mixed[:, :, hidden:].astype(jnp.bfloat16)
    ratio = lax.axis_size("row") // lax.axis_size("col")
    right_full = lax.all_gather(right_tile, "col", axis=1, tiled=True)
    received = []
    for part in range(ratio):
        received.append(broadcast(right_full, "row", col_index * ratio + part))
    right_mine = jnp.concatenate(received, axis=0)
    triangle = jnp.einsum(
        "ikh,jkh->ijh",
        lax.all_gather(left_tile, "col", axis=1, tiled=True),
        right_mine,
        preferred_element_type=jnp.float32,
    )
    tri_normed = layer_norm(triangle, norm_out_gain, norm_out_bias).astype(jnp.bfloat16)
    projected = jnp.dot(
        tri_normed.reshape(-1, hidden), proj_out, preferred_element_type=jnp.float32
    )
    gate = jax.nn.sigmoid(jnp.dot(flat, gate_out, preferred_element_type=jnp.float32))
    return (gate * projected).astype(jnp.bfloat16).reshape(row_count, col_count, channels)


def iota2(shape):
    return (
        lax.broadcasted_iota(jnp.int32, shape, 0),
        lax.broadcasted_iota(jnp.int32, shape, 1),
    )


def one_hot(condition):
    return jnp.where(condition, 1.0, 0.0).astype(BF16)


def dot(a, b, a_dim=1, b_dim=0):
    return lax.dot_general(a, b, (((a_dim,), (b_dim,)), ((), ())), preferred_element_type=F32)


def over(value, size):
    if size & (size - 1):
        return value // size
    return lax.shift_right_logical(value, jnp.full_like(value, size.bit_length() - 1))


def rest(value, size):
    return value % size if size & (size - 1) else value & (size - 1)


def over(value, size):
    if size & (size - 1):
        return value // size
    return lax.shift_right_logical(value, jnp.full_like(value, size.bit_length() - 1))


def rest(value, size):
    return value % size if size & (size - 1) else value & (size - 1)


def fetch(sources, targets, sems):
    copies = [
        pltpu.make_async_copy(source, target, sems.at[n])
        for n, (source, target) in enumerate(zip(sources, targets))
    ]
    for copy in copies:
        copy.start()
    return copies


def sigmoid(halved):
    return 0.5 + 0.5 * jnp.tanh(halved)


def exchange_blocks(arrays, cols):
    lane = over(lax.broadcasted_iota(jnp.int32, (1, LANES), 1), cols)
    arrays, step = list(arrays), 1
    while step < len(arrays):
        upper = lane & step != 0
        for n in range(len(arrays)):
            if n // step % 2 == 0:
                a, b = arrays[n], arrays[n + step]
                arrays[n] = jnp.where(upper, pltpu.roll(b, step * cols, 1), a)
                arrays[n + step] = jnp.where(upper, b, pltpu.roll(a, LANES - step * cols, 1))
        step *= 2
    return arrays


def order_kernel(order_ref):
    out, source = iota2(order_ref.shape)
    order_ref[...] = one_hot(
        (over(out, SOME) == rest(source, SOME)) & (rest(out, SOME) == over(source, SOME))
    )


def column(row):
    a, b = iota2((LANES, LANES))
    return jnp.sum(jnp.where(a == b, row, 0.0), axis=1, keepdims=True)


def cell_mask(lengths, slots, rows, cols):
    cell = lax.broadcasted_iota(jnp.int32, (1, rows * cols), 1)

    def valid(token):
        length = jnp.zeros_like(token)
        for chain in range(lengths.shape[1]):
            length = jnp.where(
                over(token, slots) == chain, lengths[:, chain : chain + 1], length
            )
        return rest(token, slots) < length

    row_ok = valid(lax.axis_index(("high", "low")) * rows + over(cell, cols))
    col_ok = valid(lax.axis_index("col") * cols + rest(cell, cols))
    return jnp.where(row_ok & col_ok, 1.0, 0.0)


def mix_kernel(
    slots,
    order_ref,
    chain_ref,
    pair_ref,
    gain_ref,
    bias_ref,
    proj_ref,
    gate_ref,
    last_gain_ref,
    last_bias_ref,
    sent_ref,
    normed_ref,
    last_gain_out,
    last_bias_out,
):
    rows, cols, channels = pair_ref.shape
    hidden = proj_ref.shape[1] // 2
    cells = rows * cols
    inner = LANES // cols
    groups = rows // inner
    chunks = sent_ref.shape[0]
    flat = pair_ref[...].reshape(cells, channels).astype(F32)
    normed = layer_norm(flat, gain_ref[...], bias_ref[...]).astype(BF16)
    normed_ref[...] = normed
    for source, target in ((last_gain_ref, last_gain_out), (last_bias_ref, last_bias_out)):
        target[...] = jnp.broadcast_to(column(source[...]), target.shape)

    weights = jnp.concatenate([proj_ref[...], gate_ref[...] * 0.5], axis=1)
    products = dot(weights, normed, 0, 1)
    values, gates = products[: 2 * hidden], products[2 * hidden :]
    mask = cell_mask(chain_ref[...], slots, rows, cols)
    mixed = (sigmoid(gates) * values * mask).astype(BF16)

    by_row = []
    for side in range(2):
        lines = []
        for g in range(groups):
            lines += exchange_blocks(
                [
                    mixed[
                        side * hidden + n * chunks : side * hidden + (n + 1) * chunks,
                        g * LANES : (g + 1) * LANES,
                    ]
                    for n in range(inner)
                ],
                cols,
            )
        by_row.append(lines)
    order = order_ref[...]
    for part in range(chunks // SOME):
        for side in range(2):
            stack = jnp.concatenate(
                [line[part * SOME : (part + 1) * SOME] for line in by_row[side]], axis=0
            )
            sent_ref[part * SOME : (part + 1) * SOME, side * rows : (side + 1) * rows] = (
                dot(order, stack).astype(BF16).reshape(SOME, rows, LANES)
            )


def triangle_kernel(split, grid_cols, rows, cols, got_ref, sent_ref):
    inner = LANES // cols

    def place(r, c):
        z, y = r // split[1], r % split[1]
        return (c * split[1] + y) * split[0] + z

    def side(which):
        return jnp.concatenate(
            [
                jnp.concatenate(
                    [
                        got_ref[place(r, c), which * rows : (which + 1) * rows]
                        for r in range(split[0] * split[1])
                    ],
                    axis=0,
                )
                for c in range(grid_cols)
            ],
            axis=1,
        )

    left, right = side(0), side(1)
    lane = lax.broadcasted_iota(jnp.int32, (1, grid_cols * LANES), 1)
    by_channel = [right * one_hot(over(rest(lane, LANES), cols) == n) for n in range(inner)]
    right_by = jnp.concatenate(
        [
            by_channel[n][c * cols : (c + 1) * cols]
            for c in range(grid_cols)
            for n in range(inner)
        ],
        axis=0,
    )
    sums = dot(left, right_by, 1, 1).astype(BF16)
    for c in range(grid_cols):
        for r in range(split[0] * split[1]):
            sent_ref[place(r, c)] = sums[r * rows : (r + 1) * rows, c * LANES : (c + 1) * LANES]


def update_kernel(
    got_ref,
    order_ref,
    normed_ref,
    gain_ref,
    bias_ref,
    proj_ref,
    gate_ref,
    out_hbm,
    out_ref,
    out_sems,
):
    rows, cols, channels = out_ref.shape
    chunks = got_ref.shape[0]
    inner = LANES // cols
    groups = rows // inner
    order = order_ref[...]
    parts = [
        dot(order, got_ref[part * SOME : (part + 1) * SOME].reshape(SOME * rows, LANES)).astype(BF16)
        for part in range(chunks // SOME)
    ]
    lines = [
        jnp.concatenate([part[row * SOME : (row + 1) * SOME] for part in parts], axis=0)
        for row in range(rows)
    ]
    gain, bias = gain_ref[...], bias_ref[...]
    opened = sigmoid(dot(normed_ref[...], gate_ref[...] * 0.5))
    results = []
    for g in range(groups):
        values = jnp.concatenate(
            exchange_blocks(lines[g * inner : (g + 1) * inner], cols), axis=0
        ).astype(F32)
        mean = jnp.mean(values, axis=0, keepdims=True)
        centered = values - mean
        variance = jnp.mean(centered * centered, axis=0, keepdims=True)
        tri_normed = (centered * lax.rsqrt(variance + 1e-05) * gain + bias).astype(BF16)
        projected = dot(tri_normed, proj_ref[...], 0, 0)
        update = (opened[g * LANES : (g + 1) * LANES] * projected).astype(BF16)
        out_ref[g * inner : (g + 1) * inner] = update.reshape(inner, cols, channels)
        if g % 2:
            here = pl.ds((g - 1) * inner, 2 * inner)
            results.append(
                pltpu.make_async_copy(out_ref.at[here], out_hbm.at[here], out_sems.at[g // 2])
            )
            results[-1].start()
    for copy in results:
        copy.wait()


VMEM = pl.BlockSpec(memory_space=pltpu.VMEM)
HBM = pl.BlockSpec(memory_space=pltpu.HBM)
PARAMS = pltpu.CompilerParams(vmem_limit_bytes=32 * 1024 * 1024)


def exchanged(
    split,
    grid_cols,
    pair,
    chain_lengths,
    norm_in_gain,
    norm_in_bias,
    proj_in,
    gate_in,
    norm_out_gain,
    norm_out_bias,
    proj_out,
    gate_out,
):
    rows, cols, channels = pair.shape
    hidden = proj_out.shape[0]
    grid_rows = split[0] * split[1]
    devices = grid_rows * grid_cols
    slots = rows * grid_rows // chain_lengths.shape[0]
    order = pl.pallas_call(
        order_kernel,
        out_shape=jax.ShapeDtypeStruct((SOME * SOME, SOME * SOME), BF16),
        out_specs=VMEM,
        compiler_params=PARAMS,
        cost_estimate=pl.CostEstimate(flops=10**9, bytes_accessed=10**6, transcendentals=0),
        name="order",
    )()
    square = jax.ShapeDtypeStruct((LANES, LANES), F32)
    sent, normed, last_gain, last_bias = pl.pallas_call(
        functools.partial(mix_kernel, slots),
        out_shape=(
            jax.ShapeDtypeStruct((devices, 2 * rows, LANES), BF16),
            jax.ShapeDtypeStruct((rows * cols, channels), BF16),
            square,
            square,
        ),
        in_specs=[VMEM] * 9,
        out_specs=[VMEM] * 4,
        compiler_params=PARAMS,
        name="mix",
    )(
        order,
        chain_lengths.reshape(1, -1),
        pair,
        norm_in_gain.reshape(1, LANES),
        norm_in_bias.reshape(1, LANES),
        proj_in,
        gate_in,
        norm_out_gain.reshape(1, LANES),
        norm_out_bias.reshape(1, LANES),
    )
    axes = ("col", "low", "high")
    got = lax.all_to_all(sent, axes, 0, 0, tiled=True)
    sums = pl.pallas_call(
        functools.partial(triangle_kernel, split, grid_cols, rows, cols),
        out_shape=jax.ShapeDtypeStruct((devices, rows, LANES), BF16),
        in_specs=[VMEM],
        out_specs=VMEM,
        compiler_params=PARAMS,
        name="triangle",
    )(got)
    mine = lax.all_to_all(sums, axes, 0, 0, tiled=True)
    return pl.pallas_call(
        update_kernel,
        out_shape=jax.ShapeDtypeStruct((rows, cols, channels), BF16),
        in_specs=[VMEM] * 7,
        out_specs=HBM,
        scratch_shapes=[
            pltpu.VMEM((rows, cols, channels), BF16),
            pltpu.SemaphoreType.DMA((rows * cols // LANES // 2,)),
        ],
        compiler_params=PARAMS,
        name="update",
    )(mine, order, normed, last_gain, last_bias, proj_out, gate_out)


def solution(mesh):
    grid_rows, grid_cols = mesh.shape["row"], mesh.shape["col"]
    split = (grid_rows // 2, 2)
    fine = jax.sharding.Mesh(
        mesh.devices.reshape(split + (grid_cols,)), ("high", "low", "col")
    )

    def fits(rows, cols, channels, hidden):
        devices = grid_rows * grid_cols
        inner = LANES // cols
        return (
            channels == LANES
            and hidden == LANES
            and inner * cols == LANES
            and inner & (inner - 1) == 0
            and inner * devices == hidden
            and rows == SOME
            and rows % (2 * inner) == 0
            and devices % SOME == 0
        )

    def call(*arrays):
        tokens, others, channels = arrays[0].shape
        hidden = arrays[8].shape[0]
        if fits(tokens // grid_rows, others // grid_cols, channels, hidden):
            return jax.shard_map(
                functools.partial(exchanged, split, grid_cols),
                mesh=fine,
                in_specs=(P(("high", "low"), "col", None),) + (P(),) * 9,
                out_specs=P(("high", "low"), "col", None),
                check_vma=False,
            )(*arrays)
        return jax.shard_map(
            gathered,
            mesh=mesh,
            in_specs=(P("row", "col", None),) + (P(),) * 9,
            out_specs=P("row", "col", None),
            check_vma=False,
        )(*arrays)

    return call
```

```python
import functools
import jax
import jax.numpy as jnp
from jax import lax
from jax.experimental import pallas as pl
from jax.experimental.pallas import tpu as pltpu
from jax.sharding import PartitionSpec as P

LANES = 128
SOME = 16
F32 = jnp.float32
BF16 = jnp.bfloat16


def broadcast(value, axis, source):
    kept = jnp.where(lax.axis_index(axis) == source, value, 0).astype(value.dtype)
    return lax.psum(kept, axis)


def layer_norm(values, gain, bias):
    mean = jnp.mean(values, axis=-1, keepdims=True)
    centered = values - mean
    variance = jnp.mean(centered * centered, axis=-1, keepdims=True)
    return centered * lax.rsqrt(variance + 1e-05) * gain + bias


def token_valid(chain_lengths, tokens_idx, slots):
    chain = tokens_idx // slots
    position = tokens_idx % slots
    chain_ids = jnp.arange(chain_lengths.shape[0], dtype=jnp.int32)
    length_of = jnp.sum(
        jnp.where(chain[:, None] == chain_ids[None, :], chain_lengths[None, :], 0), axis=1
    )
    return (position < length_of).astype(jnp.float32)


def gathered(
    pair,
    chain_lengths,
    norm_in_gain,
    norm_in_bias,
    proj_in,
    gate_in,
    norm_out_gain,
    norm_out_bias,
    proj_out,
    gate_out,
):
    row_count = pair.shape[0]
    col_count = pair.shape[1]
    channels = pair.shape[2]
    hidden = proj_out.shape[0]
    row_index = lax.axis_index("row")
    col_index = lax.axis_index("col")
    slots = row_count * lax.axis_size("row") // chain_lengths.shape[0]
    valid_rows = token_valid(
        chain_lengths, row_index * row_count + jnp.arange(row_count, dtype=jnp.int32), slots
    )
    valid_cols = token_valid(
        chain_lengths, col_index * col_count + jnp.arange(col_count, dtype=jnp.int32), slots
    )
    pair_mask = valid_rows[:, None] * valid_cols[None, :]
    normed = layer_norm(pair.astype(jnp.float32), norm_in_gain, norm_in_bias).astype(jnp.bfloat16)
    flat = normed.reshape(-1, channels)
    values = jnp.dot(flat, proj_in, preferred_element_type=jnp.float32)
    gates = jnp.dot(flat, gate_in, preferred_element_type=jnp.float32)
    mixed = (jax.nn.sigmoid(gates) * values).reshape(row_count, col_count, 2 * hidden) * pair_mask[
        :, :, None
    ]
    left_tile = mixed[:, :, :hidden].astype(jnp.bfloat16)
    right_tile = mixed[:, :, hidden:].astype(jnp.bfloat16)
    ratio = lax.axis_size("row") // lax.axis_size("col")
    right_full = lax.all_gather(right_tile, "col", axis=1, tiled=True)
    received = []
    for part in range(ratio):
        received.append(broadcast(right_full, "row", col_index * ratio + part))
    right_mine = jnp.concatenate(received, axis=0)
    triangle = jnp.einsum(
        "ikh,jkh->ijh",
        lax.all_gather(left_tile, "col", axis=1, tiled=True),
        right_mine,
        preferred_element_type=jnp.float32,
    )
    tri_normed = layer_norm(triangle, norm_out_gain, norm_out_bias).astype(jnp.bfloat16)
    projected = jnp.dot(
        tri_normed.reshape(-1, hidden), proj_out, preferred_element_type=jnp.float32
    )
    gate = jax.nn.sigmoid(jnp.dot(flat, gate_out, preferred_element_type=jnp.float32))
    return (gate * projected).astype(jnp.bfloat16).reshape(row_count, col_count, channels)


def iota2(shape):
    return (
        lax.broadcasted_iota(jnp.int32, shape, 0),
        lax.broadcasted_iota(jnp.int32, shape, 1),
    )


def one_hot(condition):
    return jnp.where(condition, 1.0, 0.0).astype(BF16)


def dot(a, b, a_dim=1, b_dim=0):
    return lax.dot_general(a, b, (((a_dim,), (b_dim,)), ((), ())), preferred_element_type=F32)


def over(value, size):
    if size & (size - 1):
        return value // size
    return lax.shift_right_logical(value, jnp.full_like(value, size.bit_length() - 1))


def rest(value, size):
    return value % size if size & (size - 1) else value & (size - 1)


def over(value, size):
    if size & (size - 1):
        return value // size
    return lax.shift_right_logical(value, jnp.full_like(value, size.bit_length() - 1))


def rest(value, size):
    return value % size if size & (size - 1) else value & (size - 1)


def fetch(sources, targets, sems):
    copies = [
        pltpu.make_async_copy(source, target, sems.at[n])
        for n, (source, target) in enumerate(zip(sources, targets))
    ]
    for copy in copies:
        copy.start()
    return copies


def sigmoid(halved):
    return 0.5 + 0.5 * jnp.tanh(halved)


def exchange_blocks(arrays, cols):
    lane = over(lax.broadcasted_iota(jnp.int32, (1, LANES), 1), cols)
    arrays, step = list(arrays), 1
    while step < len(arrays):
        upper = lane & step != 0
        for n in range(len(arrays)):
            if n // step % 2 == 0:
                a, b = arrays[n], arrays[n + step]
                arrays[n] = jnp.where(upper, pltpu.roll(b, step * cols, 1), a)
                arrays[n + step] = jnp.where(upper, b, pltpu.roll(a, LANES - step * cols, 1))
        step *= 2
    return arrays


def order_kernel(order_ref):
    out, source = iota2(order_ref.shape)
    order_ref[...] = one_hot(
        (over(out, SOME) == rest(source, SOME)) & (rest(out, SOME) == over(source, SOME))
    )


def column(row):
    a, b = iota2((LANES, LANES))
    return jnp.sum(jnp.where(a == b, row, 0.0), axis=1, keepdims=True)


def cell_mask(lengths, slots, rows, cols):
    cell = lax.broadcasted_iota(jnp.int32, (1, rows * cols), 1)

    def valid(token):
        length = jnp.zeros_like(token)
        for chain in range(lengths.shape[1]):
            length = jnp.where(
                over(token, slots) == chain, lengths[:, chain : chain + 1], length
            )
        return rest(token, slots) < length

    row_ok = valid(lax.axis_index("row") * rows + over(cell, cols))
    col_ok = valid(lax.axis_index("col") * cols + rest(cell, cols))
    return jnp.where(row_ok & col_ok, 1.0, 0.0)


def mix_kernel(
    slots,
    order_ref,
    chain_ref,
    pair_ref,
    gain_ref,
    bias_ref,
    proj_ref,
    gate_ref,
    last_gain_ref,
    last_bias_ref,
    sent_ref,
    normed_ref,
    last_gain_out,
    last_bias_out,
):
    rows, cols, channels = pair_ref.shape
    hidden = proj_ref.shape[1] // 2
    cells = rows * cols
    inner = LANES // cols
    groups = rows // inner
    chunks = sent_ref.shape[0]
    flat = pair_ref[...].reshape(cells, channels).astype(F32)
    normed = layer_norm(flat, gain_ref[...], bias_ref[...]).astype(BF16)
    normed_ref[...] = normed
    for source, target in ((last_gain_ref, last_gain_out), (last_bias_ref, last_bias_out)):
        target[...] = jnp.broadcast_to(column(source[...]), target.shape)

    weights = jnp.concatenate([proj_ref[...], gate_ref[...] * 0.5], axis=1)
    products = dot(weights, normed, 0, 1)
    values, gates = products[: 2 * hidden], products[2 * hidden :]
    mask = cell_mask(chain_ref[...], slots, rows, cols)
    mixed = (sigmoid(gates) * values * mask).astype(BF16)

    by_row = []
    for side in range(2):
        lines = []
        for g in range(groups):
            lines += exchange_blocks(
                [
                    mixed[
                        side * hidden + n * chunks : side * hidden + (n + 1) * chunks,
                        g * LANES : (g + 1) * LANES,
                    ]
                    for n in range(inner)
                ],
                cols,
            )
        by_row.append(lines)
    order = order_ref[...]
    for part in range(chunks // SOME):
        for side in range(2):
            stack = jnp.concatenate(
                [line[part * SOME : (part + 1) * SOME] for line in by_row[side]], axis=0
            )
            sent_ref[part * SOME : (part + 1) * SOME, side * rows : (side + 1) * rows] = (
                dot(order, stack).astype(BF16).reshape(SOME, rows, LANES)
            )


def triangle_kernel(ring, grid_rows, grid_cols, rows, cols, got_ref, sent_ref):
    inner = LANES // cols

    def place(r, c):
        return ring.index(r * grid_cols + c)

    def side(which):
        return jnp.concatenate(
            [
                jnp.concatenate(
                    [
                        got_ref[place(r, c), which * rows : (which + 1) * rows]
                        for r in range(grid_rows)
                    ],
                    axis=0,
                )
                for c in range(grid_cols)
            ],
            axis=1,
        )

    left, right = side(0), side(1)
    lane = lax.broadcasted_iota(jnp.int32, (1, grid_cols * LANES), 1)
    by_channel = [right * one_hot(over(rest(lane, LANES), cols) == n) for n in range(inner)]
    right_by = jnp.concatenate(
        [
            by_channel[n][c * cols : (c + 1) * cols]
            for c in range(grid_cols)
            for n in range(inner)
        ],
        axis=0,
    )
    sums = dot(left, right_by, 1, 1).astype(BF16)
    for c in range(grid_cols):
        for r in range(grid_rows):
            sent_ref[place(r, c)] = sums[r * rows : (r + 1) * rows, c * LANES : (c + 1) * LANES]


def update_kernel(
    got_ref,
    order_ref,
    normed_ref,
    gain_ref,
    bias_ref,
    proj_ref,
    gate_ref,
    out_hbm,
    out_ref,
    out_sems,
):
    rows, cols, channels = out_ref.shape
    chunks = got_ref.shape[0]
    inner = LANES // cols
    groups = rows // inner
    order = order_ref[...]
    parts = [
        dot(order, got_ref[part * SOME : (part + 1) * SOME].reshape(SOME * rows, LANES)).astype(BF16)
        for part in range(chunks // SOME)
    ]
    lines = [
        jnp.concatenate([part[row * SOME : (row + 1) * SOME] for part in parts], axis=0)
        for row in range(rows)
    ]
    gain, bias = gain_ref[...], bias_ref[...]
    opened = sigmoid(dot(normed_ref[...], gate_ref[...] * 0.5))
    results = []
    for g in range(groups):
        values = jnp.concatenate(
            exchange_blocks(lines[g * inner : (g + 1) * inner], cols), axis=0
        ).astype(F32)
        mean = jnp.mean(values, axis=0, keepdims=True)
        centered = values - mean
        variance = jnp.mean(centered * centered, axis=0, keepdims=True)
        tri_normed = (centered * lax.rsqrt(variance + 1e-05) * gain + bias).astype(BF16)
        projected = dot(tri_normed, proj_ref[...], 0, 0)
        update = (opened[g * LANES : (g + 1) * LANES] * projected).astype(BF16)
        out_ref[g * inner : (g + 1) * inner] = update.reshape(inner, cols, channels)
        if g % 2:
            here = pl.ds((g - 1) * inner, 2 * inner)
            results.append(
                pltpu.make_async_copy(out_ref.at[here], out_hbm.at[here], out_sems.at[g // 2])
            )
            results[-1].start()
    for copy in results:
        copy.wait()


VMEM = pl.BlockSpec(memory_space=pltpu.VMEM)
HBM = pl.BlockSpec(memory_space=pltpu.HBM)
PARAMS = pltpu.CompilerParams(vmem_limit_bytes=32 * 1024 * 1024)


def ring_of(grid_rows, grid_cols):
    ring = [
        (z * 2 + y) * grid_cols + c
        for c in range(grid_cols)
        for y in range(2)
        for z in range(grid_rows // 2)
    ]
    return ring[::-1]


def exchanged(
    grid_rows,
    grid_cols,
    pair,
    chain_lengths,
    norm_in_gain,
    norm_in_bias,
    proj_in,
    gate_in,
    norm_out_gain,
    norm_out_bias,
    proj_out,
    gate_out,
):
    rows, cols, channels = pair.shape
    hidden = proj_out.shape[0]
    devices = grid_rows * grid_cols
    slots = rows * grid_rows // chain_lengths.shape[0]
    order = pl.pallas_call(
        order_kernel,
        out_shape=jax.ShapeDtypeStruct((SOME * SOME, SOME * SOME), BF16),
        out_specs=VMEM,
        compiler_params=PARAMS,
        cost_estimate=pl.CostEstimate(flops=10**9, bytes_accessed=10**6, transcendentals=0),
        name="order",
    )()
    square = jax.ShapeDtypeStruct((LANES, LANES), F32)
    sent, normed, last_gain, last_bias = pl.pallas_call(
        functools.partial(mix_kernel, slots),
        out_shape=(
            jax.ShapeDtypeStruct((devices, 2 * rows, LANES), BF16),
            jax.ShapeDtypeStruct((rows * cols, channels), BF16),
            square,
            square,
        ),
        in_specs=[VMEM] * 9,
        out_specs=[VMEM] * 4,
        compiler_params=PARAMS,
        name="mix",
    )(
        order,
        chain_lengths.reshape(1, -1),
        pair,
        norm_in_gain.reshape(1, LANES),
        norm_in_bias.reshape(1, LANES),
        proj_in,
        gate_in,
        norm_out_gain.reshape(1, LANES),
        norm_out_bias.reshape(1, LANES),
    )
    ring = ring_of(grid_rows, grid_cols)

    def exchange(chunks):
        return lax.all_to_all(
            chunks, ("row", "col"), 0, 0, tiled=True, axis_index_groups=[ring]
        )

    got = exchange(sent)
    sums = pl.pallas_call(
        functools.partial(triangle_kernel, ring, grid_rows, grid_cols, rows, cols),
        out_shape=jax.ShapeDtypeStruct((devices, rows, LANES), BF16),
        in_specs=[VMEM],
        out_specs=VMEM,
        compiler_params=PARAMS,
        name="triangle",
    )(got)
    mine = exchange(sums)
    return pl.pallas_call(
        update_kernel,
        out_shape=jax.ShapeDtypeStruct((rows, cols, channels), BF16),
        in_specs=[VMEM] * 7,
        out_specs=HBM,
        scratch_shapes=[
            pltpu.VMEM((rows, cols, channels), BF16),
            pltpu.SemaphoreType.DMA((rows * cols // LANES // 2,)),
        ],
        compiler_params=PARAMS,
        name="update",
    )(mine, order, normed, last_gain, last_bias, proj_out, gate_out)


def solution(mesh):
    grid_rows, grid_cols = mesh.shape["row"], mesh.shape["col"]
    def fits(rows, cols, channels, hidden):
        devices = grid_rows * grid_cols
        inner = LANES // cols
        return (
            channels == LANES
            and hidden == LANES
            and inner * cols == LANES
            and inner & (inner - 1) == 0
            and inner * devices == hidden
            and rows == SOME
            and rows % (2 * inner) == 0
            and devices % SOME == 0
            and grid_rows % 2 == 0
        )

    def call(*arrays):
        tokens, others, channels = arrays[0].shape
        hidden = arrays[8].shape[0]
        if fits(tokens // grid_rows, others // grid_cols, channels, hidden):
            return jax.shard_map(
                functools.partial(exchanged, grid_rows, grid_cols),
                mesh=mesh,
                in_specs=(P("row", "col", None),) + (P(),) * 9,
                out_specs=P("row", "col", None),
                check_vma=False,
            )(*arrays)
        return jax.shard_map(
            gathered,
            mesh=mesh,
            in_specs=(P("row", "col", None),) + (P(),) * 9,
            out_specs=P("row", "col", None),
            check_vma=False,
        )(*arrays)

    return call
```

```python
import functools
import jax
import jax.numpy as jnp
from jax import lax
from jax.experimental import pallas as pl
from jax.experimental.pallas import tpu as pltpu
from jax.sharding import PartitionSpec as P

LANES = 128
SOME = 16
F32 = jnp.float32
BF16 = jnp.bfloat16


def broadcast(value, axis, source):
    kept = jnp.where(lax.axis_index(axis) == source, value, 0).astype(value.dtype)
    return lax.psum(kept, axis)


def layer_norm(values, gain, bias):
    mean = jnp.mean(values, axis=-1, keepdims=True)
    centered = values - mean
    variance = jnp.mean(centered * centered, axis=-1, keepdims=True)
    return centered * lax.rsqrt(variance + 1e-05) * gain + bias


def token_valid(chain_lengths, tokens_idx, slots):
    chain = tokens_idx // slots
    position = tokens_idx % slots
    chain_ids = jnp.arange(chain_lengths.shape[0], dtype=jnp.int32)
    length_of = jnp.sum(
        jnp.where(chain[:, None] == chain_ids[None, :], chain_lengths[None, :], 0), axis=1
    )
    return (position < length_of).astype(jnp.float32)


def gathered(
    pair,
    chain_lengths,
    norm_in_gain,
    norm_in_bias,
    proj_in,
    gate_in,
    norm_out_gain,
    norm_out_bias,
    proj_out,
    gate_out,
):
    row_count = pair.shape[0]
    col_count = pair.shape[1]
    channels = pair.shape[2]
    hidden = proj_out.shape[0]
    row_index = lax.axis_index("row")
    col_index = lax.axis_index("col")
    slots = row_count * lax.axis_size("row") // chain_lengths.shape[0]
    valid_rows = token_valid(
        chain_lengths, row_index * row_count + jnp.arange(row_count, dtype=jnp.int32), slots
    )
    valid_cols = token_valid(
        chain_lengths, col_index * col_count + jnp.arange(col_count, dtype=jnp.int32), slots
    )
    pair_mask = valid_rows[:, None] * valid_cols[None, :]
    normed = layer_norm(pair.astype(jnp.float32), norm_in_gain, norm_in_bias).astype(jnp.bfloat16)
    flat = normed.reshape(-1, channels)
    values = jnp.dot(flat, proj_in, preferred_element_type=jnp.float32)
    gates = jnp.dot(flat, gate_in, preferred_element_type=jnp.float32)
    mixed = (jax.nn.sigmoid(gates) * values).reshape(row_count, col_count, 2 * hidden) * pair_mask[
        :, :, None
    ]
    left_tile = mixed[:, :, :hidden].astype(jnp.bfloat16)
    right_tile = mixed[:, :, hidden:].astype(jnp.bfloat16)
    ratio = lax.axis_size("row") // lax.axis_size("col")
    right_full = lax.all_gather(right_tile, "col", axis=1, tiled=True)
    received = []
    for part in range(ratio):
        received.append(broadcast(right_full, "row", col_index * ratio + part))
    right_mine = jnp.concatenate(received, axis=0)
    triangle = jnp.einsum(
        "ikh,jkh->ijh",
        lax.all_gather(left_tile, "col", axis=1, tiled=True),
        right_mine,
        preferred_element_type=jnp.float32,
    )
    tri_normed = layer_norm(triangle, norm_out_gain, norm_out_bias).astype(jnp.bfloat16)
    projected = jnp.dot(
        tri_normed.reshape(-1, hidden), proj_out, preferred_element_type=jnp.float32
    )
    gate = jax.nn.sigmoid(jnp.dot(flat, gate_out, preferred_element_type=jnp.float32))
    return (gate * projected).astype(jnp.bfloat16).reshape(row_count, col_count, channels)


def iota2(shape):
    return (
        lax.broadcasted_iota(jnp.int32, shape, 0),
        lax.broadcasted_iota(jnp.int32, shape, 1),
    )


def one_hot(condition):
    return jnp.where(condition, 1.0, 0.0).astype(BF16)


def dot(a, b, a_dim=1, b_dim=0):
    return lax.dot_general(a, b, (((a_dim,), (b_dim,)), ((), ())), preferred_element_type=F32)


def over(value, size):
    if size & (size - 1):
        return value // size
    return lax.shift_right_logical(value, jnp.full_like(value, size.bit_length() - 1))


def rest(value, size):
    return value % size if size & (size - 1) else value & (size - 1)


def over(value, size):
    if size & (size - 1):
        return value // size
    return lax.shift_right_logical(value, jnp.full_like(value, size.bit_length() - 1))


def rest(value, size):
    return value % size if size & (size - 1) else value & (size - 1)


def fetch(sources, targets, sems):
    copies = [
        pltpu.make_async_copy(source, target, sems.at[n])
        for n, (source, target) in enumerate(zip(sources, targets))
    ]
    for copy in copies:
        copy.start()
    return copies


def sigmoid(halved):
    return 0.5 + 0.5 * jnp.tanh(halved)


def exchange_blocks(arrays, cols):
    lane = over(lax.broadcasted_iota(jnp.int32, (1, LANES), 1), cols)
    arrays, step = list(arrays), 1
    while step < len(arrays):
        upper = lane & step != 0
        for n in range(len(arrays)):
            if n // step % 2 == 0:
                a, b = arrays[n], arrays[n + step]
                arrays[n] = jnp.where(upper, pltpu.roll(b, step * cols, 1), a)
                arrays[n + step] = jnp.where(upper, b, pltpu.roll(a, LANES - step * cols, 1))
        step *= 2
    return arrays


def order_kernel(order_ref):
    out, source = iota2(order_ref.shape)
    order_ref[...] = one_hot(
        (over(out, SOME) == rest(source, SOME)) & (rest(out, SOME) == over(source, SOME))
    )


def column(row):
    a, b = iota2((LANES, LANES))
    return jnp.sum(jnp.where(a == b, row, 0.0), axis=1, keepdims=True)


def cell_mask(lengths, slots, rows, cols):
    cell = lax.broadcasted_iota(jnp.int32, (1, rows * cols), 1)

    def valid(token):
        length = jnp.zeros_like(token)
        for chain in range(lengths.shape[1]):
            length = jnp.where(
                over(token, slots) == chain, lengths[:, chain : chain + 1], length
            )
        return rest(token, slots) < length

    row_ok = valid(lax.axis_index("row") * rows + over(cell, cols))
    col_ok = valid(lax.axis_index("col") * cols + rest(cell, cols))
    return jnp.where(row_ok & col_ok, 1.0, 0.0)


def mix_kernel(
    slots,
    order_ref,
    chain_ref,
    pair_ref,
    gain_ref,
    bias_ref,
    proj_ref,
    gate_ref,
    last_gain_ref,
    last_bias_ref,
    sent_ref,
    normed_ref,
    last_gain_out,
    last_bias_out,
):
    rows, cols, channels = pair_ref.shape
    hidden = proj_ref.shape[1] // 2
    cells = rows * cols
    inner = LANES // cols
    groups = rows // inner
    chunks = sent_ref.shape[0]
    flat = pair_ref[...].reshape(cells, channels).astype(F32)
    normed = layer_norm(flat, gain_ref[...], bias_ref[...]).astype(BF16)
    normed_ref[...] = normed
    for source, target in ((last_gain_ref, last_gain_out), (last_bias_ref, last_bias_out)):
        target[...] = jnp.broadcast_to(column(source[...]), target.shape)

    weights = jnp.concatenate([proj_ref[...], gate_ref[...] * 0.5], axis=1)
    products = dot(weights, normed, 0, 1)
    values, gates = products[: 2 * hidden], products[2 * hidden :]
    mask = cell_mask(chain_ref[...], slots, rows, cols)
    mixed = (sigmoid(gates) * values * mask).astype(BF16)

    by_row = []
    for side in range(2):
        lines = []
        for g in range(groups):
            lines += exchange_blocks(
                [
                    mixed[
                        side * hidden + n * chunks : side * hidden + (n + 1) * chunks,
                        g * LANES : (g + 1) * LANES,
                    ]
                    for n in range(inner)
                ],
                cols,
            )
        by_row.append(lines)
    order = order_ref[...]
    for part in range(chunks // SOME):
        for side in range(2):
            stack = jnp.concatenate(
                [line[part * SOME : (part + 1) * SOME] for line in by_row[side]], axis=0
            )
            sent_ref[part * SOME : (part + 1) * SOME, side * rows : (side + 1) * rows] = (
                dot(order, stack).astype(BF16).reshape(SOME, rows, LANES)
            )


def triangle_kernel(ring, grid_rows, grid_cols, rows, cols, got_ref, sent_ref):
    inner = LANES // cols

    def place(r, c):
        return ring.index(r * grid_cols + c)

    def side(which):
        return jnp.concatenate(
            [
                jnp.concatenate(
                    [
                        got_ref[place(r, c), which * rows : (which + 1) * rows]
                        for r in range(grid_rows)
                    ],
                    axis=0,
                )
                for c in range(grid_cols)
            ],
            axis=1,
        )

    left, right = side(0), side(1)
    lane = lax.broadcasted_iota(jnp.int32, (1, grid_cols * LANES), 1)
    by_channel = [right * one_hot(over(rest(lane, LANES), cols) == n) for n in range(inner)]
    right_by = jnp.concatenate(
        [
            by_channel[n][c * cols : (c + 1) * cols]
            for c in range(grid_cols)
            for n in range(inner)
        ],
        axis=0,
    )
    sums = dot(left, right_by, 1, 1).astype(BF16)
    for c in range(grid_cols):
        for r in range(grid_rows):
            sent_ref[place(r, c)] = sums[r * rows : (r + 1) * rows, c * LANES : (c + 1) * LANES]


def update_kernel(
    got_ref,
    order_ref,
    normed_ref,
    gain_ref,
    bias_ref,
    proj_ref,
    gate_ref,
    out_hbm,
    out_ref,
    out_sems,
):
    rows, cols, channels = out_ref.shape
    chunks = got_ref.shape[0]
    inner = LANES // cols
    groups = rows // inner
    order = order_ref[...]
    parts = [
        dot(order, got_ref[part * SOME : (part + 1) * SOME].reshape(SOME * rows, LANES)).astype(BF16)
        for part in range(chunks // SOME)
    ]
    lines = [
        jnp.concatenate([part[row * SOME : (row + 1) * SOME] for part in parts], axis=0)
        for row in range(rows)
    ]
    gain, bias = gain_ref[...], bias_ref[...]
    opened = sigmoid(dot(normed_ref[...], gate_ref[...] * 0.5))
    results = []
    for g in range(groups):
        values = jnp.concatenate(
            exchange_blocks(lines[g * inner : (g + 1) * inner], cols), axis=0
        ).astype(F32)
        mean = jnp.mean(values, axis=0, keepdims=True)
        centered = values - mean
        variance = jnp.mean(centered * centered, axis=0, keepdims=True)
        tri_normed = (centered * lax.rsqrt(variance + 1e-05) * gain + bias).astype(BF16)
        projected = dot(tri_normed, proj_ref[...], 0, 0)
        update = (opened[g * LANES : (g + 1) * LANES] * projected).astype(BF16)
        out_ref[g * inner : (g + 1) * inner] = update.reshape(inner, cols, channels)
        if g % 2:
            here = pl.ds((g - 1) * inner, 2 * inner)
            results.append(
                pltpu.make_async_copy(out_ref.at[here], out_hbm.at[here], out_sems.at[g // 2])
            )
            results[-1].start()
    for copy in results:
        copy.wait()


VMEM = pl.BlockSpec(memory_space=pltpu.VMEM)
HBM = pl.BlockSpec(memory_space=pltpu.HBM)
PARAMS = pltpu.CompilerParams(vmem_limit_bytes=32 * 1024 * 1024)


def ring_of(grid_rows, grid_cols):
    line = [(c, y) for c in range(grid_cols) for y in range(2)]
    places = [(at + z, z, at) for at in range(len(line)) for z in range(grid_rows // 2)]
    return [(z * 2 + line[at][1]) * grid_cols + line[at][0] for _, z, at in sorted(places)]


def exchanged(
    grid_rows,
    grid_cols,
    pair,
    chain_lengths,
    norm_in_gain,
    norm_in_bias,
    proj_in,
    gate_in,
    norm_out_gain,
    norm_out_bias,
    proj_out,
    gate_out,
):
    rows, cols, channels = pair.shape
    hidden = proj_out.shape[0]
    devices = grid_rows * grid_cols
    slots = rows * grid_rows // chain_lengths.shape[0]
    order = pl.pallas_call(
        order_kernel,
        out_shape=jax.ShapeDtypeStruct((SOME * SOME, SOME * SOME), BF16),
        out_specs=VMEM,
        compiler_params=PARAMS,
        cost_estimate=pl.CostEstimate(flops=10**9, bytes_accessed=10**6, transcendentals=0),
        name="order",
    )()
    square = jax.ShapeDtypeStruct((LANES, LANES), F32)
    sent, normed, last_gain, last_bias = pl.pallas_call(
        functools.partial(mix_kernel, slots),
        out_shape=(
            jax.ShapeDtypeStruct((devices, 2 * rows, LANES), BF16),
            jax.ShapeDtypeStruct((rows * cols, channels), BF16),
            square,
            square,
        ),
        in_specs=[VMEM] * 9,
        out_specs=[VMEM] * 4,
        compiler_params=PARAMS,
        name="mix",
    )(
        order,
        chain_lengths.reshape(1, -1),
        pair,
        norm_in_gain.reshape(1, LANES),
        norm_in_bias.reshape(1, LANES),
        proj_in,
        gate_in,
        norm_out_gain.reshape(1, LANES),
        norm_out_bias.reshape(1, LANES),
    )
    ring = ring_of(grid_rows, grid_cols)

    def exchange(chunks):
        return lax.all_to_all(
            chunks, ("row", "col"), 0, 0, tiled=True, axis_index_groups=[ring]
        )

    got = exchange(sent)
    sums = pl.pallas_call(
        functools.partial(triangle_kernel, ring, grid_rows, grid_cols, rows, cols),
        out_shape=jax.ShapeDtypeStruct((devices, rows, LANES), BF16),
        in_specs=[VMEM],
        out_specs=VMEM,
        compiler_params=PARAMS,
        name="triangle",
    )(got)
    mine = exchange(sums)
    return pl.pallas_call(
        update_kernel,
        out_shape=jax.ShapeDtypeStruct((rows, cols, channels), BF16),
        in_specs=[VMEM] * 7,
        out_specs=HBM,
        scratch_shapes=[
            pltpu.VMEM((rows, cols, channels), BF16),
            pltpu.SemaphoreType.DMA((rows * cols // LANES // 2,)),
        ],
        compiler_params=PARAMS,
        name="update",
    )(mine, order, normed, last_gain, last_bias, proj_out, gate_out)


def solution(mesh):
    grid_rows, grid_cols = mesh.shape["row"], mesh.shape["col"]
    def fits(rows, cols, channels, hidden):
        devices = grid_rows * grid_cols
        inner = LANES // cols
        return (
            channels == LANES
            and hidden == LANES
            and inner * cols == LANES
            and inner & (inner - 1) == 0
            and inner * devices == hidden
            and rows == SOME
            and rows % (2 * inner) == 0
            and devices % SOME == 0
            and grid_rows % 2 == 0
        )

    def call(*arrays):
        tokens, others, channels = arrays[0].shape
        hidden = arrays[8].shape[0]
        if fits(tokens // grid_rows, others // grid_cols, channels, hidden):
            return jax.shard_map(
                functools.partial(exchanged, grid_rows, grid_cols),
                mesh=mesh,
                in_specs=(P("row", "col", None),) + (P(),) * 9,
                out_specs=P("row", "col", None),
                check_vma=False,
            )(*arrays)
        return jax.shard_map(
            gathered,
            mesh=mesh,
            in_specs=(P("row", "col", None),) + (P(),) * 9,
            out_specs=P("row", "col", None),
            check_vma=False,
        )(*arrays)

    return call
```

```python
import functools
import jax
import jax.numpy as jnp
from jax import lax
from jax.experimental import pallas as pl
from jax.experimental.pallas import tpu as pltpu
from jax.sharding import PartitionSpec as P

LANES = 128
SOME = 16
F32 = jnp.float32
BF16 = jnp.bfloat16


def broadcast(value, axis, source):
    kept = jnp.where(lax.axis_index(axis) == source, value, 0).astype(value.dtype)
    return lax.psum(kept, axis)


def layer_norm(values, gain, bias):
    mean = jnp.mean(values, axis=-1, keepdims=True)
    centered = values - mean
    variance = jnp.mean(centered * centered, axis=-1, keepdims=True)
    return centered * lax.rsqrt(variance + 1e-05) * gain + bias


def token_valid(chain_lengths, tokens_idx, slots):
    chain = tokens_idx // slots
    position = tokens_idx % slots
    chain_ids = jnp.arange(chain_lengths.shape[0], dtype=jnp.int32)
    length_of = jnp.sum(
        jnp.where(chain[:, None] == chain_ids[None, :], chain_lengths[None, :], 0), axis=1
    )
    return (position < length_of).astype(jnp.float32)


def gathered(
    pair,
    chain_lengths,
    norm_in_gain,
    norm_in_bias,
    proj_in,
    gate_in,
    norm_out_gain,
    norm_out_bias,
    proj_out,
    gate_out,
):
    row_count = pair.shape[0]
    col_count = pair.shape[1]
    channels = pair.shape[2]
    hidden = proj_out.shape[0]
    row_index = lax.axis_index("row")
    col_index = lax.axis_index("col")
    slots = row_count * lax.axis_size("row") // chain_lengths.shape[0]
    valid_rows = token_valid(
        chain_lengths, row_index * row_count + jnp.arange(row_count, dtype=jnp.int32), slots
    )
    valid_cols = token_valid(
        chain_lengths, col_index * col_count + jnp.arange(col_count, dtype=jnp.int32), slots
    )
    pair_mask = valid_rows[:, None] * valid_cols[None, :]
    normed = layer_norm(pair.astype(jnp.float32), norm_in_gain, norm_in_bias).astype(jnp.bfloat16)
    flat = normed.reshape(-1, channels)
    values = jnp.dot(flat, proj_in, preferred_element_type=jnp.float32)
    gates = jnp.dot(flat, gate_in, preferred_element_type=jnp.float32)
    mixed = (jax.nn.sigmoid(gates) * values).reshape(row_count, col_count, 2 * hidden) * pair_mask[
        :, :, None
    ]
    left_tile = mixed[:, :, :hidden].astype(jnp.bfloat16)
    right_tile = mixed[:, :, hidden:].astype(jnp.bfloat16)
    ratio = lax.axis_size("row") // lax.axis_size("col")
    right_full = lax.all_gather(right_tile, "col", axis=1, tiled=True)
    received = []
    for part in range(ratio):
        received.append(broadcast(right_full, "row", col_index * ratio + part))
    right_mine = jnp.concatenate(received, axis=0)
    triangle = jnp.einsum(
        "ikh,jkh->ijh",
        lax.all_gather(left_tile, "col", axis=1, tiled=True),
        right_mine,
        preferred_element_type=jnp.float32,
    )
    tri_normed = layer_norm(triangle, norm_out_gain, norm_out_bias).astype(jnp.bfloat16)
    projected = jnp.dot(
        tri_normed.reshape(-1, hidden), proj_out, preferred_element_type=jnp.float32
    )
    gate = jax.nn.sigmoid(jnp.dot(flat, gate_out, preferred_element_type=jnp.float32))
    return (gate * projected).astype(jnp.bfloat16).reshape(row_count, col_count, channels)


def iota2(shape):
    return (
        lax.broadcasted_iota(jnp.int32, shape, 0),
        lax.broadcasted_iota(jnp.int32, shape, 1),
    )


def one_hot(condition):
    return jnp.where(condition, 1.0, 0.0).astype(BF16)


def dot(a, b, a_dim=1, b_dim=0):
    return lax.dot_general(a, b, (((a_dim,), (b_dim,)), ((), ())), preferred_element_type=F32)


def over(value, size):
    if size & (size - 1):
        return value // size
    return lax.shift_right_logical(value, jnp.full_like(value, size.bit_length() - 1))


def rest(value, size):
    return value % size if size & (size - 1) else value & (size - 1)


def over(value, size):
    if size & (size - 1):
        return value // size
    return lax.shift_right_logical(value, jnp.full_like(value, size.bit_length() - 1))


def rest(value, size):
    return value % size if size & (size - 1) else value & (size - 1)


def fetch(sources, targets, sems):
    copies = [
        pltpu.make_async_copy(source, target, sems.at[n])
        for n, (source, target) in enumerate(zip(sources, targets))
    ]
    for copy in copies:
        copy.start()
    return copies


def sigmoid(halved):
    return 0.5 + 0.5 * jnp.tanh(halved)


def exchange_blocks(arrays, cols):
    lane = over(lax.broadcasted_iota(jnp.int32, (1, LANES), 1), cols)
    arrays, step = list(arrays), 1
    while step < len(arrays):
        upper = lane & step != 0
        for n in range(len(arrays)):
            if n // step % 2 == 0:
                a, b = arrays[n], arrays[n + step]
                arrays[n] = jnp.where(upper, pltpu.roll(b, step * cols, 1), a)
                arrays[n + step] = jnp.where(upper, b, pltpu.roll(a, LANES - step * cols, 1))
        step *= 2
    return arrays


def order_kernel(order_ref):
    out, source = iota2(order_ref.shape)
    order_ref[...] = one_hot(
        (over(out, SOME) == rest(source, SOME)) & (rest(out, SOME) == over(source, SOME))
    )


def column(row):
    a, b = iota2((LANES, LANES))
    return jnp.sum(jnp.where(a == b, row, 0.0), axis=1, keepdims=True)


def cell_mask(lengths, slots, rows, cols):
    cell = lax.broadcasted_iota(jnp.int32, (1, rows * cols), 1)

    def valid(token):
        length = jnp.zeros_like(token)
        for chain in range(lengths.shape[1]):
            length = jnp.where(
                over(token, slots) == chain, lengths[:, chain : chain + 1], length
            )
        return rest(token, slots) < length

    row_ok = valid(lax.axis_index("row") * rows + over(cell, cols))
    col_ok = valid(lax.axis_index("col") * cols + rest(cell, cols))
    return jnp.where(row_ok & col_ok, 1.0, 0.0)


def mix_kernel(
    slots,
    order_ref,
    chain_ref,
    pair_ref,
    gain_ref,
    bias_ref,
    proj_ref,
    gate_ref,
    last_gain_ref,
    last_bias_ref,
    sent_ref,
    normed_ref,
    last_gain_out,
    last_bias_out,
):
    rows, cols, channels = pair_ref.shape
    hidden = proj_ref.shape[1] // 2
    cells = rows * cols
    inner = LANES // cols
    groups = rows // inner
    chunks = sent_ref.shape[0]
    flat = pair_ref[...].reshape(cells, channels).astype(F32)
    normed = layer_norm(flat, gain_ref[...], bias_ref[...]).astype(BF16)
    normed_ref[...] = normed
    for source, target in ((last_gain_ref, last_gain_out), (last_bias_ref, last_bias_out)):
        target[...] = jnp.broadcast_to(column(source[...]), target.shape)

    weights = jnp.concatenate([proj_ref[...], gate_ref[...] * 0.5], axis=1)
    products = dot(weights, normed, 0, 1)
    values, gates = products[: 2 * hidden], products[2 * hidden :]
    mask = cell_mask(chain_ref[...], slots, rows, cols)
    mixed = (sigmoid(gates) * values * mask).astype(BF16)

    by_row = []
    for side in range(2):
        lines = []
        for g in range(groups):
            lines += exchange_blocks(
                [
                    mixed[
                        side * hidden + n * chunks : side * hidden + (n + 1) * chunks,
                        g * LANES : (g + 1) * LANES,
                    ]
                    for n in range(inner)
                ],
                cols,
            )
        by_row.append(lines)
    order = order_ref[...]
    for part in range(chunks // SOME):
        for side in range(2):
            stack = jnp.concatenate(
                [line[part * SOME : (part + 1) * SOME] for line in by_row[side]], axis=0
            )
            sent_ref[part * SOME : (part + 1) * SOME, side * rows : (side + 1) * rows] = (
                dot(order, stack).astype(BF16).reshape(SOME, rows, LANES)
            )


def triangle_kernel(ring, grid_rows, grid_cols, rows, cols, got_ref, sent_ref):
    inner = LANES // cols

    def place(r, c):
        return ring.index(r * grid_cols + c)

    def side(which):
        return jnp.concatenate(
            [
                jnp.concatenate(
                    [
                        got_ref[place(r, c), which * rows : (which + 1) * rows]
                        for r in range(grid_rows)
                    ],
                    axis=0,
                )
                for c in range(grid_cols)
            ],
            axis=1,
        )

    left, right = side(0), side(1)
    lane = lax.broadcasted_iota(jnp.int32, (1, grid_cols * LANES), 1)
    by_channel = [right * one_hot(over(rest(lane, LANES), cols) == n) for n in range(inner)]
    right_by = jnp.concatenate(
        [
            by_channel[n][c * cols : (c + 1) * cols]
            for c in range(grid_cols)
            for n in range(inner)
        ],
        axis=0,
    )
    sums = dot(left, right_by, 1, 1).astype(BF16)
    for c in range(grid_cols):
        for r in range(grid_rows):
            sent_ref[place(r, c)] = sums[r * rows : (r + 1) * rows, c * LANES : (c + 1) * LANES]


def update_kernel(
    got_ref,
    order_ref,
    normed_ref,
    gain_ref,
    bias_ref,
    proj_ref,
    gate_ref,
    out_hbm,
    out_ref,
    out_sems,
):
    rows, cols, channels = out_ref.shape
    chunks = got_ref.shape[0]
    inner = LANES // cols
    groups = rows // inner
    order = order_ref[...]
    parts = [
        dot(order, got_ref[part * SOME : (part + 1) * SOME].reshape(SOME * rows, LANES)).astype(BF16)
        for part in range(chunks // SOME)
    ]
    lines = [
        jnp.concatenate([part[row * SOME : (row + 1) * SOME] for part in parts], axis=0)
        for row in range(rows)
    ]
    gain, bias = gain_ref[...], bias_ref[...]
    opened = sigmoid(dot(normed_ref[...], gate_ref[...] * 0.5))
    results = []
    for g in range(groups):
        values = jnp.concatenate(
            exchange_blocks(lines[g * inner : (g + 1) * inner], cols), axis=0
        ).astype(F32)
        mean = jnp.mean(values, axis=0, keepdims=True)
        centered = values - mean
        variance = jnp.mean(centered * centered, axis=0, keepdims=True)
        tri_normed = (centered * lax.rsqrt(variance + 1e-05) * gain + bias).astype(BF16)
        projected = dot(tri_normed, proj_ref[...], 0, 0)
        update = (opened[g * LANES : (g + 1) * LANES] * projected).astype(BF16)
        out_ref[g * inner : (g + 1) * inner] = update.reshape(inner, cols, channels)
        if g % 2:
            here = pl.ds((g - 1) * inner, 2 * inner)
            results.append(
                pltpu.make_async_copy(out_ref.at[here], out_hbm.at[here], out_sems.at[g // 2])
            )
            results[-1].start()
    for copy in results:
        copy.wait()


VMEM = pl.BlockSpec(memory_space=pltpu.VMEM)
HBM = pl.BlockSpec(memory_space=pltpu.HBM)
PARAMS = pltpu.CompilerParams(vmem_limit_bytes=32 * 1024 * 1024)


def ring_of(grid_rows, grid_cols):
    line = [(c, y) for c in range(grid_cols) for y in range(2)]
    places = [(at + z, z, at) for at in range(len(line)) for z in range(grid_rows // 2)]
    ring = [(z * 2 + line[at][1]) * grid_cols + line[at][0] for _, z, at in sorted(places)]
    return [device for device in ring if device > 1] + [1, 0]


def exchanged(
    grid_rows,
    grid_cols,
    pair,
    chain_lengths,
    norm_in_gain,
    norm_in_bias,
    proj_in,
    gate_in,
    norm_out_gain,
    norm_out_bias,
    proj_out,
    gate_out,
):
    rows, cols, channels = pair.shape
    hidden = proj_out.shape[0]
    devices = grid_rows * grid_cols
    slots = rows * grid_rows // chain_lengths.shape[0]
    order = pl.pallas_call(
        order_kernel,
        out_shape=jax.ShapeDtypeStruct((SOME * SOME, SOME * SOME), BF16),
        out_specs=VMEM,
        compiler_params=PARAMS,
        cost_estimate=pl.CostEstimate(flops=10**9, bytes_accessed=10**6, transcendentals=0),
        name="order",
    )()
    square = jax.ShapeDtypeStruct((LANES, LANES), F32)
    sent, normed, last_gain, last_bias = pl.pallas_call(
        functools.partial(mix_kernel, slots),
        out_shape=(
            jax.ShapeDtypeStruct((devices, 2 * rows, LANES), BF16),
            jax.ShapeDtypeStruct((rows * cols, channels), BF16),
            square,
            square,
        ),
        in_specs=[VMEM] * 9,
        out_specs=[VMEM] * 4,
        compiler_params=PARAMS,
        name="mix",
    )(
        order,
        chain_lengths.reshape(1, -1),
        pair,
        norm_in_gain.reshape(1, LANES),
        norm_in_bias.reshape(1, LANES),
        proj_in,
        gate_in,
        norm_out_gain.reshape(1, LANES),
        norm_out_bias.reshape(1, LANES),
    )
    ring = ring_of(grid_rows, grid_cols)

    def exchange(chunks):
        return lax.all_to_all(
            chunks, ("row", "col"), 0, 0, tiled=True, axis_index_groups=[ring]
        )

    got = exchange(sent)
    sums = pl.pallas_call(
        functools.partial(triangle_kernel, ring, grid_rows, grid_cols, rows, cols),
        out_shape=jax.ShapeDtypeStruct((devices, rows, LANES), BF16),
        in_specs=[VMEM],
        out_specs=VMEM,
        compiler_params=PARAMS,
        name="triangle",
    )(got)
    mine = exchange(sums)
    return pl.pallas_call(
        update_kernel,
        out_shape=jax.ShapeDtypeStruct((rows, cols, channels), BF16),
        in_specs=[VMEM] * 7,
        out_specs=HBM,
        scratch_shapes=[
            pltpu.VMEM((rows, cols, channels), BF16),
            pltpu.SemaphoreType.DMA((rows * cols // LANES // 2,)),
        ],
        compiler_params=PARAMS,
        name="update",
    )(mine, order, normed, last_gain, last_bias, proj_out, gate_out)


def solution(mesh):
    grid_rows, grid_cols = mesh.shape["row"], mesh.shape["col"]
    def fits(rows, cols, channels, hidden):
        devices = grid_rows * grid_cols
        inner = LANES // cols
        return (
            channels == LANES
            and hidden == LANES
            and inner * cols == LANES
            and inner & (inner - 1) == 0
            and inner * devices == hidden
            and rows == SOME
            and rows % (2 * inner) == 0
            and devices % SOME == 0
            and grid_rows % 2 == 0
        )

    def call(*arrays):
        tokens, others, channels = arrays[0].shape
        hidden = arrays[8].shape[0]
        if fits(tokens // grid_rows, others // grid_cols, channels, hidden):
            return jax.shard_map(
                functools.partial(exchanged, grid_rows, grid_cols),
                mesh=mesh,
                in_specs=(P("row", "col", None),) + (P(),) * 9,
                out_specs=P("row", "col", None),
                check_vma=False,
            )(*arrays)
        return jax.shard_map(
            gathered,
            mesh=mesh,
            in_specs=(P("row", "col", None),) + (P(),) * 9,
            out_specs=P("row", "col", None),
            check_vma=False,
        )(*arrays)

    return call
```

```python
import functools
import jax
import jax.numpy as jnp
from jax import lax
from jax.experimental import pallas as pl
from jax.experimental.pallas import tpu as pltpu
from jax.sharding import PartitionSpec as P

LANES = 128
SOME = 16
F32 = jnp.float32
BF16 = jnp.bfloat16


def broadcast(value, axis, source):
    kept = jnp.where(lax.axis_index(axis) == source, value, 0).astype(value.dtype)
    return lax.psum(kept, axis)


def layer_norm(values, gain, bias):
    mean = jnp.mean(values, axis=-1, keepdims=True)
    centered = values - mean
    variance = jnp.mean(centered * centered, axis=-1, keepdims=True)
    return centered * lax.rsqrt(variance + 1e-05) * gain + bias


def token_valid(chain_lengths, tokens_idx, slots):
    chain = tokens_idx // slots
    position = tokens_idx % slots
    chain_ids = jnp.arange(chain_lengths.shape[0], dtype=jnp.int32)
    length_of = jnp.sum(
        jnp.where(chain[:, None] == chain_ids[None, :], chain_lengths[None, :], 0), axis=1
    )
    return (position < length_of).astype(jnp.float32)


def gathered(
    pair,
    chain_lengths,
    norm_in_gain,
    norm_in_bias,
    proj_in,
    gate_in,
    norm_out_gain,
    norm_out_bias,
    proj_out,
    gate_out,
):
    row_count = pair.shape[0]
    col_count = pair.shape[1]
    channels = pair.shape[2]
    hidden = proj_out.shape[0]
    row_index = lax.axis_index("row")
    col_index = lax.axis_index("col")
    slots = row_count * lax.axis_size("row") // chain_lengths.shape[0]
    valid_rows = token_valid(
        chain_lengths, row_index * row_count + jnp.arange(row_count, dtype=jnp.int32), slots
    )
    valid_cols = token_valid(
        chain_lengths, col_index * col_count + jnp.arange(col_count, dtype=jnp.int32), slots
    )
    pair_mask = valid_rows[:, None] * valid_cols[None, :]
    normed = layer_norm(pair.astype(jnp.float32), norm_in_gain, norm_in_bias).astype(jnp.bfloat16)
    flat = normed.reshape(-1, channels)
    values = jnp.dot(flat, proj_in, preferred_element_type=jnp.float32)
    gates = jnp.dot(flat, gate_in, preferred_element_type=jnp.float32)
    mixed = (jax.nn.sigmoid(gates) * values).reshape(row_count, col_count, 2 * hidden) * pair_mask[
        :, :, None
    ]
    left_tile = mixed[:, :, :hidden].astype(jnp.bfloat16)
    right_tile = mixed[:, :, hidden:].astype(jnp.bfloat16)
    ratio = lax.axis_size("row") // lax.axis_size("col")
    right_full = lax.all_gather(right_tile, "col", axis=1, tiled=True)
    received = []
    for part in range(ratio):
        received.append(broadcast(right_full, "row", col_index * ratio + part))
    right_mine = jnp.concatenate(received, axis=0)
    triangle = jnp.einsum(
        "ikh,jkh->ijh",
        lax.all_gather(left_tile, "col", axis=1, tiled=True),
        right_mine,
        preferred_element_type=jnp.float32,
    )
    tri_normed = layer_norm(triangle, norm_out_gain, norm_out_bias).astype(jnp.bfloat16)
    projected = jnp.dot(
        tri_normed.reshape(-1, hidden), proj_out, preferred_element_type=jnp.float32
    )
    gate = jax.nn.sigmoid(jnp.dot(flat, gate_out, preferred_element_type=jnp.float32))
    return (gate * projected).astype(jnp.bfloat16).reshape(row_count, col_count, channels)


def iota2(shape):
    return (
        lax.broadcasted_iota(jnp.int32, shape, 0),
        lax.broadcasted_iota(jnp.int32, shape, 1),
    )


def one_hot(condition):
    return jnp.where(condition, 1.0, 0.0).astype(BF16)


def dot(a, b, a_dim=1, b_dim=0):
    return lax.dot_general(a, b, (((a_dim,), (b_dim,)), ((), ())), preferred_element_type=F32)


def over(value, size):
    if size & (size - 1):
        return value // size
    return lax.shift_right_logical(value, jnp.full_like(value, size.bit_length() - 1))


def rest(value, size):
    return value % size if size & (size - 1) else value & (size - 1)


def over(value, size):
    if size & (size - 1):
        return value // size
    return lax.shift_right_logical(value, jnp.full_like(value, size.bit_length() - 1))


def rest(value, size):
    return value % size if size & (size - 1) else value & (size - 1)


def fetch(sources, targets, sems):
    copies = [
        pltpu.make_async_copy(source, target, sems.at[n])
        for n, (source, target) in enumerate(zip(sources, targets))
    ]
    for copy in copies:
        copy.start()
    return copies


def sigmoid(halved):
    return 0.5 + 0.5 * jnp.tanh(halved)


def exchange_blocks(arrays, cols):
    lane = over(lax.broadcasted_iota(jnp.int32, (1, LANES), 1), cols)
    arrays, step = list(arrays), 1
    while step < len(arrays):
        upper = lane & step != 0
        for n in range(len(arrays)):
            if n // step % 2 == 0:
                a, b = arrays[n], arrays[n + step]
                arrays[n] = jnp.where(upper, pltpu.roll(b, step * cols, 1), a)
                arrays[n + step] = jnp.where(upper, b, pltpu.roll(a, LANES - step * cols, 1))
        step *= 2
    return arrays


def order_kernel(order_ref):
    out, source = iota2(order_ref.shape)
    order_ref[...] = one_hot(
        (over(out, SOME) == rest(source, SOME)) & (rest(out, SOME) == over(source, SOME))
    )


def column(row):
    a, b = iota2((LANES, LANES))
    return jnp.sum(jnp.where(a == b, row, 0.0), axis=1, keepdims=True)


def cell_mask(lengths, slots, rows, cols):
    cell = lax.broadcasted_iota(jnp.int32, (1, rows * cols), 1)

    def valid(token):
        length = jnp.zeros_like(token)
        for chain in range(lengths.shape[1]):
            length = jnp.where(
                over(token, slots) == chain, lengths[:, chain : chain + 1], length
            )
        return rest(token, slots) < length

    row_ok = valid(lax.axis_index("row") * rows + over(cell, cols))
    col_ok = valid(lax.axis_index("col") * cols + rest(cell, cols))
    return jnp.where(row_ok & col_ok, 1.0, 0.0)


def mix_kernel(
    slots,
    order_ref,
    chain_ref,
    pair_ref,
    gain_ref,
    bias_ref,
    proj_ref,
    gate_ref,
    last_gain_ref,
    last_bias_ref,
    sent_ref,
    normed_ref,
    last_gain_out,
    last_bias_out,
):
    rows, cols, channels = pair_ref.shape
    hidden = proj_ref.shape[1] // 2
    cells = rows * cols
    inner = LANES // cols
    groups = rows // inner
    chunks = sent_ref.shape[0]
    flat = pair_ref[...].reshape(cells, channels).astype(F32)
    normed = layer_norm(flat, gain_ref[...], bias_ref[...]).astype(BF16)
    normed_ref[...] = normed
    for source, target in ((last_gain_ref, last_gain_out), (last_bias_ref, last_bias_out)):
        target[...] = jnp.broadcast_to(column(source[...]), target.shape)

    weights = jnp.concatenate([proj_ref[...], gate_ref[...] * 0.5], axis=1)
    products = dot(weights, normed, 0, 1)
    values, gates = products[: 2 * hidden], products[2 * hidden :]
    mask = cell_mask(chain_ref[...], slots, rows, cols)
    mixed = (sigmoid(gates) * values * mask).astype(BF16)

    by_row = []
    for side in range(2):
        lines = []
        for g in range(groups):
            lines += exchange_blocks(
                [
                    mixed[
                        side * hidden + n * chunks : side * hidden + (n + 1) * chunks,
                        g * LANES : (g + 1) * LANES,
                    ]
                    for n in range(inner)
                ],
                cols,
            )
        by_row.append(lines)
    order = order_ref[...]
    for part in range(chunks // SOME):
        for side in range(2):
            stack = jnp.concatenate(
                [line[part * SOME : (part + 1) * SOME] for line in by_row[side]], axis=0
            )
            sent_ref[part * SOME : (part + 1) * SOME, side * rows : (side + 1) * rows] = (
                dot(order, stack).astype(BF16).reshape(SOME, rows, LANES)
            )


def triangle_kernel(ring, grid_rows, grid_cols, rows, cols, got_ref, sent_ref):
    inner = LANES // cols

    def place(r, c):
        return ring.index(r * grid_cols + c)

    def side(which):
        return jnp.concatenate(
            [
                jnp.concatenate(
                    [
                        got_ref[place(r, c), which * rows : (which + 1) * rows]
                        for r in range(grid_rows)
                    ],
                    axis=0,
                )
                for c in range(grid_cols)
            ],
            axis=1,
        )

    left, right = side(0), side(1)
    lane = lax.broadcasted_iota(jnp.int32, (1, grid_cols * LANES), 1)
    by_channel = [right * one_hot(over(rest(lane, LANES), cols) == n) for n in range(inner)]
    right_by = jnp.concatenate(
        [
            by_channel[n][c * cols : (c + 1) * cols]
            for c in range(grid_cols)
            for n in range(inner)
        ],
        axis=0,
    )
    sums = dot(left, right_by, 1, 1).astype(BF16)
    for c in range(grid_cols):
        for r in range(grid_rows):
            sent_ref[place(r, c)] = sums[r * rows : (r + 1) * rows, c * LANES : (c + 1) * LANES]


def update_kernel(
    got_ref,
    order_ref,
    normed_ref,
    gain_ref,
    bias_ref,
    proj_ref,
    gate_ref,
    out_hbm,
    out_ref,
    out_sems,
):
    rows, cols, channels = out_ref.shape
    chunks = got_ref.shape[0]
    inner = LANES // cols
    groups = rows // inner
    order = order_ref[...]
    parts = [
        dot(order, got_ref[part * SOME : (part + 1) * SOME].reshape(SOME * rows, LANES)).astype(BF16)
        for part in range(chunks // SOME)
    ]
    lines = [
        jnp.concatenate([part[row * SOME : (row + 1) * SOME] for part in parts], axis=0)
        for row in range(rows)
    ]
    gain, bias = gain_ref[...], bias_ref[...]
    opened = sigmoid(dot(normed_ref[...], gate_ref[...] * 0.5))
    results = []
    for g in range(groups):
        values = jnp.concatenate(
            exchange_blocks(lines[g * inner : (g + 1) * inner], cols), axis=0
        ).astype(F32)
        mean = jnp.mean(values, axis=0, keepdims=True)
        centered = values - mean
        variance = jnp.mean(centered * centered, axis=0, keepdims=True)
        tri_normed = (centered * lax.rsqrt(variance + 1e-05) * gain + bias).astype(BF16)
        projected = dot(tri_normed, proj_ref[...], 0, 0)
        update = (opened[g * LANES : (g + 1) * LANES] * projected).astype(BF16)
        out_ref[g * inner : (g + 1) * inner] = update.reshape(inner, cols, channels)
        if g % 2:
            here = pl.ds((g - 1) * inner, 2 * inner)
            results.append(
                pltpu.make_async_copy(out_ref.at[here], out_hbm.at[here], out_sems.at[g // 2])
            )
            results[-1].start()
    for copy in results:
        copy.wait()


VMEM = pl.BlockSpec(memory_space=pltpu.VMEM)
HBM = pl.BlockSpec(memory_space=pltpu.HBM)
PARAMS = pltpu.CompilerParams(vmem_limit_bytes=32 * 1024 * 1024)


def ring_of(grid_rows, grid_cols):
    line = [(c, y) for c in range(grid_cols) for y in range(2)]
    places = [(at + z, z, at) for at in range(len(line)) for z in range(grid_rows // 2)]
    ring = [(z * 2 + line[at][1]) * grid_cols + line[at][0] for _, z, at in sorted(places)]
    other = ring.index(2 * grid_cols + 1)
    ring[0], ring[other] = ring[other], ring[0]
    return ring


def exchanged(
    grid_rows,
    grid_cols,
    pair,
    chain_lengths,
    norm_in_gain,
    norm_in_bias,
    proj_in,
    gate_in,
    norm_out_gain,
    norm_out_bias,
    proj_out,
    gate_out,
):
    rows, cols, channels = pair.shape
    hidden = proj_out.shape[0]
    devices = grid_rows * grid_cols
    slots = rows * grid_rows // chain_lengths.shape[0]
    order = pl.pallas_call(
        order_kernel,
        out_shape=jax.ShapeDtypeStruct((SOME * SOME, SOME * SOME), BF16),
        out_specs=VMEM,
        compiler_params=PARAMS,
        cost_estimate=pl.CostEstimate(flops=10**9, bytes_accessed=10**6, transcendentals=0),
        name="order",
    )()
    square = jax.ShapeDtypeStruct((LANES, LANES), F32)
    sent, normed, last_gain, last_bias = pl.pallas_call(
        functools.partial(mix_kernel, slots),
        out_shape=(
            jax.ShapeDtypeStruct((devices, 2 * rows, LANES), BF16),
            jax.ShapeDtypeStruct((rows * cols, channels), BF16),
            square,
            square,
        ),
        in_specs=[VMEM] * 9,
        out_specs=[VMEM] * 4,
        compiler_params=PARAMS,
        name="mix",
    )(
        order,
        chain_lengths.reshape(1, -1),
        pair,
        norm_in_gain.reshape(1, LANES),
        norm_in_bias.reshape(1, LANES),
        proj_in,
        gate_in,
        norm_out_gain.reshape(1, LANES),
        norm_out_bias.reshape(1, LANES),
    )
    ring = ring_of(grid_rows, grid_cols)

    def exchange(chunks):
        return lax.all_to_all(
            chunks, ("row", "col"), 0, 0, tiled=True, axis_index_groups=[ring]
        )

    got = exchange(sent)
    sums = pl.pallas_call(
        functools.partial(triangle_kernel, ring, grid_rows, grid_cols, rows, cols),
        out_shape=jax.ShapeDtypeStruct((devices, rows, LANES), BF16),
        in_specs=[VMEM],
        out_specs=VMEM,
        compiler_params=PARAMS,
        name="triangle",
    )(got)
    mine = exchange(sums)
    return pl.pallas_call(
        update_kernel,
        out_shape=jax.ShapeDtypeStruct((rows, cols, channels), BF16),
        in_specs=[VMEM] * 7,
        out_specs=HBM,
        scratch_shapes=[
            pltpu.VMEM((rows, cols, channels), BF16),
            pltpu.SemaphoreType.DMA((rows * cols // LANES // 2,)),
        ],
        compiler_params=PARAMS,
        name="update",
    )(mine, order, normed, last_gain, last_bias, proj_out, gate_out)


def solution(mesh):
    grid_rows, grid_cols = mesh.shape["row"], mesh.shape["col"]
    def fits(rows, cols, channels, hidden):
        devices = grid_rows * grid_cols
        inner = LANES // cols
        return (
            channels == LANES
            and hidden == LANES
            and inner * cols == LANES
            and inner & (inner - 1) == 0
            and inner * devices == hidden
            and rows == SOME
            and rows % (2 * inner) == 0
            and devices % SOME == 0
            and grid_rows % 2 == 0
        )

    def call(*arrays):
        tokens, others, channels = arrays[0].shape
        hidden = arrays[8].shape[0]
        if fits(tokens // grid_rows, others // grid_cols, channels, hidden):
            return jax.shard_map(
                functools.partial(exchanged, grid_rows, grid_cols),
                mesh=mesh,
                in_specs=(P("row", "col", None),) + (P(),) * 9,
                out_specs=P("row", "col", None),
                check_vma=False,
            )(*arrays)
        return jax.shard_map(
            gathered,
            mesh=mesh,
            in_specs=(P("row", "col", None),) + (P(),) * 9,
            out_specs=P("row", "col", None),
            check_vma=False,
        )(*arrays)

    return call
```

```python
import functools
import jax
import jax.numpy as jnp
from jax import lax
from jax.experimental import pallas as pl
from jax.experimental.pallas import tpu as pltpu
from jax.sharding import PartitionSpec as P

LANES = 128
SOME = 16
F32 = jnp.float32
BF16 = jnp.bfloat16


def broadcast(value, axis, source):
    kept = jnp.where(lax.axis_index(axis) == source, value, 0).astype(value.dtype)
    return lax.psum(kept, axis)


def layer_norm(values, gain, bias):
    mean = jnp.mean(values, axis=-1, keepdims=True)
    centered = values - mean
    variance = jnp.mean(centered * centered, axis=-1, keepdims=True)
    return centered * lax.rsqrt(variance + 1e-05) * gain + bias


def token_valid(chain_lengths, tokens_idx, slots):
    chain = tokens_idx // slots
    position = tokens_idx % slots
    chain_ids = jnp.arange(chain_lengths.shape[0], dtype=jnp.int32)
    length_of = jnp.sum(
        jnp.where(chain[:, None] == chain_ids[None, :], chain_lengths[None, :], 0), axis=1
    )
    return (position < length_of).astype(jnp.float32)


def gathered(
    pair,
    chain_lengths,
    norm_in_gain,
    norm_in_bias,
    proj_in,
    gate_in,
    norm_out_gain,
    norm_out_bias,
    proj_out,
    gate_out,
):
    row_count = pair.shape[0]
    col_count = pair.shape[1]
    channels = pair.shape[2]
    hidden = proj_out.shape[0]
    row_index = lax.axis_index("row")
    col_index = lax.axis_index("col")
    slots = row_count * lax.axis_size("row") // chain_lengths.shape[0]
    valid_rows = token_valid(
        chain_lengths, row_index * row_count + jnp.arange(row_count, dtype=jnp.int32), slots
    )
    valid_cols = token_valid(
        chain_lengths, col_index * col_count + jnp.arange(col_count, dtype=jnp.int32), slots
    )
    pair_mask = valid_rows[:, None] * valid_cols[None, :]
    normed = layer_norm(pair.astype(jnp.float32), norm_in_gain, norm_in_bias).astype(jnp.bfloat16)
    flat = normed.reshape(-1, channels)
    values = jnp.dot(flat, proj_in, preferred_element_type=jnp.float32)
    gates = jnp.dot(flat, gate_in, preferred_element_type=jnp.float32)
    mixed = (jax.nn.sigmoid(gates) * values).reshape(row_count, col_count, 2 * hidden) * pair_mask[
        :, :, None
    ]
    left_tile = mixed[:, :, :hidden].astype(jnp.bfloat16)
    right_tile = mixed[:, :, hidden:].astype(jnp.bfloat16)
    ratio = lax.axis_size("row") // lax.axis_size("col")
    right_full = lax.all_gather(right_tile, "col", axis=1, tiled=True)
    received = []
    for part in range(ratio):
        received.append(broadcast(right_full, "row", col_index * ratio + part))
    right_mine = jnp.concatenate(received, axis=0)
    triangle = jnp.einsum(
        "ikh,jkh->ijh",
        lax.all_gather(left_tile, "col", axis=1, tiled=True),
        right_mine,
        preferred_element_type=jnp.float32,
    )
    tri_normed = layer_norm(triangle, norm_out_gain, norm_out_bias).astype(jnp.bfloat16)
    projected = jnp.dot(
        tri_normed.reshape(-1, hidden), proj_out, preferred_element_type=jnp.float32
    )
    gate = jax.nn.sigmoid(jnp.dot(flat, gate_out, preferred_element_type=jnp.float32))
    return (gate * projected).astype(jnp.bfloat16).reshape(row_count, col_count, channels)


def iota2(shape):
    return (
        lax.broadcasted_iota(jnp.int32, shape, 0),
        lax.broadcasted_iota(jnp.int32, shape, 1),
    )


def one_hot(condition):
    return jnp.where(condition, 1.0, 0.0).astype(BF16)


def dot(a, b, a_dim=1, b_dim=0):
    return lax.dot_general(a, b, (((a_dim,), (b_dim,)), ((), ())), preferred_element_type=F32)


def over(value, size):
    if size & (size - 1):
        return value // size
    return lax.shift_right_logical(value, jnp.full_like(value, size.bit_length() - 1))


def rest(value, size):
    return value % size if size & (size - 1) else value & (size - 1)


def over(value, size):
    if size & (size - 1):
        return value // size
    return lax.shift_right_logical(value, jnp.full_like(value, size.bit_length() - 1))


def rest(value, size):
    return value % size if size & (size - 1) else value & (size - 1)


def fetch(sources, targets, sems):
    copies = [
        pltpu.make_async_copy(source, target, sems.at[n])
        for n, (source, target) in enumerate(zip(sources, targets))
    ]
    for copy in copies:
        copy.start()
    return copies


def sigmoid(halved):
    return 0.5 + 0.5 * jnp.tanh(halved)


def exchange_blocks(arrays, cols):
    lane = over(lax.broadcasted_iota(jnp.int32, (1, LANES), 1), cols)
    arrays, step = list(arrays), 1
    while step < len(arrays):
        upper = lane & step != 0
        for n in range(len(arrays)):
            if n // step % 2 == 0:
                a, b = arrays[n], arrays[n + step]
                arrays[n] = jnp.where(upper, pltpu.roll(b, step * cols, 1), a)
                arrays[n + step] = jnp.where(upper, b, pltpu.roll(a, LANES - step * cols, 1))
        step *= 2
    return arrays


def order_kernel(order_ref):
    out, source = iota2(order_ref.shape)
    order_ref[...] = one_hot(
        (over(out, SOME) == rest(source, SOME)) & (rest(out, SOME) == over(source, SOME))
    )


def column(row):
    a, b = iota2((LANES, LANES))
    return jnp.sum(jnp.where(a == b, row, 0.0), axis=1, keepdims=True)


def cell_mask(lengths, slots, rows, cols):
    cell = lax.broadcasted_iota(jnp.int32, (1, rows * cols), 1)

    def valid(token):
        length = jnp.zeros_like(token)
        for chain in range(lengths.shape[1]):
            length = jnp.where(
                over(token, slots) == chain, lengths[:, chain : chain + 1], length
            )
        return rest(token, slots) < length

    row_ok = valid(lax.axis_index(("z", "y")) * rows + over(cell, cols))
    col_ok = valid(lax.axis_index(("x", "c")) * cols + rest(cell, cols))
    return jnp.where(row_ok & col_ok, 1.0, 0.0)


def mix_kernel(
    slots,
    order_ref,
    chain_ref,
    pair_ref,
    gain_ref,
    bias_ref,
    proj_ref,
    gate_ref,
    last_gain_ref,
    last_bias_ref,
    sent_ref,
    normed_ref,
    last_gain_out,
    last_bias_out,
):
    rows, cols, channels = pair_ref.shape
    hidden = proj_ref.shape[1] // 2
    cells = rows * cols
    inner = LANES // cols
    groups = rows // inner
    chunks = sent_ref.shape[0]
    flat = pair_ref[...].reshape(cells, channels).astype(F32)
    normed = layer_norm(flat, gain_ref[...], bias_ref[...]).astype(BF16)
    normed_ref[...] = normed
    for source, target in ((last_gain_ref, last_gain_out), (last_bias_ref, last_bias_out)):
        target[...] = jnp.broadcast_to(column(source[...]), target.shape)

    values = dot(proj_ref[...], normed, 0, 1)
    gates = dot(gate_ref[...] * 0.5, normed, 0, 1)
    mask = cell_mask(chain_ref[...], slots, rows, cols)
    mixed = (sigmoid(gates) * values * mask).astype(BF16)

    by_row = []
    for side in range(2):
        lines = []
        for g in range(groups):
            lines += exchange_blocks(
                [
                    mixed[
                        side * hidden + n * chunks : side * hidden + (n + 1) * chunks,
                        g * LANES : (g + 1) * LANES,
                    ]
                    for n in range(inner)
                ],
                cols,
            )
        by_row.append(lines)
    order = order_ref[...]
    for part in range(chunks // SOME):
        for side in range(2):
            stack = jnp.concatenate(
                [line[part * SOME : (part + 1) * SOME] for line in by_row[side]], axis=0
            )
            sent_ref[part * SOME : (part + 1) * SOME, side * rows : (side + 1) * rows] = (
                dot(order, stack).astype(BF16).reshape(SOME, rows, LANES)
            )


def triangle_kernel(ring_in, ring_out, grid_rows, grid_cols, rows, cols, got_ref, sent_ref):
    inner = LANES // cols

    def place(ring, r, c):
        return ring.index(r * grid_cols + c)

    def side(which):
        return jnp.concatenate(
            [
                jnp.concatenate(
                    [
                        got_ref[place(ring_in, r, c), which * rows : (which + 1) * rows]
                        for r in range(grid_rows)
                    ],
                    axis=0,
                )
                for c in range(grid_cols)
            ],
            axis=1,
        )

    left, right = side(0), side(1)
    lane = lax.broadcasted_iota(jnp.int32, (1, grid_cols * LANES), 1)
    by_channel = [right * one_hot(over(rest(lane, LANES), cols) == n) for n in range(inner)]
    right_by = jnp.concatenate(
        [
            by_channel[n][c * cols : (c + 1) * cols]
            for c in range(grid_cols)
            for n in range(inner)
        ],
        axis=0,
    )
    sums = dot(left, right_by, 1, 1).astype(BF16)
    for c in range(grid_cols):
        for r in range(grid_rows):
            sent_ref[place(ring_out, r, c)] = sums[r * rows : (r + 1) * rows, c * LANES : (c + 1) * LANES]


def update_kernel(
    places,
    got_ref,
    order_ref,
    normed_ref,
    gain_ref,
    bias_ref,
    proj_ref,
    gate_ref,
    out_hbm,
    out_ref,
    out_sems,
):
    rows, cols, channels = out_ref.shape
    chunks = got_ref.shape[0]
    inner = LANES // cols
    groups = rows // inner
    order = order_ref[...]
    parts = [
        dot(
            order,
            jnp.concatenate(
                [got_ref[place] for place in places[part * SOME : (part + 1) * SOME]], axis=0
            ),
        ).astype(BF16)
        for part in range(chunks // SOME)
    ]
    lines = [
        jnp.concatenate([part[row * SOME : (row + 1) * SOME] for part in parts], axis=0)
        for row in range(rows)
    ]
    gain, bias = gain_ref[...], bias_ref[...]
    opened = sigmoid(dot(normed_ref[...], gate_ref[...] * 0.5))
    results = []
    for g in range(groups):
        values = jnp.concatenate(
            exchange_blocks(lines[g * inner : (g + 1) * inner], cols), axis=0
        ).astype(F32)
        mean = jnp.mean(values, axis=0, keepdims=True)
        centered = values - mean
        variance = jnp.mean(centered * centered, axis=0, keepdims=True)
        tri_normed = (centered * lax.rsqrt(variance + 1e-05) * gain + bias).astype(BF16)
        projected = dot(tri_normed, proj_ref[...], 0, 0)
        update = (opened[g * LANES : (g + 1) * LANES] * projected).astype(BF16)
        here = pl.ds(g * inner, inner)
        out_ref[here] = update.reshape(inner, cols, channels)
        results.append(pltpu.make_async_copy(out_ref.at[here], out_hbm.at[here], out_sems.at[g]))
        results[-1].start()
    for copy in results:
        copy.wait()


VMEM = pl.BlockSpec(memory_space=pltpu.VMEM)
HBM = pl.BlockSpec(memory_space=pltpu.HBM)
PARAMS = pltpu.CompilerParams(vmem_limit_bytes=32 * 1024 * 1024)


def ring_of(axes, grid_rows, grid_cols):
    sizes = {"z": grid_rows // 2, "y": 2, "x": grid_cols // 2, "c": 2}
    strides = {"z": 2 * grid_cols, "y": grid_cols, "x": 2, "c": 1}
    ring = [0]
    for axis in axes:
        ring = [device + n * strides[axis] for device in ring for n in range(sizes[axis])]
    return ring


def exchanged(
    grid_rows,
    grid_cols,
    pair,
    chain_lengths,
    norm_in_gain,
    norm_in_bias,
    proj_in,
    gate_in,
    norm_out_gain,
    norm_out_bias,
    proj_out,
    gate_out,
):
    rows, cols, channels = pair.shape
    hidden = proj_out.shape[0]
    devices = grid_rows * grid_cols
    slots = rows * grid_rows // chain_lengths.shape[0]
    order = pl.pallas_call(
        order_kernel,
        out_shape=jax.ShapeDtypeStruct((SOME * SOME, SOME * SOME), BF16),
        out_specs=VMEM,
        compiler_params=PARAMS,
        cost_estimate=pl.CostEstimate(flops=10**9, bytes_accessed=10**6, transcendentals=0),
        name="order",
    )()
    square = jax.ShapeDtypeStruct((LANES, LANES), F32)
    sent, normed, last_gain, last_bias = pl.pallas_call(
        functools.partial(mix_kernel, slots),
        out_shape=(
            jax.ShapeDtypeStruct((devices, 2 * rows, LANES), BF16),
            jax.ShapeDtypeStruct((rows * cols, channels), BF16),
            square,
            square,
        ),
        in_specs=[VMEM] * 9,
        out_specs=[VMEM] * 4,
        compiler_params=PARAMS,
        name="mix",
    )(
        order,
        chain_lengths.reshape(1, -1),
        pair,
        norm_in_gain.reshape(1, LANES),
        norm_in_bias.reshape(1, LANES),
        proj_in,
        gate_in,
        norm_out_gain.reshape(1, LANES),
        norm_out_bias.reshape(1, LANES),
    )
    axes_in, axes_out = "xycz", "xycz"
    ring_in = ring_of(axes_in, grid_rows, grid_cols)
    ring_out = ring_of(axes_out, grid_rows, grid_cols)
    got = lax.all_to_all(sent, tuple(axes_in), 0, 0, tiled=True)
    sums = pl.pallas_call(
        functools.partial(triangle_kernel, ring_in, ring_out, grid_rows, grid_cols, rows, cols),
        out_shape=jax.ShapeDtypeStruct((devices, rows, LANES), BF16),
        in_specs=[VMEM],
        out_specs=VMEM,
        compiler_params=PARAMS,
        name="triangle",
    )(got)
    mine = lax.all_to_all(sums, tuple(axes_out), 0, 0, tiled=True)
    places = [ring_out.index(device) for device in ring_in]
    return pl.pallas_call(
        functools.partial(update_kernel, places),
        out_shape=jax.ShapeDtypeStruct((rows, cols, channels), BF16),
        in_specs=[VMEM] * 7,
        out_specs=HBM,
        scratch_shapes=[
            pltpu.VMEM((rows, cols, channels), BF16),
            pltpu.SemaphoreType.DMA((rows * cols // LANES,)),
        ],
        compiler_params=PARAMS,
        name="update",
    )(mine, order, normed, last_gain, last_bias, proj_out, gate_out)


def solution(mesh):
    grid_rows, grid_cols = mesh.shape["row"], mesh.shape["col"]
    fine = jax.sharding.Mesh(
        mesh.devices.reshape(max(grid_rows // 2, 1), -1, max(grid_cols // 2, 1), min(grid_cols, 2)),
        ("z", "y", "x", "c"),
    )

    def fits(rows, cols, channels, hidden):
        devices = grid_rows * grid_cols
        inner = LANES // cols
        return (
            channels == LANES
            and hidden == LANES
            and inner * cols == LANES
            and inner & (inner - 1) == 0
            and inner * devices == hidden
            and rows == SOME
            and rows % inner == 0
            and devices % SOME == 0
            and grid_rows % 2 == 0
            and grid_cols % 2 == 0
        )

    def call(*arrays):
        tokens, others, channels = arrays[0].shape
        hidden = arrays[8].shape[0]
        if fits(tokens // grid_rows, others // grid_cols, channels, hidden):
            return jax.shard_map(
                functools.partial(exchanged, grid_rows, grid_cols),
                mesh=fine,
                in_specs=(P(("z", "y"), ("x", "c"), None),) + (P(),) * 9,
                out_specs=P(("z", "y"), ("x", "c"), None),
                check_vma=False,
            )(*arrays)
        return jax.shard_map(
            gathered,
            mesh=mesh,
            in_specs=(P("row", "col", None),) + (P(),) * 9,
            out_specs=P("row", "col", None),
            check_vma=False,
        )(*arrays)

    return call
```

```python
import functools
import jax
import jax.numpy as jnp
from jax import lax
from jax.experimental import pallas as pl
from jax.experimental.pallas import tpu as pltpu
from jax.sharding import PartitionSpec as P

LANES = 128
SOME = 16
F32 = jnp.float32
BF16 = jnp.bfloat16


def broadcast(value, axis, source):
    kept = jnp.where(lax.axis_index(axis) == source, value, 0).astype(value.dtype)
    return lax.psum(kept, axis)


def layer_norm(values, gain, bias):
    mean = jnp.mean(values, axis=-1, keepdims=True)
    centered = values - mean
    variance = jnp.mean(centered * centered, axis=-1, keepdims=True)
    return centered * lax.rsqrt(variance + 1e-05) * gain + bias


def token_valid(chain_lengths, tokens_idx, slots):
    chain = tokens_idx // slots
    position = tokens_idx % slots
    chain_ids = jnp.arange(chain_lengths.shape[0], dtype=jnp.int32)
    length_of = jnp.sum(
        jnp.where(chain[:, None] == chain_ids[None, :], chain_lengths[None, :], 0), axis=1
    )
    return (position < length_of).astype(jnp.float32)


def gathered(
    pair,
    chain_lengths,
    norm_in_gain,
    norm_in_bias,
    proj_in,
    gate_in,
    norm_out_gain,
    norm_out_bias,
    proj_out,
    gate_out,
):
    row_count = pair.shape[0]
    col_count = pair.shape[1]
    channels = pair.shape[2]
    hidden = proj_out.shape[0]
    row_index = lax.axis_index("row")
    col_index = lax.axis_index("col")
    slots = row_count * lax.axis_size("row") // chain_lengths.shape[0]
    valid_rows = token_valid(
        chain_lengths, row_index * row_count + jnp.arange(row_count, dtype=jnp.int32), slots
    )
    valid_cols = token_valid(
        chain_lengths, col_index * col_count + jnp.arange(col_count, dtype=jnp.int32), slots
    )
    pair_mask = valid_rows[:, None] * valid_cols[None, :]
    normed = layer_norm(pair.astype(jnp.float32), norm_in_gain, norm_in_bias).astype(jnp.bfloat16)
    flat = normed.reshape(-1, channels)
    values = jnp.dot(flat, proj_in, preferred_element_type=jnp.float32)
    gates = jnp.dot(flat, gate_in, preferred_element_type=jnp.float32)
    mixed = (jax.nn.sigmoid(gates) * values).reshape(row_count, col_count, 2 * hidden) * pair_mask[
        :, :, None
    ]
    left_tile = mixed[:, :, :hidden].astype(jnp.bfloat16)
    right_tile = mixed[:, :, hidden:].astype(jnp.bfloat16)
    ratio = lax.axis_size("row") // lax.axis_size("col")
    right_full = lax.all_gather(right_tile, "col", axis=1, tiled=True)
    received = []
    for part in range(ratio):
        received.append(broadcast(right_full, "row", col_index * ratio + part))
    right_mine = jnp.concatenate(received, axis=0)
    triangle = jnp.einsum(
        "ikh,jkh->ijh",
        lax.all_gather(left_tile, "col", axis=1, tiled=True),
        right_mine,
        preferred_element_type=jnp.float32,
    )
    tri_normed = layer_norm(triangle, norm_out_gain, norm_out_bias).astype(jnp.bfloat16)
    projected = jnp.dot(
        tri_normed.reshape(-1, hidden), proj_out, preferred_element_type=jnp.float32
    )
    gate = jax.nn.sigmoid(jnp.dot(flat, gate_out, preferred_element_type=jnp.float32))
    return (gate * projected).astype(jnp.bfloat16).reshape(row_count, col_count, channels)


def iota2(shape):
    return (
        lax.broadcasted_iota(jnp.int32, shape, 0),
        lax.broadcasted_iota(jnp.int32, shape, 1),
    )


def one_hot(condition):
    return jnp.where(condition, 1.0, 0.0).astype(BF16)


def dot(a, b, a_dim=1, b_dim=0):
    return lax.dot_general(a, b, (((a_dim,), (b_dim,)), ((), ())), preferred_element_type=F32)


def over(value, size):
    if size & (size - 1):
        return value // size
    return lax.shift_right_logical(value, jnp.full_like(value, size.bit_length() - 1))


def rest(value, size):
    return value % size if size & (size - 1) else value & (size - 1)


def over(value, size):
    if size & (size - 1):
        return value // size
    return lax.shift_right_logical(value, jnp.full_like(value, size.bit_length() - 1))


def rest(value, size):
    return value % size if size & (size - 1) else value & (size - 1)


def fetch(sources, targets, sems):
    copies = [
        pltpu.make_async_copy(source, target, sems.at[n])
        for n, (source, target) in enumerate(zip(sources, targets))
    ]
    for copy in copies:
        copy.start()
    return copies


def sigmoid(halved):
    return 0.5 + 0.5 * jnp.tanh(halved)


def exchange_blocks(arrays, cols):
    lane = over(lax.broadcasted_iota(jnp.int32, (1, LANES), 1), cols)
    arrays, step = list(arrays), 1
    while step < len(arrays):
        upper = lane & step != 0
        for n in range(len(arrays)):
            if n // step % 2 == 0:
                a, b = arrays[n], arrays[n + step]
                arrays[n] = jnp.where(upper, pltpu.roll(b, step * cols, 1), a)
                arrays[n + step] = jnp.where(upper, b, pltpu.roll(a, LANES - step * cols, 1))
        step *= 2
    return arrays


def order_kernel(order_ref):
    out, source = iota2(order_ref.shape)
    order_ref[...] = one_hot(
        (over(out, SOME) == rest(source, SOME)) & (rest(out, SOME) == over(source, SOME))
    )


def column(row):
    a, b = iota2((LANES, LANES))
    return jnp.sum(jnp.where(a == b, row, 0.0), axis=1, keepdims=True)


def cell_mask(lengths, slots, rows, cols):
    cell = lax.broadcasted_iota(jnp.int32, (1, rows * cols), 1)

    def valid(token):
        length = jnp.zeros_like(token)
        for chain in range(lengths.shape[1]):
            length = jnp.where(
                over(token, slots) == chain, lengths[:, chain : chain + 1], length
            )
        return rest(token, slots) < length

    row_ok = valid(lax.axis_index(("z", "y")) * rows + over(cell, cols))
    col_ok = valid(lax.axis_index(("x", "c")) * cols + rest(cell, cols))
    return jnp.where(row_ok & col_ok, 1.0, 0.0)


def mix_kernel(
    slots,
    order_ref,
    chain_ref,
    pair_ref,
    gain_ref,
    bias_ref,
    proj_ref,
    gate_ref,
    last_gain_ref,
    last_bias_ref,
    sent_ref,
    normed_ref,
    last_gain_out,
    last_bias_out,
):
    rows, cols, channels = pair_ref.shape
    hidden = proj_ref.shape[1] // 2
    cells = rows * cols
    inner = LANES // cols
    groups = rows // inner
    chunks = sent_ref.shape[0]
    flat = pair_ref[...].reshape(cells, channels).astype(F32)
    normed = layer_norm(flat, gain_ref[...], bias_ref[...]).astype(BF16)
    normed_ref[...] = normed
    for source, target in ((last_gain_ref, last_gain_out), (last_bias_ref, last_bias_out)):
        target[...] = jnp.broadcast_to(column(source[...]), target.shape)

    values = dot(proj_ref[...], normed, 0, 1)
    gates = dot(gate_ref[...] * 0.5, normed, 0, 1)
    mask = cell_mask(chain_ref[...], slots, rows, cols)
    mixed = (sigmoid(gates) * values * mask).astype(BF16)

    by_row = []
    for side in range(2):
        lines = []
        for g in range(groups):
            lines += exchange_blocks(
                [
                    mixed[
                        side * hidden + n * chunks : side * hidden + (n + 1) * chunks,
                        g * LANES : (g + 1) * LANES,
                    ]
                    for n in range(inner)
                ],
                cols,
            )
        by_row.append(lines)
    order = order_ref[...]
    for part in range(chunks // SOME):
        for side in range(2):
            stack = jnp.concatenate(
                [line[part * SOME : (part + 1) * SOME] for line in by_row[side]], axis=0
            )
            sent_ref[part * SOME : (part + 1) * SOME, side * rows : (side + 1) * rows] = (
                dot(order, stack).astype(BF16).reshape(SOME, rows, LANES)
            )


def triangle_kernel(ring_in, ring_out, grid_rows, grid_cols, rows, cols, got_ref, sent_ref):
    inner = LANES // cols

    def place(ring, r, c):
        return ring.index(r * grid_cols + c)

    def side(which):
        return jnp.concatenate(
            [
                jnp.concatenate(
                    [
                        got_ref[place(ring_in, r, c), which * rows : (which + 1) * rows]
                        for r in range(grid_rows)
                    ],
                    axis=0,
                )
                for c in range(grid_cols)
            ],
            axis=1,
        )

    left, right = side(0), side(1)
    lane = lax.broadcasted_iota(jnp.int32, (1, grid_cols * LANES), 1)
    by_channel = [right * one_hot(over(rest(lane, LANES), cols) == n) for n in range(inner)]
    right_by = jnp.concatenate(
        [
            by_channel[n][c * cols : (c + 1) * cols]
            for c in range(grid_cols)
            for n in range(inner)
        ],
        axis=0,
    )
    sums = dot(left, right_by, 1, 1).astype(BF16)
    for c in range(grid_cols):
        for r in range(grid_rows):
            sent_ref[place(ring_out, r, c)] = sums[r * rows : (r + 1) * rows, c * LANES : (c + 1) * LANES]


def update_kernel(
    places,
    got_ref,
    order_ref,
    normed_ref,
    gain_ref,
    bias_ref,
    proj_ref,
    gate_ref,
    out_hbm,
    out_ref,
    out_sems,
):
    rows, cols, channels = out_ref.shape
    chunks = got_ref.shape[0]
    inner = LANES // cols
    groups = rows // inner
    order = order_ref[...]
    parts = [
        dot(
            order,
            jnp.concatenate(
                [got_ref[place] for place in places[part * SOME : (part + 1) * SOME]], axis=0
            ),
        ).astype(BF16)
        for part in range(chunks // SOME)
    ]
    lines = [
        jnp.concatenate([part[row * SOME : (row + 1) * SOME] for part in parts], axis=0)
        for row in range(rows)
    ]
    gain, bias = gain_ref[...], bias_ref[...]
    opened = sigmoid(dot(normed_ref[...], gate_ref[...] * 0.5))
    results = []
    for g in range(groups):
        values = jnp.concatenate(
            exchange_blocks(lines[g * inner : (g + 1) * inner], cols), axis=0
        ).astype(F32)
        mean = jnp.mean(values, axis=0, keepdims=True)
        centered = values - mean
        variance = jnp.mean(centered * centered, axis=0, keepdims=True)
        tri_normed = (centered * lax.rsqrt(variance + 1e-05) * gain + bias).astype(BF16)
        projected = dot(tri_normed, proj_ref[...], 0, 0)
        update = (opened[g * LANES : (g + 1) * LANES] * projected).astype(BF16)
        here = pl.ds(g * inner, inner)
        out_ref[here] = update.reshape(inner, cols, channels)
        results.append(pltpu.make_async_copy(out_ref.at[here], out_hbm.at[here], out_sems.at[g]))
        results[-1].start()
    for copy in results:
        copy.wait()


VMEM = pl.BlockSpec(memory_space=pltpu.VMEM)
HBM = pl.BlockSpec(memory_space=pltpu.HBM)
PARAMS = pltpu.CompilerParams(vmem_limit_bytes=32 * 1024 * 1024)


def ring_of(axes, grid_rows, grid_cols):
    sizes = {"z": grid_rows // 2, "y": 2, "x": grid_cols // 2, "c": 2}
    strides = {"z": 2 * grid_cols, "y": grid_cols, "x": 2, "c": 1}
    ring = [0]
    for axis in axes:
        ring = [device + n * strides[axis] for device in ring for n in range(sizes[axis])]
    return ring


def exchanged(
    grid_rows,
    grid_cols,
    pair,
    chain_lengths,
    norm_in_gain,
    norm_in_bias,
    proj_in,
    gate_in,
    norm_out_gain,
    norm_out_bias,
    proj_out,
    gate_out,
):
    rows, cols, channels = pair.shape
    hidden = proj_out.shape[0]
    devices = grid_rows * grid_cols
    slots = rows * grid_rows // chain_lengths.shape[0]
    order = pl.pallas_call(
        order_kernel,
        out_shape=jax.ShapeDtypeStruct((SOME * SOME, SOME * SOME), BF16),
        out_specs=VMEM,
        compiler_params=PARAMS,
        cost_estimate=pl.CostEstimate(flops=10**9, bytes_accessed=10**6, transcendentals=0),
        name="order",
    )()
    square = jax.ShapeDtypeStruct((LANES, LANES), F32)
    sent, normed, last_gain, last_bias = pl.pallas_call(
        functools.partial(mix_kernel, slots),
        out_shape=(
            jax.ShapeDtypeStruct((devices, 2 * rows, LANES), BF16),
            jax.ShapeDtypeStruct((rows * cols, channels), BF16),
            square,
            square,
        ),
        in_specs=[VMEM] * 9,
        out_specs=[VMEM] * 4,
        compiler_params=PARAMS,
        name="mix",
    )(
        order,
        chain_lengths.reshape(1, -1),
        pair,
        norm_in_gain.reshape(1, LANES),
        norm_in_bias.reshape(1, LANES),
        proj_in,
        gate_in,
        norm_out_gain.reshape(1, LANES),
        norm_out_bias.reshape(1, LANES),
    )
    axes_in, axes_out = "cyxz", "cyxz"
    ring_in = ring_of(axes_in, grid_rows, grid_cols)
    ring_out = ring_of(axes_out, grid_rows, grid_cols)
    got = lax.all_to_all(sent, tuple(axes_in), 0, 0, tiled=True)
    sums = pl.pallas_call(
        functools.partial(triangle_kernel, ring_in, ring_out, grid_rows, grid_cols, rows, cols),
        out_shape=jax.ShapeDtypeStruct((devices, rows, LANES), BF16),
        in_specs=[VMEM],
        out_specs=VMEM,
        compiler_params=PARAMS,
        name="triangle",
    )(got)
    mine = lax.all_to_all(sums, tuple(axes_out), 0, 0, tiled=True)
    places = [ring_out.index(device) for device in ring_in]
    return pl.pallas_call(
        functools.partial(update_kernel, places),
        out_shape=jax.ShapeDtypeStruct((rows, cols, channels), BF16),
        in_specs=[VMEM] * 7,
        out_specs=HBM,
        scratch_shapes=[
            pltpu.VMEM((rows, cols, channels), BF16),
            pltpu.SemaphoreType.DMA((rows * cols // LANES,)),
        ],
        compiler_params=PARAMS,
        name="update",
    )(mine, order, normed, last_gain, last_bias, proj_out, gate_out)


def solution(mesh):
    grid_rows, grid_cols = mesh.shape["row"], mesh.shape["col"]
    fine = jax.sharding.Mesh(
        mesh.devices.reshape(max(grid_rows // 2, 1), -1, max(grid_cols // 2, 1), min(grid_cols, 2)),
        ("z", "y", "x", "c"),
    )

    def fits(rows, cols, channels, hidden):
        devices = grid_rows * grid_cols
        inner = LANES // cols
        return (
            channels == LANES
            and hidden == LANES
            and inner * cols == LANES
            and inner & (inner - 1) == 0
            and inner * devices == hidden
            and rows == SOME
            and rows % inner == 0
            and devices % SOME == 0
            and grid_rows % 2 == 0
            and grid_cols % 2 == 0
        )

    def call(*arrays):
        tokens, others, channels = arrays[0].shape
        hidden = arrays[8].shape[0]
        if fits(tokens // grid_rows, others // grid_cols, channels, hidden):
            return jax.shard_map(
                functools.partial(exchanged, grid_rows, grid_cols),
                mesh=fine,
                in_specs=(P(("z", "y"), ("x", "c"), None),) + (P(),) * 9,
                out_specs=P(("z", "y"), ("x", "c"), None),
                check_vma=False,
            )(*arrays)
        return jax.shard_map(
            gathered,
            mesh=mesh,
            in_specs=(P("row", "col", None),) + (P(),) * 9,
            out_specs=P("row", "col", None),
            check_vma=False,
        )(*arrays)

    return call
```

```python
import functools
import jax
import jax.numpy as jnp
from jax import lax
from jax.experimental import pallas as pl
from jax.experimental.pallas import tpu as pltpu
from jax.sharding import PartitionSpec as P

LANES = 128
SOME = 16
F32 = jnp.float32
BF16 = jnp.bfloat16


def broadcast(value, axis, source):
    kept = jnp.where(lax.axis_index(axis) == source, value, 0).astype(value.dtype)
    return lax.psum(kept, axis)


def layer_norm(values, gain, bias):
    mean = jnp.mean(values, axis=-1, keepdims=True)
    centered = values - mean
    variance = jnp.mean(centered * centered, axis=-1, keepdims=True)
    return centered * lax.rsqrt(variance + 1e-05) * gain + bias


def token_valid(chain_lengths, tokens_idx, slots):
    chain = tokens_idx // slots
    position = tokens_idx % slots
    chain_ids = jnp.arange(chain_lengths.shape[0], dtype=jnp.int32)
    length_of = jnp.sum(
        jnp.where(chain[:, None] == chain_ids[None, :], chain_lengths[None, :], 0), axis=1
    )
    return (position < length_of).astype(jnp.float32)


def gathered(
    pair,
    chain_lengths,
    norm_in_gain,
    norm_in_bias,
    proj_in,
    gate_in,
    norm_out_gain,
    norm_out_bias,
    proj_out,
    gate_out,
):
    row_count = pair.shape[0]
    col_count = pair.shape[1]
    channels = pair.shape[2]
    hidden = proj_out.shape[0]
    row_index = lax.axis_index("row")
    col_index = lax.axis_index("col")
    slots = row_count * lax.axis_size("row") // chain_lengths.shape[0]
    valid_rows = token_valid(
        chain_lengths, row_index * row_count + jnp.arange(row_count, dtype=jnp.int32), slots
    )
    valid_cols = token_valid(
        chain_lengths, col_index * col_count + jnp.arange(col_count, dtype=jnp.int32), slots
    )
    pair_mask = valid_rows[:, None] * valid_cols[None, :]
    normed = layer_norm(pair.astype(jnp.float32), norm_in_gain, norm_in_bias).astype(jnp.bfloat16)
    flat = normed.reshape(-1, channels)
    values = jnp.dot(flat, proj_in, preferred_element_type=jnp.float32)
    gates = jnp.dot(flat, gate_in, preferred_element_type=jnp.float32)
    mixed = (jax.nn.sigmoid(gates) * values).reshape(row_count, col_count, 2 * hidden) * pair_mask[
        :, :, None
    ]
    left_tile = mixed[:, :, :hidden].astype(jnp.bfloat16)
    right_tile = mixed[:, :, hidden:].astype(jnp.bfloat16)
    ratio = lax.axis_size("row") // lax.axis_size("col")
    right_full = lax.all_gather(right_tile, "col", axis=1, tiled=True)
    received = []
    for part in range(ratio):
        received.append(broadcast(right_full, "row", col_index * ratio + part))
    right_mine = jnp.concatenate(received, axis=0)
    triangle = jnp.einsum(
        "ikh,jkh->ijh",
        lax.all_gather(left_tile, "col", axis=1, tiled=True),
        right_mine,
        preferred_element_type=jnp.float32,
    )
    tri_normed = layer_norm(triangle, norm_out_gain, norm_out_bias).astype(jnp.bfloat16)
    projected = jnp.dot(
        tri_normed.reshape(-1, hidden), proj_out, preferred_element_type=jnp.float32
    )
    gate = jax.nn.sigmoid(jnp.dot(flat, gate_out, preferred_element_type=jnp.float32))
    return (gate * projected).astype(jnp.bfloat16).reshape(row_count, col_count, channels)


def iota2(shape):
    return (
        lax.broadcasted_iota(jnp.int32, shape, 0),
        lax.broadcasted_iota(jnp.int32, shape, 1),
    )


def one_hot(condition):
    return jnp.where(condition, 1.0, 0.0).astype(BF16)


def dot(a, b, a_dim=1, b_dim=0):
    return lax.dot_general(a, b, (((a_dim,), (b_dim,)), ((), ())), preferred_element_type=F32)


def over(value, size):
    if size & (size - 1):
        return value // size
    return lax.shift_right_logical(value, jnp.full_like(value, size.bit_length() - 1))


def rest(value, size):
    return value % size if size & (size - 1) else value & (size - 1)


def over(value, size):
    if size & (size - 1):
        return value // size
    return lax.shift_right_logical(value, jnp.full_like(value, size.bit_length() - 1))


def rest(value, size):
    return value % size if size & (size - 1) else value & (size - 1)


def fetch(sources, targets, sems):
    copies = [
        pltpu.make_async_copy(source, target, sems.at[n])
        for n, (source, target) in enumerate(zip(sources, targets))
    ]
    for copy in copies:
        copy.start()
    return copies


def sigmoid(halved):
    return 0.5 + 0.5 * jnp.tanh(halved)


def exchange_blocks(arrays, cols):
    lane = over(lax.broadcasted_iota(jnp.int32, (1, LANES), 1), cols)
    arrays, step = list(arrays), 1
    while step < len(arrays):
        upper = lane & step != 0
        for n in range(len(arrays)):
            if n // step % 2 == 0:
                a, b = arrays[n], arrays[n + step]
                arrays[n] = jnp.where(upper, pltpu.roll(b, step * cols, 1), a)
                arrays[n + step] = jnp.where(upper, b, pltpu.roll(a, LANES - step * cols, 1))
        step *= 2
    return arrays


def order_kernel(order_ref):
    out, source = iota2(order_ref.shape)
    order_ref[...] = one_hot(
        (over(out, SOME) == rest(source, SOME)) & (rest(out, SOME) == over(source, SOME))
    )


def column(row):
    a, b = iota2((LANES, LANES))
    return jnp.sum(jnp.where(a == b, row, 0.0), axis=1, keepdims=True)


def cell_mask(lengths, slots, rows, cols):
    cell = lax.broadcasted_iota(jnp.int32, (1, rows * cols), 1)

    def valid(token):
        length = jnp.zeros_like(token)
        for chain in range(lengths.shape[1]):
            length = jnp.where(
                over(token, slots) == chain, lengths[:, chain : chain + 1], length
            )
        return rest(token, slots) < length

    row_ok = valid(lax.axis_index(("high", "low")) * rows + over(cell, cols))
    col_ok = valid(lax.axis_index("col") * cols + rest(cell, cols))
    return jnp.where(row_ok & col_ok, 1.0, 0.0)


def mix_kernel(
    slots,
    order_ref,
    chain_ref,
    gain_ref,
    bias_ref,
    last_gain_ref,
    last_bias_ref,
    proj_ref,
    gate_ref,
    pair_ref,
    sent_ref,
    normed_ref,
    last_gain_out,
    last_bias_out,
):
    rows, cols, channels = pair_ref.shape
    hidden = proj_ref.shape[1] // 2
    cells = rows * cols
    inner = LANES // cols
    groups = rows // inner
    chunks = sent_ref.shape[0]
    flat = pair_ref[...].reshape(cells, channels).astype(F32)
    normed = layer_norm(flat, gain_ref[...], bias_ref[...]).astype(BF16)
    normed_ref[...] = normed
    last_gain_out[...] = last_gain_ref[...]
    last_bias_out[...] = last_bias_ref[...]
    weights = jnp.concatenate([proj_ref[...], gate_ref[...] * 0.5], axis=1)
    products = dot(weights, normed, 0, 1)
    values, gates = products[: 2 * hidden], products[2 * hidden :]
    mask = cell_mask(chain_ref[...], slots, rows, cols)
    mixed = (sigmoid(gates) * values * mask).astype(BF16)

    by_row = []
    for side in range(2):
        lines = []
        for g in range(groups):
            lines += exchange_blocks(
                [
                    mixed[
                        side * hidden + n * chunks : side * hidden + (n + 1) * chunks,
                        g * LANES : (g + 1) * LANES,
                    ]
                    for n in range(inner)
                ],
                cols,
            )
        by_row.append(lines)
    order = order_ref[...]
    for part in range(chunks // SOME):
        for side in range(2):
            stack = jnp.concatenate(
                [line[part * SOME : (part + 1) * SOME] for line in by_row[side]], axis=0
            )
            sent_ref[part * SOME : (part + 1) * SOME, side * rows : (side + 1) * rows] = (
                dot(order, stack).astype(BF16).reshape(SOME, rows, LANES)
            )


def triangle_kernel(split, grid_cols, rows, cols, got_ref, sent_ref):
    inner = LANES // cols

    def place(r, c):
        z, y = r // split[1], r % split[1]
        return (c * split[1] + y) * split[0] + z

    def side(which):
        return jnp.concatenate(
            [
                jnp.concatenate(
                    [
                        got_ref[place(r, c), which * rows : (which + 1) * rows]
                        for r in range(split[0] * split[1])
                    ],
                    axis=0,
                )
                for c in range(grid_cols)
            ],
            axis=1,
        )

    left, right = side(0), side(1)
    lane = lax.broadcasted_iota(jnp.int32, (1, grid_cols * LANES), 1)
    by_channel = [right * one_hot(over(rest(lane, LANES), cols) == n) for n in range(inner)]
    right_by = jnp.concatenate(
        [
            by_channel[n][c * cols : (c + 1) * cols]
            for c in range(grid_cols)
            for n in range(inner)
        ],
        axis=0,
    )
    sums = dot(left, right_by, 1, 1).astype(BF16)
    for c in range(grid_cols):
        for r in range(split[0] * split[1]):
            sent_ref[place(r, c)] = sums[r * rows : (r + 1) * rows, c * LANES : (c + 1) * LANES]


def update_kernel(
    got_ref,
    order_ref,
    normed_ref,
    gain_ref,
    bias_ref,
    proj_ref,
    gate_ref,
    out_hbm,
    out_ref,
    out_sems,
):
    rows, cols, channels = out_ref.shape
    chunks = got_ref.shape[0]
    inner = LANES // cols
    groups = rows // inner
    order = order_ref[...]
    parts = [
        dot(order, got_ref[part * SOME : (part + 1) * SOME].reshape(SOME * rows, LANES)).astype(BF16)
        for part in range(chunks // SOME)
    ]
    lines = [
        jnp.concatenate([part[row * SOME : (row + 1) * SOME] for part in parts], axis=0)
        for row in range(rows)
    ]
    gain, bias = column(gain_ref[...]), column(bias_ref[...])
    opened = sigmoid(dot(normed_ref[...], gate_ref[...] * 0.5))
    results = []
    for g in range(groups):
        values = jnp.concatenate(
            exchange_blocks(lines[g * inner : (g + 1) * inner], cols), axis=0
        ).astype(F32)
        mean = jnp.mean(values, axis=0, keepdims=True)
        centered = values - mean
        variance = jnp.mean(centered * centered, axis=0, keepdims=True)
        tri_normed = (centered * lax.rsqrt(variance + 1e-05) * gain + bias).astype(BF16)
        projected = dot(tri_normed, proj_ref[...], 0, 0)
        update = (opened[g * LANES : (g + 1) * LANES] * projected).astype(BF16)
        out_ref[g * inner : (g + 1) * inner] = update.reshape(inner, cols, channels)
        if g % 2:
            here = pl.ds((g - 1) * inner, 2 * inner)
            results.append(
                pltpu.make_async_copy(out_ref.at[here], out_hbm.at[here], out_sems.at[g // 2])
            )
            results[-1].start()
    for copy in results:
        copy.wait()


VMEM = pl.BlockSpec(memory_space=pltpu.VMEM)
HBM = pl.BlockSpec(memory_space=pltpu.HBM)
PARAMS = pltpu.CompilerParams(vmem_limit_bytes=32 * 1024 * 1024)


def exchanged(
    split,
    grid_cols,
    pair,
    chain_lengths,
    norm_in_gain,
    norm_in_bias,
    proj_in,
    gate_in,
    norm_out_gain,
    norm_out_bias,
    proj_out,
    gate_out,
):
    rows, cols, channels = pair.shape
    hidden = proj_out.shape[0]
    grid_rows = split[0] * split[1]
    devices = grid_rows * grid_cols
    slots = rows * grid_rows // chain_lengths.shape[0]
    order = pl.pallas_call(
        order_kernel,
        out_shape=jax.ShapeDtypeStruct((SOME * SOME, SOME * SOME), BF16),
        out_specs=VMEM,
        compiler_params=PARAMS,
        cost_estimate=pl.CostEstimate(flops=10**9, bytes_accessed=10**6, transcendentals=0),
        name="order",
    )()
    row = jax.ShapeDtypeStruct((1, LANES), F32)
    sent, normed, last_gain, last_bias = pl.pallas_call(
        functools.partial(mix_kernel, slots),
        out_shape=(
            jax.ShapeDtypeStruct((devices, 2 * rows, LANES), BF16),
            jax.ShapeDtypeStruct((rows * cols, channels), BF16),
            row,
            row,
        ),
        in_specs=[VMEM] * 9,
        out_specs=[VMEM] * 4,
        compiler_params=PARAMS,
        name="mix",
    )(
        order,
        chain_lengths.reshape(1, -1),
        norm_in_gain.reshape(1, LANES),
        norm_in_bias.reshape(1, LANES),
        norm_out_gain.reshape(1, LANES),
        norm_out_bias.reshape(1, LANES),
        proj_in,
        gate_in,
        pair,
    )
    axes = ("col", "low", "high")
    got = lax.all_to_all(sent, axes, 0, 0, tiled=True)
    sums = pl.pallas_call(
        functools.partial(triangle_kernel, split, grid_cols, rows, cols),
        out_shape=jax.ShapeDtypeStruct((devices, rows, LANES), BF16),
        in_specs=[VMEM],
        out_specs=VMEM,
        compiler_params=PARAMS,
        name="triangle",
    )(got)
    mine = lax.all_to_all(sums, axes, 0, 0, tiled=True)
    return pl.pallas_call(
        update_kernel,
        out_shape=jax.ShapeDtypeStruct((rows, cols, channels), BF16),
        in_specs=[VMEM] * 7,
        out_specs=HBM,
        scratch_shapes=[
            pltpu.VMEM((rows, cols, channels), BF16),
            pltpu.SemaphoreType.DMA((rows * cols // LANES // 2,)),
        ],
        compiler_params=PARAMS,
        name="update",
    )(mine, order, normed, last_gain, last_bias, proj_out, gate_out)


def solution(mesh):
    grid_rows, grid_cols = mesh.shape["row"], mesh.shape["col"]
    split = (grid_rows // 2, 2)
    fine = jax.sharding.Mesh(
        mesh.devices.reshape(split + (grid_cols,)), ("high", "low", "col")
    )

    def fits(rows, cols, channels, hidden):
        devices = grid_rows * grid_cols
        inner = LANES // cols
        return (
            channels == LANES
            and hidden == LANES
            and inner * cols == LANES
            and inner & (inner - 1) == 0
            and inner * devices == hidden
            and rows == SOME
            and rows % (2 * inner) == 0
            and devices % SOME == 0
        )

    def call(*arrays):
        tokens, others, channels = arrays[0].shape
        hidden = arrays[8].shape[0]
        if fits(tokens // grid_rows, others // grid_cols, channels, hidden):
            return jax.shard_map(
                functools.partial(exchanged, split, grid_cols),
                mesh=fine,
                in_specs=(P(("high", "low"), "col", None),) + (P(),) * 9,
                out_specs=P(("high", "low"), "col", None),
                check_vma=False,
            )(*arrays)
        return jax.shard_map(
            gathered,
            mesh=mesh,
            in_specs=(P("row", "col", None),) + (P(),) * 9,
            out_specs=P("row", "col", None),
            check_vma=False,
        )(*arrays)

    return call
```

```python
import functools
import jax
import jax.numpy as jnp
from jax import lax
from jax.experimental import pallas as pl
from jax.experimental.pallas import tpu as pltpu
from jax.sharding import PartitionSpec as P

LANES = 128
SOME = 16
F32 = jnp.float32
BF16 = jnp.bfloat16


def broadcast(value, axis, source):
    kept = jnp.where(lax.axis_index(axis) == source, value, 0).astype(value.dtype)
    return lax.psum(kept, axis)


def layer_norm(values, gain, bias):
    mean = jnp.mean(values, axis=-1, keepdims=True)
    centered = values - mean
    variance = jnp.mean(centered * centered, axis=-1, keepdims=True)
    return centered * lax.rsqrt(variance + 1e-05) * gain + bias


def token_valid(chain_lengths, tokens_idx, slots):
    chain = tokens_idx // slots
    position = tokens_idx % slots
    chain_ids = jnp.arange(chain_lengths.shape[0], dtype=jnp.int32)
    length_of = jnp.sum(
        jnp.where(chain[:, None] == chain_ids[None, :], chain_lengths[None, :], 0), axis=1
    )
    return (position < length_of).astype(jnp.float32)


def gathered(
    pair,
    chain_lengths,
    norm_in_gain,
    norm_in_bias,
    proj_in,
    gate_in,
    norm_out_gain,
    norm_out_bias,
    proj_out,
    gate_out,
):
    row_count = pair.shape[0]
    col_count = pair.shape[1]
    channels = pair.shape[2]
    hidden = proj_out.shape[0]
    row_index = lax.axis_index("row")
    col_index = lax.axis_index("col")
    slots = row_count * lax.axis_size("row") // chain_lengths.shape[0]
    valid_rows = token_valid(
        chain_lengths, row_index * row_count + jnp.arange(row_count, dtype=jnp.int32), slots
    )
    valid_cols = token_valid(
        chain_lengths, col_index * col_count + jnp.arange(col_count, dtype=jnp.int32), slots
    )
    pair_mask = valid_rows[:, None] * valid_cols[None, :]
    normed = layer_norm(pair.astype(jnp.float32), norm_in_gain, norm_in_bias).astype(jnp.bfloat16)
    flat = normed.reshape(-1, channels)
    values = jnp.dot(flat, proj_in, preferred_element_type=jnp.float32)
    gates = jnp.dot(flat, gate_in, preferred_element_type=jnp.float32)
    mixed = (jax.nn.sigmoid(gates) * values).reshape(row_count, col_count, 2 * hidden) * pair_mask[
        :, :, None
    ]
    left_tile = mixed[:, :, :hidden].astype(jnp.bfloat16)
    right_tile = mixed[:, :, hidden:].astype(jnp.bfloat16)
    ratio = lax.axis_size("row") // lax.axis_size("col")
    right_full = lax.all_gather(right_tile, "col", axis=1, tiled=True)
    received = []
    for part in range(ratio):
        received.append(broadcast(right_full, "row", col_index * ratio + part))
    right_mine = jnp.concatenate(received, axis=0)
    triangle = jnp.einsum(
        "ikh,jkh->ijh",
        lax.all_gather(left_tile, "col", axis=1, tiled=True),
        right_mine,
        preferred_element_type=jnp.float32,
    )
    tri_normed = layer_norm(triangle, norm_out_gain, norm_out_bias).astype(jnp.bfloat16)
    projected = jnp.dot(
        tri_normed.reshape(-1, hidden), proj_out, preferred_element_type=jnp.float32
    )
    gate = jax.nn.sigmoid(jnp.dot(flat, gate_out, preferred_element_type=jnp.float32))
    return (gate * projected).astype(jnp.bfloat16).reshape(row_count, col_count, channels)


def iota2(shape):
    return (
        lax.broadcasted_iota(jnp.int32, shape, 0),
        lax.broadcasted_iota(jnp.int32, shape, 1),
    )


def one_hot(condition):
    return jnp.where(condition, 1.0, 0.0).astype(BF16)


def dot(a, b, a_dim=1, b_dim=0):
    return lax.dot_general(a, b, (((a_dim,), (b_dim,)), ((), ())), preferred_element_type=F32)


def over(value, size):
    if size & (size - 1):
        return value // size
    return lax.shift_right_logical(value, jnp.full_like(value, size.bit_length() - 1))


def rest(value, size):
    return value % size if size & (size - 1) else value & (size - 1)


def over(value, size):
    if size & (size - 1):
        return value // size
    return lax.shift_right_logical(value, jnp.full_like(value, size.bit_length() - 1))


def rest(value, size):
    return value % size if size & (size - 1) else value & (size - 1)


def fetch(sources, targets, sems):
    copies = [
        pltpu.make_async_copy(source, target, sems.at[n])
        for n, (source, target) in enumerate(zip(sources, targets))
    ]
    for copy in copies:
        copy.start()
    return copies


def sigmoid(halved):
    return 0.5 + 0.5 * jnp.tanh(halved)


def exchange_blocks(arrays, cols):
    lane = over(lax.broadcasted_iota(jnp.int32, (1, LANES), 1), cols)
    arrays, step = list(arrays), 1
    while step < len(arrays):
        upper = lane & step != 0
        for n in range(len(arrays)):
            if n // step % 2 == 0:
                a, b = arrays[n], arrays[n + step]
                arrays[n] = jnp.where(upper, pltpu.roll(b, step * cols, 1), a)
                arrays[n + step] = jnp.where(upper, b, pltpu.roll(a, LANES - step * cols, 1))
        step *= 2
    return arrays


def order_kernel(order_ref):
    out, source = iota2(order_ref.shape)
    order_ref[...] = one_hot(
        (over(out, SOME) == rest(source, SOME)) & (rest(out, SOME) == over(source, SOME))
    )


def column(row):
    a, b = iota2((LANES, LANES))
    return jnp.sum(jnp.where(a == b, row, 0.0), axis=1, keepdims=True)


def cell_mask(lengths, slots, rows, cols):
    cell = lax.broadcasted_iota(jnp.int32, (1, rows * cols), 1)

    def valid(token):
        length = jnp.zeros_like(token)
        for chain in range(lengths.shape[1]):
            length = jnp.where(
                over(token, slots) == chain, lengths[:, chain : chain + 1], length
            )
        return rest(token, slots) < length

    row_ok = valid(lax.axis_index(("high", "low")) * rows + over(cell, cols))
    col_ok = valid(lax.axis_index("col") * cols + rest(cell, cols))
    return jnp.where(row_ok & col_ok, 1.0, 0.0)


def mix_kernel(
    slots,
    order_ref,
    chain_ref,
    gain_ref,
    bias_ref,
    last_gain_ref,
    last_bias_ref,
    proj_ref,
    gate_ref,
    pair_ref,
    sent_ref,
    normed_ref,
    last_gain_out,
    last_bias_out,
):
    rows, cols, channels = pair_ref.shape
    hidden = proj_ref.shape[1] // 2
    cells = rows * cols
    inner = LANES // cols
    groups = rows // inner
    chunks = sent_ref.shape[0]
    flat = pair_ref[...].reshape(cells, channels).astype(F32)
    normed = layer_norm(flat, gain_ref[...], bias_ref[...]).astype(BF16)
    normed_ref[...] = normed
    last_gain_out[...] = last_gain_ref[...]
    last_bias_out[...] = last_bias_ref[...]
    mask = cell_mask(chain_ref[...], slots, rows, cols)
    order = order_ref[...]
    for side in range(2):
        own = slice(side * hidden, (side + 1) * hidden)
        values = dot(proj_ref[:, own], normed, 0, 1)
        gates = dot(gate_ref[:, own] * 0.5, normed, 0, 1)
        mixed = (sigmoid(gates) * values * mask).astype(BF16)
        lines = []
        for g in range(groups):
            lines += exchange_blocks(
                [
                    mixed[n * chunks : (n + 1) * chunks, g * LANES : (g + 1) * LANES]
                    for n in range(inner)
                ],
                cols,
            )
        for part in range(chunks // SOME):
            stack = jnp.concatenate(
                [line[part * SOME : (part + 1) * SOME] for line in lines], axis=0
            )
            sent_ref[part * SOME : (part + 1) * SOME, side * rows : (side + 1) * rows] = (
                dot(order, stack).astype(BF16).reshape(SOME, rows, LANES)
            )


def triangle_kernel(split, grid_cols, rows, cols, got_ref, sent_ref):
    inner = LANES // cols

    def place(r, c):
        z, y = r // split[1], r % split[1]
        return (c * split[1] + y) * split[0] + z

    def side(which):
        return jnp.concatenate(
            [
                jnp.concatenate(
                    [
                        got_ref[place(r, c), which * rows : (which + 1) * rows]
                        for r in range(split[0] * split[1])
                    ],
                    axis=0,
                )
                for c in range(grid_cols)
            ],
            axis=1,
        )

    left, right = side(0), side(1)
    lane = lax.broadcasted_iota(jnp.int32, (1, grid_cols * LANES), 1)
    by_channel = [right * one_hot(over(rest(lane, LANES), cols) == n) for n in range(inner)]
    right_by = jnp.concatenate(
        [
            by_channel[n][c * cols : (c + 1) * cols]
            for c in range(grid_cols)
            for n in range(inner)
        ],
        axis=0,
    )
    sums = dot(left, right_by, 1, 1).astype(BF16)
    for c in range(grid_cols):
        for r in range(split[0] * split[1]):
            sent_ref[place(r, c)] = sums[r * rows : (r + 1) * rows, c * LANES : (c + 1) * LANES]


def update_kernel(
    got_ref,
    order_ref,
    normed_ref,
    gain_ref,
    bias_ref,
    proj_ref,
    gate_ref,
    out_hbm,
    out_ref,
    out_sems,
):
    rows, cols, channels = out_ref.shape
    chunks = got_ref.shape[0]
    inner = LANES // cols
    groups = rows // inner
    order = order_ref[...]
    parts = [
        dot(order, got_ref[part * SOME : (part + 1) * SOME].reshape(SOME * rows, LANES)).astype(BF16)
        for part in range(chunks // SOME)
    ]
    lines = [
        jnp.concatenate([part[row * SOME : (row + 1) * SOME] for part in parts], axis=0)
        for row in range(rows)
    ]
    gain, bias = column(gain_ref[...]), column(bias_ref[...])
    opened = sigmoid(dot(normed_ref[...], gate_ref[...] * 0.5))
    results = []
    for g in range(groups):
        values = jnp.concatenate(
            exchange_blocks(lines[g * inner : (g + 1) * inner], cols), axis=0
        ).astype(F32)
        mean = jnp.mean(values, axis=0, keepdims=True)
        centered = values - mean
        variance = jnp.mean(centered * centered, axis=0, keepdims=True)
        tri_normed = (centered * lax.rsqrt(variance + 1e-05) * gain + bias).astype(BF16)
        projected = dot(tri_normed, proj_ref[...], 0, 0)
        update = (opened[g * LANES : (g + 1) * LANES] * projected).astype(BF16)
        out_ref[g * inner : (g + 1) * inner] = update.reshape(inner, cols, channels)
        if g % 2:
            here = pl.ds((g - 1) * inner, 2 * inner)
            results.append(
                pltpu.make_async_copy(out_ref.at[here], out_hbm.at[here], out_sems.at[g // 2])
            )
            results[-1].start()
    for copy in results:
        copy.wait()


VMEM = pl.BlockSpec(memory_space=pltpu.VMEM)
HBM = pl.BlockSpec(memory_space=pltpu.HBM)
PARAMS = pltpu.CompilerParams(vmem_limit_bytes=32 * 1024 * 1024)


def exchanged(
    split,
    grid_cols,
    pair,
    chain_lengths,
    norm_in_gain,
    norm_in_bias,
    proj_in,
    gate_in,
    norm_out_gain,
    norm_out_bias,
    proj_out,
    gate_out,
):
    rows, cols, channels = pair.shape
    hidden = proj_out.shape[0]
    grid_rows = split[0] * split[1]
    devices = grid_rows * grid_cols
    slots = rows * grid_rows // chain_lengths.shape[0]
    order = pl.pallas_call(
        order_kernel,
        out_shape=jax.ShapeDtypeStruct((SOME * SOME, SOME * SOME), BF16),
        out_specs=VMEM,
        compiler_params=PARAMS,
        cost_estimate=pl.CostEstimate(flops=10**9, bytes_accessed=10**6, transcendentals=0),
        name="order",
    )()
    row = jax.ShapeDtypeStruct((1, LANES), F32)
    sent, normed, last_gain, last_bias = pl.pallas_call(
        functools.partial(mix_kernel, slots),
        out_shape=(
            jax.ShapeDtypeStruct((devices, 2 * rows, LANES), BF16),
            jax.ShapeDtypeStruct((rows * cols, channels), BF16),
            row,
            row,
        ),
        in_specs=[VMEM] * 9,
        out_specs=[VMEM] * 4,
        compiler_params=PARAMS,
        name="mix",
    )(
        order,
        chain_lengths.reshape(1, -1),
        norm_in_gain.reshape(1, LANES),
        norm_in_bias.reshape(1, LANES),
        norm_out_gain.reshape(1, LANES),
        norm_out_bias.reshape(1, LANES),
        proj_in,
        gate_in,
        pair,
    )
    axes = ("col", "low", "high")
    got = lax.all_to_all(sent, axes, 0, 0, tiled=True)
    sums = pl.pallas_call(
        functools.partial(triangle_kernel, split, grid_cols, rows, cols),
        out_shape=jax.ShapeDtypeStruct((devices, rows, LANES), BF16),
        in_specs=[VMEM],
        out_specs=VMEM,
        compiler_params=PARAMS,
        name="triangle",
    )(got)
    mine = lax.all_to_all(sums, axes, 0, 0, tiled=True)
    return pl.pallas_call(
        update_kernel,
        out_shape=jax.ShapeDtypeStruct((rows, cols, channels), BF16),
        in_specs=[VMEM] * 7,
        out_specs=HBM,
        scratch_shapes=[
            pltpu.VMEM((rows, cols, channels), BF16),
            pltpu.SemaphoreType.DMA((rows * cols // LANES // 2,)),
        ],
        compiler_params=PARAMS,
        name="update",
    )(mine, order, normed, last_gain, last_bias, proj_out, gate_out)


def solution(mesh):
    grid_rows, grid_cols = mesh.shape["row"], mesh.shape["col"]
    split = (grid_rows // 2, 2)
    fine = jax.sharding.Mesh(
        mesh.devices.reshape(split + (grid_cols,)), ("high", "low", "col")
    )

    def fits(rows, cols, channels, hidden):
        devices = grid_rows * grid_cols
        inner = LANES // cols
        return (
            channels == LANES
            and hidden == LANES
            and inner * cols == LANES
            and inner & (inner - 1) == 0
            and inner * devices == hidden
            and rows == SOME
            and rows % (2 * inner) == 0
            and devices % SOME == 0
        )

    def call(*arrays):
        tokens, others, channels = arrays[0].shape
        hidden = arrays[8].shape[0]
        if fits(tokens // grid_rows, others // grid_cols, channels, hidden):
            return jax.shard_map(
                functools.partial(exchanged, split, grid_cols),
                mesh=fine,
                in_specs=(P(("high", "low"), "col", None),) + (P(),) * 9,
                out_specs=P(("high", "low"), "col", None),
                check_vma=False,
            )(*arrays)
        return jax.shard_map(
            gathered,
            mesh=mesh,
            in_specs=(P("row", "col", None),) + (P(),) * 9,
            out_specs=P("row", "col", None),
            check_vma=False,
        )(*arrays)

    return call
```

```python
import functools
import jax
import jax.numpy as jnp
from jax import lax
from jax.experimental import pallas as pl
from jax.experimental.pallas import tpu as pltpu
from jax.sharding import PartitionSpec as P

LANES = 128
SOME = 16
F32 = jnp.float32
BF16 = jnp.bfloat16


def broadcast(value, axis, source):
    kept = jnp.where(lax.axis_index(axis) == source, value, 0).astype(value.dtype)
    return lax.psum(kept, axis)


def layer_norm(values, gain, bias):
    mean = jnp.mean(values, axis=-1, keepdims=True)
    centered = values - mean
    variance = jnp.mean(centered * centered, axis=-1, keepdims=True)
    return centered * lax.rsqrt(variance + 1e-05) * gain + bias


def token_valid(chain_lengths, tokens_idx, slots):
    chain = tokens_idx // slots
    position = tokens_idx % slots
    chain_ids = jnp.arange(chain_lengths.shape[0], dtype=jnp.int32)
    length_of = jnp.sum(
        jnp.where(chain[:, None] == chain_ids[None, :], chain_lengths[None, :], 0), axis=1
    )
    return (position < length_of).astype(jnp.float32)


def gathered(
    pair,
    chain_lengths,
    norm_in_gain,
    norm_in_bias,
    proj_in,
    gate_in,
    norm_out_gain,
    norm_out_bias,
    proj_out,
    gate_out,
):
    row_count = pair.shape[0]
    col_count = pair.shape[1]
    channels = pair.shape[2]
    hidden = proj_out.shape[0]
    row_index = lax.axis_index("row")
    col_index = lax.axis_index("col")
    slots = row_count * lax.axis_size("row") // chain_lengths.shape[0]
    valid_rows = token_valid(
        chain_lengths, row_index * row_count + jnp.arange(row_count, dtype=jnp.int32), slots
    )
    valid_cols = token_valid(
        chain_lengths, col_index * col_count + jnp.arange(col_count, dtype=jnp.int32), slots
    )
    pair_mask = valid_rows[:, None] * valid_cols[None, :]
    normed = layer_norm(pair.astype(jnp.float32), norm_in_gain, norm_in_bias).astype(jnp.bfloat16)
    flat = normed.reshape(-1, channels)
    values = jnp.dot(flat, proj_in, preferred_element_type=jnp.float32)
    gates = jnp.dot(flat, gate_in, preferred_element_type=jnp.float32)
    mixed = (jax.nn.sigmoid(gates) * values).reshape(row_count, col_count, 2 * hidden) * pair_mask[
        :, :, None
    ]
    left_tile = mixed[:, :, :hidden].astype(jnp.bfloat16)
    right_tile = mixed[:, :, hidden:].astype(jnp.bfloat16)
    ratio = lax.axis_size("row") // lax.axis_size("col")
    right_full = lax.all_gather(right_tile, "col", axis=1, tiled=True)
    received = []
    for part in range(ratio):
        received.append(broadcast(right_full, "row", col_index * ratio + part))
    right_mine = jnp.concatenate(received, axis=0)
    triangle = jnp.einsum(
        "ikh,jkh->ijh",
        lax.all_gather(left_tile, "col", axis=1, tiled=True),
        right_mine,
        preferred_element_type=jnp.float32,
    )
    tri_normed = layer_norm(triangle, norm_out_gain, norm_out_bias).astype(jnp.bfloat16)
    projected = jnp.dot(
        tri_normed.reshape(-1, hidden), proj_out, preferred_element_type=jnp.float32
    )
    gate = jax.nn.sigmoid(jnp.dot(flat, gate_out, preferred_element_type=jnp.float32))
    return (gate * projected).astype(jnp.bfloat16).reshape(row_count, col_count, channels)


def iota2(shape):
    return (
        lax.broadcasted_iota(jnp.int32, shape, 0),
        lax.broadcasted_iota(jnp.int32, shape, 1),
    )


def one_hot(condition):
    return jnp.where(condition, 1.0, 0.0).astype(BF16)


def dot(a, b, a_dim=1, b_dim=0):
    return lax.dot_general(a, b, (((a_dim,), (b_dim,)), ((), ())), preferred_element_type=F32)


def over(value, size):
    if size & (size - 1):
        return value // size
    return lax.shift_right_logical(value, jnp.full_like(value, size.bit_length() - 1))


def rest(value, size):
    return value % size if size & (size - 1) else value & (size - 1)


def over(value, size):
    if size & (size - 1):
        return value // size
    return lax.shift_right_logical(value, jnp.full_like(value, size.bit_length() - 1))


def rest(value, size):
    return value % size if size & (size - 1) else value & (size - 1)


def fetch(sources, targets, sems):
    copies = [
        pltpu.make_async_copy(source, target, sems.at[n])
        for n, (source, target) in enumerate(zip(sources, targets))
    ]
    for copy in copies:
        copy.start()
    return copies


def sigmoid(halved):
    return 0.5 + 0.5 * jnp.tanh(halved)


def exchange_blocks(arrays, cols):
    lane = over(lax.broadcasted_iota(jnp.int32, (1, LANES), 1), cols)
    arrays, step = list(arrays), 1
    while step < len(arrays):
        upper = lane & step != 0
        for n in range(len(arrays)):
            if n // step % 2 == 0:
                a, b = arrays[n], arrays[n + step]
                arrays[n] = jnp.where(upper, pltpu.roll(b, step * cols, 1), a)
                arrays[n + step] = jnp.where(upper, b, pltpu.roll(a, LANES - step * cols, 1))
        step *= 2
    return arrays


def order_kernel(order_ref):
    out, source = iota2(order_ref.shape)
    order_ref[...] = one_hot(
        (over(out, SOME) == rest(source, SOME)) & (rest(out, SOME) == over(source, SOME))
    )


def column(row):
    a, b = iota2((LANES, LANES))
    return jnp.sum(jnp.where(a == b, row, 0.0), axis=1, keepdims=True)


def cell_mask(lengths, slots, rows, cols):
    cell = lax.broadcasted_iota(jnp.int32, (1, rows * cols), 1)

    def valid(token):
        length = jnp.zeros_like(token)
        for chain in range(lengths.shape[1]):
            length = jnp.where(
                over(token, slots) == chain, lengths[:, chain : chain + 1], length
            )
        return rest(token, slots) < length

    row_ok = valid(lax.axis_index(("high", "low")) * rows + over(cell, cols))
    col_ok = valid(lax.axis_index("col") * cols + rest(cell, cols))
    return jnp.where(row_ok & col_ok, 1.0, 0.0)


def mix_kernel(
    slots,
    order_ref,
    chain_ref,
    gain_ref,
    bias_ref,
    last_gain_ref,
    last_bias_ref,
    proj_ref,
    gate_ref,
    pair_ref,
    sent_ref,
    normed_ref,
    last_gain_out,
    last_bias_out,
):
    rows, cols, channels = pair_ref.shape
    hidden = proj_ref.shape[1] // 2
    cells = rows * cols
    inner = LANES // cols
    groups = rows // inner
    chunks = sent_ref.shape[0]
    flat = pair_ref[...].reshape(cells, channels).astype(F32)
    normed = layer_norm(flat, gain_ref[...], bias_ref[...]).astype(BF16)
    normed_ref[...] = normed
    last_gain_out[...] = last_gain_ref[...]
    last_bias_out[...] = last_bias_ref[...]
    weights = jnp.concatenate([proj_ref[...], gate_ref[...] * 0.5], axis=1)
    products = dot(weights, normed, 0, 1)
    values, gates = products[: 2 * hidden], products[2 * hidden :]
    mask = cell_mask(chain_ref[...], slots, rows, cols)
    mixed = (sigmoid(gates) * values * mask).astype(BF16)

    by_row = []
    for side in range(2):
        lines = []
        for g in range(groups):
            lines += exchange_blocks(
                [
                    mixed[
                        side * hidden + n * chunks : side * hidden + (n + 1) * chunks,
                        g * LANES : (g + 1) * LANES,
                    ]
                    for n in range(inner)
                ],
                cols,
            )
        by_row.append(lines)
    blocks = [(part, side) for part in range(chunks // SOME) for side in range(2)]
    stacks = [
        jnp.concatenate(
            [line[part * SOME : (part + 1) * SOME] for line in by_row[side]], axis=0
        )
        for part, side in blocks
    ]
    moved = dot(order_ref[...], jnp.concatenate(stacks, axis=1)).astype(BF16)
    for n, (part, side) in enumerate(blocks):
        sent_ref[part * SOME : (part + 1) * SOME, side * rows : (side + 1) * rows] = moved[
            :, n * LANES : (n + 1) * LANES
        ].reshape(SOME, rows, LANES)


def triangle_kernel(split, grid_cols, rows, cols, got_ref, sent_ref):
    inner = LANES // cols

    def place(r, c):
        z, y = r // split[1], r % split[1]
        return (c * split[1] + y) * split[0] + z

    def side(which):
        return jnp.concatenate(
            [
                jnp.concatenate(
                    [
                        got_ref[place(r, c), which * rows : (which + 1) * rows]
                        for r in range(split[0] * split[1])
                    ],
                    axis=0,
                )
                for c in range(grid_cols)
            ],
            axis=1,
        )

    left, right = side(0), side(1)
    lane = lax.broadcasted_iota(jnp.int32, (1, grid_cols * LANES), 1)
    by_channel = [right * one_hot(over(rest(lane, LANES), cols) == n) for n in range(inner)]
    right_by = jnp.concatenate(
        [
            by_channel[n][c * cols : (c + 1) * cols]
            for c in range(grid_cols)
            for n in range(inner)
        ],
        axis=0,
    )
    sums = dot(left, right_by, 1, 1).astype(BF16)
    for c in range(grid_cols):
        for r in range(split[0] * split[1]):
            sent_ref[place(r, c)] = sums[r * rows : (r + 1) * rows, c * LANES : (c + 1) * LANES]


def update_kernel(
    got_ref,
    order_ref,
    normed_ref,
    gain_ref,
    bias_ref,
    proj_ref,
    gate_ref,
    out_hbm,
    out_ref,
    out_sems,
):
    rows, cols, channels = out_ref.shape
    chunks = got_ref.shape[0]
    inner = LANES // cols
    groups = rows // inner
    got = jnp.concatenate(
        [
            got_ref[part * SOME : (part + 1) * SOME].reshape(SOME * rows, LANES)
            for part in range(chunks // SOME)
        ],
        axis=1,
    )
    moved = dot(order_ref[...], got).astype(BF16)
    parts = [moved[:, part * LANES : (part + 1) * LANES] for part in range(chunks // SOME)]
    lines = [
        jnp.concatenate([part[row * SOME : (row + 1) * SOME] for part in parts], axis=0)
        for row in range(rows)
    ]
    gain, bias = column(gain_ref[...]), column(bias_ref[...])
    opened = sigmoid(dot(normed_ref[...], gate_ref[...] * 0.5))
    results = []
    for g in range(groups):
        values = jnp.concatenate(
            exchange_blocks(lines[g * inner : (g + 1) * inner], cols), axis=0
        ).astype(F32)
        mean = jnp.mean(values, axis=0, keepdims=True)
        centered = values - mean
        variance = jnp.mean(centered * centered, axis=0, keepdims=True)
        tri_normed = (centered * lax.rsqrt(variance + 1e-05) * gain + bias).astype(BF16)
        projected = dot(tri_normed, proj_ref[...], 0, 0)
        update = (opened[g * LANES : (g + 1) * LANES] * projected).astype(BF16)
        out_ref[g * inner : (g + 1) * inner] = update.reshape(inner, cols, channels)
        if g % 2:
            here = pl.ds((g - 1) * inner, 2 * inner)
            results.append(
                pltpu.make_async_copy(out_ref.at[here], out_hbm.at[here], out_sems.at[g // 2])
            )
            results[-1].start()
    for copy in results:
        copy.wait()


VMEM = pl.BlockSpec(memory_space=pltpu.VMEM)
HBM = pl.BlockSpec(memory_space=pltpu.HBM)
PARAMS = pltpu.CompilerParams(vmem_limit_bytes=32 * 1024 * 1024)


def exchanged(
    split,
    grid_cols,
    pair,
    chain_lengths,
    norm_in_gain,
    norm_in_bias,
    proj_in,
    gate_in,
    norm_out_gain,
    norm_out_bias,
    proj_out,
    gate_out,
):
    rows, cols, channels = pair.shape
    hidden = proj_out.shape[0]
    grid_rows = split[0] * split[1]
    devices = grid_rows * grid_cols
    slots = rows * grid_rows // chain_lengths.shape[0]
    order = pl.pallas_call(
        order_kernel,
        out_shape=jax.ShapeDtypeStruct((SOME * SOME, SOME * SOME), BF16),
        out_specs=VMEM,
        compiler_params=PARAMS,
        cost_estimate=pl.CostEstimate(flops=10**9, bytes_accessed=10**6, transcendentals=0),
        name="order",
    )()
    row = jax.ShapeDtypeStruct((1, LANES), F32)
    sent, normed, last_gain, last_bias = pl.pallas_call(
        functools.partial(mix_kernel, slots),
        out_shape=(
            jax.ShapeDtypeStruct((devices, 2 * rows, LANES), BF16),
            jax.ShapeDtypeStruct((rows * cols, channels), BF16),
            row,
            row,
        ),
        in_specs=[VMEM] * 9,
        out_specs=[VMEM] * 4,
        compiler_params=PARAMS,
        name="mix",
    )(
        order,
        chain_lengths.reshape(1, -1),
        norm_in_gain.reshape(1, LANES),
        norm_in_bias.reshape(1, LANES),
        norm_out_gain.reshape(1, LANES),
        norm_out_bias.reshape(1, LANES),
        proj_in,
        gate_in,
        pair,
    )
    axes = ("col", "low", "high")
    got = lax.all_to_all(sent, axes, 0, 0, tiled=True)
    sums = pl.pallas_call(
        functools.partial(triangle_kernel, split, grid_cols, rows, cols),
        out_shape=jax.ShapeDtypeStruct((devices, rows, LANES), BF16),
        in_specs=[VMEM],
        out_specs=VMEM,
        compiler_params=PARAMS,
        name="triangle",
    )(got)
    mine = lax.all_to_all(sums, axes, 0, 0, tiled=True)
    return pl.pallas_call(
        update_kernel,
        out_shape=jax.ShapeDtypeStruct((rows, cols, channels), BF16),
        in_specs=[VMEM] * 7,
        out_specs=HBM,
        scratch_shapes=[
            pltpu.VMEM((rows, cols, channels), BF16),
            pltpu.SemaphoreType.DMA((rows * cols // LANES // 2,)),
        ],
        compiler_params=PARAMS,
        name="update",
    )(mine, order, normed, last_gain, last_bias, proj_out, gate_out)


def solution(mesh):
    grid_rows, grid_cols = mesh.shape["row"], mesh.shape["col"]
    split = (grid_rows // 2, 2)
    fine = jax.sharding.Mesh(
        mesh.devices.reshape(split + (grid_cols,)), ("high", "low", "col")
    )

    def fits(rows, cols, channels, hidden):
        devices = grid_rows * grid_cols
        inner = LANES // cols
        return (
            channels == LANES
            and hidden == LANES
            and inner * cols == LANES
            and inner & (inner - 1) == 0
            and inner * devices == hidden
            and rows == SOME
            and rows % (2 * inner) == 0
            and devices % SOME == 0
        )

    def call(*arrays):
        tokens, others, channels = arrays[0].shape
        hidden = arrays[8].shape[0]
        if fits(tokens // grid_rows, others // grid_cols, channels, hidden):
            return jax.shard_map(
                functools.partial(exchanged, split, grid_cols),
                mesh=fine,
                in_specs=(P(("high", "low"), "col", None),) + (P(),) * 9,
                out_specs=P(("high", "low"), "col", None),
                check_vma=False,
            )(*arrays)
        return jax.shard_map(
            gathered,
            mesh=mesh,
            in_specs=(P("row", "col", None),) + (P(),) * 9,
            out_specs=P("row", "col", None),
            check_vma=False,
        )(*arrays)

    return call
```

```python
import functools
import jax
import jax.numpy as jnp
from jax import lax
from jax.experimental import pallas as pl
from jax.experimental.pallas import tpu as pltpu
from jax.sharding import PartitionSpec as P

LANES = 128
SOME = 16
F32 = jnp.float32
BF16 = jnp.bfloat16


def broadcast(value, axis, source):
    kept = jnp.where(lax.axis_index(axis) == source, value, 0).astype(value.dtype)
    return lax.psum(kept, axis)


def layer_norm(values, gain, bias):
    mean = jnp.mean(values, axis=-1, keepdims=True)
    centered = values - mean
    variance = jnp.mean(centered * centered, axis=-1, keepdims=True)
    return centered * lax.rsqrt(variance + 1e-05) * gain + bias


def token_valid(chain_lengths, tokens_idx, slots):
    chain = tokens_idx // slots
    position = tokens_idx % slots
    chain_ids = jnp.arange(chain_lengths.shape[0], dtype=jnp.int32)
    length_of = jnp.sum(
        jnp.where(chain[:, None] == chain_ids[None, :], chain_lengths[None, :], 0), axis=1
    )
    return (position < length_of).astype(jnp.float32)


def gathered(
    pair,
    chain_lengths,
    norm_in_gain,
    norm_in_bias,
    proj_in,
    gate_in,
    norm_out_gain,
    norm_out_bias,
    proj_out,
    gate_out,
):
    row_count = pair.shape[0]
    col_count = pair.shape[1]
    channels = pair.shape[2]
    hidden = proj_out.shape[0]
    row_index = lax.axis_index("row")
    col_index = lax.axis_index("col")
    slots = row_count * lax.axis_size("row") // chain_lengths.shape[0]
    valid_rows = token_valid(
        chain_lengths, row_index * row_count + jnp.arange(row_count, dtype=jnp.int32), slots
    )
    valid_cols = token_valid(
        chain_lengths, col_index * col_count + jnp.arange(col_count, dtype=jnp.int32), slots
    )
    pair_mask = valid_rows[:, None] * valid_cols[None, :]
    normed = layer_norm(pair.astype(jnp.float32), norm_in_gain, norm_in_bias).astype(jnp.bfloat16)
    flat = normed.reshape(-1, channels)
    values = jnp.dot(flat, proj_in, preferred_element_type=jnp.float32)
    gates = jnp.dot(flat, gate_in, preferred_element_type=jnp.float32)
    mixed = (jax.nn.sigmoid(gates) * values).reshape(row_count, col_count, 2 * hidden) * pair_mask[
        :, :, None
    ]
    left_tile = mixed[:, :, :hidden].astype(jnp.bfloat16)
    right_tile = mixed[:, :, hidden:].astype(jnp.bfloat16)
    ratio = lax.axis_size("row") // lax.axis_size("col")
    right_full = lax.all_gather(right_tile, "col", axis=1, tiled=True)
    received = []
    for part in range(ratio):
        received.append(broadcast(right_full, "row", col_index * ratio + part))
    right_mine = jnp.concatenate(received, axis=0)
    triangle = jnp.einsum(
        "ikh,jkh->ijh",
        lax.all_gather(left_tile, "col", axis=1, tiled=True),
        right_mine,
        preferred_element_type=jnp.float32,
    )
    tri_normed = layer_norm(triangle, norm_out_gain, norm_out_bias).astype(jnp.bfloat16)
    projected = jnp.dot(
        tri_normed.reshape(-1, hidden), proj_out, preferred_element_type=jnp.float32
    )
    gate = jax.nn.sigmoid(jnp.dot(flat, gate_out, preferred_element_type=jnp.float32))
    return (gate * projected).astype(jnp.bfloat16).reshape(row_count, col_count, channels)


def iota2(shape):
    return (
        lax.broadcasted_iota(jnp.int32, shape, 0),
        lax.broadcasted_iota(jnp.int32, shape, 1),
    )


def one_hot(condition):
    return jnp.where(condition, 1.0, 0.0).astype(BF16)


def dot(a, b, a_dim=1, b_dim=0):
    return lax.dot_general(a, b, (((a_dim,), (b_dim,)), ((), ())), preferred_element_type=F32)


def over(value, size):
    if size & (size - 1):
        return value // size
    return lax.shift_right_logical(value, jnp.full_like(value, size.bit_length() - 1))


def rest(value, size):
    return value % size if size & (size - 1) else value & (size - 1)


def over(value, size):
    if size & (size - 1):
        return value // size
    return lax.shift_right_logical(value, jnp.full_like(value, size.bit_length() - 1))


def rest(value, size):
    return value % size if size & (size - 1) else value & (size - 1)


def fetch(sources, targets, sems):
    copies = [
        pltpu.make_async_copy(source, target, sems.at[n])
        for n, (source, target) in enumerate(zip(sources, targets))
    ]
    for copy in copies:
        copy.start()
    return copies


def sigmoid(halved):
    return 0.5 + 0.5 * jnp.tanh(halved)


def exchange_blocks(arrays, cols):
    lane = over(lax.broadcasted_iota(jnp.int32, (1, LANES), 1), cols)
    arrays, step = list(arrays), 1
    while step < len(arrays):
        upper = lane & step != 0
        for n in range(len(arrays)):
            if n // step % 2 == 0:
                a, b = arrays[n], arrays[n + step]
                arrays[n] = jnp.where(upper, pltpu.roll(b, step * cols, 1), a)
                arrays[n + step] = jnp.where(upper, b, pltpu.roll(a, LANES - step * cols, 1))
        step *= 2
    return arrays


def order_kernel(order_ref):
    out, source = iota2(order_ref.shape)
    order_ref[...] = one_hot(
        (over(out, SOME) == rest(source, SOME)) & (rest(out, SOME) == over(source, SOME))
    )


def column(row):
    a, b = iota2((LANES, LANES))
    return jnp.sum(jnp.where(a == b, row, 0.0), axis=1, keepdims=True)


def cell_mask(lengths, slots, rows, cols):
    cell = lax.broadcasted_iota(jnp.int32, (1, rows * cols), 1)

    def valid(token):
        length = jnp.zeros_like(token)
        for chain in range(lengths.shape[1]):
            length = jnp.where(
                over(token, slots) == chain, lengths[:, chain : chain + 1], length
            )
        return rest(token, slots) < length

    row_ok = valid(lax.axis_index(("high", "low")) * rows + over(cell, cols))
    col_ok = valid(lax.axis_index("col") * cols + rest(cell, cols))
    return jnp.where(row_ok & col_ok, 1.0, 0.0)


def mix_kernel(
    slots,
    order_ref,
    chain_ref,
    gain_ref,
    bias_ref,
    last_gain_ref,
    last_bias_ref,
    proj_ref,
    gate_ref,
    pair_ref,
    sent_ref,
    normed_ref,
    last_gain_out,
    last_bias_out,
):
    rows, cols, channels = pair_ref.shape
    hidden = proj_ref.shape[1] // 2
    cells = rows * cols
    inner = LANES // cols
    groups = rows // inner
    chunks = sent_ref.shape[0]
    flat = pair_ref[...].reshape(cells, channels).astype(F32)
    normed = layer_norm(flat, gain_ref[...], bias_ref[...]).astype(BF16)
    normed_ref[...] = normed
    last_gain_out[...] = last_gain_ref[...]
    last_bias_out[...] = last_bias_ref[...]
    weights = jnp.concatenate([proj_ref[...], gate_ref[...] * 0.5], axis=1)
    products = dot(weights, normed, 0, 1)
    values, gates = products[: 2 * hidden], products[2 * hidden :]
    mask = cell_mask(chain_ref[...], slots, rows, cols)
    mixed = (sigmoid(gates) * values * mask).astype(BF16)

    by_row = []
    for side in range(2):
        lines = []
        for g in range(groups):
            lines += exchange_blocks(
                [
                    mixed[
                        side * hidden + n * chunks : side * hidden + (n + 1) * chunks,
                        g * LANES : (g + 1) * LANES,
                    ]
                    for n in range(inner)
                ],
                cols,
            )
        by_row.append(lines)
    blocks = [(part, side) for part in range(chunks // SOME) for side in range(2)]
    stacks = [
        jnp.concatenate(
            [line[part * SOME : (part + 1) * SOME] for line in by_row[side]], axis=0
        )
        for part, side in blocks
    ]
    moved = dot(order_ref[...], jnp.concatenate(stacks, axis=1)).astype(BF16)
    for n, (part, side) in enumerate(blocks):
        sent_ref[part * SOME : (part + 1) * SOME, side * rows : (side + 1) * rows] = moved[
            :, n * LANES : (n + 1) * LANES
        ].reshape(SOME, rows, LANES)


def triangle_kernel(split, grid_cols, rows, cols, got_ref, sent_ref):
    inner = LANES // cols

    def place(r, c):
        z, y = r // split[1], r % split[1]
        return (c * split[1] + y) * split[0] + z

    def side(which):
        return jnp.concatenate(
            [
                jnp.concatenate(
                    [
                        got_ref[place(r, c), which * rows : (which + 1) * rows]
                        for r in range(split[0] * split[1])
                    ],
                    axis=0,
                )
                for c in range(grid_cols)
            ],
            axis=1,
        )

    left, right = side(0), side(1)
    lane = lax.broadcasted_iota(jnp.int32, (1, grid_cols * LANES), 1)
    by_channel = [right * one_hot(over(rest(lane, LANES), cols) == n) for n in range(inner)]
    right_by = jnp.concatenate(
        [
            by_channel[n][c * cols : (c + 1) * cols]
            for c in range(grid_cols)
            for n in range(inner)
        ],
        axis=0,
    )
    sums = dot(left, right_by, 1, 1).astype(BF16)
    for c in range(grid_cols):
        for r in range(split[0] * split[1]):
            sent_ref[place(r, c)] = sums[r * rows : (r + 1) * rows, c * LANES : (c + 1) * LANES]


def update_kernel(
    got_ref,
    order_ref,
    normed_ref,
    gain_ref,
    bias_ref,
    proj_ref,
    gate_ref,
    out_hbm,
    out_ref,
    out_sems,
):
    rows, cols, channels = out_ref.shape
    chunks = got_ref.shape[0]
    inner = LANES // cols
    groups = rows // inner
    order = order_ref[...]
    parts = [
        dot(order, got_ref[part * SOME : (part + 1) * SOME].reshape(SOME * rows, LANES)).astype(BF16)
        for part in range(chunks // SOME)
    ]
    lines = [
        jnp.concatenate([part[row * SOME : (row + 1) * SOME] for part in parts], axis=0)
        for row in range(rows)
    ]
    gain, bias = column(gain_ref[...]), column(bias_ref[...])
    opened = sigmoid(dot(normed_ref[...], gate_ref[...] * 0.5))
    results = []
    for g in range(groups):
        values = jnp.concatenate(
            exchange_blocks(lines[g * inner : (g + 1) * inner], cols), axis=0
        ).astype(F32)
        mean = jnp.mean(values, axis=0, keepdims=True)
        centered = values - mean
        variance = jnp.mean(centered * centered, axis=0, keepdims=True)
        tri_normed = (centered * lax.rsqrt(variance + 1e-05) * gain + bias).astype(BF16)
        projected = dot(tri_normed, proj_ref[...], 0, 0)
        update = (opened[g * LANES : (g + 1) * LANES] * projected).astype(BF16)
        out_ref[g * inner : (g + 1) * inner] = update.reshape(inner, cols, channels)
        if g % 2:
            here = pl.ds((g - 1) * inner, 2 * inner)
            results.append(
                pltpu.make_async_copy(out_ref.at[here], out_hbm.at[here], out_sems.at[g // 2])
            )
            results[-1].start()
    for copy in results:
        copy.wait()


VMEM = pl.BlockSpec(memory_space=pltpu.VMEM)
HBM = pl.BlockSpec(memory_space=pltpu.HBM)
PARAMS = pltpu.CompilerParams(vmem_limit_bytes=32 * 1024 * 1024)


def exchanged(
    split,
    grid_cols,
    pair,
    chain_lengths,
    norm_in_gain,
    norm_in_bias,
    proj_in,
    gate_in,
    norm_out_gain,
    norm_out_bias,
    proj_out,
    gate_out,
):
    rows, cols, channels = pair.shape
    hidden = proj_out.shape[0]
    grid_rows = split[0] * split[1]
    devices = grid_rows * grid_cols
    slots = rows * grid_rows // chain_lengths.shape[0]
    order = pl.pallas_call(
        order_kernel,
        out_shape=jax.ShapeDtypeStruct((SOME * SOME, SOME * SOME), BF16),
        out_specs=VMEM,
        compiler_params=PARAMS,
        cost_estimate=pl.CostEstimate(flops=10**9, bytes_accessed=10**6, transcendentals=0),
        name="order",
    )()
    row = jax.ShapeDtypeStruct((1, LANES), F32)
    sent, normed, last_gain, last_bias = pl.pallas_call(
        functools.partial(mix_kernel, slots),
        out_shape=(
            jax.ShapeDtypeStruct((devices, 2 * rows, LANES), BF16),
            jax.ShapeDtypeStruct((rows * cols, channels), BF16),
            row,
            row,
        ),
        in_specs=[VMEM] * 9,
        out_specs=[VMEM] * 4,
        compiler_params=PARAMS,
        name="mix",
    )(
        order,
        chain_lengths.reshape(1, -1),
        norm_in_gain.reshape(1, LANES),
        norm_in_bias.reshape(1, LANES),
        norm_out_gain.reshape(1, LANES),
        norm_out_bias.reshape(1, LANES),
        proj_in,
        gate_in,
        pair,
    )
    axes = ("col", "low", "high")
    got = lax.all_to_all(sent, axes, 0, 0, tiled=True)
    sums = pl.pallas_call(
        functools.partial(triangle_kernel, split, grid_cols, rows, cols),
        out_shape=jax.ShapeDtypeStruct((devices, rows, LANES), BF16),
        in_specs=[VMEM],
        out_specs=VMEM,
        compiler_params=PARAMS,
        name="triangle",
    )(got)
    mine = lax.all_to_all(sums, axes, 0, 0, tiled=True)
    return pl.pallas_call(
        update_kernel,
        out_shape=jax.ShapeDtypeStruct((rows, cols, channels), BF16),
        in_specs=[VMEM] * 7,
        out_specs=HBM,
        scratch_shapes=[
            pltpu.VMEM((rows, cols, channels), BF16),
            pltpu.SemaphoreType.DMA((rows * cols // LANES // 2,)),
        ],
        compiler_params=PARAMS,
        name="update",
    )(mine, order, normed, last_gain, last_bias, proj_out, gate_out)


def solution(mesh):
    grid_rows, grid_cols = mesh.shape["row"], mesh.shape["col"]
    split = (grid_rows // 2, 2)
    fine = jax.sharding.Mesh(
        mesh.devices.reshape(split + (grid_cols,)), ("high", "low", "col")
    )

    def fits(rows, cols, channels, hidden):
        devices = grid_rows * grid_cols
        inner = LANES // cols
        return (
            channels == LANES
            and hidden == LANES
            and inner * cols == LANES
            and inner & (inner - 1) == 0
            and inner * devices == hidden
            and rows == SOME
            and rows % (2 * inner) == 0
            and devices % SOME == 0
        )

    def call(*arrays):
        tokens, others, channels = arrays[0].shape
        hidden = arrays[8].shape[0]
        if fits(tokens // grid_rows, others // grid_cols, channels, hidden):
            return jax.shard_map(
                functools.partial(exchanged, split, grid_cols),
                mesh=fine,
                in_specs=(P(("high", "low"), "col", None),) + (P(),) * 9,
                out_specs=P(("high", "low"), "col", None),
                check_vma=False,
            )(*arrays)
        return jax.shard_map(
            gathered,
            mesh=mesh,
            in_specs=(P("row", "col", None),) + (P(),) * 9,
            out_specs=P("row", "col", None),
            check_vma=False,
        )(*arrays)

    return call
```

```python
import functools
import jax
import jax.numpy as jnp
from jax import lax
from jax.experimental import pallas as pl
from jax.experimental.pallas import tpu as pltpu
from jax.sharding import PartitionSpec as P

LANES = 128
SOME = 16
F32 = jnp.float32
BF16 = jnp.bfloat16


def broadcast(value, axis, source):
    kept = jnp.where(lax.axis_index(axis) == source, value, 0).astype(value.dtype)
    return lax.psum(kept, axis)


def layer_norm(values, gain, bias):
    mean = jnp.mean(values, axis=-1, keepdims=True)
    centered = values - mean
    variance = jnp.mean(centered * centered, axis=-1, keepdims=True)
    return centered * lax.rsqrt(variance + 1e-05) * gain + bias


def token_valid(chain_lengths, tokens_idx, slots):
    chain = tokens_idx // slots
    position = tokens_idx % slots
    chain_ids = jnp.arange(chain_lengths.shape[0], dtype=jnp.int32)
    length_of = jnp.sum(
        jnp.where(chain[:, None] == chain_ids[None, :], chain_lengths[None, :], 0), axis=1
    )
    return (position < length_of).astype(jnp.float32)


def gathered(
    pair,
    chain_lengths,
    norm_in_gain,
    norm_in_bias,
    proj_in,
    gate_in,
    norm_out_gain,
    norm_out_bias,
    proj_out,
    gate_out,
):
    row_count = pair.shape[0]
    col_count = pair.shape[1]
    channels = pair.shape[2]
    hidden = proj_out.shape[0]
    row_index = lax.axis_index("row")
    col_index = lax.axis_index("col")
    slots = row_count * lax.axis_size("row") // chain_lengths.shape[0]
    valid_rows = token_valid(
        chain_lengths, row_index * row_count + jnp.arange(row_count, dtype=jnp.int32), slots
    )
    valid_cols = token_valid(
        chain_lengths, col_index * col_count + jnp.arange(col_count, dtype=jnp.int32), slots
    )
    pair_mask = valid_rows[:, None] * valid_cols[None, :]
    normed = layer_norm(pair.astype(jnp.float32), norm_in_gain, norm_in_bias).astype(jnp.bfloat16)
    flat = normed.reshape(-1, channels)
    values = jnp.dot(flat, proj_in, preferred_element_type=jnp.float32)
    gates = jnp.dot(flat, gate_in, preferred_element_type=jnp.float32)
    mixed = (jax.nn.sigmoid(gates) * values).reshape(row_count, col_count, 2 * hidden) * pair_mask[
        :, :, None
    ]
    left_tile = mixed[:, :, :hidden].astype(jnp.bfloat16)
    right_tile = mixed[:, :, hidden:].astype(jnp.bfloat16)
    ratio = lax.axis_size("row") // lax.axis_size("col")
    right_full = lax.all_gather(right_tile, "col", axis=1, tiled=True)
    received = []
    for part in range(ratio):
        received.append(broadcast(right_full, "row", col_index * ratio + part))
    right_mine = jnp.concatenate(received, axis=0)
    triangle = jnp.einsum(
        "ikh,jkh->ijh",
        lax.all_gather(left_tile, "col", axis=1, tiled=True),
        right_mine,
        preferred_element_type=jnp.float32,
    )
    tri_normed = layer_norm(triangle, norm_out_gain, norm_out_bias).astype(jnp.bfloat16)
    projected = jnp.dot(
        tri_normed.reshape(-1, hidden), proj_out, preferred_element_type=jnp.float32
    )
    gate = jax.nn.sigmoid(jnp.dot(flat, gate_out, preferred_element_type=jnp.float32))
    return (gate * projected).astype(jnp.bfloat16).reshape(row_count, col_count, channels)


def iota2(shape):
    return (
        lax.broadcasted_iota(jnp.int32, shape, 0),
        lax.broadcasted_iota(jnp.int32, shape, 1),
    )


def one_hot(condition):
    return jnp.where(condition, 1.0, 0.0).astype(BF16)


def dot(a, b, a_dim=1, b_dim=0):
    return lax.dot_general(a, b, (((a_dim,), (b_dim,)), ((), ())), preferred_element_type=F32)


def over(value, size):
    if size & (size - 1):
        return value // size
    return lax.shift_right_logical(value, jnp.full_like(value, size.bit_length() - 1))


def rest(value, size):
    return value % size if size & (size - 1) else value & (size - 1)


def over(value, size):
    if size & (size - 1):
        return value // size
    return lax.shift_right_logical(value, jnp.full_like(value, size.bit_length() - 1))


def rest(value, size):
    return value % size if size & (size - 1) else value & (size - 1)


def fetch(sources, targets, sems):
    copies = [
        pltpu.make_async_copy(source, target, sems.at[n])
        for n, (source, target) in enumerate(zip(sources, targets))
    ]
    for copy in copies:
        copy.start()
    return copies


def sigmoid(halved):
    return 0.5 + 0.5 * jnp.tanh(halved)


def exchange_blocks(arrays, cols):
    lane = over(lax.broadcasted_iota(jnp.int32, (1, LANES), 1), cols)
    arrays, step = list(arrays), 1
    while step < len(arrays):
        upper = lane & step != 0
        for n in range(len(arrays)):
            if n // step % 2 == 0:
                a, b = arrays[n], arrays[n + step]
                arrays[n] = jnp.where(upper, pltpu.roll(b, step * cols, 1), a)
                arrays[n + step] = jnp.where(upper, b, pltpu.roll(a, LANES - step * cols, 1))
        step *= 2
    return arrays


def order_kernel(order_ref):
    out, source = iota2(order_ref.shape)
    order_ref[...] = one_hot(
        (over(out, SOME) == rest(source, SOME)) & (rest(out, SOME) == over(source, SOME))
    )


def column(row):
    a, b = iota2((LANES, LANES))
    return jnp.sum(jnp.where(a == b, row, 0.0), axis=1, keepdims=True)


def cell_mask(lengths, slots, rows, cols):
    cell = lax.broadcasted_iota(jnp.int32, (1, rows * cols), 1)

    def valid(token):
        length = jnp.zeros_like(token)
        for chain in range(lengths.shape[1]):
            length = jnp.where(
                over(token, slots) == chain, lengths[:, chain : chain + 1], length
            )
        return rest(token, slots) < length

    row_ok = valid(lax.axis_index(("high", "low")) * rows + over(cell, cols))
    col_ok = valid(lax.axis_index("col") * cols + rest(cell, cols))
    return jnp.where(row_ok & col_ok, 1.0, 0.0)


def mix_kernel(
    slots,
    order_ref,
    chain_ref,
    pair_ref,
    gain_ref,
    bias_ref,
    proj_ref,
    gate_ref,
    last_gain_ref,
    last_bias_ref,
    sent_ref,
    normed_ref,
    last_gain_out,
    last_bias_out,
):
    rows, cols, channels = pair_ref.shape
    hidden = proj_ref.shape[1] // 2
    cells = rows * cols
    inner = LANES // cols
    groups = rows // inner
    chunks = sent_ref.shape[0]
    flat = pair_ref[...].reshape(cells, channels).astype(F32)
    normed = layer_norm(flat, gain_ref[...], bias_ref[...]).astype(BF16)
    normed_ref[...] = normed
    for source, target in ((last_gain_ref, last_gain_out), (last_bias_ref, last_bias_out)):
        target[...] = jnp.broadcast_to(column(source[...]), target.shape)

    weights = jnp.concatenate([proj_ref[...], gate_ref[...] * 0.5], axis=1)
    products = dot(weights, normed, 0, 1)
    values, gates = products[: 2 * hidden], products[2 * hidden :]
    mask = cell_mask(chain_ref[...], slots, rows, cols)
    mixed = (sigmoid(gates) * values * mask).astype(BF16)

    by_row = []
    for side in range(2):
        lines = []
        for g in range(groups):
            lines += exchange_blocks(
                [
                    mixed[
                        side * hidden + n * chunks : side * hidden + (n + 1) * chunks,
                        g * LANES : (g + 1) * LANES,
                    ]
                    for n in range(inner)
                ],
                cols,
            )
        by_row.append(lines)
    blocks = [(part, side) for part in range(chunks // SOME) for side in range(2)]
    stacks = [
        jnp.concatenate(
            [line[part * SOME : (part + 1) * SOME] for line in by_row[side]], axis=0
        )
        for part, side in blocks
    ]
    moved = dot(order_ref[...], jnp.concatenate(stacks, axis=1)).astype(BF16)
    for n, (part, side) in enumerate(blocks):
        sent_ref[part * SOME : (part + 1) * SOME, side * rows : (side + 1) * rows] = moved[
            :, n * LANES : (n + 1) * LANES
        ].reshape(SOME, rows, LANES)


def triangle_kernel(split, grid_cols, rows, cols, got_ref, sent_ref):
    inner = LANES // cols

    def place(r, c):
        z, y = r // split[1], r % split[1]
        return (c * split[1] + y) * split[0] + z

    def side(which):
        return jnp.concatenate(
            [
                jnp.concatenate(
                    [
                        got_ref[place(r, c), which * rows : (which + 1) * rows]
                        for r in range(split[0] * split[1])
                    ],
                    axis=0,
                )
                for c in range(grid_cols)
            ],
            axis=1,
        )

    left, right = side(0), side(1)
    lane = lax.broadcasted_iota(jnp.int32, (1, grid_cols * LANES), 1)
    by_channel = [right * one_hot(over(rest(lane, LANES), cols) == n) for n in range(inner)]
    right_by = jnp.concatenate(
        [
            by_channel[n][c * cols : (c + 1) * cols]
            for c in range(grid_cols)
            for n in range(inner)
        ],
        axis=0,
    )
    sums = dot(left, right_by, 1, 1).astype(BF16)
    for c in range(grid_cols):
        for r in range(split[0] * split[1]):
            sent_ref[place(r, c)] = sums[r * rows : (r + 1) * rows, c * LANES : (c + 1) * LANES]


def update_kernel(
    got_ref,
    order_ref,
    normed_ref,
    gain_ref,
    bias_ref,
    proj_ref,
    gate_ref,
    out_hbm,
    out_ref,
    out_sems,
):
    rows, cols, channels = out_ref.shape
    chunks = got_ref.shape[0]
    inner = LANES // cols
    groups = rows // inner
    order = order_ref[...]
    parts = [
        dot(order, got_ref[part * SOME : (part + 1) * SOME].reshape(SOME * rows, LANES)).astype(BF16)
        for part in range(chunks // SOME)
    ]
    lines = [
        jnp.concatenate([part[row * SOME : (row + 1) * SOME] for part in parts], axis=0)
        for row in range(rows)
    ]
    gain, bias = gain_ref[...], bias_ref[...]
    opened = sigmoid(dot(normed_ref[...], gate_ref[...] * 0.5))
    results = []
    for g in range(groups):
        values = jnp.concatenate(
            exchange_blocks(lines[g * inner : (g + 1) * inner], cols), axis=0
        ).astype(F32)
        mean = jnp.mean(values, axis=0, keepdims=True)
        centered = values - mean
        variance = jnp.mean(centered * centered, axis=0, keepdims=True)
        tri_normed = (centered * lax.rsqrt(variance + 1e-05) * gain + bias).astype(BF16)
        projected = dot(tri_normed, proj_ref[...], 0, 0)
        update = (opened[g * LANES : (g + 1) * LANES] * projected).astype(BF16)
        out_ref[g * inner : (g + 1) * inner] = update.reshape(inner, cols, channels)
        if g % 2:
            here = pl.ds((g - 1) * inner, 2 * inner)
            results.append(
                pltpu.make_async_copy(out_ref.at[here], out_hbm.at[here], out_sems.at[g // 2])
            )
            results[-1].start()
    for copy in results:
        copy.wait()


VMEM = pl.BlockSpec(memory_space=pltpu.VMEM)
HBM = pl.BlockSpec(memory_space=pltpu.HBM)
PARAMS = pltpu.CompilerParams(vmem_limit_bytes=32 * 1024 * 1024)


def exchanged(
    split,
    grid_cols,
    pair,
    chain_lengths,
    norm_in_gain,
    norm_in_bias,
    proj_in,
    gate_in,
    norm_out_gain,
    norm_out_bias,
    proj_out,
    gate_out,
):
    rows, cols, channels = pair.shape
    hidden = proj_out.shape[0]
    grid_rows = split[0] * split[1]
    devices = grid_rows * grid_cols
    slots = rows * grid_rows // chain_lengths.shape[0]
    order = pl.pallas_call(
        order_kernel,
        out_shape=jax.ShapeDtypeStruct((SOME * SOME, SOME * SOME), BF16),
        out_specs=VMEM,
        compiler_params=PARAMS,
        cost_estimate=pl.CostEstimate(flops=10**9, bytes_accessed=10**6, transcendentals=0),
        name="order",
    )()
    square = jax.ShapeDtypeStruct((LANES, LANES), F32)
    sent, normed, last_gain, last_bias = pl.pallas_call(
        functools.partial(mix_kernel, slots),
        out_shape=(
            jax.ShapeDtypeStruct((devices, 2 * rows, LANES), BF16),
            jax.ShapeDtypeStruct((rows * cols, channels), BF16),
            square,
            square,
        ),
        in_specs=[VMEM] * 9,
        out_specs=[VMEM] * 4,
        compiler_params=PARAMS,
        name="mix",
    )(
        order,
        chain_lengths.reshape(1, -1),
        pair,
        norm_in_gain.reshape(1, LANES),
        norm_in_bias.reshape(1, LANES),
        proj_in,
        gate_in,
        norm_out_gain.reshape(1, LANES),
        norm_out_bias.reshape(1, LANES),
    )
    axes = ("col", "low", "high")
    got = lax.all_to_all(sent, axes, 0, 0, tiled=True)
    sums = pl.pallas_call(
        functools.partial(triangle_kernel, split, grid_cols, rows, cols),
        out_shape=jax.ShapeDtypeStruct((devices, rows, LANES), BF16),
        in_specs=[VMEM],
        out_specs=VMEM,
        compiler_params=PARAMS,
        name="triangle",
    )(got)
    mine = lax.all_to_all(sums, axes, 0, 0, tiled=True)
    return pl.pallas_call(
        update_kernel,
        out_shape=jax.ShapeDtypeStruct((rows, cols, channels), BF16),
        in_specs=[VMEM] * 7,
        out_specs=HBM,
        scratch_shapes=[
            pltpu.VMEM((rows, cols, channels), BF16),
            pltpu.SemaphoreType.DMA((rows * cols // LANES // 2,)),
        ],
        compiler_params=PARAMS,
        name="update",
    )(mine, order, normed, last_gain, last_bias, proj_out, gate_out)


def solution(mesh):
    grid_rows, grid_cols = mesh.shape["row"], mesh.shape["col"]
    split = (grid_rows // 2, 2)
    fine = jax.sharding.Mesh(
        mesh.devices.reshape(split + (grid_cols,)), ("high", "low", "col")
    )

    def fits(rows, cols, channels, hidden):
        devices = grid_rows * grid_cols
        inner = LANES // cols
        return (
            channels == LANES
            and hidden == LANES
            and inner * cols == LANES
            and inner & (inner - 1) == 0
            and inner * devices == hidden
            and rows == SOME
            and rows % (2 * inner) == 0
            and devices % SOME == 0
        )

    def call(*arrays):
        tokens, others, channels = arrays[0].shape
        hidden = arrays[8].shape[0]
        if fits(tokens // grid_rows, others // grid_cols, channels, hidden):
            return jax.shard_map(
                functools.partial(exchanged, split, grid_cols),
                mesh=fine,
                in_specs=(P(("high", "low"), "col", None),) + (P(),) * 9,
                out_specs=P(("high", "low"), "col", None),
                check_vma=False,
            )(*arrays)
        return jax.shard_map(
            gathered,
            mesh=mesh,
            in_specs=(P("row", "col", None),) + (P(),) * 9,
            out_specs=P("row", "col", None),
            check_vma=False,
        )(*arrays)

    return call
```
